32 devices in a mesh: img: 4 (over y, x), row: 8 (over z, core).
Axes of the slice: x: 2, y: 2, z: 4, core: 2. Of those that a mesh axis runs over, the one named last changes fastest.
Arguments:
- pixels: bfloat16 [8, 32, 64, 256], P('img', 'row'), may hold values from -6 to 6
- heights: int32 [8], P('img'), may hold values from 1 to 32, as said below
- timesteps: int32 [8], P('img'), may hold values from 0 to 999
- norm1_gain: bfloat16 [256], replicated, may hold values from 0.25 to 1.75
- norm1_bias: bfloat16 [256], replicated, may hold values from -1.75 to 1.75
- conv1_weight: bfloat16 [3, 3, 256, 256], replicated, may hold values from -0.125 to 0.125
- conv1_bias: bfloat16 [256], replicated, may hold values from -3 to 3
- time_weight: bfloat16 [1024, 512], replicated, may hold values from -0.1875 to 0.1875
- time_bias: bfloat16 [512], replicated, may hold values from -3 to 3
- norm2_gain: bfloat16 [256], replicated, may hold values from 0.25 to 1.75
- norm2_bias: bfloat16 [256], replicated, may hold values from -1.75 to 1.75
- conv2_weight: bfloat16 [3, 3, 256, 256], replicated, may hold values from -0.125 to 0.125
- conv2_bias: bfloat16 [256], replicated, may hold values from -3 to 3
- norm3_gain: bfloat16 [256], replicated, may hold values from 0.25 to 1.75
- norm3_bias: bfloat16 [256], replicated, may hold values from -1.75 to 1.75
- qkv_weight: bfloat16 [256, 768], replicated, may hold values from -0.375 to 0.375
- qv_bias: bfloat16 [512], replicated, may hold values from -3 to 3
- out_weight: bfloat16 [256, 256], replicated, may hold values from -7 to 7
- out_bias: bfloat16 [256], replicated, may hold values from -3 to 3
- grad_out: bfloat16 [8, 32, 64, 256], P('img', 'row'), may hold values from -6 to 6
Outputs:
- block_out: bfloat16 [8, 32, 64, 256], P('img', 'row')
- grad_pixels: bfloat16 [8, 32, 64, 256], P('img', 'row')
- norm1_gain_grad: float32 [256], replicated
- norm1_bias_grad: float32 [256], replicated
- conv1_weight_grad: float32 [3, 3, 256, 256], replicated
- conv1_bias_grad: float32 [256], replicated
- time_weight_grad: float32 [1024, 512], replicated
- time_bias_grad: float32 [512], replicated
- norm2_gain_grad: float32 [256], replicated
- norm2_bias_grad: float32 [256], replicated
- conv2_weight_grad: float32 [3, 3, 256, 256], replicated
- conv2_bias_grad: float32 [256], replicated
- norm3_gain_grad: float32 [256], replicated
- norm3_bias_grad: float32 [256], replicated
- qkv_weight_grad: float32 [256, 768], replicated
- qv_bias_grad: float32 [512], replicated
- out_weight_grad: float32 [256, 256], replicated
- out_bias_grad: float32 [256], replicated
The draws below stay inside these ranges and needn't reach their ends.
Inputs may be any that keep to these rules, and one draw needn't show every extreme that they name: `heights`: each image has at least one valid row; in every block of 2 consecutive images one image has all 32 rows valid.
All inputs are finite; a program needn't handle non-finite values.
Results may differ from the reference program's by a relative error of at most 0.015.
Values may be sent and summed in bfloat16 or wider, within the bound.
No kernel may reach another device: no remote copies, remote signals or barrier semaphores. Data moves between devices by JAX's collectives and lax.ppermute only.
A program may use at most 384 MiB of HBM per device.

```python
import math
import jax
import jax.numpy as jnp
from jax import lax

CHANNELS = 256
GROUPS = 32
HEADS = 4
HEAD_DIM = 64
TIME_DIM = 1024
COLUMNS = 64
IMG_GRP = 2
HEIGHT = 32
IMAGES = 8


def draw_heights(key, part):
    key = jax.random.fold_in(key, 11)
    draw_key, pick_key = jax.random.split(key)
    random_rows = jax.random.randint(draw_key, (IMAGES,), 1, HEIGHT + 1, dtype=jnp.int32)
    chosen = jax.random.randint(pick_key, (IMAGES // IMG_GRP,), 0, IMG_GRP, dtype=jnp.int32)
    position = jnp.arange(IMAGES, dtype=jnp.int32) % IMG_GRP
    full_mask = position == jnp.repeat(chosen, IMG_GRP)
    return jnp.where(full_mask, HEIGHT, random_rows).astype(jnp.int32)


def with_ends(values, stream_key, least, largest):
    spot = [jax.random.randint(jax.random.fold_in(stream_key, axis), (), 0, length) for axis, length in enumerate(values.shape)]
    main_axis = values.shape.index(max(values.shape))
    beside = spot[:main_axis] + [(spot[main_axis] + 1) % values.shape[main_axis]] + spot[main_axis + 1:]
    return values.at[tuple(spot)].set(least).at[tuple(beside)].set(largest)


def level_of(stream_key, shape, pieces, low, high):
    def one(axis_at, blocks):
        steps = jax.random.uniform(jax.random.fold_in(jax.random.fold_in(stream_key, 6), axis_at), (blocks,), jnp.float32, low / len(pieces), high / len(pieces))
        return jnp.repeat(jnp.exp(steps), shape[axis_at] // blocks).reshape((-1,) + (1,) * (len(shape) - axis_at - 1))

    gain = one(*pieces[0])
    for cut in pieces[1:]:
        gain = gain * one(*cut)
    return gain


def bell_draw(own_key, shape, deviation, limit, pieces=(), kind=jnp.bfloat16):
    values = jax.random.normal(own_key, shape, jnp.float32) * deviation
    if len(pieces) > 0:
        values = level_of(own_key, shape, pieces, -0.22, 0.18) * values
    return jnp.clip(values, min=-limit, max=limit).astype(kind)


def setup_inputs(seed: int = 0) -> dict:
    seeds = jax.random.split(jax.random.key(seed), 21)
    return {
        "pixels": bell_draw(seeds[0], (IMAGES, HEIGHT, COLUMNS, CHANNELS), 1.0, 6.0, ((0, 4), (1, 8))),
        "heights": draw_heights(jax.random.fold_in(seeds[20], 71), 0),
        "timesteps": with_ends(jax.random.randint(seeds[2], (IMAGES,), 0, 1000), jax.random.fold_in(seeds[2], 1), 0, 999).astype(jnp.int32),
        "norm1_gain": jnp.clip(1.0 + 0.15 * jax.random.normal(seeds[3], (CHANNELS,), jnp.float32), 0.25, 1.75).astype(jnp.bfloat16),
        "norm1_bias": bell_draw(seeds[4], (CHANNELS,), 0.3, 1.75),
        "conv1_weight": bell_draw(seeds[5], (3, 3, CHANNELS, CHANNELS), (9 * CHANNELS) ** -0.5, 0.125),
        "conv1_bias": bell_draw(seeds[6], (CHANNELS,), 0.5, 3.0),
        "time_weight": bell_draw(seeds[7], (TIME_DIM, 2 * CHANNELS), TIME_DIM ** -0.5, 0.1875),
        "time_bias": bell_draw(seeds[8], (2 * CHANNELS,), 0.5, 3.0),
        "norm2_gain": jnp.clip(1.0 + 0.15 * jax.random.normal(seeds[9], (CHANNELS,), jnp.float32), 0.25, 1.75).astype(jnp.bfloat16),
        "norm2_bias": bell_draw(seeds[10], (CHANNELS,), 0.3, 1.75),
        "conv2_weight": bell_draw(seeds[11], (3, 3, CHANNELS, CHANNELS), (9 * CHANNELS) ** -0.5, 0.125),
        "conv2_bias": bell_draw(seeds[12], (CHANNELS,), 0.5, 3.0),
        "norm3_gain": jnp.clip(1.0 + 0.15 * jax.random.normal(seeds[13], (CHANNELS,), jnp.float32), 0.25, 1.75).astype(jnp.bfloat16),
        "norm3_bias": bell_draw(seeds[14], (CHANNELS,), 0.3, 1.75),
        "qkv_weight": bell_draw(seeds[15], (CHANNELS, 3 * CHANNELS), CHANNELS ** -0.5, 0.375),
        "qv_bias": bell_draw(seeds[16], (2 * CHANNELS,), 0.5, 3.0),
        "out_weight": bell_draw(seeds[17], (CHANNELS, CHANNELS), ((HEIGHT * COLUMNS) ** 0.5 * 0.025), 7.0),
        "out_bias": bell_draw(seeds[18], (CHANNELS,), 0.5, 3.0),
        "grad_out": bell_draw(seeds[19], (IMAGES, HEIGHT, COLUMNS, CHANNELS), 1.0, 6.0, ((0, 4), (1, 8))),
    }


@jax.custom_vjp
def low(v):
    return lax.optimization_barrier(v.astype(jnp.bfloat16)).astype(jnp.float32)

@jax.custom_vjp
def low_back(v):
    return v

def low_keep(v):
    return (low(v), None)

def low_pass(kept, grad):
    return (grad,)

def back_keep(v):
    return (v, None)

def back_low(kept, grad):
    return (low(grad),)
low.defvjp(low_keep, low_pass)
low_back.defvjp(back_keep, back_low)
EPSILON = 1e-05
MASKED = -1000000000.0
PRECISE = lax.Precision.HIGHEST

def rounded(values_in):
    return low(low_back(values_in))

def embed_steps(timesteps):
    half_dim = TIME_DIM // 2
    frequency = jnp.exp(-math.log(10000.0) * jnp.arange(half_dim, dtype=jnp.float32) / half_dim)
    angles = timesteps.astype(jnp.float32)[:, None] * frequency[None, :]
    return jnp.concatenate([jnp.cos(angles), jnp.sin(angles)], axis=1)

def group_norm(field_in, row_mask, cell_count, gain_in, shift_in):
    shaped = field_in.reshape(HEIGHT, COLUMNS, GROUPS, CHANNELS // GROUPS)
    weight = row_mask[:, None, None, None]
    center = lax.optimization_barrier(jnp.sum(shaped * weight, axis=(0, 1, 3))) / cell_count
    centred = shaped - center[None, None, :, None]
    spread = lax.optimization_barrier(jnp.sum(jnp.square(centred * weight), axis=(0, 1, 3))) / cell_count
    normed = centred * lax.rsqrt(spread + EPSILON)[None, None, :, None]
    return normed.reshape(HEIGHT, COLUMNS, CHANNELS) * gain_in + shift_in

def conv_same(field_in, kernel):
    result = lax.conv_general_dilated(field_in[None], kernel, (1, 1), 'SAME', dimension_numbers=('NHWC', 'HWIO', 'NHWC'), precision=PRECISE)
    return result[0]

def attend(queries, keys_all, values_all, key_valid):
    block_rows = math.gcd(queries.shape[0], 512)
    query_blocks = queries.reshape(-1, block_rows, HEADS, HEAD_DIM)
    key_heads = keys_all.reshape(-1, HEADS, HEAD_DIM)
    value_heads = values_all.reshape(-1, HEADS, HEAD_DIM)
    scaling = HEAD_DIM ** (-0.5)

    def score_block(rows_in):
        scores = low_back(jnp.einsum('qhd,khd->hqk', rows_in, key_heads, precision=PRECISE) * scaling)
        scores = jnp.where(key_valid[None, None, :], scores, MASKED)
        weights = low(jax.nn.softmax(scores, axis=-1))
        return jnp.einsum('hqk,khd->qhd', weights, value_heads, precision=PRECISE)
    mixed_out = lax.map(jax.checkpoint(score_block), query_blocks)
    return mixed_out.reshape(queries.shape[0], CHANNELS)

def image_forward(field_in, row_mask, key_valid, cell_count, embedded, params):
    norm1_gain, norm1_bias, conv1_weight, conv1_bias, time_weight, time_bias, norm2_gain, norm2_bias, conv2_weight, conv2_bias, norm3_gain, norm3_bias, qkv_weight, qv_bias, out_weight, out_bias = params
    row_cells = row_mask[:, None, None]
    first_act = low(jax.nn.silu(group_norm(field_in, row_mask, cell_count, norm1_gain, norm1_bias)) * row_cells)
    conv_one = low_back(conv_same(first_act, conv1_weight)) + conv1_bias
    shifts = jnp.dot(jax.nn.silu(embedded), time_weight, precision=PRECISE) + time_bias
    affine_two = group_norm(conv_one, row_mask, cell_count, norm2_gain, norm2_bias)
    second_pre = affine_two * (1.0 + shifts[:CHANNELS]) + shifts[CHANNELS:]
    second_act = low(jax.nn.silu(second_pre) * row_cells)
    conv_two = low_back(conv_same(second_act, conv2_weight)) + conv2_bias
    residual = field_in + conv_two
    third_act = low(group_norm(residual, row_mask, cell_count, norm3_gain, norm3_bias)).reshape(HEIGHT * COLUMNS, CHANNELS)
    projected = jnp.dot(third_act, qkv_weight, precision=PRECISE)
    queries = rounded(projected[:, :CHANNELS] + qv_bias[:CHANNELS])
    keys_all = rounded(projected[:, CHANNELS:2 * CHANNELS])
    values_all = rounded(projected[:, 2 * CHANNELS:] + qv_bias[CHANNELS:])
    attended = rounded(attend(queries, keys_all, values_all, key_valid))
    output_proj = jnp.dot(attended, out_weight, precision=PRECISE) + out_bias
    return (residual + output_proj.reshape(HEIGHT, COLUMNS, CHANNELS)) * row_cells

def add_arrays(left_arr, right_arr):
    return left_arr + right_arr

def reference(pixels, heights, timesteps, norm1_gain, norm1_bias, conv1_weight, conv1_bias, time_weight, time_bias, norm2_gain, norm2_bias, conv2_weight, conv2_bias, norm3_gain, norm3_bias, qkv_weight, qv_bias, out_weight, out_bias, grad_out):
    params = (norm1_gain.astype(jnp.float32), norm1_bias.astype(jnp.float32), conv1_weight.astype(jnp.float32), conv1_bias.astype(jnp.float32), time_weight.astype(jnp.float32), time_bias.astype(jnp.float32), norm2_gain.astype(jnp.float32), norm2_bias.astype(jnp.float32), conv2_weight.astype(jnp.float32), conv2_bias.astype(jnp.float32), norm3_gain.astype(jnp.float32), norm3_bias.astype(jnp.float32), qkv_weight.astype(jnp.float32), qv_bias.astype(jnp.float32), out_weight.astype(jnp.float32), out_bias.astype(jnp.float32))
    embedded_all = embed_steps(timesteps)

    def per_image(totals, item_in):
        field_in, height_one, embedded, cotangent = item_in
        row_ids = jnp.arange(HEIGHT, dtype=jnp.int32)
        row_valid = row_ids < height_one
        row_mask = row_valid.astype(jnp.float32)
        key_valid = jnp.repeat(row_valid, COLUMNS)
        cell_count = height_one.astype(jnp.float32) * (COLUMNS * (CHANNELS // GROUPS))

        def forward(field_arg, param_arg):
            return image_forward(field_arg, row_mask, key_valid, cell_count, embedded, param_arg)
        output, pullback = jax.vjp(forward, field_in, params)
        field_grad, param_grads = pullback(cotangent)
        totals = jax.tree.map(add_arrays, totals, param_grads)
        return (totals, (output.astype(jnp.bfloat16), field_grad.astype(jnp.bfloat16)))
    zeros_init = jax.tree.map(jnp.zeros_like, params)
    totals, (outputs, field_grads) = lax.scan(per_image, zeros_init, (pixels.astype(jnp.float32), heights, embedded_all, grad_out.astype(jnp.float32)))
    return (outputs, field_grads, totals[0], totals[1], totals[2], totals[3], totals[4], totals[5], totals[6], totals[7], totals[8], totals[9], totals[10], totals[11], totals[12], totals[13], totals[14], totals[15])
```

```python
import math

import jax
import jax.numpy as jnp
from jax import lax
from jax.experimental import pallas as pl
from jax.experimental.pallas import tpu as pltpu
from jax.sharding import PartitionSpec as P

GROUPS = 32
HEADS = 4


EPSILON = 1e-05
MASKED = -1000000000.0
PRECISE = lax.Precision.HIGHEST


def with_halo(cells, sides, width):
    for axis, dim in sides:
        count = lax.axis_size(axis)
        ends = count - 1
        head = lax.slice_in_dim(cells, 0, width, axis=dim)
        tail = lax.slice_in_dim(cells, cells.shape[dim] - width, cells.shape[dim], axis=dim)
        cells = jnp.concatenate(
            [
                lax.ppermute(tail, axis, [(i, (i + 1) % count) for i in range(ends)]),
                cells,
                lax.ppermute(head, axis, [((i + 1) % count, i) for i in range(ends)]),
            ],
            axis=dim,
        )
    return cells


def embed_steps(timesteps, time_width):
    half_dim = time_width // 2
    frequency = jnp.exp(-math.log(10000.0) * jnp.arange(half_dim, dtype=jnp.float32) / half_dim)
    angles = timesteps.astype(jnp.float32)[:, None] * frequency[None, :]
    return jnp.concatenate([jnp.cos(angles), jnp.sin(angles)], axis=1)


def silu_slope(pre_act):
    sigmoid = jax.nn.sigmoid(pre_act)
    return sigmoid * (1.0 + pre_act * (1.0 - sigmoid))


def with_rims(field_in):
    return with_halo(field_in, (("row", 1),), 1)


def conv_rows(padded, kernel):
    return lax.conv_general_dilated(
        padded,
        kernel,
        (1, 1),
        ((0, 0), (1, 1)),
        dimension_numbers=("NHWC", "HWIO", "NHWC"),
        preferred_element_type=jnp.float32,
    )


def flipped(kernel):
    return jnp.transpose(kernel[::-1, ::-1], (0, 1, 3, 2))


def kernel_grad(padded, grad_field):
    row_count = grad_field.shape[1]
    col_count = grad_field.shape[2]
    widened = jnp.pad(padded, ((0, 0), (0, 0), (1, 1), (0, 0)))
    tap_rows = []
    for tap_row in range(3):
        tap_line = []
        for tap_col in range(3):
            window = widened[:, tap_row : tap_row + row_count, tap_col : tap_col + col_count, :]
            tap_line.append(
                jnp.einsum("brwc,brwd->cd", window, grad_field, preferred_element_type=jnp.float32)
            )
        tap_rows.append(jnp.stack(tap_line))
    return jnp.stack(tap_rows)


def norm_forward(field_in, cell_mask, cell_count, group_count):
    shaped = field_in.reshape(field_in.shape[:3] + (group_count, field_in.shape[3] // group_count))
    first_sum = lax.psum(jnp.sum(shaped * cell_mask, axis=(1, 2, 4)), "row")
    center = first_sum / cell_count[:, None]
    centred = shaped - center[:, None, None, :, None]
    spread_sum = lax.psum(jnp.sum(jnp.square(centred * cell_mask), axis=(1, 2, 4)), "row")
    spread = spread_sum / cell_count[:, None]
    inverse = lax.rsqrt(spread + EPSILON)
    return (centred * inverse[:, None, None, :, None], inverse)


def norm_backward(grad_normed, normalized, inverse, gain_in, cell_mask, cell_count):
    full_shape = grad_normed.shape
    flat_norm = normalized.reshape(full_shape)
    gain_grad = jnp.sum(grad_normed * flat_norm, axis=(0, 1, 2))
    shift_grad = jnp.sum(grad_normed, axis=(0, 1, 2))
    scaled = (grad_normed * gain_in).reshape(normalized.shape)
    sum_plain, sum_cross = lax.psum(
        (
            jnp.sum(scaled * cell_mask, axis=(1, 2, 4)),
            jnp.sum(scaled * normalized * cell_mask, axis=(1, 2, 4)),
        ),
        "row",
    )
    mean_plain = sum_plain / cell_count[:, None]
    mean_cross = sum_cross / cell_count[:, None]
    grad_in = (
        (
            scaled
            - mean_plain[:, None, None, :, None]
            - normalized * mean_cross[:, None, None, :, None]
        )
        * inverse[:, None, None, :, None]
        * cell_mask
    )
    return (grad_in.reshape(full_shape), gain_grad, shift_grad)


def local_rows(
    pixels,
    heights,
    timesteps,
    norm1_gain,
    norm1_bias,
    conv1_weight,
    conv1_bias,
    time_weight,
    time_bias,
    norm2_gain,
    norm2_bias,
    conv2_weight,
    conv2_bias,
    norm3_gain,
    norm3_bias,
    qkv_weight,
    qv_bias,
    out_weight,
    out_bias,
    grad_out,
):
    image_count, row_count, col_count, channels = pixels.shape
    group_count = GROUPS
    head_count = HEADS
    head_width = channels // head_count
    query_count = row_count * col_count
    scaling = head_width ** (-0.5)
    head_shape = (image_count, query_count, head_count, head_width)
    row_ids = lax.axis_index("row") * row_count + jnp.arange(row_count, dtype=jnp.int32)
    row_valid = row_ids[None, :] < heights[:, None]
    row_mask = row_valid.astype(jnp.float32)
    cell_rows = row_mask[:, :, None, None]
    cell_mask = row_mask[:, :, None, None, None]
    own_valid = jnp.repeat(row_valid, col_count, axis=1)[:, None, None, :]
    cell_count = heights.astype(jnp.float32) * (col_count * (channels // group_count))
    gain_one = norm1_gain.astype(jnp.float32)
    gain_two = norm2_gain.astype(jnp.float32)
    gain_three = norm3_gain.astype(jnp.float32)
    field_in = pixels.astype(jnp.float32)
    normed_one, inverse_one = norm_forward(field_in, cell_mask, cell_count, group_count)
    pre_one = normed_one.reshape(field_in.shape) * gain_one + norm1_bias.astype(jnp.float32)
    act_one = (jax.nn.silu(pre_one) * cell_rows).astype(jnp.bfloat16)
    padded_one = with_rims(act_one)
    conv_one = conv_rows(padded_one, conv1_weight) + conv1_bias.astype(jnp.float32)
    time_act = jax.nn.silu(embed_steps(timesteps, time_weight.shape[0]))
    shifts = jnp.dot(
        time_act, time_weight.astype(jnp.float32), precision=PRECISE
    ) + time_bias.astype(jnp.float32)
    scale_part = 1.0 + shifts[:, None, None, :channels]
    shift_part = shifts[:, None, None, channels:]
    normed_two, inverse_two = norm_forward(conv_one, cell_mask, cell_count, group_count)
    affine_two = normed_two.reshape(field_in.shape) * gain_two + norm2_bias.astype(jnp.float32)
    pre_two = affine_two * scale_part + shift_part
    act_two = (jax.nn.silu(pre_two) * cell_rows).astype(jnp.bfloat16)
    padded_two = with_rims(act_two)
    residual = field_in + (conv_rows(padded_two, conv2_weight) + conv2_bias.astype(jnp.float32))
    normed_three, inverse_three = norm_forward(residual, cell_mask, cell_count, group_count)
    act_three = (
        normed_three.reshape(field_in.shape) * gain_three + norm3_bias.astype(jnp.float32)
    ).astype(jnp.bfloat16)
    projected = jnp.einsum(
        "brwc,cd->brwd", act_three, qkv_weight, preferred_element_type=jnp.float32
    )
    qv_float = qv_bias.astype(jnp.float32)
    queries = (projected[..., :channels] + qv_float[:channels]).astype(jnp.bfloat16)
    keys_own = projected[..., channels : 2 * channels].astype(jnp.bfloat16)
    values_own = (projected[..., 2 * channels :] + qv_float[channels:]).astype(jnp.bfloat16)
    query_heads = queries.reshape(head_shape)
    key_heads = keys_own.reshape(head_shape)
    value_heads = values_own.reshape(head_shape)

    def flatten_rows(piece_arr):
        return piece_arr.reshape(
            image_count, piece_arr.shape[1] * col_count, head_count, head_width
        )

    def key_mask(span_rows):
        key_rows = jnp.arange(span_rows, dtype=jnp.int32)
        return jnp.repeat(key_rows[None, :] < heights[:, None], col_count, axis=1)[:, None, None, :]

    top_init = jnp.full((image_count, query_count, head_count), MASKED, jnp.float32)
    piece_keys = lax.all_gather(keys_own, "row", axis=1, tiled=True)
    piece_values = lax.all_gather(values_own, "row", axis=1, tiled=True)
    key_valid = key_mask(piece_keys.shape[1])
    scores = (
        jnp.einsum(
            "bqhd,bkhd->bqhk",
            query_heads,
            flatten_rows(piece_keys),
            preferred_element_type=jnp.float32,
        )
        * scaling
    )
    scores = jnp.where(key_valid, scores, MASKED)
    new_top = jnp.maximum(top_init, jnp.max(scores, axis=3))
    weights = jnp.where(key_valid, jnp.exp(scores - new_top[..., None]), 0.0)
    running_total = jnp.sum(weights, axis=3)
    running_acc = jnp.einsum(
        "bqhk,bkhd->bqhd",
        weights.astype(jnp.bfloat16),
        flatten_rows(piece_values),
        preferred_element_type=jnp.float32,
    )
    attn_float = running_acc / running_total[..., None]
    log_total = new_top + jnp.log(running_total)
    attended = attn_float.reshape(pixels.shape).astype(jnp.bfloat16)
    output_proj = jnp.einsum(
        "brwc,cd->brwd", attended, out_weight, preferred_element_type=jnp.float32
    ) + out_bias.astype(jnp.float32)
    block_out = ((residual + output_proj) * cell_rows).astype(jnp.bfloat16)
    grad_proj = grad_out.astype(jnp.float32) * cell_rows
    grad_proj_low = grad_proj.astype(jnp.bfloat16)
    out_weight_grad = jnp.einsum(
        "brwc,brwd->cd", attended, grad_proj_low, preferred_element_type=jnp.float32
    )
    out_bias_grad = jnp.sum(grad_proj, axis=(0, 1, 2))
    grad_attended = jnp.einsum(
        "brwd,cd->brwc", grad_proj_low, out_weight, preferred_element_type=jnp.float32
    ).astype(jnp.bfloat16)
    grad_heads = grad_attended.reshape(head_shape)
    delta_own = jnp.sum(grad_heads.astype(jnp.float32) * attn_float, axis=3)
    stat_shape = (image_count, row_count, col_count, head_count)
    all_lse, all_delta = (
        lax.all_gather(log_total.reshape(stat_shape), "row", axis=1, tiled=True),
        lax.all_gather(delta_own.reshape(stat_shape), "row", axis=1, tiled=True),
    )
    piece_keys = lax.all_gather(keys_own, "row", axis=1, tiled=True)
    piece_values = lax.all_gather(values_own, "row", axis=1, tiled=True)
    flat_keys = flatten_rows(piece_keys)
    key_valid = key_mask(piece_keys.shape[1])
    scores = (
        jnp.einsum("bqhd,bkhd->bqhk", query_heads, flat_keys, preferred_element_type=jnp.float32)
        * scaling
    )
    soft_weights = jnp.where(key_valid, jnp.exp(scores - log_total[..., None]), 0.0)
    grad_probs = jnp.einsum(
        "bqhd,bkhd->bqhk",
        grad_heads,
        flatten_rows(piece_values),
        preferred_element_type=jnp.float32,
    )
    grad_scores = (soft_weights * (grad_probs - delta_own[..., None])).astype(jnp.bfloat16)
    grad_query_sum = jnp.einsum(
        "bqhk,bkhd->bqhd", grad_scores, flat_keys, preferred_element_type=jnp.float32
    )
    piece_queries = lax.all_gather(queries, "row", axis=1, tiled=True)
    piece_grads = lax.all_gather(grad_attended, "row", axis=1, tiled=True)
    flat_queries = flatten_rows(piece_queries)
    flat_grads = flatten_rows(piece_grads)
    span_rows = piece_queries.shape[1]
    piece_lse = all_lse.reshape(image_count, span_rows * col_count, head_count)
    piece_delta = all_delta.reshape(image_count, span_rows * col_count, head_count)
    scores = (
        jnp.einsum("bqhd,bkhd->bqhk", flat_queries, key_heads, preferred_element_type=jnp.float32)
        * scaling
    )
    soft_weights = jnp.where(own_valid, jnp.exp(scores - piece_lse[..., None]), 0.0)
    value_term = jnp.einsum(
        "bqhk,bqhd->bkhd",
        soft_weights.astype(jnp.bfloat16),
        flat_grads,
        preferred_element_type=jnp.float32,
    )
    grad_probs = jnp.einsum(
        "bqhd,bkhd->bqhk", flat_grads, value_heads, preferred_element_type=jnp.float32
    )
    grad_scores = (soft_weights * (grad_probs - piece_delta[..., None])).astype(jnp.bfloat16)
    key_term = jnp.einsum(
        "bqhk,bqhd->bkhd", grad_scores, flat_queries, preferred_element_type=jnp.float32
    )
    key_term, value_term = (key_term, value_term)
    grad_queries = (grad_query_sum * scaling).reshape(pixels.shape).astype(jnp.bfloat16)
    grad_keys = (key_term * scaling).reshape(pixels.shape).astype(jnp.bfloat16)
    grad_values = value_term.reshape(pixels.shape).astype(jnp.bfloat16)
    grad_projected = jnp.concatenate([grad_queries, grad_keys, grad_values], axis=3)
    qkv_weight_grad = jnp.einsum(
        "brwc,brwd->cd", act_three, grad_projected, preferred_element_type=jnp.float32
    )
    qv_bias_grad = jnp.concatenate(
        [
            jnp.sum(grad_queries.astype(jnp.float32), axis=(0, 1, 2)),
            jnp.sum(grad_values.astype(jnp.float32), axis=(0, 1, 2)),
        ]
    )
    grad_act_three = jnp.einsum(
        "brwd,cd->brwc", grad_projected, qkv_weight, preferred_element_type=jnp.float32
    )
    grad_res_attn, norm3_gain_grad, norm3_bias_grad = norm_backward(
        grad_act_three, normed_three, inverse_three, gain_three, cell_mask, cell_count
    )
    grad_residual = grad_proj + grad_res_attn
    grad_conv_two = grad_residual.astype(jnp.bfloat16)
    conv2_bias_grad = jnp.sum(grad_residual, axis=(0, 1, 2))
    conv2_weight_grad = kernel_grad(padded_two, grad_conv_two)
    grad_act_two = conv_rows(with_rims(grad_conv_two), flipped(conv2_weight)) * cell_rows
    grad_pre_two = grad_act_two * silu_slope(pre_two)
    scale_grad = jnp.sum(grad_pre_two * affine_two, axis=(1, 2))
    shift_grad = jnp.sum(grad_pre_two, axis=(1, 2))
    shift_grads = jnp.concatenate([scale_grad, shift_grad], axis=1)
    grad_conv_one, norm2_gain_grad, norm2_bias_grad = norm_backward(
        grad_pre_two * scale_part, normed_two, inverse_two, gain_two, cell_mask, cell_count
    )
    conv_one_low = grad_conv_one.astype(jnp.bfloat16)
    conv1_bias_grad = jnp.sum(grad_conv_one, axis=(0, 1, 2))
    conv1_weight_grad = kernel_grad(padded_one, conv_one_low)
    grad_act_one = conv_rows(with_rims(conv_one_low), flipped(conv1_weight)) * cell_rows
    grad_pre_one = grad_act_one * silu_slope(pre_one)
    grad_field_norm, norm1_gain_grad, norm1_bias_grad = norm_backward(
        grad_pre_one, normed_one, inverse_one, gain_one, cell_mask, cell_count
    )
    grad_pixels = (grad_residual + grad_field_norm).astype(jnp.bfloat16)
    time_weight_grad = jnp.dot(time_act.T, shift_grads, precision=PRECISE)
    time_bias_grad = jnp.sum(shift_grads, axis=0)
    summed = lax.psum(
        (
            norm1_gain_grad,
            norm1_bias_grad,
            conv1_weight_grad,
            conv1_bias_grad,
            time_weight_grad,
            time_bias_grad,
            norm2_gain_grad,
            norm2_bias_grad,
            conv2_weight_grad,
            conv2_bias_grad,
            norm3_gain_grad,
            norm3_bias_grad,
            qkv_weight_grad,
            qv_bias_grad,
            out_weight_grad,
            out_bias_grad,
        ),
        ("img", "row"),
    )
    return (
        block_out,
        grad_pixels,
        summed[0],
        summed[1],
        summed[2],
        summed[3],
        summed[4],
        summed[5],
        summed[6],
        summed[7],
        summed[8],
        summed[9],
        summed[10],
        summed[11],
        summed[12],
        summed[13],
        summed[14],
        summed[15],
    )


def mib(count):
    return pltpu.CompilerParams(vmem_limit_bytes=count * 2**20)


def dot(left, right):
    return jnp.dot(left, right, preferred_element_type=jnp.float32)


def dot_rows(left, right):
    return lax.dot_general(
        left, right, (((1,), (1,)), ((), ())), preferred_element_type=jnp.float32
    )


def fold(tile):
    return jnp.sum(tile.reshape(-1, 8, tile.shape[1]), axis=0)


def group_sums(row, width):
    channels = row.shape[1]
    rows = lax.broadcasted_iota(jnp.int32, (channels, channels), 0) // width
    cols = lax.broadcasted_iota(jnp.int32, (channels, channels), 1) // width
    same = jnp.where(rows == cols, 1.0, 0.0).astype(jnp.float32)
    wide = jnp.broadcast_to(row, (8, channels))
    return jnp.dot(wide, same, precision=PRECISE, preferred_element_type=jnp.float32)[0:1]


def row_at(index, cols):
    return pl.ds(pl.multiple_of(index * cols, cols), cols)


def total_of(tile):
    return jnp.sum(tile, axis=0, keepdims=True)


def field_stats(read, height, rows, cols, channels):
    width = channels // GROUPS
    cells = (height * (cols * width)).astype(jnp.float32)
    zero = jnp.zeros((8, channels), jnp.float32)

    def valid(index):
        return jnp.where(index < height, 1.0, 0.0).astype(jnp.float32)

    def add(index, total):
        return total + fold(read(index) * valid(index))

    total = lax.fori_loop(0, rows, add, zero, unroll=2)
    mean = group_sums(total_of(total), width) / cells

    def add_square(index, total):
        return total + fold(jnp.square((read(index) - mean) * valid(index)))

    total = lax.fori_loop(0, rows, add_square, zero, unroll=2)
    spread = group_sums(total_of(total), width) / cells
    return mean, lax.rsqrt(spread + EPSILON)


def put_shifted(ref, index, tile, cols):
    channels = tile.shape[1]
    column = lax.broadcasted_iota(jnp.int32, tile.shape, 0)
    before = jnp.where(column == 0, 0.0, pltpu.roll(tile, 1, 0))
    after = jnp.where(column == cols - 1, 0.0, pltpu.roll(tile, cols - 1, 0))
    at = row_at(index + 1, cols)
    ref[at, 0:channels] = before.astype(jnp.bfloat16)
    ref[at, channels : 2 * channels] = tile.astype(jnp.bfloat16)
    ref[at, 2 * channels : 3 * channels] = after.astype(jnp.bfloat16)


def clear_rims(ref, cols):
    edge = jnp.zeros((cols, ref.shape[1]), ref.dtype)
    ref[0:cols, :] = edge
    ref[ref.shape[0] - cols : ref.shape[0], :] = edge


def conv_shifted(shifted, weight, out, bias, cols):
    step = 8 * cols

    def block(index, carry):
        base = index * step
        total = bias
        for tap in range(3):
            at = pl.ds(pl.multiple_of(base + tap * cols, cols), step)
            total = total + dot(shifted[at, :], weight[tap])
        out[pl.ds(pl.multiple_of(base, step), step), :] = total
        return carry

    lax.fori_loop(0, out.shape[0] // step, block, 0)


def pick_own(shifted, chosen, out):
    step = out.shape[0] // 4

    def block(index, carry):
        at = pl.ds(pl.multiple_of(index * step, 16), step)
        out[at, :] = dot(shifted[at, :], chosen[...]).astype(jnp.bfloat16)
        return carry

    lax.fori_loop(0, 4, block, 0)


def kernel_quarter(grad, shifted_own, grad_t, out, cols):
    cells = grad.shape[0]
    for start in range(0, cells, 256):
        grad_t[:, start : start + 256] = jnp.transpose(grad[start : start + 256, :]).astype(
            jnp.bfloat16
        )
    width = shifted_own.shape[1]
    for tap in range(3):
        part = dot(grad_t[...], shifted_own[tap * cols : tap * cols + cells, :])
        out[tap * width : (tap + 1) * width, :] = jnp.transpose(part).astype(jnp.bfloat16)


def forward_kernel(place, *refs):
    blocks = refs[:8]
    w_one, w_two, vec, chosen = refs[8:12]
    pix, conv_one, residual, act_three, own_one, own_two, stats, shifted = refs[12:]
    cells, channels = pix.shape
    block_cells = blocks[0].shape[0]
    cols = (own_one.shape[0] - cells) // 2
    rows = cells // cols
    spot, height = place[0], place[1]
    for step, block in enumerate(blocks):
        at = pl.ds(pl.multiple_of((spot ^ step) * block_cells, block_cells), block_cells)
        pix[at, :] = block[...]
    gain_one, bias_one, conv_bias_one, gain_two, bias_two = (vec[k : k + 1, :] for k in range(5))
    scale, shift, conv_bias_two, gain_three, bias_three = (vec[k : k + 1, :] for k in range(5, 10))

    def valid(index):
        return jnp.where(index < height, 1.0, 0.0).astype(jnp.float32)

    def read_pix(index):
        return pix[row_at(index, cols), :].astype(jnp.float32)

    def read_conv(index):
        return conv_one[row_at(index, cols), :]

    def read_res(index):
        return residual[row_at(index, cols), :]

    clear_rims(shifted, cols)
    mean_one, inv_one = field_stats(read_pix, height, rows, cols, channels)

    def first(index, carry):
        pre = (read_pix(index) - mean_one) * inv_one * gain_one + bias_one
        put_shifted(shifted, index, pre / (1.0 + jnp.exp(-pre)) * valid(index), cols)
        return carry

    lax.fori_loop(0, rows, first, 0, unroll=2)
    conv_shifted(shifted, w_one, conv_one, conv_bias_one, cols)
    pick_own(shifted, chosen, own_one)
    mean_two, inv_two = field_stats(read_conv, height, rows, cols, channels)

    def second(index, carry):
        affine = (read_conv(index) - mean_two) * inv_two * gain_two + bias_two
        pre = affine * scale + shift
        put_shifted(shifted, index, pre / (1.0 + jnp.exp(-pre)) * valid(index), cols)
        return carry

    lax.fori_loop(0, rows, second, 0, unroll=2)
    conv_shifted(shifted, w_two, residual, conv_bias_two, cols)
    pick_own(shifted, chosen, own_two)

    def join(index, carry):
        at = row_at(index, cols)
        residual[at, :] = residual[at, :] + read_pix(index)
        return carry

    lax.fori_loop(0, rows, join, 0, unroll=2)
    mean_three, inv_three = field_stats(read_res, height, rows, cols, channels)

    def third(index, carry):
        normed = (read_res(index) - mean_three) * inv_three
        act_three[row_at(index, cols), :] = (normed * gain_three + bias_three).astype(jnp.bfloat16)
        return carry

    lax.fori_loop(0, rows, third, 0, unroll=2)
    stats[...] = jnp.concatenate(
        [mean_one, inv_one, mean_two, inv_two, mean_three, inv_three, mean_one, mean_one], axis=0
    )


def attention_kernel(place, *refs):
    blocks = refs[:8]
    act_three, w_heads, w_out, biases = refs[8:12]
    grad_proj, attended, packed, weight_rows, sums = refs[12:17]
    query_grad, query_grad_t, key_pad, value_pad, heads_t, mixed, mask_row = refs[17:]
    cells, channels = act_three.shape
    block_cells = blocks[0].shape[0]
    spot, height, cols = place[0], place[1], place[4]
    half = mixed.shape[1] // 2
    scaling = half**-0.5
    valid_cells = height * cols
    step = 256
    total = jnp.zeros((8, channels), jnp.float32)
    for index, block in enumerate(blocks):
        base = pl.multiple_of((spot ^ index) * block_cells, block_cells)
        cell = base + lax.broadcasted_iota(jnp.int32, (block_cells, channels), 0)
        kept = jnp.where(cell < valid_cells, block[...].astype(jnp.float32), 0.0)
        total = total + fold(kept)
        grad_proj[pl.ds(base, block_cells), :] = kept.astype(jnp.bfloat16)
    sums[...] = jnp.concatenate([total_of(total), jnp.zeros((7, channels), jnp.float32)], axis=0)

    def project(index, carry):
        at = pl.ds(pl.multiple_of(index * 512, 512), 512)
        act = act_three[at, :]
        parts = dot(act, w_heads[...]) + biases[0:1, :]
        query = (parts[:, 0 : 2 * half].astype(jnp.bfloat16)) * jnp.bfloat16(scaling)
        query_grad[at, :] = query + dot(grad_proj[at, :], w_out[...]).astype(jnp.bfloat16)
        key_pad[at, :] = parts[:, 2 * half : 4 * half].astype(jnp.bfloat16)
        value_pad[at, :] = parts[:, 4 * half : 6 * half].astype(jnp.bfloat16)
        return carry

    lax.fori_loop(0, cells // 512, project, 0)
    lane = lax.broadcasted_iota(jnp.int32, (1, cells), 1)
    mask_row[...] = jnp.where(lane < valid_cells, 0.0, MASKED)
    for start in range(0, cells, step):
        query_grad_t[:, start : start + step] = jnp.transpose(
            query_grad[start : start + step, :].astype(jnp.float32)
        ).astype(jnp.bfloat16)
    heads_t[...] = jnp.zeros(heads_t.shape, jnp.float32)
    mixed[...] = jnp.zeros(mixed.shape, jnp.bfloat16)

    def query_block(index, carry):
        at = pl.ds(pl.multiple_of(index * step, step), step)
        both = query_grad[at, :]
        scores = dot_rows(both, key_pad[...]) + mask_row[...]
        top = jnp.max(scores, axis=1, keepdims=True)
        weights = jnp.exp(scores - top)
        probs = weights * (1.0 / jnp.sum(weights, axis=1, keepdims=True))
        low = probs.astype(jnp.bfloat16)
        out = dot(low, value_pad[...])
        delta = jnp.sum(both.astype(jnp.float32) * out, axis=1, keepdims=True)
        grad_probs = dot_rows(both, value_pad[...])
        grad_scores = (probs * (grad_probs - delta)).astype(jnp.bfloat16)
        mixed[at, :] = (out + dot(grad_scores, key_pad[...]) * scaling).astype(jnp.bfloat16)
        heads_t[0:half, :] += dot(query_grad_t[0:half, at], grad_scores)
        heads_t[half : 2 * half, :] += dot(query_grad_t[half : 2 * half, at], low)
        return carry

    lax.fori_loop(0, (valid_cells + step - 1) // step, query_block, 0)
    for start in range(0, cells, step):
        packed[start : start + step, :] = jnp.transpose(heads_t[:, start : start + step]).astype(
            jnp.bfloat16
        )
    packed[cells : cells + cells // 2, 0:half] = mixed[0 : cells // 2, 0:half]
    packed[cells : cells + cells // 2, half : 2 * half] = mixed[cells // 2 : cells, 0:half]
    attended[...] = mixed[:, half : 2 * half]
    for start in range(0, cells, step):
        query_grad_t[:, start : start + step] = jnp.transpose(
            mixed[start : start + step, :].astype(jnp.float32)
        ).astype(jnp.bfloat16)
    low_heads = heads_t[...].astype(jnp.bfloat16)
    from_query = dot(query_grad_t[...], act_three[...])
    from_heads = dot(low_heads, act_three[...])
    from_out = dot(query_grad_t[...], grad_proj[...])
    weight_rows[0:half, :] = from_query[0:half].astype(jnp.bfloat16)
    weight_rows[half : 3 * half, :] = from_heads.astype(jnp.bfloat16)
    weight_rows[3 * half : 4 * half, :] = from_out[half : 2 * half].astype(jnp.bfloat16)
    ones = jnp.ones((8, cells), jnp.bfloat16)
    query_sum = dot(ones, mixed[...])
    value_sum = lax.dot_general(
        ones, low_heads, (((1,), (1,)), ((), ())), preferred_element_type=jnp.float32
    )
    row = jnp.concatenate([query_sum, value_sum], axis=1)[0:1]
    weight_rows[4 * half :, :] = jnp.concatenate(
        [row, jnp.zeros((weight_rows.shape[0] - 4 * half - 1, channels), jnp.float32)], axis=0
    ).astype(jnp.bfloat16)


def residual_kernel(place, *refs):
    heads = refs[:4]
    w_key_value, w_query, grad_proj, residual, stats, vec, own_two = refs[4:11]
    grad_res, shifted, quarter, sums, grad_act, grad_t = refs[11:]
    cells, channels = grad_proj.shape
    cols = (own_two.shape[0] - cells) // 2
    rows = cells // cols
    height, head = place[1], place[2]
    width = channels // GROUPS
    count = (height * (cols * width)).astype(jnp.float32)
    half = w_query.shape[1]
    zeros = jnp.zeros((half, channels), jnp.bfloat16)
    halfway = cells // 2
    step = 512
    pairs = ((0, 1), (2, 3))
    w_main = [
        jnp.concatenate([w_key_value[head ^ a], w_key_value[head ^ b]], axis=0) for a, b in pairs
    ]
    for part in range(2):
        w_side = []
        for a, b in pairs:
            left, right = w_query[head ^ a], w_query[head ^ b]
            order = [left, zeros, right, zeros] if part == 0 else [zeros, left, zeros, right]
            w_side.append(jnp.concatenate(order, axis=0))
        for base in range(0, halfway, step):
            start = part * halfway + base
            total = None
            for k, (a, b) in enumerate(pairs):
                main = jnp.concatenate(
                    [heads[a][start : start + step, :], heads[b][start : start + step, :]], axis=1
                )
                spot = cells + base
                side = jnp.concatenate(
                    [heads[a][spot : spot + step, :], heads[b][spot : spot + step, :]], axis=1
                )
                term = dot(main, w_main[k]) + dot(side, w_side[k])
                total = term if total is None else total + term
            grad_act[start : start + step, :] = total
    mean, inverse = stats[4:5, :], stats[5:6, :]
    gain = vec[8:9, :]
    zero = jnp.zeros((8, channels), jnp.float32)

    def normed(index):
        return (residual[row_at(index, cols), :] - mean) * inverse

    def add(index, totals):
        grad = grad_act[row_at(index, cols), :]
        return totals[0] + fold(grad), totals[1] + fold(grad * normed(index))

    plain, cross = lax.fori_loop(0, rows, add, (zero, zero), unroll=2)
    plain, cross = total_of(plain), total_of(cross)
    mean_plain = group_sums(plain * gain, width) / count
    mean_cross = group_sums(cross * gain, width) / count
    clear_rims(shifted, cols)

    def finish(index, total):
        at = row_at(index, cols)
        inner = (grad_act[at, :] * gain - mean_plain - normed(index) * mean_cross) * inverse
        inner = inner * jnp.where(index < height, 1.0, 0.0).astype(jnp.float32)
        grad = grad_proj[at, :].astype(jnp.float32) + inner
        grad_res[at, :] = grad
        put_shifted(shifted, index, grad, cols)
        return total + fold(grad)

    total = total_of(lax.fori_loop(0, rows, finish, zero, unroll=2))
    kernel_quarter(grad_res, own_two, grad_t, quarter, cols)
    sums[...] = jnp.concatenate([cross, plain, total, jnp.zeros((5, channels), jnp.float32)], axis=0)


def second_kernel(place, shifted, weight, conv_one, stats, vec, own_one, *refs):
    shifted_one, quarter, sums, grad_act, grad_t = refs
    cells, channels = conv_one.shape
    cols = (own_one.shape[0] - cells) // 2
    rows = cells // cols
    height = place[1]
    width = channels // GROUPS
    count = (height * (cols * width)).astype(jnp.float32)
    mean, inverse = stats[2:3, :], stats[3:4, :]
    gain, bias, scale, shift = (vec[k : k + 1, :] for k in range(3, 7))
    zero = jnp.zeros((8, channels), jnp.float32)

    def valid(index):
        return jnp.where(index < height, 1.0, 0.0).astype(jnp.float32)

    def normed(index):
        return (conv_one[row_at(index, cols), :] - mean) * inverse

    conv_shifted(shifted, weight, grad_act, 0.0, cols)

    def add(index, totals):
        at = row_at(index, cols)
        unit = normed(index)
        pre = (unit * gain + bias) * scale + shift
        sigmoid = 1.0 / (1.0 + jnp.exp(-pre))
        grad = grad_act[at, :] * valid(index) * (sigmoid * (1.0 + pre * (1.0 - sigmoid)))
        grad_act[at, :] = grad
        return totals[0] + fold(grad), totals[1] + fold(grad * unit)

    plain, cross = lax.fori_loop(0, rows, add, (zero, zero), unroll=2)
    plain, cross = total_of(plain), total_of(cross)
    factor = gain * scale
    mean_plain = group_sums(plain * factor, width) / count
    mean_cross = group_sums(cross * factor, width) / count
    clear_rims(shifted_one, cols)

    def finish(index, total):
        at = row_at(index, cols)
        grad = (grad_act[at, :] * factor - mean_plain - normed(index) * mean_cross) * inverse
        grad = grad * valid(index)
        grad_act[at, :] = grad
        put_shifted(shifted_one, index, grad, cols)
        return total + fold(grad)

    total = total_of(lax.fori_loop(0, rows, finish, zero, unroll=2))
    kernel_quarter(grad_act, own_one, grad_t, quarter, cols)
    sums[...] = jnp.concatenate([cross, plain, total, jnp.zeros((5, channels), jnp.float32)], axis=0)


def first_kernel(place, shifted, weight, pix, grad_res, stats, vec, out, sums, grad_act):
    cells, channels = pix.shape
    block_cells = out.shape[1]
    cols = (shifted.shape[0] - cells) // 2
    rows = cells // cols
    spot, height = place[0], place[1]
    width = channels // GROUPS
    count = (height * (cols * width)).astype(jnp.float32)
    mean, inverse = stats[0:1, :], stats[1:2, :]
    gain, bias = vec[0:1, :], vec[1:2, :]
    zero = jnp.zeros((8, channels), jnp.float32)

    def valid(index):
        return jnp.where(index < height, 1.0, 0.0).astype(jnp.float32)

    def normed(at):
        return (pix[at, :].astype(jnp.float32) - mean) * inverse

    conv_shifted(shifted, weight, grad_act, 0.0, cols)

    def add(index, totals):
        at = row_at(index, cols)
        unit = normed(at)
        pre = unit * gain + bias
        sigmoid = 1.0 / (1.0 + jnp.exp(-pre))
        grad = grad_act[at, :] * valid(index) * (sigmoid * (1.0 + pre * (1.0 - sigmoid)))
        grad_act[at, :] = grad
        return totals[0] + fold(grad), totals[1] + fold(grad * unit)

    plain, cross = lax.fori_loop(0, rows, add, (zero, zero), unroll=2)
    plain, cross = total_of(plain), total_of(cross)
    mean_plain = group_sums(plain * gain, width) / count
    mean_cross = group_sums(cross * gain, width) / count
    block_rows = block_cells // cols
    for part in range(2):
        first_row = (spot ^ (4 * part)) * block_rows
        for line in range(block_rows):
            at = row_at(first_row + line, cols)
            grad = (grad_act[at, :] * gain - mean_plain - normed(at) * mean_cross) * inverse
            grad = grad_res[at, :] + grad * valid(first_row + line)
            out[part, line * cols : (line + 1) * cols, :] = grad.astype(jnp.bfloat16)
    sums[...] = jnp.concatenate([cross, plain, jnp.zeros((6, channels), jnp.float32)], axis=0)


def block_kernel(place, *refs):
    heads = refs[:4]
    w_out, residual, vec, out = refs[4:]
    channels = residual.shape[1]
    block_cells = out.shape[1]
    spot, height, head, cols = place[0], place[1], place[2], place[4]
    for part in range(2):
        base = pl.multiple_of((spot ^ (4 * part)) * block_cells, block_cells)
        total = residual[pl.ds(base, block_cells), :] + vec[10:11, :]
        for step in range(4):
            total = total + dot(heads[step][part], w_out[head ^ step])
        cell = base + lax.broadcasted_iota(jnp.int32, (block_cells, channels), 0)
        out[part] = jnp.where(cell < height * cols, total, 0.0).astype(jnp.bfloat16)


def place_kernel(place, *refs):
    parts, out, gathered = refs[:8], refs[8], refs[9]
    head, column = place[2], place[3]
    lines = parts[0].shape[1]
    for far in range(4):
        for near in range(2):
            part = parts[far * 2 + near]
            for other in range(2):
                quarter = head ^ (near + 2 * other)
                at = pl.ds(pl.multiple_of((column ^ far) * lines, 16), lines)
                gathered[quarter, at, :] = part[other]
    return out


def swap(value, axis, step):
    count = lax.axis_size(axis)
    return lax.ppermute(value, axis, [(k, k ^ step) for k in range(count)])


def pick(stacked, index):
    return lax.dynamic_index_in_dim(stacked, index, 0, keepdims=False)


def reduce_quarters(value, column, image):
    lines = value.shape[0] // 4
    parts = value.reshape(4, lines, value.shape[1])
    total = pick(parts, column).astype(jnp.float32)
    got = [swap(pick(parts, column ^ step), "img", step) for step in (1, 2, 3)]
    for part in got:
        total = total + part.astype(jnp.float32)
    halves = total.reshape(2, lines // 2, value.shape[1])
    away = swap(pick(halves, 1 - image).astype(jnp.bfloat16), "row", 4)
    return (pick(halves, image) + away.astype(jnp.float32)).astype(jnp.bfloat16)


def gather_quarters(chunk, image, column, head):
    other = swap(chunk, "row", 4)
    first = jnp.where(image == 0, chunk, other)
    second = jnp.where(image == 0, other, chunk)
    own = jnp.concatenate([first, second], axis=0)
    pair = jnp.stack([own, swap(own, "row", 2)])
    columns = [pair] + [swap(pair, "img", step) for step in (1, 2, 3)]
    return columns, [swap(part, "row", 1) for part in columns]


def ordered(columns, mates, column, head):
    near = jnp.stack(columns)
    far = jnp.stack(mates)
    both = jnp.stack([near, far])
    chunks = [pick(jnp.swapaxes(both, 0, 1), column ^ k) for k in range(4)]
    line = jnp.stack(chunks)
    line = jnp.transpose(line, (2, 1, 0, 3, 4)).reshape(4, -1, line.shape[-1])
    return jnp.stack([pick(line, head ^ k) for k in range(4)])


def tiled_out(*shapes):
    return [jax.ShapeDtypeStruct(shape, kind) for shape, kind in shapes]


def call(kernel, outs, scratch, limit, place, *operands):
    spec = pl.BlockSpec(memory_space=pltpu.VMEM)
    return pl.pallas_call(
        kernel,
        out_shape=tiled_out(*outs),
        in_specs=[pl.BlockSpec(memory_space=pltpu.SMEM)] + [spec] * len(operands),
        out_specs=[spec] * len(outs),
        scratch_shapes=scratch,
        compiler_params=mib(limit),
    )(place, *operands)


def gather_field(mine, theirs):
    near = swap(mine, "row", 2)
    far = swap(theirs, "row", 4)
    far_near = swap(far, "row", 2)
    return [
        mine,
        swap(mine, "row", 1),
        near,
        swap(near, "row", 1),
        far,
        swap(far, "row", 1),
        far_near,
        swap(far_near, "row", 1),
    ]


def local_image(
    pixels,
    heights,
    timesteps,
    norm1_gain,
    norm1_bias,
    conv1_weight,
    conv1_bias,
    time_weight,
    time_bias,
    norm2_gain,
    norm2_bias,
    conv2_weight,
    conv2_bias,
    norm3_gain,
    norm3_bias,
    qkv_weight,
    qv_bias,
    out_weight,
    out_bias,
    grad_out,
):
    images, row_count, cols, channels = pixels.shape
    block_cells = row_count * cols
    cells = block_cells * lax.axis_size("row")
    half = channels // HEADS
    spot = lax.axis_index("row")
    column = lax.axis_index("img")
    image = spot // HEADS
    head = spot % HEADS
    low, full = jnp.bfloat16, jnp.float32
    height = pick(heights, image)
    place = jnp.stack([spot, height, head, column, jnp.int32(cols)]).astype(jnp.int32)
    pixel_blocks = pixels.reshape(images, block_cells, channels)
    grad_blocks = grad_out.reshape(images, block_cells, channels)
    field = gather_field(pick(pixel_blocks, image), pick(pixel_blocks, 1 - image))
    field = list(lax.optimization_barrier(tuple(field)))
    grad_mine, grad_theirs = pick(grad_blocks, image), pick(grad_blocks, 1 - image)
    grads = gather_field(grad_mine, grad_theirs)

    time_act = jax.nn.silu(embed_steps(timesteps, time_weight.shape[0]))
    own_time = lax.dynamic_slice_in_dim(time_act, image, 1, axis=0)
    shifts = jnp.dot(own_time, time_weight.astype(full), precision=PRECISE) + time_bias.astype(full)
    vec = jnp.concatenate(
        [
            jnp.stack(
                [
                    norm1_gain.astype(full),
                    norm1_bias.astype(full),
                    conv1_bias.astype(full),
                    norm2_gain.astype(full),
                    norm2_bias.astype(full),
                    1.0 + shifts[0, :channels],
                    shifts[0, channels:],
                    conv2_bias.astype(full),
                    norm3_gain.astype(full),
                    norm3_bias.astype(full),
                    out_bias.astype(full),
                ]
            ),
            jnp.zeros((5, channels), full),
        ],
        axis=0,
    )
    w_one = conv1_weight.reshape(3, 3 * channels, channels)
    w_two = conv2_weight.reshape(3, 3 * channels, channels)
    w_one_back = flipped(conv1_weight).reshape(3, 3 * channels, channels)
    w_two_back = flipped(conv2_weight).reshape(3, 3 * channels, channels)
    source = jnp.arange(3 * channels)[:, None]
    target = jnp.arange(3 * half)[None, :]
    wanted = target // half * channels + head * half + target % half
    chosen = (source == wanted).astype(low)
    rim_cells = cells + 2 * cols

    pix, conv_one, residual, act_three, own_one, own_two, stats = call(
        forward_kernel,
        (
            ((cells, channels), low),
            ((cells, channels), full),
            ((cells, channels), full),
            ((cells, channels), low),
            ((rim_cells, 3 * half), low),
            ((rim_cells, 3 * half), low),
            ((8, channels), full),
        ),
        [pltpu.VMEM((rim_cells, 3 * channels), low)],
        40,
        place,
        *field,
        w_one,
        w_two,
        vec,
        chosen,
    )

    head_weight = pick(jnp.moveaxis(qkv_weight.reshape(channels, 3, HEADS, half), 2, 0), head)
    empty = jnp.zeros((channels, half), low)
    w_heads = jnp.concatenate(
        [head_weight[:, 0], empty, head_weight[:, 1], empty, empty, head_weight[:, 2]], axis=1
    )
    head_bias = pick(jnp.moveaxis(qv_bias.reshape(2, HEADS, half), 1, 0), head).astype(full)
    none = jnp.zeros((half,), full)
    biases = jnp.concatenate([head_bias[0], none, none, none, none, head_bias[1]])[None, :]
    out_heads = out_weight.reshape(HEADS, half, channels)
    w_out = jnp.concatenate([empty, pick(out_heads, head).T], axis=1)
    grad_proj, attended, packed, weight_rows, out_sums = call(
        attention_kernel,
        (
            ((cells, channels), low),
            ((cells, half), low),
            ((cells + cells // 2, 2 * half), low),
            ((5 * half, channels), low),
            ((8, channels), full),
        ),
        [
            pltpu.VMEM((cells, 2 * half), low),
            pltpu.VMEM((2 * half, cells), low),
            pltpu.VMEM((cells, 2 * half), low),
            pltpu.VMEM((cells, 2 * half), low),
            pltpu.VMEM((2 * half, cells), full),
            pltpu.VMEM((cells, 2 * half), low),
            pltpu.VMEM((1, cells), full),
        ],
        48,
        place,
        *grads,
        act_three,
        w_heads,
        w_out,
        biases,
    )

    packed_near = swap(packed, "row", 2)
    packed_all = [packed, swap(packed, "row", 1), packed_near, swap(packed_near, "row", 1)]
    qkv_t = jnp.transpose(qkv_weight).reshape(3, HEADS, half, channels)
    w_key_value = jnp.concatenate([qkv_t[1], qkv_t[2]], axis=1)
    grad_res, shifted_two, quarter_two, sums_three = call(
        residual_kernel,
        (
            ((cells, channels), full),
            ((rim_cells, 3 * channels), low),
            ((9 * half, channels), low),
            ((8, channels), full),
        ),
        [pltpu.VMEM((cells, channels), full), pltpu.VMEM((channels, cells), low)],
        40,
        place,
        *packed_all,
        w_key_value,
        qkv_t[0],
        grad_proj,
        residual,
        stats,
        vec,
        own_two,
    )
    early = jnp.concatenate([quarter_two, weight_rows], axis=0)
    early_chunk = reduce_quarters(early, column, image)

    shifted_one, quarter_one, sums_two = call(
        second_kernel,
        (
            ((rim_cells, 3 * channels), low),
            ((9 * half, channels), low),
            ((8, channels), full),
        ),
        [pltpu.VMEM((cells, channels), full), pltpu.VMEM((channels, cells), low)],
        40,
        place,
        shifted_two,
        w_two_back,
        conv_one,
        stats,
        vec,
        own_one,
    )
    late_chunk = reduce_quarters(quarter_one, column, image)

    grad_pair, sums_one = call(
        first_kernel,
        (((2, block_cells, channels), low), ((8, channels), full)),
        [pltpu.VMEM((cells, channels), full)],
        40,
        place,
        shifted_one,
        w_one_back,
        pix,
        grad_res,
        stats,
        vec,
    )

    by_block = attended.reshape(2, HEADS, block_cells, half)

    def blocks_for(step):
        target = head ^ step
        return jnp.stack(
            [pick(pick(by_block, image), target), pick(pick(by_block, 1 - image), target)]
        )

    heads_got = [blocks_for(0)] + [swap(blocks_for(step), "row", step) for step in (1, 2, 3)]
    (block_pair,) = call(
        block_kernel,
        (((2, block_cells, channels), low),),
        [],
        24,
        place,
        *heads_got,
        out_heads,
        residual,
        vec,
    )
    out_pair = jnp.stack([block_pair[0], grad_pair[0]])
    away_pair = swap(jnp.stack([block_pair[1], grad_pair[1]]), "row", 4)
    first_pair = jnp.where(image == 0, out_pair, away_pair)
    second_pair = jnp.where(image == 0, away_pair, out_pair)
    finished = jnp.stack([first_pair, second_pair], axis=1).reshape((2,) + pixels.shape)

    plain, cross = sums_two[1], sums_two[0]
    scale_grad = vec[3] * cross + vec[4] * plain
    which = column * images + image
    all_images = images * lax.axis_size("img")
    own_line = (jnp.arange(all_images) == which).astype(full)
    shift_lines = own_line[:, None] * jnp.concatenate([scale_grad, plain])[None, :]
    own_step = pick(timesteps, image).astype(full)
    step_line = jnp.pad(own_line * own_step, (0, channels - all_images))
    small = jnp.concatenate(
        [
            jnp.stack(
                [
                    sums_one[0],
                    sums_one[1],
                    sums_two[2],
                    vec[5] * cross,
                    vec[5] * plain,
                    sums_three[2],
                    sums_three[0],
                    sums_three[1],
                    out_sums[0],
                    step_line,
                ]
            ),
            shift_lines.reshape(2 * all_images, channels),
        ],
        axis=0,
    )
    small = jnp.where(head == 0, small, 0.0)
    for axis, step in (("row", 1), ("row", 2), ("row", 4), ("img", 1), ("img", 2)):
        small = small + swap(small, axis, step)
    steps_all = small[9, :all_images]
    shift_grads = small[10:].reshape(all_images, 2 * channels)
    time_all = jax.nn.silu(embed_steps(steps_all, time_weight.shape[0]))
    time_weight_grad = jnp.dot(time_all.T, shift_grads, precision=PRECISE)
    time_bias_grad = jnp.sum(shift_grads, axis=0)

    early_all = ordered(*gather_quarters(early_chunk, image, column, head), column, head)
    late_all = ordered(*gather_quarters(late_chunk, image, column, head), column, head)

    def kernel_full(rows_of):
        taps = rows_of.reshape(HEADS, 3, 3, half, channels)
        taps = jnp.transpose(taps, (1, 2, 0, 3, 4)).reshape(3, 3, channels, channels)
        return taps.astype(full)

    nine = 9 * half
    conv1_weight_grad = kernel_full(late_all)
    conv2_weight_grad = kernel_full(early_all[:, :nine])
    proj_rows = early_all[:, nine : nine + 3 * half].reshape(HEADS, 3, half, channels)
    qkv_weight_grad = jnp.transpose(proj_rows, (3, 1, 0, 2)).reshape(channels, -1).astype(full)
    out_weight_grad = (
        early_all[:, nine + 3 * half : nine + 4 * half].reshape(channels, channels).astype(full)
    )
    bias_row = early_all[:, nine + 4 * half].astype(full)
    qv_bias_grad = jnp.concatenate(
        [bias_row[:, :half].reshape(-1), bias_row[:, 3 * half :].reshape(-1)]
    )
    return (
        finished[0],
        finished[1],
        small[0],
        small[1],
        conv1_weight_grad,
        small[2],
        time_weight_grad,
        time_bias_grad,
        small[3],
        small[4],
        conv2_weight_grad,
        small[5],
        small[6],
        small[7],
        qkv_weight_grad,
        qv_bias_grad,
        out_weight_grad,
        small[8],
    )


def local(*arrays):
    pixels = arrays[0]
    if lax.axis_size("row") == pixels.shape[0] * HEADS and lax.axis_size("img") == 4:
        return local_image(*arrays)
    return local_rows(*arrays)


def solution(mesh):
    placed = (
        P("img", "row", None, None),
        P("img"),
        P("img"),
        P(),
        P(),
        P(),
        P(),
        P(),
        P(),
        P(),
        P(),
        P(),
        P(),
        P(),
        P(),
        P(),
        P(),
        P(),
        P(),
        P("img", "row", None, None),
    )
    return jax.shard_map(
        local,
        mesh=mesh,
        in_specs=placed,
        out_specs=(
            P("img", "row", None, None),
            P("img", "row", None, None),
            P(),
            P(),
            P(),
            P(),
            P(),
            P(),
            P(),
            P(),
            P(),
            P(),
            P(),
            P(),
            P(),
            P(),
            P(),
            P(),
        ),
        check_vma=False,
    )
```

```python
import functools
import math

import jax
import jax.numpy as jnp
from jax import lax
from jax.experimental import pallas as pl
from jax.experimental.pallas import tpu as pltpu
from jax.sharding import PartitionSpec as P

GROUPS = 32
HEADS = 4


EPSILON = 1e-05
MASKED = -1000000000.0
PRECISE = lax.Precision.HIGHEST


def with_halo(cells, sides, width):
    for axis, dim in sides:
        count = lax.axis_size(axis)
        ends = count - 1
        head = lax.slice_in_dim(cells, 0, width, axis=dim)
        tail = lax.slice_in_dim(cells, cells.shape[dim] - width, cells.shape[dim], axis=dim)
        cells = jnp.concatenate(
            [
                lax.ppermute(tail, axis, [(i, (i + 1) % count) for i in range(ends)]),
                cells,
                lax.ppermute(head, axis, [((i + 1) % count, i) for i in range(ends)]),
            ],
            axis=dim,
        )
    return cells


def embed_steps(timesteps, time_width):
    half_dim = time_width // 2
    frequency = jnp.exp(-math.log(10000.0) * jnp.arange(half_dim, dtype=jnp.float32) / half_dim)
    angles = timesteps.astype(jnp.float32)[:, None] * frequency[None, :]
    return jnp.concatenate([jnp.cos(angles), jnp.sin(angles)], axis=1)


def silu_slope(pre_act):
    sigmoid = jax.nn.sigmoid(pre_act)
    return sigmoid * (1.0 + pre_act * (1.0 - sigmoid))


def with_rims(field_in):
    return with_halo(field_in, (("row", 1),), 1)


def conv_rows(padded, kernel):
    return lax.conv_general_dilated(
        padded,
        kernel,
        (1, 1),
        ((0, 0), (1, 1)),
        dimension_numbers=("NHWC", "HWIO", "NHWC"),
        preferred_element_type=jnp.float32,
    )


def flipped(kernel):
    return jnp.transpose(kernel[::-1, ::-1], (0, 1, 3, 2))


def kernel_grad(padded, grad_field):
    row_count = grad_field.shape[1]
    col_count = grad_field.shape[2]
    widened = jnp.pad(padded, ((0, 0), (0, 0), (1, 1), (0, 0)))
    tap_rows = []
    for tap_row in range(3):
        tap_line = []
        for tap_col in range(3):
            window = widened[:, tap_row : tap_row + row_count, tap_col : tap_col + col_count, :]
            tap_line.append(
                jnp.einsum("brwc,brwd->cd", window, grad_field, preferred_element_type=jnp.float32)
            )
        tap_rows.append(jnp.stack(tap_line))
    return jnp.stack(tap_rows)


def norm_forward(field_in, cell_mask, cell_count, group_count):
    shaped = field_in.reshape(field_in.shape[:3] + (group_count, field_in.shape[3] // group_count))
    first_sum = lax.psum(jnp.sum(shaped * cell_mask, axis=(1, 2, 4)), "row")
    center = first_sum / cell_count[:, None]
    centred = shaped - center[:, None, None, :, None]
    spread_sum = lax.psum(jnp.sum(jnp.square(centred * cell_mask), axis=(1, 2, 4)), "row")
    spread = spread_sum / cell_count[:, None]
    inverse = lax.rsqrt(spread + EPSILON)
    return (centred * inverse[:, None, None, :, None], inverse)


def norm_backward(grad_normed, normalized, inverse, gain_in, cell_mask, cell_count):
    full_shape = grad_normed.shape
    flat_norm = normalized.reshape(full_shape)
    gain_grad = jnp.sum(grad_normed * flat_norm, axis=(0, 1, 2))
    shift_grad = jnp.sum(grad_normed, axis=(0, 1, 2))
    scaled = (grad_normed * gain_in).reshape(normalized.shape)
    sum_plain, sum_cross = lax.psum(
        (
            jnp.sum(scaled * cell_mask, axis=(1, 2, 4)),
            jnp.sum(scaled * normalized * cell_mask, axis=(1, 2, 4)),
        ),
        "row",
    )
    mean_plain = sum_plain / cell_count[:, None]
    mean_cross = sum_cross / cell_count[:, None]
    grad_in = (
        (
            scaled
            - mean_plain[:, None, None, :, None]
            - normalized * mean_cross[:, None, None, :, None]
        )
        * inverse[:, None, None, :, None]
        * cell_mask
    )
    return (grad_in.reshape(full_shape), gain_grad, shift_grad)


def local_rows(
    pixels,
    heights,
    timesteps,
    norm1_gain,
    norm1_bias,
    conv1_weight,
    conv1_bias,
    time_weight,
    time_bias,
    norm2_gain,
    norm2_bias,
    conv2_weight,
    conv2_bias,
    norm3_gain,
    norm3_bias,
    qkv_weight,
    qv_bias,
    out_weight,
    out_bias,
    grad_out,
):
    image_count, row_count, col_count, channels = pixels.shape
    group_count = GROUPS
    head_count = HEADS
    head_width = channels // head_count
    query_count = row_count * col_count
    scaling = head_width ** (-0.5)
    head_shape = (image_count, query_count, head_count, head_width)
    row_ids = lax.axis_index("row") * row_count + jnp.arange(row_count, dtype=jnp.int32)
    row_valid = row_ids[None, :] < heights[:, None]
    row_mask = row_valid.astype(jnp.float32)
    cell_rows = row_mask[:, :, None, None]
    cell_mask = row_mask[:, :, None, None, None]
    own_valid = jnp.repeat(row_valid, col_count, axis=1)[:, None, None, :]
    cell_count = heights.astype(jnp.float32) * (col_count * (channels // group_count))
    gain_one = norm1_gain.astype(jnp.float32)
    gain_two = norm2_gain.astype(jnp.float32)
    gain_three = norm3_gain.astype(jnp.float32)
    field_in = pixels.astype(jnp.float32)
    normed_one, inverse_one = norm_forward(field_in, cell_mask, cell_count, group_count)
    pre_one = normed_one.reshape(field_in.shape) * gain_one + norm1_bias.astype(jnp.float32)
    act_one = (jax.nn.silu(pre_one) * cell_rows).astype(jnp.bfloat16)
    padded_one = with_rims(act_one)
    conv_one = conv_rows(padded_one, conv1_weight) + conv1_bias.astype(jnp.float32)
    time_act = jax.nn.silu(embed_steps(timesteps, time_weight.shape[0]))
    shifts = jnp.dot(
        time_act, time_weight.astype(jnp.float32), precision=PRECISE
    ) + time_bias.astype(jnp.float32)
    scale_part = 1.0 + shifts[:, None, None, :channels]
    shift_part = shifts[:, None, None, channels:]
    normed_two, inverse_two = norm_forward(conv_one, cell_mask, cell_count, group_count)
    affine_two = normed_two.reshape(field_in.shape) * gain_two + norm2_bias.astype(jnp.float32)
    pre_two = affine_two * scale_part + shift_part
    act_two = (jax.nn.silu(pre_two) * cell_rows).astype(jnp.bfloat16)
    padded_two = with_rims(act_two)
    residual = field_in + (conv_rows(padded_two, conv2_weight) + conv2_bias.astype(jnp.float32))
    normed_three, inverse_three = norm_forward(residual, cell_mask, cell_count, group_count)
    act_three = (
        normed_three.reshape(field_in.shape) * gain_three + norm3_bias.astype(jnp.float32)
    ).astype(jnp.bfloat16)
    projected = jnp.einsum(
        "brwc,cd->brwd", act_three, qkv_weight, preferred_element_type=jnp.float32
    )
    qv_float = qv_bias.astype(jnp.float32)
    queries = (projected[..., :channels] + qv_float[:channels]).astype(jnp.bfloat16)
    keys_own = projected[..., channels : 2 * channels].astype(jnp.bfloat16)
    values_own = (projected[..., 2 * channels :] + qv_float[channels:]).astype(jnp.bfloat16)
    query_heads = queries.reshape(head_shape)
    key_heads = keys_own.reshape(head_shape)
    value_heads = values_own.reshape(head_shape)

    def flatten_rows(piece_arr):
        return piece_arr.reshape(
            image_count, piece_arr.shape[1] * col_count, head_count, head_width
        )

    def key_mask(span_rows):
        key_rows = jnp.arange(span_rows, dtype=jnp.int32)
        return jnp.repeat(key_rows[None, :] < heights[:, None], col_count, axis=1)[:, None, None, :]

    top_init = jnp.full((image_count, query_count, head_count), MASKED, jnp.float32)
    piece_keys = lax.all_gather(keys_own, "row", axis=1, tiled=True)
    piece_values = lax.all_gather(values_own, "row", axis=1, tiled=True)
    key_valid = key_mask(piece_keys.shape[1])
    scores = (
        jnp.einsum(
            "bqhd,bkhd->bqhk",
            query_heads,
            flatten_rows(piece_keys),
            preferred_element_type=jnp.float32,
        )
        * scaling
    )
    scores = jnp.where(key_valid, scores, MASKED)
    new_top = jnp.maximum(top_init, jnp.max(scores, axis=3))
    weights = jnp.where(key_valid, jnp.exp(scores - new_top[..., None]), 0.0)
    running_total = jnp.sum(weights, axis=3)
    running_acc = jnp.einsum(
        "bqhk,bkhd->bqhd",
        weights.astype(jnp.bfloat16),
        flatten_rows(piece_values),
        preferred_element_type=jnp.float32,
    )
    attn_float = running_acc / running_total[..., None]
    log_total = new_top + jnp.log(running_total)
    attended = attn_float.reshape(pixels.shape).astype(jnp.bfloat16)
    output_proj = jnp.einsum(
        "brwc,cd->brwd", attended, out_weight, preferred_element_type=jnp.float32
    ) + out_bias.astype(jnp.float32)
    block_out = ((residual + output_proj) * cell_rows).astype(jnp.bfloat16)
    grad_proj = grad_out.astype(jnp.float32) * cell_rows
    grad_proj_low = grad_proj.astype(jnp.bfloat16)
    out_weight_grad = jnp.einsum(
        "brwc,brwd->cd", attended, grad_proj_low, preferred_element_type=jnp.float32
    )
    out_bias_grad = jnp.sum(grad_proj, axis=(0, 1, 2))
    grad_attended = jnp.einsum(
        "brwd,cd->brwc", grad_proj_low, out_weight, preferred_element_type=jnp.float32
    ).astype(jnp.bfloat16)
    grad_heads = grad_attended.reshape(head_shape)
    delta_own = jnp.sum(grad_heads.astype(jnp.float32) * attn_float, axis=3)
    stat_shape = (image_count, row_count, col_count, head_count)
    all_lse, all_delta = (
        lax.all_gather(log_total.reshape(stat_shape), "row", axis=1, tiled=True),
        lax.all_gather(delta_own.reshape(stat_shape), "row", axis=1, tiled=True),
    )
    piece_keys = lax.all_gather(keys_own, "row", axis=1, tiled=True)
    piece_values = lax.all_gather(values_own, "row", axis=1, tiled=True)
    flat_keys = flatten_rows(piece_keys)
    key_valid = key_mask(piece_keys.shape[1])
    scores = (
        jnp.einsum("bqhd,bkhd->bqhk", query_heads, flat_keys, preferred_element_type=jnp.float32)
        * scaling
    )
    soft_weights = jnp.where(key_valid, jnp.exp(scores - log_total[..., None]), 0.0)
    grad_probs = jnp.einsum(
        "bqhd,bkhd->bqhk",
        grad_heads,
        flatten_rows(piece_values),
        preferred_element_type=jnp.float32,
    )
    grad_scores = (soft_weights * (grad_probs - delta_own[..., None])).astype(jnp.bfloat16)
    grad_query_sum = jnp.einsum(
        "bqhk,bkhd->bqhd", grad_scores, flat_keys, preferred_element_type=jnp.float32
    )
    piece_queries = lax.all_gather(queries, "row", axis=1, tiled=True)
    piece_grads = lax.all_gather(grad_attended, "row", axis=1, tiled=True)
    flat_queries = flatten_rows(piece_queries)
    flat_grads = flatten_rows(piece_grads)
    span_rows = piece_queries.shape[1]
    piece_lse = all_lse.reshape(image_count, span_rows * col_count, head_count)
    piece_delta = all_delta.reshape(image_count, span_rows * col_count, head_count)
    scores = (
        jnp.einsum("bqhd,bkhd->bqhk", flat_queries, key_heads, preferred_element_type=jnp.float32)
        * scaling
    )
    soft_weights = jnp.where(own_valid, jnp.exp(scores - piece_lse[..., None]), 0.0)
    value_term = jnp.einsum(
        "bqhk,bqhd->bkhd",
        soft_weights.astype(jnp.bfloat16),
        flat_grads,
        preferred_element_type=jnp.float32,
    )
    grad_probs = jnp.einsum(
        "bqhd,bkhd->bqhk", flat_grads, value_heads, preferred_element_type=jnp.float32
    )
    grad_scores = (soft_weights * (grad_probs - piece_delta[..., None])).astype(jnp.bfloat16)
    key_term = jnp.einsum(
        "bqhk,bqhd->bkhd", grad_scores, flat_queries, preferred_element_type=jnp.float32
    )
    key_term, value_term = (key_term, value_term)
    grad_queries = (grad_query_sum * scaling).reshape(pixels.shape).astype(jnp.bfloat16)
    grad_keys = (key_term * scaling).reshape(pixels.shape).astype(jnp.bfloat16)
    grad_values = value_term.reshape(pixels.shape).astype(jnp.bfloat16)
    grad_projected = jnp.concatenate([grad_queries, grad_keys, grad_values], axis=3)
    qkv_weight_grad = jnp.einsum(
        "brwc,brwd->cd", act_three, grad_projected, preferred_element_type=jnp.float32
    )
    qv_bias_grad = jnp.concatenate(
        [
            jnp.sum(grad_queries.astype(jnp.float32), axis=(0, 1, 2)),
            jnp.sum(grad_values.astype(jnp.float32), axis=(0, 1, 2)),
        ]
    )
    grad_act_three = jnp.einsum(
        "brwd,cd->brwc", grad_projected, qkv_weight, preferred_element_type=jnp.float32
    )
    grad_res_attn, norm3_gain_grad, norm3_bias_grad = norm_backward(
        grad_act_three, normed_three, inverse_three, gain_three, cell_mask, cell_count
    )
    grad_residual = grad_proj + grad_res_attn
    grad_conv_two = grad_residual.astype(jnp.bfloat16)
    conv2_bias_grad = jnp.sum(grad_residual, axis=(0, 1, 2))
    conv2_weight_grad = kernel_grad(padded_two, grad_conv_two)
    grad_act_two = conv_rows(with_rims(grad_conv_two), flipped(conv2_weight)) * cell_rows
    grad_pre_two = grad_act_two * silu_slope(pre_two)
    scale_grad = jnp.sum(grad_pre_two * affine_two, axis=(1, 2))
    shift_grad = jnp.sum(grad_pre_two, axis=(1, 2))
    shift_grads = jnp.concatenate([scale_grad, shift_grad], axis=1)
    grad_conv_one, norm2_gain_grad, norm2_bias_grad = norm_backward(
        grad_pre_two * scale_part, normed_two, inverse_two, gain_two, cell_mask, cell_count
    )
    conv_one_low = grad_conv_one.astype(jnp.bfloat16)
    conv1_bias_grad = jnp.sum(grad_conv_one, axis=(0, 1, 2))
    conv1_weight_grad = kernel_grad(padded_one, conv_one_low)
    grad_act_one = conv_rows(with_rims(conv_one_low), flipped(conv1_weight)) * cell_rows
    grad_pre_one = grad_act_one * silu_slope(pre_one)
    grad_field_norm, norm1_gain_grad, norm1_bias_grad = norm_backward(
        grad_pre_one, normed_one, inverse_one, gain_one, cell_mask, cell_count
    )
    grad_pixels = (grad_residual + grad_field_norm).astype(jnp.bfloat16)
    time_weight_grad = jnp.dot(time_act.T, shift_grads, precision=PRECISE)
    time_bias_grad = jnp.sum(shift_grads, axis=0)
    summed = lax.psum(
        (
            norm1_gain_grad,
            norm1_bias_grad,
            conv1_weight_grad,
            conv1_bias_grad,
            time_weight_grad,
            time_bias_grad,
            norm2_gain_grad,
            norm2_bias_grad,
            conv2_weight_grad,
            conv2_bias_grad,
            norm3_gain_grad,
            norm3_bias_grad,
            qkv_weight_grad,
            qv_bias_grad,
            out_weight_grad,
            out_bias_grad,
        ),
        ("img", "row"),
    )
    return (
        block_out,
        grad_pixels,
        summed[0],
        summed[1],
        summed[2],
        summed[3],
        summed[4],
        summed[5],
        summed[6],
        summed[7],
        summed[8],
        summed[9],
        summed[10],
        summed[11],
        summed[12],
        summed[13],
        summed[14],
        summed[15],
    )


def mib(count):
    return pltpu.CompilerParams(vmem_limit_bytes=count * 2**20)


def dot(left, right):
    return jnp.dot(left, right, preferred_element_type=jnp.float32)


def dot_rows(left, right):
    return lax.dot_general(
        left, right, (((1,), (1,)), ((), ())), preferred_element_type=jnp.float32
    )


def fold(tile):
    return jnp.sum(tile.reshape(-1, 8, tile.shape[1]), axis=0)


def group_sums(row, width):
    channels = row.shape[1]
    rows = lax.broadcasted_iota(jnp.int32, (channels, channels), 0) // width
    cols = lax.broadcasted_iota(jnp.int32, (channels, channels), 1) // width
    same = jnp.where(rows == cols, 1.0, 0.0).astype(jnp.bfloat16)
    wide = jnp.broadcast_to(row, (16, channels))
    total = None
    for _ in range(3):
        term = wide.astype(jnp.bfloat16)
        wide = wide - term.astype(jnp.float32)
        part = dot(term, same)
        total = part if total is None else total + part
    return total[0:1]


def row_at(index, cols):
    return pl.ds(pl.multiple_of(index * cols, cols), cols)


def total_of(tile):
    return jnp.sum(tile, axis=0, keepdims=True)


def field_stats(read, height, rows, cols, channels):
    width = channels // GROUPS
    each = (height * cols).astype(jnp.float32)
    about = jnp.sum(read(0), axis=0, keepdims=True) * (1.0 / cols)
    zero = jnp.zeros((8, channels), jnp.float32)

    def add(index, totals):
        off = (read(index) - about) * valid_row(index, height)
        return totals[0] + fold(off), totals[1] + fold(off * off)

    first, square = lax.fori_loop(0, rows, add, (zero, zero), unroll=4)
    first, square = total_of(first), total_of(square)
    mean = group_sums(first + about * each, width) / (each * width)
    shift = about - mean
    spread = group_sums(square + 2.0 * first * shift + each * shift * shift, width)
    return mean, lax.rsqrt(spread / (each * width) + EPSILON)


def half_line(mean, inverse, gain, bias, scale=1.0, shift=0.0):
    slope = inverse * gain
    start = bias - mean * slope
    return 0.5 * slope * scale, 0.5 * (start * scale + shift)


def put_shifted(ref, index, tile, cols):
    channels = tile.shape[1]
    column = lax.broadcasted_iota(jnp.int32, tile.shape, 0)
    before = jnp.where(column == 0, 0.0, pltpu.roll(tile, 1, 0))
    after = jnp.where(column == cols - 1, 0.0, pltpu.roll(tile, cols - 1, 0))
    at = row_at(index + 1, cols)
    ref[at, 0:channels] = before.astype(jnp.bfloat16)
    ref[at, channels : 2 * channels] = tile.astype(jnp.bfloat16)
    ref[at, 2 * channels : 3 * channels] = after.astype(jnp.bfloat16)


def clear_rims(ref, cols):
    edge = jnp.zeros((cols, ref.shape[1]), ref.dtype)
    ref[0:cols, :] = edge
    ref[ref.shape[0] - cols : ref.shape[0], :] = edge


def conv_shifted(shifted, weight, out, bias, cols, added=None):
    step = 8 * cols

    def block(index, carry):
        base = index * step
        total = bias
        for tap in range(3):
            at = pl.ds(pl.multiple_of(base + tap * cols, cols), step)
            total = total + dot(shifted[at, :], weight[tap])
        if added is not None:
            total = total + added[pl.ds(pl.multiple_of(base, step), step), :].astype(jnp.float32)
        out[pl.ds(pl.multiple_of(base, step), step), :] = total
        return carry

    lax.fori_loop(0, out.shape[0] // step, block, 0)


def kernel_quarter(shifted, own_t, out, cols):
    cells = own_t.shape[2]
    channels = shifted.shape[1] // 3
    width = own_t.shape[1]
    grad = shifted[cols : cols + cells, channels : 2 * channels]
    for tap in range(3):
        out[tap * width : (tap + 1) * width, :] = dot(own_t[tap], grad).astype(jnp.bfloat16)


def own_place(vec):
    spot = lax.axis_index("row")
    image, head = spot // HEADS, spot % HEADS
    return spot, head, image, jnp.max(vec[11:12, :]).astype(jnp.int32)


def started(sems, *pairs):
    copies = [pltpu.make_async_copy(src, dst, sems.at[k]) for k, (src, dst) in enumerate(pairs)]
    for copy in copies:
        copy.start()
    return copies


def finish_all(copies):
    for copy in copies:
        copy.wait()


def valid_row(index, height):
    return jnp.where(index < height, 1.0, 0.0).astype(jnp.float32)


def forward_kernel(vec, *refs):
    blocks, (w_one_far, w_two_far) = refs[:8], refs[8:10]
    act_three, pix_far, conv_far, residual_far, act_one_far, act_two_far, stats_far = refs[10:17]
    pix, conv_one, residual, stats, w_one, w_two, shift_one, shift_two, in_sems, out_sems = refs[17:]
    cells, channels = pix.shape
    block_cells = blocks[0].shape[0]
    cols = (shift_one.shape[0] - cells) // 2
    rows = cells // cols
    spot, _, _, height = own_place(vec)
    pairs = []
    for step, block in enumerate(blocks):
        base = pl.multiple_of((spot ^ step) * block_cells, block_cells)
        pairs.append((block, pix.at[pl.ds(base, block_cells), :]))
    arriving = started(in_sems, *pairs, (w_one_far, w_one), (w_two_far, w_two))
    gain_one, bias_one, conv_bias_one, gain_two, bias_two = (vec[k : k + 1, :] for k in range(5))
    scale, shift, conv_bias_two, gain_three, bias_three = (vec[k : k + 1, :] for k in range(5, 10))
    inner = (pl.ds(cols, cells), pl.ds(channels, channels))

    def read_pix(index):
        return pix[row_at(index, cols), :].astype(jnp.float32)

    def read_conv(index):
        return conv_one[row_at(index, cols), :]

    def read_res(index):
        return residual[row_at(index, cols), :]

    def activate(read, line, shifted):
        def body(index, carry):
            part = read(index) * line[0] + line[1]
            part = (part + part * jnp.tanh(part)) * valid_row(index, height)
            put_shifted(shifted, index, part, cols)
            return carry

        lax.fori_loop(0, rows, body, 0, unroll=2)

    clear_rims(shift_one, cols)
    clear_rims(shift_two, cols)
    finish_all(arriving[:8])
    leaving = started(out_sems, (pix, pix_far))
    mean_one, inv_one = field_stats(read_pix, height, rows, cols, channels)
    activate(read_pix, half_line(mean_one, inv_one, gain_one, bias_one), shift_one)
    leaving += started(out_sems.at[1:2], (shift_one.at[inner], act_one_far))
    arriving[8].wait()
    conv_shifted(shift_one, w_one, conv_one, conv_bias_one, cols)
    leaving += started(out_sems.at[2:3], (conv_one, conv_far))
    mean_two, inv_two = field_stats(read_conv, height, rows, cols, channels)
    line = half_line(mean_two, inv_two, gain_two, bias_two, scale, shift)
    activate(read_conv, line, shift_two)
    leaving += started(out_sems.at[3:4], (shift_two.at[inner], act_two_far))
    arriving[9].wait()
    conv_shifted(shift_two, w_two, residual, conv_bias_two, cols, pix)
    leaving += started(out_sems.at[4:5], (residual, residual_far))
    mean_three, inv_three = field_stats(read_res, height, rows, cols, channels)
    stats[...] = jnp.concatenate(
        [mean_one, inv_one, mean_two, inv_two, mean_three, inv_three, mean_one, mean_one], axis=0
    )
    leaving += started(out_sems.at[5:6], (stats, stats_far))
    slope = inv_three * gain_three
    start = bias_three - mean_three * slope

    def third(index, carry):
        act_three[row_at(index, cols), :] = (read_res(index) * slope + start).astype(jnp.bfloat16)
        return carry

    lax.fori_loop(0, rows, third, 0, unroll=4)
    finish_all(leaving)


def attention_kernel(columns, vec, act_three, w_heads, w_out, biases, *refs):
    blocks = refs[:8]
    value_key_far, query_far, grad_far, mixed_far, sums_far = refs[8:13]
    (
        grad_blocks, grad_proj, value_key, query_part, sums,
        query_grad, key_pad, value_pad, heads_t, mixed, mask_row, in_sems, out_sems,
    ) = refs[13:]
    cells, channels = act_three.shape
    block_cells = blocks[0].shape[0]
    spot, _, _, height = own_place(vec)
    half = mixed.shape[1] // 2
    cols = columns
    scaling = half**-0.5
    valid_cells = height * cols
    step = 256
    pairs = []
    for index, block in enumerate(blocks):
        base = pl.multiple_of((spot ^ index) * block_cells, block_cells)
        pairs.append((block, grad_blocks.at[pl.ds(base, block_cells), :]))
    arriving = started(in_sems, *pairs)

    def project(index, carry):
        at = pl.ds(pl.multiple_of(index * 512, 512), 512)
        parts = dot(act_three[at, :], w_heads[...]) + biases[0:1, :]
        query_grad[at, :] = parts[:, 0 : 2 * half].astype(jnp.bfloat16) * jnp.bfloat16(scaling)
        key_pad[at, :] = parts[:, 2 * half : 4 * half].astype(jnp.bfloat16)
        value_pad[at, :] = parts[:, 4 * half : 6 * half].astype(jnp.bfloat16)
        query, key = parts[:, 0 : 2 * half], parts[:, 2 * half : 4 * half]
        query_size = jnp.sum(query * query, axis=1, keepdims=True) * (scaling * scaling)
        key_size = jnp.sum(key * key, axis=1, keepdims=True)
        return jnp.maximum(carry[0], jnp.max(query_size)), jnp.maximum(carry[1], jnp.max(key_size))

    norms = lax.fori_loop(0, cells // 512, project, (jnp.float32(0.0), jnp.float32(0.0)))
    lane = lax.broadcasted_iota(jnp.int32, (1, cells), 1)
    mask_row[...] = jnp.where(lane < valid_cells, 0.0, MASKED)
    heads_t[...] = jnp.zeros(heads_t.shape, jnp.float32)
    mixed[...] = jnp.zeros(mixed.shape, jnp.bfloat16)
    finish_all(arriving)

    def clean(index, total):
        at = pl.ds(pl.multiple_of(index * block_cells, block_cells), block_cells)
        cell = index * block_cells + lax.broadcasted_iota(jnp.int32, (block_cells, channels), 0)
        kept = jnp.where(cell < valid_cells, grad_blocks[at, :].astype(jnp.float32), 0.0)
        low = kept.astype(jnp.bfloat16)
        grad_proj[at, :] = low
        query_grad[at, :] = query_grad[at, :] + dot(low, w_out[...]).astype(jnp.bfloat16)
        return total + fold(kept)

    total = lax.fori_loop(
        0, cells // block_cells, clean, jnp.zeros((8, channels), jnp.float32)
    )
    sums[...] = jnp.concatenate([total_of(total), jnp.zeros((7, channels), jnp.float32)], axis=0)
    leaving = started(out_sems, (grad_proj, grad_far), (sums, sums_far))

    def query_block(shifted, index, carry):
        at = pl.ds(pl.multiple_of(index * step, step), step)
        both = query_grad[at, :]
        scores = dot_rows(both, key_pad[...]) + mask_row[...]
        if shifted:
            scores = scores - jnp.max(scores, axis=1, keepdims=True)
        weights = jnp.exp(scores)
        total = jnp.zeros((step, 2 * half), jnp.float32)
        for start in range(0, cells, 2 * half):
            total = total + weights[:, start : start + 2 * half]
        inverse = 1.0 / jnp.sum(total, axis=1, keepdims=True)
        low = weights.astype(jnp.bfloat16)
        out = dot(low, value_pad[...]) * inverse
        wide = both.astype(jnp.float32)
        delta = jnp.sum(wide * out, axis=1, keepdims=True)
        turned = jnp.transpose(wide * inverse).astype(jnp.bfloat16)
        grad_probs = dot_rows(both, value_pad[...])
        grad_scores = (low.astype(jnp.float32) * (grad_probs - delta)).astype(jnp.bfloat16)
        grad_query = dot(grad_scores, key_pad[...]) * (inverse * scaling)
        mixed[at, :] = (out + grad_query).astype(jnp.bfloat16)
        heads_t[0:half, :] += dot(turned[0:half], grad_scores)
        heads_t[half : 2 * half, :] += dot(turned[half : 2 * half], low)
        return carry

    query_most, key_most = norms
    narrow = query_most * key_most <= 3600.0

    @pl.when(narrow)
    def _():
        lax.fori_loop(0, cells // step, functools.partial(query_block, False), 0, unroll=2)

    @pl.when(jnp.logical_not(narrow))
    def _():
        count = (valid_cells + step - 1) // step
        lax.fori_loop(0, count, functools.partial(query_block, True), 0)

    for start in range(0, cells, step):
        value_key[start : start + step, :] = jnp.transpose(heads_t[:, start : start + step]).astype(
            jnp.bfloat16
        )
    query_part[:, 0:half] = mixed[0 : cells // 2, 0:half]
    query_part[:, half : 2 * half] = mixed[cells // 2 : cells, 0:half]
    leaving += started(
        out_sems.at[2:5], (value_key, value_key_far), (query_part, query_far), (mixed, mixed_far)
    )
    finish_all(leaving)


def aside_kernel(vec, *refs):
    act_far, (mixed_far, value_key_far, act_three_far, grad_far) = refs[0:2], refs[2:6]
    own_far, weight_far, sends = refs[6:8], refs[8], refs[9:13]
    acts, mixed, value_key, act_three, grad_proj, padded, own, weight_rows, in_sems, out_sems = (
        refs[13:]
    )
    cells, channels = act_three.shape
    cols = (padded.shape[0] - cells) // 2
    lanes = mixed.shape[1]
    half = lanes // 2
    spot, head, image, _ = own_place(vec)
    arriving = started(
        in_sems,
        (mixed_far, mixed),
        (value_key_far, value_key),
        (act_three_far, act_three),
        (grad_far, grad_proj),
        (act_far[0], acts.at[0]),
        (act_far[1], acts.at[1]),
    )
    block_cells = sends[0].shape[1]
    step = 256
    arriving[0].wait()
    for k, send in enumerate(sends):
        for part in range(2):
            block = (head ^ k) + HEADS * (image ^ part)
            at = pl.ds(pl.multiple_of(block * block_cells, block_cells), block_cells)
            send[part] = mixed[at, :]
    finish_all(arriving[1:4])

    def gather(index, totals):
        at = pl.ds(pl.multiple_of(index * step, step), step)
        low_mixed, low_heads, act = mixed[at, :], value_key[at, :], act_three[at, :]
        mixed_t = jnp.transpose(low_mixed.astype(jnp.float32)).astype(jnp.bfloat16)
        heads_t = jnp.transpose(low_heads.astype(jnp.float32)).astype(jnp.bfloat16)
        return (
            totals[0] + dot(mixed_t, act),
            totals[1] + dot(heads_t, act),
            totals[2] + dot(mixed_t, grad_proj[at, :]),
            totals[3] + fold(low_mixed.astype(jnp.float32)),
            totals[4] + fold(low_heads.astype(jnp.float32)),
        )

    square = jnp.zeros((lanes, channels), jnp.float32)
    line = jnp.zeros((8, lanes), jnp.float32)
    from_query, from_heads, from_out, query_sum, value_sum = lax.fori_loop(
        0, cells // step, gather, (square, square, square, line, line)
    )
    weight_rows[0:half, :] = from_query[0:half].astype(jnp.bfloat16)
    weight_rows[half : 3 * half, :] = from_heads.astype(jnp.bfloat16)
    weight_rows[3 * half : 4 * half, :] = from_out[half:lanes].astype(jnp.bfloat16)
    which = lax.axis_index("img") * 2 + image
    lane = lax.broadcasted_iota(jnp.int32, (1, channels), 1)
    now = jnp.max(vec[12:13, :]).astype(jnp.int32)
    high = jnp.where(lane == which, (now // 32).astype(jnp.float32), 0.0)
    rest = jnp.where(lane == which, (now % 32).astype(jnp.float32), 0.0)
    row = jnp.concatenate([total_of(query_sum), total_of(value_sum)], axis=1)
    below = jnp.zeros((weight_rows.shape[0] - 4 * half - 3, channels), jnp.float32)
    weight_rows[4 * half :, :] = jnp.concatenate([row, high, rest, below], axis=0).astype(
        jnp.bfloat16
    )
    source = lax.broadcasted_iota(jnp.int32, (channels, 3 * half), 0)
    target = lax.broadcasted_iota(jnp.int32, (channels, 3 * half), 1)
    chosen = jnp.where(source == head * half + target % half, 1.0, 0.0).astype(jnp.bfloat16)
    lane = lax.broadcasted_iota(jnp.int32, (step, 3 * half), 1)
    column = lax.broadcasted_iota(jnp.int32, (step, 3 * half), 0) % cols
    leaving = started(out_sems.at[2:3], (weight_rows, weight_far))
    for k in range(2):
        arriving[4 + k].wait()
        clear_rims(padded, cols)

        def widen(index, carry):
            at = pl.ds(pl.multiple_of(index * step, step), step)
            tile = dot(acts[k, at, :], chosen)
            before = jnp.where(column == 0, 0.0, pltpu.roll(tile, 1, 0))
            after = jnp.where(column == cols - 1, 0.0, pltpu.roll(tile, step - 1, 0))
            tile = jnp.where(lane < half, before, jnp.where(lane < 2 * half, tile, after))
            padded[pl.ds(pl.multiple_of(index * step + cols, cols), step), :] = tile
            return carry

        lax.fori_loop(0, cells // step, widen, 0)
        for tap in range(3):

            def turn(index, carry):
                at = pl.ds(pl.multiple_of(index * step + tap * cols, cols), step)
                to = pl.ds(pl.multiple_of(index * step, step), step)
                own[k, tap, :, to] = jnp.transpose(padded[at, :]).astype(jnp.bfloat16)
                return carry

            lax.fori_loop(0, cells // step, turn, 0)
        leaving += started(out_sems.at[k : k + 1], (own.at[k], own_far[k]))
    finish_all(leaving)


def residual_kernel(vec, qkv_t, *refs):
    heads_far, sides_far = refs[0:8:2], refs[1:8:2]
    grad_far, residual_far, stats_far, own_far, weight_far = refs[8:13]
    shifted, grad_res_far, quarter_far, sums_far = refs[13:17]
    (
        heads, sides, grad_proj, residual, stats, own_two, grad_res, quarter, sums, grad_act,
        in_sems, out_sems,
    ) = refs[17:]
    cells, channels = grad_proj.shape
    cols = (shifted.shape[0] - cells) // 2
    rows = cells // cols
    _, head, _, height = own_place(vec)
    width = channels // GROUPS
    count = (height * (cols * width)).astype(jnp.float32)
    half = qkv_t.shape[1]
    pairs = [(far, heads.at[head ^ k]) for k, far in enumerate(heads_far)]
    pairs += [(far, sides.at[head ^ k]) for k, far in enumerate(sides_far)]
    arriving = started(
        in_sems,
        *pairs,
        (stats_far, stats),
        (residual_far, residual),
        (grad_far, grad_proj),
        (own_far, own_two),
        (weight_far, quarter.at[pl.ds(9 * half, 5 * half), :]),
    )
    zeros = jnp.zeros((half, channels), jnp.bfloat16)
    halfway = cells // 2
    step = 512
    pairs = ((0, 1), (2, 3))
    w_main = []
    for a, b in pairs:
        order = [HEADS + a, 2 * HEADS + a, HEADS + b, 2 * HEADS + b]
        w_main.append(jnp.concatenate([qkv_t[k] for k in order], axis=0))
    finish_all(arriving[:8])
    for part in range(2):
        w_side = []
        for a, b in pairs:
            left, right = qkv_t[a], qkv_t[b]
            order = [left, zeros, right, zeros] if part == 0 else [zeros, left, zeros, right]
            w_side.append(jnp.concatenate(order, axis=0))
        for base in range(0, halfway, step):
            start = part * halfway + base
            total = None
            for k, (a, b) in enumerate(pairs):
                main = jnp.concatenate(
                    [heads[a][start : start + step, :], heads[b][start : start + step, :]], axis=1
                )
                side = jnp.concatenate(
                    [sides[a][base : base + step, :], sides[b][base : base + step, :]], axis=1
                )
                term = dot(main, w_main[k]) + dot(side, w_side[k])
                total = term if total is None else total + term
            grad_act[start : start + step, :] = total
    finish_all(arriving[8:10])
    mean, inverse = stats[4:5, :], stats[5:6, :]
    gain = vec[8:9, :]
    zero = jnp.zeros((8, channels), jnp.float32)

    def normed(index):
        return (residual[row_at(index, cols), :] - mean) * inverse

    def add(index, totals):
        grad = grad_act[row_at(index, cols), :]
        return totals[0] + fold(grad), totals[1] + fold(grad * normed(index))

    plain, cross = lax.fori_loop(0, rows, add, (zero, zero), unroll=2)
    plain, cross = total_of(plain), total_of(cross)
    mean_plain = group_sums(plain * gain, width) / count
    mean_cross = group_sums(cross * gain, width) / count
    clear_rims(shifted, cols)
    arriving[10].wait()

    def finish(index, total):
        at = row_at(index, cols)
        inner = (grad_act[at, :] * gain - mean_plain - normed(index) * mean_cross) * inverse
        grad = grad_proj[at, :].astype(jnp.float32) + inner * valid_row(index, height)
        grad_res[at, :] = grad
        put_shifted(shifted, index, grad, cols)
        return total + fold(grad)

    total = total_of(lax.fori_loop(0, rows, finish, zero, unroll=2))
    sums[...] = jnp.concatenate([cross, plain, total, jnp.zeros((5, channels), jnp.float32)], axis=0)
    leaving = started(out_sems, (grad_res, grad_res_far), (sums, sums_far))
    finish_all(arriving[11:])
    kernel_quarter(shifted, own_two, quarter, cols)
    leaving += started(out_sems.at[2:3], (quarter, quarter_far))
    finish_all(leaving)


def second_kernel(vec, shifted, weight_far, conv_far, stats_far, own_far, *refs):
    sums_three_far, out_sums_far = refs[0:2]
    shifted_one, quarter_far = refs[2:4]
    (
        weight, conv_one, stats, own_one, sums_three, out_sums, quarter, grad_act, in_sems, out_sems,
    ) = refs[4:]
    cells, channels = conv_one.shape
    cols = (shifted.shape[0] - cells) // 2
    rows = cells // cols
    _, _, image, height = own_place(vec)
    width = channels // GROUPS
    count = (height * (cols * width)).astype(jnp.float32)
    arriving = started(
        in_sems,
        (weight_far, weight),
        (stats_far, stats),
        (conv_far, conv_one),
        (own_far, own_one),
        (sums_three_far, sums_three),
        (out_sums_far, out_sums),
    )
    gain, bias, scale, shift = (vec[k : k + 1, :] for k in range(3, 7))
    zero = jnp.zeros((8, channels), jnp.float32)
    clear_rims(shifted_one, cols)
    arriving[0].wait()
    conv_shifted(shifted, weight, grad_act, 0.0, cols)
    finish_all(arriving[1:3])
    mean, inverse = stats[2:3, :], stats[3:4, :]
    line = half_line(mean, inverse, gain, bias, scale, shift)
    begin = mean * inverse

    def add(index, totals):
        at = row_at(index, cols)
        value = conv_one[at, :]
        unit = value * inverse - begin
        part = value * line[0] + line[1]
        sigmoid = 0.5 + 0.5 * jnp.tanh(part)
        slope = sigmoid + 2.0 * part * sigmoid * (1.0 - sigmoid)
        grad = grad_act[at, :] * valid_row(index, height) * slope
        grad_act[at, :] = grad
        return totals[0] + fold(grad), totals[1] + fold(grad * unit)

    plain, cross = lax.fori_loop(0, rows, add, (zero, zero), unroll=2)
    plain, cross = total_of(plain), total_of(cross)
    factor = gain * scale
    mean_plain = group_sums(plain * factor, width) / count
    mean_cross = group_sums(cross * factor, width) / count
    one, two = factor * inverse, mean_cross * inverse * inverse
    three = (mean_plain - begin * mean_cross) * inverse

    def finish(index, total):
        at = row_at(index, cols)
        grad = grad_act[at, :] * one - conv_one[at, :] * two - three
        grad = grad * valid_row(index, height)
        put_shifted(shifted_one, index, grad, cols)
        return total + fold(grad)

    total = total_of(lax.fori_loop(0, rows, finish, zero, unroll=2))
    finish_all(arriving[3:])
    kernel_quarter(shifted_one, own_one, quarter, cols)
    lines = [
        sums_three[0:3, :], out_sums[0:1, :], cross * scale, plain * scale, total,
        jnp.zeros((9, channels), jnp.float32),
    ]
    mine = 2 * (lax.axis_index("img") * 2 + image)
    place = lax.broadcasted_iota(jnp.int32, (16, channels), 0)
    both = jnp.where(place == mine, gain * cross + bias * plain, 0.0)
    lines.append(jnp.where(place == mine + 1, plain, both))
    base = 3 * own_one.shape[1]
    lines.append(jnp.zeros((quarter.shape[0] - base - 32, channels), jnp.float32))
    quarter[base:, :] = jnp.concatenate(lines, axis=0).astype(jnp.bfloat16)
    finish_all(started(out_sems, (quarter, quarter_far)))


def first_kernel(vec, shifted, weight_far, pix_far, grad_far, stats_far, *refs):
    out_own_far, out_away_far, sums_far = refs[:3]
    weight, pix, grad_res, stats, out, sums, grad_act, in_sems, out_sems = refs[3:]
    cells, channels = pix.shape
    block_cells = out.shape[1]
    cols = (shifted.shape[0] - cells) // 2
    rows = cells // cols
    spot, _, _, height = own_place(vec)
    width = channels // GROUPS
    count = (height * (cols * width)).astype(jnp.float32)
    arriving = started(
        in_sems,
        (weight_far, weight),
        (stats_far, stats),
        (pix_far, pix),
        (grad_far, grad_res),
    )
    gain, bias = vec[0:1, :], vec[1:2, :]
    zero = jnp.zeros((8, channels), jnp.float32)
    arriving[0].wait()
    conv_shifted(shifted, weight, grad_act, 0.0, cols)
    finish_all(arriving[1:])
    mean, inverse = stats[0:1, :], stats[1:2, :]
    line = half_line(mean, inverse, gain, bias)
    begin = mean * inverse

    def normed(at):
        return pix[at, :].astype(jnp.float32) * inverse - begin

    def add(index, totals):
        at = row_at(index, cols)
        value = pix[at, :].astype(jnp.float32)
        unit = value * inverse - begin
        part = value * line[0] + line[1]
        sigmoid = 0.5 + 0.5 * jnp.tanh(part)
        slope = sigmoid + 2.0 * part * sigmoid * (1.0 - sigmoid)
        grad = grad_act[at, :] * valid_row(index, height) * slope
        grad_act[at, :] = grad
        return totals[0] + fold(grad), totals[1] + fold(grad * unit)

    plain, cross = lax.fori_loop(0, rows, add, (zero, zero), unroll=2)
    plain, cross = total_of(plain), total_of(cross)
    mean_plain = group_sums(plain * gain, width) / count
    mean_cross = group_sums(cross * gain, width) / count
    block_rows = block_cells // cols
    for part in range(2):
        first_row = (spot ^ (4 * part)) * block_rows
        for line in range(block_rows):
            at = row_at(first_row + line, cols)
            grad = (grad_act[at, :] * gain - mean_plain - normed(at) * mean_cross) * inverse
            grad = grad_res[at, :] + grad * valid_row(first_row + line, height)
            out[part, line * cols : (line + 1) * cols, :] = grad.astype(jnp.bfloat16)
    sums[...] = jnp.concatenate([cross, plain, jnp.zeros((6, channels), jnp.float32)], axis=0)
    finish_all(
        started(
            out_sems, (out.at[0], out_own_far), (out.at[1], out_away_far), (sums, sums_far)
        )
    )


def block_kernel(columns, vec, w_out, *refs):
    heads, residual_far = refs[:4], refs[4]
    out_own, out_away, residual, in_sems = refs[5:]
    block_cells, channels = out_own.shape
    spot, head, _, height = own_place(vec)
    cols = columns
    bases = [
        pl.multiple_of((spot ^ (4 * part)) * block_cells, block_cells) for part in range(2)
    ]
    pairs = [
        (residual_far.at[pl.ds(base, block_cells), :], residual.at[part])
        for part, base in enumerate(bases)
    ]
    finish_all(started(in_sems, *pairs))
    for part, out in enumerate((out_own, out_away)):
        total = residual[part] + vec[10:11, :]
        for step in range(4):
            tile = heads[step][part]
            total = total + dot(tile[:, tile.shape[1] // 2 :], w_out[head ^ step])
        cell = bases[part] + lax.broadcasted_iota(jnp.int32, (block_cells, channels), 0)
        out[...] = jnp.where(cell < height * cols, total, 0.0).astype(jnp.bfloat16)


def prepare_kernel(*refs):
    shifts, lines_far, kernels_far = refs[0], refs[1:15], refs[15:17]
    vec, w_heads, w_out, biases, qkv_t = refs[17:22]
    backs_far = refs[22:24]
    kernels, backs, qkv_weight, out_weight, heights, timesteps, qv_bias, *lines = refs[24:40]
    line_sems, in_sems, out_sems = refs[40:]
    channels = out_weight.shape[0]
    half = channels // HEADS
    small = started(
        line_sems,
        *zip(lines_far, (*lines, qv_bias, qkv_weight, out_weight, heights, timesteps)),
    )
    arriving = started(
        in_sems, *[(far, kernels.at[k]) for k, far in enumerate(kernels_far)]
    )
    finish_all(small)
    spot = lax.axis_index("row")
    image, head = spot // HEADS, spot % HEADS
    shift_row = shifts[pl.ds(image, 1), :]
    order = list(range(5)) + [None, None] + list(range(5, 9))
    for line, k in enumerate(order):
        if k is not None:
            vec[line : line + 1, :] = lines[k][...].astype(jnp.float32).reshape(1, channels)
    vec[5:6, :] = 1.0 + shift_row[:, :channels]
    vec[6:7, :] = shift_row[:, channels:]
    vec[11:12, :] = jnp.full((1, channels), heights[image].astype(jnp.float32))
    vec[12:13, :] = jnp.full((1, channels), timesteps[image].astype(jnp.float32))
    vec[13:16, :] = jnp.zeros((3, channels), jnp.float32)
    source = lax.broadcasted_iota(jnp.int32, (channels, 2 * half), 0)
    lane = lax.broadcasted_iota(jnp.int32, (channels, 2 * half), 1)
    first = jnp.where((lane < half) & (source == head * half + lane), 1.0, 0.0)
    second = jnp.where((lane >= half) & (source == head * half + lane - half), 1.0, 0.0)
    first, second = first.astype(jnp.bfloat16), second.astype(jnp.bfloat16)
    lanes = 2 * half
    for part, taken in enumerate((first, first, second)):
        whole = qkv_weight[:, part * channels : (part + 1) * channels]
        w_heads[:, part * lanes : (part + 1) * lanes] = dot(whole, taken).astype(jnp.bfloat16)
    turned = jnp.transpose(out_weight[...].astype(jnp.float32)).astype(jnp.bfloat16)
    w_out[...] = dot(turned, second).astype(jnp.bfloat16)
    both = qv_bias[...].astype(jnp.float32).reshape(1, 2 * channels)
    wide = jnp.broadcast_to(both, (16, 2 * channels)).astype(jnp.bfloat16)
    biases[:, 0:lanes] = dot(wide[:, :channels], first)[0:8]
    biases[:, lanes : 2 * lanes] = jnp.zeros((8, lanes), jnp.float32)
    biases[:, 2 * lanes : 3 * lanes] = dot(wide[:, channels:], second)[0:8]
    for block in range(0, 3 * HEADS, 2):
        whole = qkv_weight[:, block // 2 * lanes : (block // 2 + 1) * lanes].astype(jnp.float32)
        whole = jnp.transpose(whole).astype(jnp.bfloat16)
        qkv_t[block] = whole[0:half]
        qkv_t[block + 1] = whole[half:lanes]
    leaving = []
    for k in range(2):
        arriving[k].wait()

        def turn(tap, carry):
            tile = kernels[k, 2 - tap // 3, 2 - tap % 3].astype(jnp.float32)
            at = pl.ds(pl.multiple_of(tap % 3 * channels, channels), channels)
            backs[k, tap // 3, at, :] = jnp.transpose(tile).astype(jnp.bfloat16)
            return carry

        lax.fori_loop(0, 9, turn, 0)
        leaving += started(out_sems.at[k : k + 1], (backs.at[k], backs_far[k]))
    finish_all(leaving)


def gathered_rows(parts, gathered):
    spot = lax.axis_index("row")
    head, column = spot % HEADS, lax.axis_index("img")
    lines = parts[0].shape[1]
    for index, part in enumerate(parts):
        at = pl.ds(pl.multiple_of((column ^ (index // 2)) * lines, 16), lines)
        for pair in range(2):
            gathered[head ^ (index % 2 + 2 * pair), at, :] = part[pair]


def place_taps(gathered, out):
    half = out.shape[2] // HEADS
    for quarter in range(HEADS):
        for tap in range(9):
            base = tap * half
            out[tap // 3, tap % 3, quarter * half : (quarter + 1) * half, :] = gathered[
                quarter, base : base + half, :
            ].astype(jnp.float32)


def late_kernel(*refs):
    parts, ones, time_all, (out, time_out, time_bias), rows = (
        refs[:8], refs[8:12], refs[12], refs[13:16], refs[16:25],
    )
    gathered, norm_one = refs[-2:]
    gathered_rows(parts, gathered)
    place_taps(gathered, out)
    rest = gathered[0, 9 * (out.shape[3] // HEADS) :, :]
    column = lax.axis_index("img")
    for step, part in enumerate(ones):
        norm_one[column ^ step] = part[...]
    total = norm_one[0] + norm_one[1] + norm_one[2] + norm_one[3]
    lines = rest[0:16, :].astype(jnp.float32)
    whole = jnp.concatenate([total[0:2], lines[0:7]], axis=0)
    for k, row in enumerate(rows):
        row[...] = whole[k : k + 1].reshape(row.shape)
    shifts = rest[16:32, :].astype(jnp.float32)
    images = time_all.shape[0]
    channels = shifts.shape[1]
    pair = jnp.concatenate([shifts[2 * k : 2 * k + 1, :] for k in range(images)], axis=0)
    other = jnp.concatenate([shifts[2 * k + 1 : 2 * k + 2, :] for k in range(images)], axis=0)
    time_bias[...] = jnp.concatenate([total_of(pair), total_of(other)], axis=1).reshape(
        time_bias.shape
    )
    for k, lines in enumerate((pair, other)):
        time_out[:, k * channels : (k + 1) * channels] = lax.dot_general(
            time_all[...], lines, (((0,), (0,)), ((), ())), precision=PRECISE,
            preferred_element_type=jnp.float32,
        )


def early_kernel(*refs):
    parts, (out, qkv_out, out_out, bias_out, step_out) = refs[:8], refs[8:13]
    (gathered,) = refs[13:]
    gathered_rows(parts, gathered)
    place_taps(gathered, out)
    half = out_out.shape[0] // HEADS
    nine = 9 * half
    sums = []
    for quarter in range(HEADS):
        out_out[quarter * half : (quarter + 1) * half, :] = gathered[
            quarter, nine + 3 * half : nine + 4 * half, :
        ].astype(jnp.float32)
        sums.append(gathered[quarter, nine + 4 * half : nine + 4 * half + 16].astype(jnp.float32))
    parts = [part[0:1, :half] for part in sums] + [part[0:1, 3 * half :] for part in sums]
    bias_out[...] = jnp.concatenate(parts, axis=1).reshape(bias_out.shape)
    step_out[...] = sums[0][0:8]
    for part in range(3):
        block = jnp.concatenate(
            [
                gathered[quarter, nine + part * half : nine + (part + 1) * half, :]
                for quarter in range(HEADS)
            ],
            axis=0,
        )
        width = HEADS * half
        qkv_out[:, part * width : (part + 1) * width] = jnp.transpose(block.astype(jnp.float32))


def swap(value, axis, step):
    count = lax.axis_size(axis)
    return lax.ppermute(value, axis, [(k, k ^ step) for k in range(count)])


def pick(stacked, index):
    return lax.dynamic_index_in_dim(stacked, index, 0, keepdims=False)


def reduce_columns(value, column):
    lines = value.shape[0] // 4
    parts = value.reshape(4, lines, value.shape[1])
    got = [swap(pick(parts, column ^ step), "img", step) for step in (1, 2, 3)]
    total = pick(parts, column).astype(jnp.float32)
    for part in got:
        total = total + part.astype(jnp.float32)
    return total.astype(jnp.bfloat16)


def both_images(total):
    away = swap(total, "row", 4)
    return (total.astype(jnp.float32) + away.astype(jnp.float32)).astype(jnp.bfloat16)


def gather_quarters(own):
    pair = jnp.stack([own, swap(own, "row", 2)])
    near = [pair] + [swap(pair, "img", step) for step in (1, 2, 3)]
    return [part for mine in near for part in (mine, swap(mine, "row", 1))]


def call(kernel, near_outs, far_outs, scratch, limit, work, scalars, near, far, last_outs=()):
    close = pl.BlockSpec(memory_space=pltpu.VMEM)
    distant = pl.BlockSpec(memory_space=pltpu.HBM)
    operands = list(near) + [pltpu.with_memory_space_constraint(array, pltpu.HBM) for array in far]
    moved = sum(array.size * array.dtype.itemsize for array in operands)
    return pl.pallas_call(
        kernel,
        out_shape=[jax.ShapeDtypeStruct(*kind) for kind in near_outs]
        + [pltpu.HBM(*kind) for kind in far_outs]
        + [jax.ShapeDtypeStruct(*kind) for kind in last_outs],
        in_specs=[pl.BlockSpec(memory_space=pltpu.SMEM)] * len(scalars)
        + [close] * len(near)
        + [distant] * len(far),
        out_specs=[close] * len(near_outs)
        + [distant] * len(far_outs)
        + [close] * len(last_outs),
        scratch_shapes=[pltpu.VMEM(*kind) if isinstance(kind, tuple) else kind for kind in scratch],
        compiler_params=mib(limit),
        cost_estimate=pl.CostEstimate(flops=work, bytes_accessed=moved, transcendentals=0),
    )(*scalars, *operands)


def sems(count):
    return pltpu.SemaphoreType.DMA((count,))


def gather_field(mine, theirs):
    far, far_near = swap(theirs, "row", 4), swap(theirs, "row", 6)
    return [mine, swap(mine, "row", 1), swap(mine, "row", 2), None, far, None, far_near, None]


def relayed(blocks, after=None):
    sent = [blocks[2], blocks[4], blocks[6]]
    if after is not None:
        sent = lax.optimization_barrier((*sent, after))[:3]
    odd = [swap(block, "row", 1) for block in sent]
    return [
        blocks[0], blocks[1], blocks[2], odd[0], blocks[4], odd[1], blocks[6], odd[2],
    ]


def local_image(
    pixels,
    heights,
    timesteps,
    norm1_gain,
    norm1_bias,
    conv1_weight,
    conv1_bias,
    time_weight,
    time_bias,
    norm2_gain,
    norm2_bias,
    conv2_weight,
    conv2_bias,
    norm3_gain,
    norm3_bias,
    qkv_weight,
    qv_bias,
    out_weight,
    out_bias,
    grad_out,
):
    images, row_count, cols, channels = pixels.shape
    block_cells = row_count * cols
    cells = block_cells * lax.axis_size("row")
    half = channels // HEADS
    column = lax.axis_index("img")
    image = lax.axis_index("row") // HEADS
    low, full = jnp.bfloat16, jnp.float32
    pixel_blocks = pixels.reshape(images, block_cells, channels)
    grad_blocks = grad_out.reshape(images, block_cells, channels)
    field = gather_field(pick(pixel_blocks, image), pick(pixel_blocks, 1 - image))
    later = (pick(grad_blocks, image), pick(grad_blocks, 1 - image), field[4], field[6])
    later = lax.optimization_barrier(later)
    grads = gather_field(later[0], later[1])
    field[4], field[6] = later[2], later[3]
    time_act = jax.nn.silu(embed_steps(timesteps, time_weight.shape[0]))
    shifts = jnp.dot(time_act, time_weight.astype(full), precision=PRECISE) + time_bias.astype(full)
    kernel_shape = (3, 3 * channels, channels)
    lanes = 2 * half
    vec, w_heads, w_out, biases, qkv_t, w_one_back, w_two_back = call(
        prepare_kernel,
        [
            ((16, channels), full), ((channels, 3 * lanes), low), ((channels, lanes), low),
            ((8, 3 * lanes), full), ((3 * HEADS, half, channels), low),
        ],
        [(kernel_shape, low), (kernel_shape, low)],
        [
            ((2, 3, 3, channels, channels), low), ((2,) + kernel_shape, low),
            ((channels, 3 * channels), low), ((channels, channels), low),
            pltpu.SMEM((images,), jnp.int32), pltpu.SMEM((images,), jnp.int32),
            ((2 * channels,), low), *[((channels,), low)] * 9,
            sems(14), sems(2), sems(2),
        ],
        16,
        channels,
        [],
        [shifts],
        [
            norm1_gain, norm1_bias, conv1_bias, norm2_gain, norm2_bias, conv2_bias, norm3_gain,
            norm3_bias, out_bias, qv_bias, qkv_weight, out_weight, heights, timesteps,
            conv1_weight,
            conv2_weight,
        ],
    )
    field = relayed(field, vec)
    w_one, w_two = conv1_weight.reshape(kernel_shape), conv2_weight.reshape(kernel_shape)
    rim_cells = cells + 2 * cols
    cost = 9 * cells * channels * channels // 2

    wide, tall = (cells, channels), (rim_cells, 3 * channels)
    rows_eight = ((8, channels), full)
    act_three, pix, conv_one, residual, act_one, act_two, stats = call(
        forward_kernel,
        [(wide, low)],
        [(wide, low), (wide, full), (wide, full), (wide, low), (wide, low), rows_eight],
        [
            (wide, low), (wide, full), (wide, full), rows_eight, (kernel_shape, low),
            (kernel_shape, low), (tall, low), (tall, low), sems(10), sems(6),
        ],
        28,
        cost * 16,
        [],
        [vec],
        [*field, w_one, w_two],
    )
    grads = relayed(grads, act_three)
    query_shape, head_shape = (cells // 2, lanes), (cells, lanes)
    value_key, query_part, grad_proj, mixed, out_sums = call(
        functools.partial(attention_kernel, cols),
        [],
        [(head_shape, low), (query_shape, low), (wide, low), (head_shape, low), rows_eight],
        [
            (wide, low), (wide, low), (head_shape, low), (query_shape, low), rows_eight,
            (head_shape, low), (head_shape, low), (head_shape, low), ((lanes, cells), full),
            (head_shape, low), ((1, cells), full), sems(8), sems(5),
        ],
        36,
        cost * 20,
        [],
        [vec, act_three, w_heads, w_out, biases],
        grads,
    )

    key_near, query_near = swap(value_key, "row", 2), swap(query_part, "row", 2)
    key_mate, query_mate = swap(value_key, "row", 1), swap(query_part, "row", 1)
    own_shape = (3, 3 * half, cells)
    send_shape = ((2, block_cells, lanes), low)
    own_one, own_two, weight_rows, *sends = call(
        aside_kernel,
        [],
        [(own_shape, low), (own_shape, low), ((5 * half, channels), low)],
        [
            ((2,) + wide, low), (head_shape, low), (head_shape, low), (wide, low), (wide, low),
            ((rim_cells, 3 * half), full), ((2,) + own_shape, low), ((5 * half, channels), low),
            sems(6), sems(3),
        ],
        28,
        cost * 6,
        [],
        [vec],
        [act_one, act_two, mixed, value_key, act_three, grad_proj],
        [send_shape] * 4,
    )
    key_near, query_near, own_two = lax.optimization_barrier((key_near, query_near, own_two))
    packed_all = [
        value_key, query_part, key_mate, query_mate,
        key_near, query_near, swap(key_near, "row", 1), swap(query_near, "row", 1),
    ]
    shifted_two, grad_res, quarter_two, sums_three = call(
        residual_kernel,
        [(tall, low)],
        [(wide, full), ((14 * half, channels), low), rows_eight],
        [
            ((HEADS,) + head_shape, low), ((HEADS,) + query_shape, low),
            (wide, low), (wide, full), rows_eight, (own_shape, low), (wide, full),
            ((14 * half, channels), low), rows_eight, (wide, full), sems(13), sems(3),
        ],
        24,
        cost * 6,
        [],
        [vec, qkv_t],
        [*packed_all, grad_proj, residual, stats, own_two, weight_rows],
    )
    early_total = reduce_columns(quarter_two, column)
    *sends, shifted_two = lax.optimization_barrier((*sends, shifted_two))
    heads_got = [sends[0]] + [swap(sends[step], "row", step) for step in (1, 2, 3)]
    shifted_one, quarter_one = call(
        second_kernel,
        [(tall, low)],
        [((10 * half, channels), low)],
        [
            (kernel_shape, low), (wide, full), rows_eight, (own_shape, low), rows_eight, rows_eight,
            ((10 * half, channels), low), (wide, full), sems(6), sems(1),
        ],
        20,
        cost * 7,
        [],
        [vec, shifted_two],
        [w_two_back, conv_one, stats, own_one, sums_three, out_sums],
    )
    late_total = reduce_columns(quarter_one, column)
    shifted_one, early_total, late_total = lax.optimization_barrier(
        (shifted_one, early_total, late_total)
    )
    early_lines = early_total.shape[0]
    both = both_images(jnp.concatenate([early_total, late_total], axis=0))
    early_chunk, late_chunk = both[:early_lines], both[early_lines:]
    grad_own, grad_away, sums_one = call(
        first_kernel,
        [],
        [((block_cells, channels), low), ((block_cells, channels), low), rows_eight],
        [
            (kernel_shape, low), (wide, low), (wide, full), rows_eight,
            ((2, block_cells, channels), low), rows_eight, (wide, full), sems(4), sems(3),
        ],
        20,
        cost * 5,
        [],
        [vec, shifted_one],
        [w_one_back, pix, grad_res, stats],
    )
    block_own, block_away = call(
        functools.partial(block_kernel, cols),
        [((block_cells, channels), low), ((block_cells, channels), low)],
        [],
        [((2, block_cells, channels), full), sems(2)],
        8,
        cost,
        [],
        [vec, out_weight.reshape(HEADS, half, channels), *heads_got],
        [residual],
    )
    early_parts = gather_quarters(early_chunk)
    late_parts = gather_quarters(late_chunk)
    out_pair = jnp.stack([block_own, grad_own])
    away_pair = swap(jnp.stack([block_away, grad_away]), "row", 4)
    first_pair = jnp.where(image == 0, out_pair, away_pair)
    second_pair = jnp.where(image == 0, away_pair, out_pair)
    finished = jnp.stack([first_pair, second_pair], axis=1).reshape((2,) + pixels.shape)
    norm_one = sums_one + swap(sums_one, "row", 4)
    norm_parts = [norm_one] + [swap(norm_one, "img", step) for step in (1, 2, 3)]

    nine = 9 * half
    conv2_weight_grad, qkv_weight_grad, out_weight_grad, qv_bias_grad, steps = call(
        early_kernel,
        [
            ((3, 3, channels, channels), full), ((channels, 3 * channels), full),
            ((channels, channels), full), ((2 * channels,), full), rows_eight,
        ],
        [],
        [((HEADS, nine + 5 * half, channels), low)],
        12,
        cost,
        [],
        early_parts,
        [],
    )
    all_images = images * lax.axis_size("img")
    steps_all = steps[1, :all_images] * 32.0 + steps[2, :all_images]
    time_all = jax.nn.silu(embed_steps(steps_all, time_weight.shape[0]))
    line = ((channels,), full)
    conv1_weight_grad, time_weight_grad, time_bias_grad, *lines = call(
        late_kernel,
        [
            ((3, 3, channels, channels), full), ((time_weight.shape[0], 2 * channels), full),
            ((2 * channels,), full), line, line, line, line, line, line, line, line, line,
        ],
        [],
        [((HEADS, 10 * half, channels), low), ((4, 8, channels), full)],
        12,
        cost,
        [],
        [*late_parts, *norm_parts, time_all],
        [],
    )
    norm1_gain_grad, norm1_bias_grad, norm3_gain_grad, norm3_bias_grad, conv2_bias_grad = lines[:5]
    out_bias_grad, norm2_gain_grad, norm2_bias_grad, conv1_bias_grad = lines[5:]
    return (
        finished[0],
        finished[1],
        norm1_gain_grad,
        norm1_bias_grad,
        conv1_weight_grad,
        conv1_bias_grad,
        time_weight_grad,
        time_bias_grad,
        norm2_gain_grad,
        norm2_bias_grad,
        conv2_weight_grad,
        conv2_bias_grad,
        norm3_gain_grad,
        norm3_bias_grad,
        qkv_weight_grad,
        qv_bias_grad,
        out_weight_grad,
        out_bias_grad,
    )


def local(*arrays):
    pixels = arrays[0]
    if lax.axis_size("row") == pixels.shape[0] * HEADS and lax.axis_size("img") == 4:
        return local_image(*arrays)
    return local_rows(*arrays)


def solution(mesh):
    placed = (
        P("img", "row", None, None),
        P("img"),
        P("img"),
        P(),
        P(),
        P(),
        P(),
        P(),
        P(),
        P(),
        P(),
        P(),
        P(),
        P(),
        P(),
        P(),
        P(),
        P(),
        P(),
        P("img", "row", None, None),
    )
    return jax.shard_map(
        local,
        mesh=mesh,
        in_specs=placed,
        out_specs=(
            P("img", "row", None, None),
            P("img", "row", None, None),
            P(),
            P(),
            P(),
            P(),
            P(),
            P(),
            P(),
            P(),
            P(),
            P(),
            P(),
            P(),
            P(),
            P(),
            P(),
            P(),
        ),
        check_vma=False,
    )
```

```python
import functools
import math

import jax
import jax.numpy as jnp
from jax import lax
from jax.experimental import pallas as pl
from jax.experimental.pallas import tpu as pltpu
from jax.sharding import PartitionSpec as P

GROUPS = 32
HEADS = 4


EPSILON = 1e-05
MASKED = -1000000000.0
PRECISE = lax.Precision.HIGHEST


def with_halo(cells, sides, width):
    for axis, dim in sides:
        count = lax.axis_size(axis)
        ends = count - 1
        head = lax.slice_in_dim(cells, 0, width, axis=dim)
        tail = lax.slice_in_dim(cells, cells.shape[dim] - width, cells.shape[dim], axis=dim)
        cells = jnp.concatenate(
            [
                lax.ppermute(tail, axis, [(i, (i + 1) % count) for i in range(ends)]),
                cells,
                lax.ppermute(head, axis, [((i + 1) % count, i) for i in range(ends)]),
            ],
            axis=dim,
        )
    return cells


def embed_steps(timesteps, time_width):
    half_dim = time_width // 2
    frequency = jnp.exp(-math.log(10000.0) * jnp.arange(half_dim, dtype=jnp.float32) / half_dim)
    angles = timesteps.astype(jnp.float32)[:, None] * frequency[None, :]
    return jnp.concatenate([jnp.cos(angles), jnp.sin(angles)], axis=1)


def silu_slope(pre_act):
    sigmoid = jax.nn.sigmoid(pre_act)
    return sigmoid * (1.0 + pre_act * (1.0 - sigmoid))


def with_rims(field_in):
    return with_halo(field_in, (("row", 1),), 1)


def conv_rows(padded, kernel):
    return lax.conv_general_dilated(
        padded,
        kernel,
        (1, 1),
        ((0, 0), (1, 1)),
        dimension_numbers=("NHWC", "HWIO", "NHWC"),
        preferred_element_type=jnp.float32,
    )


def flipped(kernel):
    return jnp.transpose(kernel[::-1, ::-1], (0, 1, 3, 2))


def kernel_grad(padded, grad_field):
    row_count = grad_field.shape[1]
    col_count = grad_field.shape[2]
    widened = jnp.pad(padded, ((0, 0), (0, 0), (1, 1), (0, 0)))
    tap_rows = []
    for tap_row in range(3):
        tap_line = []
        for tap_col in range(3):
            window = widened[:, tap_row : tap_row + row_count, tap_col : tap_col + col_count, :]
            tap_line.append(
                jnp.einsum("brwc,brwd->cd", window, grad_field, preferred_element_type=jnp.float32)
            )
        tap_rows.append(jnp.stack(tap_line))
    return jnp.stack(tap_rows)


def norm_forward(field_in, cell_mask, cell_count, group_count):
    shaped = field_in.reshape(field_in.shape[:3] + (group_count, field_in.shape[3] // group_count))
    first_sum = lax.psum(jnp.sum(shaped * cell_mask, axis=(1, 2, 4)), "row")
    center = first_sum / cell_count[:, None]
    centred = shaped - center[:, None, None, :, None]
    spread_sum = lax.psum(jnp.sum(jnp.square(centred * cell_mask), axis=(1, 2, 4)), "row")
    spread = spread_sum / cell_count[:, None]
    inverse = lax.rsqrt(spread + EPSILON)
    return (centred * inverse[:, None, None, :, None], inverse)


def norm_backward(grad_normed, normalized, inverse, gain_in, cell_mask, cell_count):
    full_shape = grad_normed.shape
    flat_norm = normalized.reshape(full_shape)
    gain_grad = jnp.sum(grad_normed * flat_norm, axis=(0, 1, 2))
    shift_grad = jnp.sum(grad_normed, axis=(0, 1, 2))
    scaled = (grad_normed * gain_in).reshape(normalized.shape)
    sum_plain, sum_cross = lax.psum(
        (
            jnp.sum(scaled * cell_mask, axis=(1, 2, 4)),
            jnp.sum(scaled * normalized * cell_mask, axis=(1, 2, 4)),
        ),
        "row",
    )
    mean_plain = sum_plain / cell_count[:, None]
    mean_cross = sum_cross / cell_count[:, None]
    grad_in = (
        (
            scaled
            - mean_plain[:, None, None, :, None]
            - normalized * mean_cross[:, None, None, :, None]
        )
        * inverse[:, None, None, :, None]
        * cell_mask
    )
    return (grad_in.reshape(full_shape), gain_grad, shift_grad)


def local_rows(
    pixels,
    heights,
    timesteps,
    norm1_gain,
    norm1_bias,
    conv1_weight,
    conv1_bias,
    time_weight,
    time_bias,
    norm2_gain,
    norm2_bias,
    conv2_weight,
    conv2_bias,
    norm3_gain,
    norm3_bias,
    qkv_weight,
    qv_bias,
    out_weight,
    out_bias,
    grad_out,
):
    image_count, row_count, col_count, channels = pixels.shape
    group_count = GROUPS
    head_count = HEADS
    head_width = channels // head_count
    query_count = row_count * col_count
    scaling = head_width ** (-0.5)
    head_shape = (image_count, query_count, head_count, head_width)
    row_ids = lax.axis_index("row") * row_count + jnp.arange(row_count, dtype=jnp.int32)
    row_valid = row_ids[None, :] < heights[:, None]
    row_mask = row_valid.astype(jnp.float32)
    cell_rows = row_mask[:, :, None, None]
    cell_mask = row_mask[:, :, None, None, None]
    own_valid = jnp.repeat(row_valid, col_count, axis=1)[:, None, None, :]
    cell_count = heights.astype(jnp.float32) * (col_count * (channels // group_count))
    gain_one = norm1_gain.astype(jnp.float32)
    gain_two = norm2_gain.astype(jnp.float32)
    gain_three = norm3_gain.astype(jnp.float32)
    field_in = pixels.astype(jnp.float32)
    normed_one, inverse_one = norm_forward(field_in, cell_mask, cell_count, group_count)
    pre_one = normed_one.reshape(field_in.shape) * gain_one + norm1_bias.astype(jnp.float32)
    act_one = (jax.nn.silu(pre_one) * cell_rows).astype(jnp.bfloat16)
    padded_one = with_rims(act_one)
    conv_one = conv_rows(padded_one, conv1_weight) + conv1_bias.astype(jnp.float32)
    time_act = jax.nn.silu(embed_steps(timesteps, time_weight.shape[0]))
    shifts = jnp.dot(
        time_act, time_weight.astype(jnp.float32), precision=PRECISE
    ) + time_bias.astype(jnp.float32)
    scale_part = 1.0 + shifts[:, None, None, :channels]
    shift_part = shifts[:, None, None, channels:]
    normed_two, inverse_two = norm_forward(conv_one, cell_mask, cell_count, group_count)
    affine_two = normed_two.reshape(field_in.shape) * gain_two + norm2_bias.astype(jnp.float32)
    pre_two = affine_two * scale_part + shift_part
    act_two = (jax.nn.silu(pre_two) * cell_rows).astype(jnp.bfloat16)
    padded_two = with_rims(act_two)
    residual = field_in + (conv_rows(padded_two, conv2_weight) + conv2_bias.astype(jnp.float32))
    normed_three, inverse_three = norm_forward(residual, cell_mask, cell_count, group_count)
    act_three = (
        normed_three.reshape(field_in.shape) * gain_three + norm3_bias.astype(jnp.float32)
    ).astype(jnp.bfloat16)
    projected = jnp.einsum(
        "brwc,cd->brwd", act_three, qkv_weight, preferred_element_type=jnp.float32
    )
    qv_float = qv_bias.astype(jnp.float32)
    queries = (projected[..., :channels] + qv_float[:channels]).astype(jnp.bfloat16)
    keys_own = projected[..., channels : 2 * channels].astype(jnp.bfloat16)
    values_own = (projected[..., 2 * channels :] + qv_float[channels:]).astype(jnp.bfloat16)
    query_heads = queries.reshape(head_shape)
    key_heads = keys_own.reshape(head_shape)
    value_heads = values_own.reshape(head_shape)

    def flatten_rows(piece_arr):
        return piece_arr.reshape(
            image_count, piece_arr.shape[1] * col_count, head_count, head_width
        )

    def key_mask(span_rows):
        key_rows = jnp.arange(span_rows, dtype=jnp.int32)
        return jnp.repeat(key_rows[None, :] < heights[:, None], col_count, axis=1)[:, None, None, :]

    top_init = jnp.full((image_count, query_count, head_count), MASKED, jnp.float32)
    piece_keys = lax.all_gather(keys_own, "row", axis=1, tiled=True)
    piece_values = lax.all_gather(values_own, "row", axis=1, tiled=True)
    key_valid = key_mask(piece_keys.shape[1])
    scores = (
        jnp.einsum(
            "bqhd,bkhd->bqhk",
            query_heads,
            flatten_rows(piece_keys),
            preferred_element_type=jnp.float32,
        )
        * scaling
    )
    scores = jnp.where(key_valid, scores, MASKED)
    new_top = jnp.maximum(top_init, jnp.max(scores, axis=3))
    weights = jnp.where(key_valid, jnp.exp(scores - new_top[..., None]), 0.0)
    running_total = jnp.sum(weights, axis=3)
    running_acc = jnp.einsum(
        "bqhk,bkhd->bqhd",
        weights.astype(jnp.bfloat16),
        flatten_rows(piece_values),
        preferred_element_type=jnp.float32,
    )
    attn_float = running_acc / running_total[..., None]
    log_total = new_top + jnp.log(running_total)
    attended = attn_float.reshape(pixels.shape).astype(jnp.bfloat16)
    output_proj = jnp.einsum(
        "brwc,cd->brwd", attended, out_weight, preferred_element_type=jnp.float32
    ) + out_bias.astype(jnp.float32)
    block_out = ((residual + output_proj) * cell_rows).astype(jnp.bfloat16)
    grad_proj = grad_out.astype(jnp.float32) * cell_rows
    grad_proj_low = grad_proj.astype(jnp.bfloat16)
    out_weight_grad = jnp.einsum(
        "brwc,brwd->cd", attended, grad_proj_low, preferred_element_type=jnp.float32
    )
    out_bias_grad = jnp.sum(grad_proj, axis=(0, 1, 2))
    grad_attended = jnp.einsum(
        "brwd,cd->brwc", grad_proj_low, out_weight, preferred_element_type=jnp.float32
    ).astype(jnp.bfloat16)
    grad_heads = grad_attended.reshape(head_shape)
    delta_own = jnp.sum(grad_heads.astype(jnp.float32) * attn_float, axis=3)
    stat_shape = (image_count, row_count, col_count, head_count)
    all_lse, all_delta = (
        lax.all_gather(log_total.reshape(stat_shape), "row", axis=1, tiled=True),
        lax.all_gather(delta_own.reshape(stat_shape), "row", axis=1, tiled=True),
    )
    piece_keys = lax.all_gather(keys_own, "row", axis=1, tiled=True)
    piece_values = lax.all_gather(values_own, "row", axis=1, tiled=True)
    flat_keys = flatten_rows(piece_keys)
    key_valid = key_mask(piece_keys.shape[1])
    scores = (
        jnp.einsum("bqhd,bkhd->bqhk", query_heads, flat_keys, preferred_element_type=jnp.float32)
        * scaling
    )
    soft_weights = jnp.where(key_valid, jnp.exp(scores - log_total[..., None]), 0.0)
    grad_probs = jnp.einsum(
        "bqhd,bkhd->bqhk",
        grad_heads,
        flatten_rows(piece_values),
        preferred_element_type=jnp.float32,
    )
    grad_scores = (soft_weights * (grad_probs - delta_own[..., None])).astype(jnp.bfloat16)
    grad_query_sum = jnp.einsum(
        "bqhk,bkhd->bqhd", grad_scores, flat_keys, preferred_element_type=jnp.float32
    )
    piece_queries = lax.all_gather(queries, "row", axis=1, tiled=True)
    piece_grads = lax.all_gather(grad_attended, "row", axis=1, tiled=True)
    flat_queries = flatten_rows(piece_queries)
    flat_grads = flatten_rows(piece_grads)
    span_rows = piece_queries.shape[1]
    piece_lse = all_lse.reshape(image_count, span_rows * col_count, head_count)
    piece_delta = all_delta.reshape(image_count, span_rows * col_count, head_count)
    scores = (
        jnp.einsum("bqhd,bkhd->bqhk", flat_queries, key_heads, preferred_element_type=jnp.float32)
        * scaling
    )
    soft_weights = jnp.where(own_valid, jnp.exp(scores - piece_lse[..., None]), 0.0)
    value_term = jnp.einsum(
        "bqhk,bqhd->bkhd",
        soft_weights.astype(jnp.bfloat16),
        flat_grads,
        preferred_element_type=jnp.float32,
    )
    grad_probs = jnp.einsum(
        "bqhd,bkhd->bqhk", flat_grads, value_heads, preferred_element_type=jnp.float32
    )
    grad_scores = (soft_weights * (grad_probs - piece_delta[..., None])).astype(jnp.bfloat16)
    key_term = jnp.einsum(
        "bqhk,bqhd->bkhd", grad_scores, flat_queries, preferred_element_type=jnp.float32
    )
    key_term, value_term = (key_term, value_term)
    grad_queries = (grad_query_sum * scaling).reshape(pixels.shape).astype(jnp.bfloat16)
    grad_keys = (key_term * scaling).reshape(pixels.shape).astype(jnp.bfloat16)
    grad_values = value_term.reshape(pixels.shape).astype(jnp.bfloat16)
    grad_projected = jnp.concatenate([grad_queries, grad_keys, grad_values], axis=3)
    qkv_weight_grad = jnp.einsum(
        "brwc,brwd->cd", act_three, grad_projected, preferred_element_type=jnp.float32
    )
    qv_bias_grad = jnp.concatenate(
        [
            jnp.sum(grad_queries.astype(jnp.float32), axis=(0, 1, 2)),
            jnp.sum(grad_values.astype(jnp.float32), axis=(0, 1, 2)),
        ]
    )
    grad_act_three = jnp.einsum(
        "brwd,cd->brwc", grad_projected, qkv_weight, preferred_element_type=jnp.float32
    )
    grad_res_attn, norm3_gain_grad, norm3_bias_grad = norm_backward(
        grad_act_three, normed_three, inverse_three, gain_three, cell_mask, cell_count
    )
    grad_residual = grad_proj + grad_res_attn
    grad_conv_two = grad_residual.astype(jnp.bfloat16)
    conv2_bias_grad = jnp.sum(grad_residual, axis=(0, 1, 2))
    conv2_weight_grad = kernel_grad(padded_two, grad_conv_two)
    grad_act_two = conv_rows(with_rims(grad_conv_two), flipped(conv2_weight)) * cell_rows
    grad_pre_two = grad_act_two * silu_slope(pre_two)
    scale_grad = jnp.sum(grad_pre_two * affine_two, axis=(1, 2))
    shift_grad = jnp.sum(grad_pre_two, axis=(1, 2))
    shift_grads = jnp.concatenate([scale_grad, shift_grad], axis=1)
    grad_conv_one, norm2_gain_grad, norm2_bias_grad = norm_backward(
        grad_pre_two * scale_part, normed_two, inverse_two, gain_two, cell_mask, cell_count
    )
    conv_one_low = grad_conv_one.astype(jnp.bfloat16)
    conv1_bias_grad = jnp.sum(grad_conv_one, axis=(0, 1, 2))
    conv1_weight_grad = kernel_grad(padded_one, conv_one_low)
    grad_act_one = conv_rows(with_rims(conv_one_low), flipped(conv1_weight)) * cell_rows
    grad_pre_one = grad_act_one * silu_slope(pre_one)
    grad_field_norm, norm1_gain_grad, norm1_bias_grad = norm_backward(
        grad_pre_one, normed_one, inverse_one, gain_one, cell_mask, cell_count
    )
    grad_pixels = (grad_residual + grad_field_norm).astype(jnp.bfloat16)
    time_weight_grad = jnp.dot(time_act.T, shift_grads, precision=PRECISE)
    time_bias_grad = jnp.sum(shift_grads, axis=0)
    summed = lax.psum(
        (
            norm1_gain_grad,
            norm1_bias_grad,
            conv1_weight_grad,
            conv1_bias_grad,
            time_weight_grad,
            time_bias_grad,
            norm2_gain_grad,
            norm2_bias_grad,
            conv2_weight_grad,
            conv2_bias_grad,
            norm3_gain_grad,
            norm3_bias_grad,
            qkv_weight_grad,
            qv_bias_grad,
            out_weight_grad,
            out_bias_grad,
        ),
        ("img", "row"),
    )
    return (
        block_out,
        grad_pixels,
        summed[0],
        summed[1],
        summed[2],
        summed[3],
        summed[4],
        summed[5],
        summed[6],
        summed[7],
        summed[8],
        summed[9],
        summed[10],
        summed[11],
        summed[12],
        summed[13],
        summed[14],
        summed[15],
    )


def mib(count):
    return pltpu.CompilerParams(vmem_limit_bytes=count * 2**20)


def dot(left, right):
    return jnp.dot(left, right, preferred_element_type=jnp.float32)


def dot_rows(left, right):
    return lax.dot_general(
        left, right, (((1,), (1,)), ((), ())), preferred_element_type=jnp.float32
    )


def fold(tile):
    return jnp.sum(tile.reshape(-1, 8, tile.shape[1]), axis=0)


def group_sums(row, width):
    channels = row.shape[1]
    rows = lax.broadcasted_iota(jnp.int32, (channels, channels), 0) // width
    cols = lax.broadcasted_iota(jnp.int32, (channels, channels), 1) // width
    same = jnp.where(rows == cols, 1.0, 0.0).astype(jnp.bfloat16)
    wide = jnp.broadcast_to(row, (16, channels))
    total = None
    for _ in range(3):
        term = wide.astype(jnp.bfloat16)
        wide = wide - term.astype(jnp.float32)
        part = dot(term, same)
        total = part if total is None else total + part
    return total[0:1]


def row_at(index, cols):
    return pl.ds(pl.multiple_of(index * cols, cols), cols)


def total_of(tile):
    return jnp.sum(tile, axis=0, keepdims=True)


def field_stats(read, height, rows, cols, channels):
    width = channels // GROUPS
    each = (height * cols).astype(jnp.float32)
    about = jnp.sum(read(0), axis=0, keepdims=True) * (1.0 / cols)
    zero = jnp.zeros((8, channels), jnp.float32)

    def add(index, totals):
        off = (read(index) - about) * valid_row(index, height)
        return totals[0] + fold(off), totals[1] + fold(off * off)

    first, square = lax.fori_loop(0, rows, add, (zero, zero), unroll=4)
    first, square = total_of(first), total_of(square)
    mean = group_sums(first + about * each, width) / (each * width)
    shift = about - mean
    spread = group_sums(square + 2.0 * first * shift + each * shift * shift, width)
    return mean, lax.rsqrt(spread / (each * width) + EPSILON)


def half_line(mean, inverse, gain, bias, scale=1.0, shift=0.0):
    slope = inverse * gain
    start = bias - mean * slope
    return 0.5 * slope * scale, 0.5 * (start * scale + shift)


def put_shifted(ref, index, tile, cols):
    channels = tile.shape[1]
    column = lax.broadcasted_iota(jnp.int32, tile.shape, 0)
    before = jnp.where(column == 0, 0.0, pltpu.roll(tile, 1, 0))
    after = jnp.where(column == cols - 1, 0.0, pltpu.roll(tile, cols - 1, 0))
    at = row_at(index + 1, cols)
    ref[at, 0:channels] = before.astype(jnp.bfloat16)
    ref[at, channels : 2 * channels] = tile.astype(jnp.bfloat16)
    ref[at, 2 * channels : 3 * channels] = after.astype(jnp.bfloat16)


def clear_rims(ref, cols):
    edge = jnp.zeros((cols, ref.shape[1]), ref.dtype)
    ref[0:cols, :] = edge
    ref[ref.shape[0] - cols : ref.shape[0], :] = edge


def conv_shifted(shifted, weight, out, bias, cols, added=None):
    step = 8 * cols

    def block(index, carry):
        base = index * step
        total = bias
        for tap in range(3):
            at = pl.ds(pl.multiple_of(base + tap * cols, cols), step)
            total = total + dot(shifted[at, :], weight[tap])
        if added is not None:
            total = total + added[pl.ds(pl.multiple_of(base, step), step), :].astype(jnp.float32)
        out[pl.ds(pl.multiple_of(base, step), step), :] = total
        return carry

    lax.fori_loop(0, out.shape[0] // step, block, 0, unroll=True)


def kernel_quarter(shifted, own_t, out, cols):
    cells = own_t.shape[2]
    channels = shifted.shape[1] // 3
    width = own_t.shape[1]
    grad = shifted[cols : cols + cells, channels : 2 * channels]
    for tap in range(3):
        out[tap * width : (tap + 1) * width, :] = dot(own_t[tap], grad).astype(jnp.bfloat16)


def own_place(vec):
    spot = lax.axis_index("row")
    image, head = spot // HEADS, spot % HEADS
    return spot, head, image, jnp.max(vec[11:12, :]).astype(jnp.int32)


def started(sems, *pairs):
    copies = [pltpu.make_async_copy(src, dst, sems.at[k]) for k, (src, dst) in enumerate(pairs)]
    for copy in copies:
        copy.start()
    return copies


def finish_all(copies):
    for copy in copies:
        copy.wait()


def valid_row(index, height):
    return jnp.where(index < height, 1.0, 0.0).astype(jnp.float32)


def forward_kernel(vec, *refs):
    blocks, (w_one_far, w_two_far) = refs[:8], refs[8:10]
    act_three, pix_far, conv_far, residual_far, act_one_far, act_two_far, stats_far = refs[10:17]
    pix, conv_one, residual, stats, w_one, w_two, shift_one, shift_two, in_sems, out_sems = refs[17:]
    cells, channels = pix.shape
    block_cells = blocks[0].shape[0]
    cols = (shift_one.shape[0] - cells) // 2
    rows = cells // cols
    spot, _, _, height = own_place(vec)
    pairs = []
    for step, block in enumerate(blocks):
        base = pl.multiple_of((spot ^ step) * block_cells, block_cells)
        pairs.append((block, pix.at[pl.ds(base, block_cells), :]))
    arriving = started(in_sems, *pairs, (w_one_far, w_one), (w_two_far, w_two))
    gain_one, bias_one, conv_bias_one, gain_two, bias_two = (vec[k : k + 1, :] for k in range(5))
    scale, shift, conv_bias_two, gain_three, bias_three = (vec[k : k + 1, :] for k in range(5, 10))
    inner = (pl.ds(cols, cells), pl.ds(channels, channels))

    def read_pix(index):
        return pix[row_at(index, cols), :].astype(jnp.float32)

    def read_conv(index):
        return conv_one[row_at(index, cols), :]

    def read_res(index):
        return residual[row_at(index, cols), :]

    def activate(read, line, shifted):
        def body(index, carry):
            part = read(index) * line[0] + line[1]
            part = (part + part * jnp.tanh(part)) * valid_row(index, height)
            put_shifted(shifted, index, part, cols)
            return carry

        lax.fori_loop(0, rows, body, 0, unroll=2)

    clear_rims(shift_one, cols)
    clear_rims(shift_two, cols)
    finish_all(arriving[:8])
    leaving = started(out_sems, (pix, pix_far))
    mean_one, inv_one = field_stats(read_pix, height, rows, cols, channels)
    activate(read_pix, half_line(mean_one, inv_one, gain_one, bias_one), shift_one)
    leaving += started(out_sems.at[1:2], (shift_one.at[inner], act_one_far))
    arriving[8].wait()
    conv_shifted(shift_one, w_one, conv_one, conv_bias_one, cols)
    leaving += started(out_sems.at[2:3], (conv_one, conv_far))
    mean_two, inv_two = field_stats(read_conv, height, rows, cols, channels)
    line = half_line(mean_two, inv_two, gain_two, bias_two, scale, shift)
    activate(read_conv, line, shift_two)
    leaving += started(out_sems.at[3:4], (shift_two.at[inner], act_two_far))
    arriving[9].wait()
    conv_shifted(shift_two, w_two, residual, conv_bias_two, cols, pix)
    leaving += started(out_sems.at[4:5], (residual, residual_far))
    mean_three, inv_three = field_stats(read_res, height, rows, cols, channels)
    stats[...] = jnp.concatenate(
        [mean_one, inv_one, mean_two, inv_two, mean_three, inv_three, mean_one, mean_one], axis=0
    )
    leaving += started(out_sems.at[5:6], (stats, stats_far))
    slope = inv_three * gain_three
    start = bias_three - mean_three * slope

    def third(index, carry):
        act_three[row_at(index, cols), :] = (read_res(index) * slope + start).astype(jnp.bfloat16)
        return carry

    lax.fori_loop(0, rows, third, 0, unroll=4)
    finish_all(leaving)


def attention_kernel(columns, vec, act_three, w_heads, w_out, biases, *refs):
    blocks = refs[:8]
    value_key_far, query_far, grad_far, mixed_far, sums_far = refs[8:13]
    (
        grad_blocks, grad_proj, value_key, query_part, sums,
        query_grad, key_pad, value_pad, heads_t, mixed, mask_row, in_sems, out_sems,
    ) = refs[13:]
    cells, channels = act_three.shape
    block_cells = blocks[0].shape[0]
    spot, _, _, height = own_place(vec)
    half = mixed.shape[1] // 2
    cols = columns
    scaling = half**-0.5
    valid_cells = height * cols
    step = 256
    pairs = []
    for index, block in enumerate(blocks):
        base = pl.multiple_of((spot ^ index) * block_cells, block_cells)
        pairs.append((block, grad_blocks.at[pl.ds(base, block_cells), :]))
    arriving = started(in_sems, *pairs)

    def project(index, carry):
        at = pl.ds(pl.multiple_of(index * 512, 512), 512)
        parts = dot(act_three[at, :], w_heads[...]) + biases[0:1, :]
        query_grad[at, :] = parts[:, 0 : 2 * half].astype(jnp.bfloat16) * jnp.bfloat16(scaling)
        key_pad[at, :] = parts[:, 2 * half : 4 * half].astype(jnp.bfloat16)
        value_pad[at, :] = parts[:, 4 * half : 6 * half].astype(jnp.bfloat16)
        query, key = parts[:, 0 : 2 * half], parts[:, 2 * half : 4 * half]
        query_size = jnp.sum(query * query, axis=1, keepdims=True) * (scaling * scaling)
        key_size = jnp.sum(key * key, axis=1, keepdims=True)
        return jnp.maximum(carry[0], jnp.max(query_size)), jnp.maximum(carry[1], jnp.max(key_size))

    norms = lax.fori_loop(0, cells // 512, project, (jnp.float32(0.0), jnp.float32(0.0)))
    lane = lax.broadcasted_iota(jnp.int32, (1, cells), 1)
    mask_row[...] = jnp.where(lane < valid_cells, 0.0, MASKED)
    heads_t[...] = jnp.zeros(heads_t.shape, jnp.float32)
    mixed[...] = jnp.zeros(mixed.shape, jnp.bfloat16)
    finish_all(arriving)

    def clean(index, total):
        at = pl.ds(pl.multiple_of(index * block_cells, block_cells), block_cells)
        cell = index * block_cells + lax.broadcasted_iota(jnp.int32, (block_cells, channels), 0)
        kept = jnp.where(cell < valid_cells, grad_blocks[at, :].astype(jnp.float32), 0.0)
        low = kept.astype(jnp.bfloat16)
        grad_proj[at, :] = low
        query_grad[at, :] = query_grad[at, :] + dot(low, w_out[...]).astype(jnp.bfloat16)
        return total + fold(kept)

    total = lax.fori_loop(
        0, cells // block_cells, clean, jnp.zeros((8, channels), jnp.float32)
    )
    sums[...] = jnp.concatenate([total_of(total), jnp.zeros((7, channels), jnp.float32)], axis=0)
    leaving = started(out_sems, (grad_proj, grad_far), (sums, sums_far))

    def query_block(shifted, index, carry):
        at = pl.ds(pl.multiple_of(index * step, step), step)
        both = query_grad[at, :]
        scores = dot_rows(both, key_pad[...]) + mask_row[...]
        if shifted:
            scores = scores - jnp.max(scores, axis=1, keepdims=True)
        weights = jnp.exp(scores)
        total = jnp.zeros((step, 2 * half), jnp.float32)
        for start in range(0, cells, 2 * half):
            total = total + weights[:, start : start + 2 * half]
        inverse = 1.0 / jnp.sum(total, axis=1, keepdims=True)
        low = weights.astype(jnp.bfloat16)
        out = dot(low, value_pad[...]) * inverse
        wide = both.astype(jnp.float32)
        delta = jnp.sum(wide * out, axis=1, keepdims=True)
        turned = jnp.transpose(wide * inverse).astype(jnp.bfloat16)
        grad_probs = dot_rows(both, value_pad[...])
        grad_scores = (low.astype(jnp.float32) * (grad_probs - delta)).astype(jnp.bfloat16)
        grad_query = dot(grad_scores, key_pad[...]) * (inverse * scaling)
        mixed[at, :] = (out + grad_query).astype(jnp.bfloat16)
        heads_t[0:half, :] += dot(turned[0:half], grad_scores)
        heads_t[half : 2 * half, :] += dot(turned[half : 2 * half], low)
        return carry

    query_most, key_most = norms
    narrow = query_most * key_most <= 3600.0

    @pl.when(narrow)
    def _():
        lax.fori_loop(0, cells // step, functools.partial(query_block, False), 0, unroll=2)

    @pl.when(jnp.logical_not(narrow))
    def _():
        count = (valid_cells + step - 1) // step
        lax.fori_loop(0, count, functools.partial(query_block, True), 0)

    for start in range(0, cells, step):
        value_key[start : start + step, :] = jnp.transpose(heads_t[:, start : start + step]).astype(
            jnp.bfloat16
        )
    query_part[:, 0:half] = mixed[0 : cells // 2, 0:half]
    query_part[:, half : 2 * half] = mixed[cells // 2 : cells, 0:half]
    leaving += started(
        out_sems.at[2:5], (value_key, value_key_far), (query_part, query_far), (mixed, mixed_far)
    )
    finish_all(leaving)


def aside_kernel(vec, *refs):
    act_far, (mixed_far, value_key_far, act_three_far, grad_far) = refs[0:2], refs[2:6]
    own_far, weight_far, sends = refs[6:8], refs[8], refs[9:13]
    acts, mixed, value_key, act_three, grad_proj, padded, own, weight_rows, in_sems, out_sems = (
        refs[13:]
    )
    cells, channels = act_three.shape
    cols = (padded.shape[0] - cells) // 2
    lanes = mixed.shape[1]
    half = lanes // 2
    spot, head, image, _ = own_place(vec)
    arriving = started(
        in_sems,
        (mixed_far, mixed),
        (value_key_far, value_key),
        (act_three_far, act_three),
        (grad_far, grad_proj),
        (act_far[0], acts.at[0]),
        (act_far[1], acts.at[1]),
    )
    block_cells = sends[0].shape[0]
    step = 256
    arriving[0].wait()
    for k, send in enumerate(sends):
        tiles = []
        for part in range(2):
            block = (head ^ k) + HEADS * (image ^ part)
            at = pl.ds(pl.multiple_of(block * block_cells, block_cells), block_cells)
            tiles.append(mixed[at, half:lanes])
        send[...] = jnp.concatenate(tiles, axis=1)
    finish_all(arriving[1:4])

    def gather(index, totals):
        at = pl.ds(pl.multiple_of(index * step, step), step)
        low_mixed, low_heads, act = mixed[at, :], value_key[at, :], act_three[at, :]
        mixed_t = jnp.transpose(low_mixed.astype(jnp.float32)).astype(jnp.bfloat16)
        heads_t = jnp.transpose(low_heads.astype(jnp.float32)).astype(jnp.bfloat16)
        return (
            totals[0] + dot(mixed_t, act),
            totals[1] + dot(heads_t, act),
            totals[2] + dot(mixed_t, grad_proj[at, :]),
            totals[3] + fold(low_mixed.astype(jnp.float32)),
            totals[4] + fold(low_heads.astype(jnp.float32)),
        )

    square = jnp.zeros((lanes, channels), jnp.float32)
    line = jnp.zeros((8, lanes), jnp.float32)
    from_query, from_heads, from_out, query_sum, value_sum = lax.fori_loop(
        0, cells // step, gather, (square, square, square, line, line)
    )
    weight_rows[0:half, :] = from_query[0:half].astype(jnp.bfloat16)
    weight_rows[half : 3 * half, :] = from_heads.astype(jnp.bfloat16)
    weight_rows[3 * half : 4 * half, :] = from_out[half:lanes].astype(jnp.bfloat16)
    which = lax.axis_index("img") * 2 + image
    lane = lax.broadcasted_iota(jnp.int32, (1, channels), 1)
    now = jnp.max(vec[12:13, :]).astype(jnp.int32)
    high = jnp.where(lane == which, (now // 32).astype(jnp.float32), 0.0)
    rest = jnp.where(lane == which, (now % 32).astype(jnp.float32), 0.0)
    row = jnp.concatenate([total_of(query_sum), total_of(value_sum)], axis=1)
    below = jnp.zeros((weight_rows.shape[0] - 4 * half - 3, channels), jnp.float32)
    weight_rows[4 * half :, :] = jnp.concatenate([row, high, rest, below], axis=0).astype(
        jnp.bfloat16
    )
    source = lax.broadcasted_iota(jnp.int32, (channels, 3 * half), 0)
    target = lax.broadcasted_iota(jnp.int32, (channels, 3 * half), 1)
    chosen = jnp.where(source == head * half + target % half, 1.0, 0.0).astype(jnp.bfloat16)
    lane = lax.broadcasted_iota(jnp.int32, (step, 3 * half), 1)
    column = lax.broadcasted_iota(jnp.int32, (step, 3 * half), 0) % cols
    leaving = started(out_sems.at[2:3], (weight_rows, weight_far))
    for k in range(2):
        arriving[4 + k].wait()
        clear_rims(padded, cols)

        def widen(index, carry):
            at = pl.ds(pl.multiple_of(index * step, step), step)
            tile = dot(acts[k, at, :], chosen)
            before = jnp.where(column == 0, 0.0, pltpu.roll(tile, 1, 0))
            after = jnp.where(column == cols - 1, 0.0, pltpu.roll(tile, step - 1, 0))
            tile = jnp.where(lane < half, before, jnp.where(lane < 2 * half, tile, after))
            padded[pl.ds(pl.multiple_of(index * step + cols, cols), step), :] = tile
            return carry

        lax.fori_loop(0, cells // step, widen, 0)
        for tap in range(3):

            def turn(index, carry):
                at = pl.ds(pl.multiple_of(index * step + tap * cols, cols), step)
                to = pl.ds(pl.multiple_of(index * step, step), step)
                own[k, tap, :, to] = jnp.transpose(padded[at, :]).astype(jnp.bfloat16)
                return carry

            lax.fori_loop(0, cells // step, turn, 0)
        leaving += started(out_sems.at[k : k + 1], (own.at[k], own_far[k]))
    finish_all(leaving)


def middle_kernel(vec, qkv_t, *refs):
    heads_far, sides_far = refs[0:8:2], refs[1:8:2]
    grad_far, residual_far, stats_far, own_two_far, rows_far = refs[8:13]
    weight_far, conv_far, own_one_far, out_sums_far = refs[13:17]
    shifted_one, grad_res_far, payload_far = refs[17], refs[18], refs[19:23]
    (
        heads, sides, grad_proj, residual, stats, own_two, grad_res, early, grad_act, shifted,
        weight, conv_one, own_one, out_sums, late, in_sems, out_sems,
    ) = refs[23:]
    cells, channels = grad_proj.shape
    cols = (shifted.shape[0] - cells) // 2
    rows = cells // cols
    _, head, image, height = own_place(vec)
    column = lax.axis_index("img")
    width = channels // GROUPS
    count = (height * (cols * width)).astype(jnp.float32)
    half = qkv_t.shape[1]
    pairs = [(far, heads.at[head ^ k]) for k, far in enumerate(heads_far)]
    pairs += [(far, sides.at[head ^ k]) for k, far in enumerate(sides_far)]
    arriving = started(
        in_sems,
        *pairs,
        (stats_far, stats),
        (residual_far, residual),
        (grad_far, grad_proj),
        (own_two_far, own_two),
        (rows_far, early.at[pl.ds(9 * half, 5 * half), :]),
        (weight_far, weight),
        (conv_far, conv_one),
        (own_one_far, own_one),
        (out_sums_far, out_sums),
    )
    zeros = jnp.zeros((half, channels), jnp.bfloat16)
    halfway = cells // 2
    step = 512
    pairs = ((0, 1), (2, 3))
    w_main = []
    for a, b in pairs:
        order = [HEADS + a, 2 * HEADS + a, HEADS + b, 2 * HEADS + b]
        w_main.append(jnp.concatenate([qkv_t[k] for k in order], axis=0))
    finish_all(arriving[:8])
    for part in range(2):
        w_side = []
        for a, b in pairs:
            left, right = qkv_t[a], qkv_t[b]
            order = [left, zeros, right, zeros] if part == 0 else [zeros, left, zeros, right]
            w_side.append(jnp.concatenate(order, axis=0))
        for base in range(0, halfway, step):
            start = part * halfway + base
            total = None
            for k, (a, b) in enumerate(pairs):
                main = jnp.concatenate(
                    [heads[a][start : start + step, :], heads[b][start : start + step, :]], axis=1
                )
                side = jnp.concatenate(
                    [sides[a][base : base + step, :], sides[b][base : base + step, :]], axis=1
                )
                term = dot(main, w_main[k]) + dot(side, w_side[k])
                total = term if total is None else total + term
            grad_act[start : start + step, :] = total
    finish_all(arriving[8:10])
    mean, inverse = stats[4:5, :], stats[5:6, :]
    gain = vec[8:9, :]
    zero = jnp.zeros((8, channels), jnp.float32)

    def normed(index):
        return (residual[row_at(index, cols), :] - mean) * inverse

    def add(index, totals):
        grad = grad_act[row_at(index, cols), :]
        return totals[0] + fold(grad), totals[1] + fold(grad * normed(index))

    plain, cross = lax.fori_loop(0, rows, add, (zero, zero), unroll=2)
    plain, cross = total_of(plain), total_of(cross)
    mean_plain = group_sums(plain * gain, width) / count
    mean_cross = group_sums(cross * gain, width) / count
    clear_rims(shifted, cols)
    arriving[10].wait()

    def finish(index, total):
        at = row_at(index, cols)
        inner = (grad_act[at, :] * gain - mean_plain - normed(index) * mean_cross) * inverse
        grad = grad_proj[at, :].astype(jnp.float32) + inner * valid_row(index, height)
        grad_res[at, :] = grad
        put_shifted(shifted, index, grad, cols)
        return total + fold(grad)

    total = total_of(lax.fori_loop(0, rows, finish, zero, unroll=2))
    three_lines = [cross, plain, total]
    leaving = started(out_sems, (grad_res, grad_res_far))
    finish_all(arriving[11:13])
    kernel_quarter(shifted, own_two, early, cols)
    before = early.shape[0] // 4
    chunks = [pl.ds(pl.multiple_of((column ^ k) * before, 16), before) for k in range(4)]
    leaving += started(
        out_sems.at[1:5],
        *[(early.at[at, :], far.at[pl.ds(0, before), :]) for at, far in zip(chunks, payload_far)],
    )

    gain, bias, scale, shift = (vec[k : k + 1, :] for k in range(3, 7))
    clear_rims(shifted_one, cols)
    arriving[13].wait()
    conv_shifted(shifted, weight, grad_act, 0.0, cols)
    arriving[14].wait()
    mean, inverse = stats[2:3, :], stats[3:4, :]
    line = half_line(mean, inverse, gain, bias, scale, shift)
    begin = mean * inverse

    def add(index, totals):
        at = row_at(index, cols)
        value = conv_one[at, :]
        unit = value * inverse - begin
        part = value * line[0] + line[1]
        sigmoid = 0.5 + 0.5 * jnp.tanh(part)
        slope = sigmoid + 2.0 * part * sigmoid * (1.0 - sigmoid)
        grad = grad_act[at, :] * valid_row(index, height) * slope
        grad_act[at, :] = grad
        return totals[0] + fold(grad), totals[1] + fold(grad * unit)

    plain, cross = lax.fori_loop(0, rows, add, (zero, zero), unroll=2)
    plain, cross = total_of(plain), total_of(cross)
    factor = gain * scale
    mean_plain = group_sums(plain * factor, width) / count
    mean_cross = group_sums(cross * factor, width) / count
    one, two = factor * inverse, mean_cross * inverse * inverse
    three = (mean_plain - begin * mean_cross) * inverse

    def finish(index, total):
        at = row_at(index, cols)
        grad = grad_act[at, :] * one - conv_one[at, :] * two - three
        grad = grad * valid_row(index, height)
        put_shifted(shifted_one, index, grad, cols)
        return total + fold(grad)

    total = total_of(lax.fori_loop(0, rows, finish, zero, unroll=2))
    finish_all(arriving[15:])
    kernel_quarter(shifted_one, own_one, late, cols)
    lines = [
        *three_lines, out_sums[0:1, :], cross * scale, plain * scale, total,
        jnp.zeros((9, channels), jnp.float32),
    ]
    mine = 2 * (column * 2 + image)
    place = lax.broadcasted_iota(jnp.int32, (16, channels), 0)
    both = jnp.where(place == mine, gain * cross + bias * plain, 0.0)
    lines.append(jnp.where(place == mine + 1, plain, both))
    base = 3 * own_one.shape[1]
    lines.append(jnp.zeros((late.shape[0] - base - 32, channels), jnp.float32))
    late[base:, :] = jnp.concatenate(lines, axis=0).astype(jnp.bfloat16)
    after = late.shape[0] // 4
    chunks = [pl.ds(pl.multiple_of((column ^ k) * after, 16), after) for k in range(4)]
    leaving += started(
        out_sems.at[5:9],
        *[
            (late.at[at, :], far.at[pl.ds(before, after), :])
            for at, far in zip(chunks, payload_far)
        ],
    )
    finish_all(leaving)


def first_kernel(vec, shifted, weight_far, pix_far, grad_far, stats_far, *refs):
    out_own_far, out_away_far, sums_far = refs[:3]
    weight, pix, grad_res, stats, out, sums, grad_act, in_sems, out_sems = refs[3:]
    cells, channels = pix.shape
    block_cells = out.shape[1]
    cols = (shifted.shape[0] - cells) // 2
    rows = cells // cols
    spot, _, _, height = own_place(vec)
    width = channels // GROUPS
    count = (height * (cols * width)).astype(jnp.float32)
    arriving = started(
        in_sems,
        (weight_far, weight),
        (stats_far, stats),
        (pix_far, pix),
        (grad_far, grad_res),
    )
    gain, bias = vec[0:1, :], vec[1:2, :]
    zero = jnp.zeros((8, channels), jnp.float32)
    arriving[0].wait()
    conv_shifted(shifted, weight, grad_act, 0.0, cols)
    finish_all(arriving[1:])
    mean, inverse = stats[0:1, :], stats[1:2, :]
    line = half_line(mean, inverse, gain, bias)
    begin = mean * inverse

    def normed(at):
        return pix[at, :].astype(jnp.float32) * inverse - begin

    def add(index, totals):
        at = row_at(index, cols)
        value = pix[at, :].astype(jnp.float32)
        unit = value * inverse - begin
        part = value * line[0] + line[1]
        sigmoid = 0.5 + 0.5 * jnp.tanh(part)
        slope = sigmoid + 2.0 * part * sigmoid * (1.0 - sigmoid)
        grad = grad_act[at, :] * valid_row(index, height) * slope
        grad_act[at, :] = grad
        return totals[0] + fold(grad), totals[1] + fold(grad * unit)

    plain, cross = lax.fori_loop(0, rows, add, (zero, zero), unroll=2)
    plain, cross = total_of(plain), total_of(cross)
    mean_plain = group_sums(plain * gain, width) / count
    mean_cross = group_sums(cross * gain, width) / count
    block_rows = block_cells // cols
    for part in range(2):
        first_row = (spot ^ (4 * part)) * block_rows
        for line in range(block_rows):
            at = row_at(first_row + line, cols)
            grad = (grad_act[at, :] * gain - mean_plain - normed(at) * mean_cross) * inverse
            grad = grad_res[at, :] + grad * valid_row(first_row + line, height)
            out[part, line * cols : (line + 1) * cols, :] = grad.astype(jnp.bfloat16)
    sums[...] = jnp.concatenate([cross, plain, jnp.zeros((6, channels), jnp.float32)], axis=0)
    finish_all(
        started(
            out_sems, (out.at[0], out_own_far), (out.at[1], out_away_far), (sums, sums_far)
        )
    )


def block_kernel(columns, vec, w_out, *refs):
    heads, residual_far = refs[:4], refs[4]
    out_own, out_away, residual, in_sems = refs[5:]
    block_cells, channels = out_own.shape
    spot, head, _, height = own_place(vec)
    cols = columns
    bases = [
        pl.multiple_of((spot ^ (4 * part)) * block_cells, block_cells) for part in range(2)
    ]
    pairs = [
        (residual_far.at[pl.ds(base, block_cells), :], residual.at[part])
        for part, base in enumerate(bases)
    ]
    finish_all(started(in_sems, *pairs))
    for part, out in enumerate((out_own, out_away)):
        total = residual[part] + vec[10:11, :]
        for step in range(4):
            width = w_out.shape[1]
            tile = heads[step][:, part * width : (part + 1) * width]
            total = total + dot(tile, w_out[head ^ step])
        cell = bases[part] + lax.broadcasted_iota(jnp.int32, (block_cells, channels), 0)
        out[...] = jnp.where(cell < height * cols, total, 0.0).astype(jnp.bfloat16)


def prepare_kernel(*refs):
    shifts, lines_far, kernels_far = refs[0], refs[1:15], refs[15:17]
    vec, w_heads, w_out, biases, qkv_t = refs[17:22]
    backs_far = refs[22:24]
    kernels, backs, qkv_weight, out_weight, heights, timesteps, qv_bias, *lines = refs[24:40]
    line_sems, in_sems, out_sems = refs[40:]
    channels = out_weight.shape[0]
    half = channels // HEADS
    small = started(
        line_sems,
        *zip(lines_far, (*lines, qv_bias, qkv_weight, out_weight, heights, timesteps)),
    )
    arriving = started(
        in_sems, *[(far, kernels.at[k]) for k, far in enumerate(kernels_far)]
    )
    finish_all(small)
    spot = lax.axis_index("row")
    image, head = spot // HEADS, spot % HEADS
    shift_row = shifts[pl.ds(image, 1), :]
    order = list(range(5)) + [None, None] + list(range(5, 9))
    for line, k in enumerate(order):
        if k is not None:
            vec[line : line + 1, :] = lines[k][...].astype(jnp.float32).reshape(1, channels)
    vec[5:6, :] = 1.0 + shift_row[:, :channels]
    vec[6:7, :] = shift_row[:, channels:]
    vec[11:12, :] = jnp.full((1, channels), heights[image].astype(jnp.float32))
    vec[12:13, :] = jnp.full((1, channels), timesteps[image].astype(jnp.float32))
    vec[13:16, :] = jnp.zeros((3, channels), jnp.float32)
    source = lax.broadcasted_iota(jnp.int32, (channels, 2 * half), 0)
    lane = lax.broadcasted_iota(jnp.int32, (channels, 2 * half), 1)
    first = jnp.where((lane < half) & (source == head * half + lane), 1.0, 0.0)
    second = jnp.where((lane >= half) & (source == head * half + lane - half), 1.0, 0.0)
    first, second = first.astype(jnp.bfloat16), second.astype(jnp.bfloat16)
    lanes = 2 * half
    for part, taken in enumerate((first, first, second)):
        whole = qkv_weight[:, part * channels : (part + 1) * channels]
        w_heads[:, part * lanes : (part + 1) * lanes] = dot(whole, taken).astype(jnp.bfloat16)
    turned = jnp.transpose(out_weight[...].astype(jnp.float32)).astype(jnp.bfloat16)
    w_out[...] = dot(turned, second).astype(jnp.bfloat16)
    both = qv_bias[...].astype(jnp.float32).reshape(1, 2 * channels)
    wide = jnp.broadcast_to(both, (16, 2 * channels)).astype(jnp.bfloat16)
    biases[:, 0:lanes] = dot(wide[:, :channels], first)[0:8]
    biases[:, lanes : 2 * lanes] = jnp.zeros((8, lanes), jnp.float32)
    biases[:, 2 * lanes : 3 * lanes] = dot(wide[:, channels:], second)[0:8]
    for block in range(0, 3 * HEADS, 2):
        whole = qkv_weight[:, block // 2 * lanes : (block // 2 + 1) * lanes].astype(jnp.float32)
        whole = jnp.transpose(whole).astype(jnp.bfloat16)
        qkv_t[block] = whole[0:half]
        qkv_t[block + 1] = whole[half:lanes]
    leaving = []
    for k in range(2):
        arriving[k].wait()

        def turn(tap, carry):
            tile = kernels[k, 2 - tap // 3, 2 - tap % 3].astype(jnp.float32)
            at = pl.ds(pl.multiple_of(tap % 3 * channels, channels), channels)
            backs[k, tap // 3, at, :] = jnp.transpose(tile).astype(jnp.bfloat16)
            return carry

        lax.fori_loop(0, 9, turn, 0)
        leaving += started(out_sems.at[k : k + 1], (backs.at[k], backs_far[k]))
    finish_all(leaving)


def gathered_rows(parts, early, late):
    spot = lax.axis_index("row")
    head, column = spot % HEADS, lax.axis_index("img")
    early_lines, late_lines = early.shape[1] // 4, late.shape[1] // 4
    lines = early_lines + late_lines
    for index, part in enumerate(parts):
        away = column ^ (index // 2)
        early_at = pl.ds(pl.multiple_of(away * early_lines, 16), early_lines)
        late_at = pl.ds(pl.multiple_of(away * late_lines, 16), late_lines)
        for pair in range(2):
            quarter, base = head ^ (index % 2 + 2 * pair), pair * lines
            early[quarter, early_at, :] = part[base : base + early_lines]
            late[quarter, late_at, :] = part[base + early_lines : base + lines]


def place_taps(gathered, out):
    half = out.shape[2] // HEADS
    for quarter in range(HEADS):
        for tap in range(9):
            base = tap * half
            out[tap // 3, tap % 3, quarter * half : (quarter + 1) * half, :] = gathered[
                quarter, base : base + half, :
            ].astype(jnp.float32)


def final_kernel(*refs):
    parts, frequency = refs[:8], refs[8]
    one_far, two_far, qkv_far, out_far, time_far = refs[9:14]
    bias_out, time_bias, rows = refs[14], refs[15], refs[16:25]
    early, late, norm_one, one, two, qkv_out, out_out, time_out, out_sems = refs[25:]
    gathered_rows(parts, early, late)
    place_taps(late, one)
    leaving = started(out_sems, (one, one_far))
    place_taps(early, two)
    leaving += started(out_sems.at[1:2], (two, two_far))
    half = out_out.shape[0] // HEADS
    nine = 9 * half
    sums = []
    for quarter in range(HEADS):
        out_out[quarter * half : (quarter + 1) * half, :] = early[
            quarter, nine + 3 * half : nine + 4 * half, :
        ].astype(jnp.float32)
        sums.append(early[quarter, nine + 4 * half : nine + 4 * half + 16].astype(jnp.float32))
    pieces = [part[0:1, :half] for part in sums] + [part[0:1, 3 * half :] for part in sums]
    bias_out[...] = jnp.concatenate(pieces, axis=1).reshape(bias_out.shape)
    for part in range(3):
        block = jnp.concatenate(
            [
                early[quarter, nine + part * half : nine + (part + 1) * half, :]
                for quarter in range(HEADS)
            ],
            axis=0,
        )
        width = HEADS * half
        qkv_out[:, part * width : (part + 1) * width] = jnp.transpose(block.astype(jnp.float32))
    leaving += started(out_sems.at[2:4], (qkv_out, qkv_far), (out_out, out_far))
    column = lax.axis_index("img")
    lines = (early.shape[1] + late.shape[1]) // 2
    for step in range(4):
        norm_one[column ^ step] = parts[2 * step][lines : lines + 16, :].astype(jnp.float32)
    total = norm_one[0] + norm_one[1] + norm_one[2] + norm_one[3]
    rest = late[0, nine:, :]
    whole = jnp.concatenate([total[0:2], rest[0:16, :].astype(jnp.float32)[0:7]], axis=0)
    for k, row in enumerate(rows):
        row[...] = whole[k : k + 1].reshape(row.shape)
    shifts = rest[16:32, :].astype(jnp.float32)
    pair = jnp.concatenate([shifts[k : k + 1, :] for k in range(0, 16, 2)], axis=0)
    other = jnp.concatenate([shifts[k : k + 1, :] for k in range(1, 16, 2)], axis=0)
    both = jnp.concatenate([pair, other], axis=1)
    time_bias[...] = total_of(both).reshape(time_bias.shape)
    steps = sums[0][1:2, :] * 32.0 + sums[0][2:3, :]
    image = lax.broadcasted_iota(jnp.int32, (8, steps.shape[1]), 0)
    lane = lax.broadcasted_iota(jnp.int32, (8, steps.shape[1]), 1)
    now = jnp.sum(jnp.where(image == lane, steps, 0.0), axis=1, keepdims=True)
    angles = now * frequency[...]
    left = jnp.concatenate([jnp.cos(angles), jnp.sin(angles)], axis=1)
    left = left / (1.0 + jnp.exp(-left))
    terms = []
    for _ in range(3):
        terms.append(left.astype(jnp.bfloat16).astype(jnp.float32))
        left = left - terms[-1]
    terms = jnp.concatenate(terms + [jnp.zeros_like(left)], axis=0)
    both = jnp.concatenate([both] * 3 + [jnp.zeros_like(both)], axis=0).astype(jnp.bfloat16)
    time_out[...] = lax.dot_general(
        terms.astype(jnp.bfloat16), both, (((0,), (0,)), ((), ())),
        preferred_element_type=jnp.float32,
    )
    leaving += started(out_sems.at[4:5], (time_out, time_far))
    finish_all(leaving)


def swap(value, axis, step):
    count = lax.axis_size(axis)
    return lax.ppermute(value, axis, [(k, k ^ step) for k in range(count)])


def pick(stacked, index):
    return lax.dynamic_index_in_dim(stacked, index, 0, keepdims=False)


def add_up(*parts):
    total = parts[0].astype(jnp.float32)
    for part in parts[1:]:
        total = total + part.astype(jnp.float32)
    return total.astype(jnp.bfloat16)


def from_columns(pair):
    return [pair] + [swap(pair, "img", step) for step in (1, 2, 3)]


def with_mates(columns):
    return [part for mine in columns for part in (mine, swap(mine, "row", 1))]


def gather_columns(pair):
    return with_mates(from_columns(pair))


def call(kernel, near_outs, far_outs, scratch, limit, work, scalars, near, far, last_outs=()):
    close = pl.BlockSpec(memory_space=pltpu.VMEM)
    distant = pl.BlockSpec(memory_space=pltpu.HBM)
    operands = list(near) + [pltpu.with_memory_space_constraint(array, pltpu.HBM) for array in far]
    moved = sum(array.size * array.dtype.itemsize for array in operands)
    return pl.pallas_call(
        kernel,
        out_shape=[jax.ShapeDtypeStruct(*kind) for kind in near_outs]
        + [pltpu.HBM(*kind) for kind in far_outs]
        + [jax.ShapeDtypeStruct(*kind) for kind in last_outs],
        in_specs=[pl.BlockSpec(memory_space=pltpu.SMEM)] * len(scalars)
        + [close] * len(near)
        + [distant] * len(far),
        out_specs=[close] * len(near_outs)
        + [distant] * len(far_outs)
        + [close] * len(last_outs),
        scratch_shapes=[pltpu.VMEM(*kind) if isinstance(kind, tuple) else kind for kind in scratch],
        compiler_params=mib(limit),
        cost_estimate=pl.CostEstimate(flops=work, bytes_accessed=moved, transcendentals=0),
    )(*scalars, *operands)


def sems(count):
    return pltpu.SemaphoreType.DMA((count,))


def gather_field(mine, theirs):
    far, far_near = swap(theirs, "row", 4), swap(theirs, "row", 6)
    return [mine, swap(mine, "row", 1), swap(mine, "row", 2), None, far, None, far_near, None]


def relayed(blocks, after=None):
    sent = [blocks[2], blocks[4], blocks[6]]
    if after is not None:
        sent = lax.optimization_barrier((*sent, after))[:3]
    odd = [swap(block, "row", 1) for block in sent]
    return [
        blocks[0], blocks[1], blocks[2], odd[0], blocks[4], odd[1], blocks[6], odd[2],
    ]


def local_image(
    pixels,
    heights,
    timesteps,
    norm1_gain,
    norm1_bias,
    conv1_weight,
    conv1_bias,
    time_weight,
    time_bias,
    norm2_gain,
    norm2_bias,
    conv2_weight,
    conv2_bias,
    norm3_gain,
    norm3_bias,
    qkv_weight,
    qv_bias,
    out_weight,
    out_bias,
    grad_out,
):
    images, row_count, cols, channels = pixels.shape
    block_cells = row_count * cols
    cells = block_cells * lax.axis_size("row")
    half = channels // HEADS
    column = lax.axis_index("img")
    image = lax.axis_index("row") // HEADS
    low, full = jnp.bfloat16, jnp.float32
    pixel_blocks = pixels.reshape(images, block_cells, channels)
    grad_blocks = grad_out.reshape(images, block_cells, channels)
    field = gather_field(pick(pixel_blocks, image), pick(pixel_blocks, 1 - image))
    later = (pick(grad_blocks, image), pick(grad_blocks, 1 - image), field[4], field[6])
    later = lax.optimization_barrier(later)
    grads = gather_field(later[0], later[1])
    field[4], field[6] = later[2], later[3]
    time_act = jax.nn.silu(embed_steps(timesteps, time_weight.shape[0]))
    shifts = jnp.dot(time_act, time_weight.astype(full), precision=PRECISE) + time_bias.astype(full)
    kernel_shape = (3, 3 * channels, channels)
    lanes = 2 * half
    vec, w_heads, w_out, biases, qkv_t, w_one_back, w_two_back = call(
        prepare_kernel,
        [
            ((16, channels), full), ((channels, 3 * lanes), low), ((channels, lanes), low),
            ((8, 3 * lanes), full), ((3 * HEADS, half, channels), low),
        ],
        [(kernel_shape, low), (kernel_shape, low)],
        [
            ((2, 3, 3, channels, channels), low), ((2,) + kernel_shape, low),
            ((channels, 3 * channels), low), ((channels, channels), low),
            pltpu.SMEM((images,), jnp.int32), pltpu.SMEM((images,), jnp.int32),
            ((2 * channels,), low), *[((channels,), low)] * 9,
            sems(14), sems(2), sems(2),
        ],
        16,
        channels,
        [],
        [shifts],
        [
            norm1_gain, norm1_bias, conv1_bias, norm2_gain, norm2_bias, conv2_bias, norm3_gain,
            norm3_bias, out_bias, qv_bias, qkv_weight, out_weight, heights, timesteps,
            conv1_weight,
            conv2_weight,
        ],
    )
    field = relayed(field, vec)
    w_one, w_two = conv1_weight.reshape(kernel_shape), conv2_weight.reshape(kernel_shape)
    rim_cells = cells + 2 * cols
    cost = 9 * cells * channels * channels // 2

    wide, tall = (cells, channels), (rim_cells, 3 * channels)
    rows_eight = ((8, channels), full)
    act_three, pix, conv_one, residual, act_one, act_two, stats = call(
        forward_kernel,
        [(wide, low)],
        [(wide, low), (wide, full), (wide, full), (wide, low), (wide, low), rows_eight],
        [
            (wide, low), (wide, full), (wide, full), rows_eight, (kernel_shape, low),
            (kernel_shape, low), (tall, low), (tall, low), sems(10), sems(6),
        ],
        28,
        cost * 25,
        [],
        [vec],
        [*field, w_one, w_two],
    )
    grads = relayed(grads, act_three)
    query_shape, head_shape = (cells // 2, lanes), (cells, lanes)
    value_key, query_part, grad_proj, mixed, out_sums = call(
        functools.partial(attention_kernel, cols),
        [],
        [(head_shape, low), (query_shape, low), (wide, low), (head_shape, low), rows_eight],
        [
            (wide, low), (wide, low), (head_shape, low), (query_shape, low), rows_eight,
            (head_shape, low), (head_shape, low), (head_shape, low), ((lanes, cells), full),
            (head_shape, low), ((1, cells), full), sems(8), sems(5),
        ],
        36,
        cost * 34,
        [],
        [vec, act_three, w_heads, w_out, biases],
        grads,
    )

    key_near, query_near = swap(value_key, "row", 2), swap(query_part, "row", 2)
    key_mate, query_mate = swap(value_key, "row", 1), swap(query_part, "row", 1)
    own_shape = (3, 3 * half, cells)
    send_shape = ((block_cells, lanes), low)
    own_one, own_two, weight_rows, *sends = call(
        aside_kernel,
        [],
        [(own_shape, low), (own_shape, low), ((5 * half, channels), low)],
        [
            ((2,) + wide, low), (head_shape, low), (head_shape, low), (wide, low), (wide, low),
            ((rim_cells, 3 * half), full), ((2,) + own_shape, low), ((5 * half, channels), low),
            sems(6), sems(3),
        ],
        28,
        cost * 27,
        [],
        [vec],
        [act_one, act_two, mixed, value_key, act_three, grad_proj],
        [send_shape] * 4,
    )
    key_near, query_near, own_two = lax.optimization_barrier((key_near, query_near, own_two))
    packed_all = [
        value_key, query_part, key_mate, query_mate,
        key_near, query_near, swap(key_near, "row", 1), swap(query_near, "row", 1),
    ]
    early_lines, late_lines = 14 * half // 4, 10 * half // 4
    lines = early_lines + late_lines
    shifted_one, grad_res, *payload = call(
        middle_kernel,
        [(tall, low)],
        [(wide, full)] + [((lines, channels), low)] * 4,
        [
            ((HEADS,) + head_shape, low), ((HEADS,) + query_shape, low),
            (wide, low), (wide, full), rows_eight, (own_shape, low), (wide, full),
            ((14 * half, channels), low), (wide, full), (tall, low), (kernel_shape, low),
            (wide, full), (own_shape, low), rows_eight, ((10 * half, channels), low),
            sems(17), sems(9),
        ],
        40,
        cost * 26,
        [],
        [vec, qkv_t],
        [
            *packed_all, grad_proj, residual, stats, own_two, weight_rows, w_two_back, conv_one,
            own_one, out_sums,
        ],
    )
    *sends, shifted_one = lax.optimization_barrier((*sends, shifted_one))
    total = add_up(payload[0], *[swap(payload[step], "img", step) for step in (1, 2, 3)])
    heads_got = [sends[0]] + [swap(sends[step], "row", step) for step in (1, 2, 3)]
    shifted_one, total, *heads_got = lax.optimization_barrier((shifted_one, total, *heads_got))
    both = add_up(total, swap(total, "row", 4))
    grad_own, grad_away, sums_one = call(
        first_kernel,
        [],
        [((block_cells, channels), low), ((block_cells, channels), low), rows_eight],
        [
            (kernel_shape, low), (wide, low), (wide, full), rows_eight,
            ((2, block_cells, channels), low), rows_eight, (wide, full), sems(4), sems(3),
        ],
        20,
        cost * 12,
        [],
        [vec, shifted_one],
        [w_one_back, pix, grad_res, stats],
    )
    block_own, block_away = call(
        functools.partial(block_kernel, cols),
        [((block_cells, channels), low), ((block_cells, channels), low)],
        [],
        [((2, block_cells, channels), full), sems(2)],
        8,
        cost,
        [],
        [vec, out_weight.reshape(HEADS, half, channels), *heads_got],
        [residual],
    )
    out_pair = jnp.stack([block_own, grad_own])
    away_pair = swap(jnp.stack([block_away, grad_away]), "row", 4)
    first_pair = jnp.where(image == 0, out_pair, away_pair)
    second_pair = jnp.where(image == 0, away_pair, out_pair)
    finished = jnp.stack([first_pair, second_pair], axis=1).reshape((2,) + pixels.shape)
    norm_one = jnp.concatenate([sums_one, jnp.zeros_like(sums_one)], axis=0).astype(low)
    norm_one = add_up(norm_one, swap(norm_one, "row", 4))
    other = swap(both, "row", 2)
    pair = jnp.concatenate([both, other, norm_one], axis=0)
    parts = gather_columns(pair)
    line = ((channels,), full)
    kernel_out = ((3, 3, channels, channels), full)
    time_out = ((time_weight.shape[0], 2 * channels), full)
    qkv_out, out_out = ((channels, 3 * channels), full), ((channels, channels), full)
    half_time = time_weight.shape[0] // 2
    frequency = jnp.exp(-math.log(10000.0) * jnp.arange(half_time, dtype=full) / half_time)
    (
        conv1_weight_grad, conv2_weight_grad, qkv_weight_grad, out_weight_grad, time_weight_grad,
        qv_bias_grad, time_bias_grad, *lines,
    ) = call(
        final_kernel,
        [],
        [kernel_out, kernel_out, qkv_out, out_out, time_out],
        [
            ((HEADS, 14 * half, channels), low), ((HEADS, 10 * half, channels), low),
            ((4, 16, channels), full), kernel_out, kernel_out, qkv_out, out_out, time_out, sems(5),
        ],
        28,
        cost,
        [],
        [*parts, frequency[None, :]],
        [],
        [((2 * channels,), full)] * 2 + [line] * 9,
    )
    norm1_gain_grad, norm1_bias_grad, norm3_gain_grad, norm3_bias_grad, conv2_bias_grad = lines[:5]
    out_bias_grad, norm2_gain_grad, norm2_bias_grad, conv1_bias_grad = lines[5:]
    return (
        finished[0],
        finished[1],
        norm1_gain_grad,
        norm1_bias_grad,
        conv1_weight_grad,
        conv1_bias_grad,
        time_weight_grad,
        time_bias_grad,
        norm2_gain_grad,
        norm2_bias_grad,
        conv2_weight_grad,
        conv2_bias_grad,
        norm3_gain_grad,
        norm3_bias_grad,
        qkv_weight_grad,
        qv_bias_grad,
        out_weight_grad,
        out_bias_grad,
    )


def local(*arrays):
    pixels = arrays[0]
    if lax.axis_size("row") == pixels.shape[0] * HEADS and lax.axis_size("img") == 4:
        return local_image(*arrays)
    return local_rows(*arrays)


def solution(mesh):
    placed = (
        P("img", "row", None, None),
        P("img"),
        P("img"),
        P(),
        P(),
        P(),
        P(),
        P(),
        P(),
        P(),
        P(),
        P(),
        P(),
        P(),
        P(),
        P(),
        P(),
        P(),
        P(),
        P("img", "row", None, None),
    )
    return jax.shard_map(
        local,
        mesh=mesh,
        in_specs=placed,
        out_specs=(
            P("img", "row", None, None),
            P("img", "row", None, None),
            P(),
            P(),
            P(),
            P(),
            P(),
            P(),
            P(),
            P(),
            P(),
            P(),
            P(),
            P(),
            P(),
            P(),
            P(),
            P(),
        ),
        check_vma=False,
    )
```

```python
import functools
import math

import jax
import jax.numpy as jnp
from jax import lax
from jax.experimental import pallas as pl
from jax.experimental.pallas import tpu as pltpu
from jax.sharding import PartitionSpec as P

GROUPS = 32
HEADS = 4


EPSILON = 1e-05
MASKED = -1000000000.0
PRECISE = lax.Precision.HIGHEST


def with_halo(cells, sides, width):
    for axis, dim in sides:
        count = lax.axis_size(axis)
        ends = count - 1
        head = lax.slice_in_dim(cells, 0, width, axis=dim)
        tail = lax.slice_in_dim(cells, cells.shape[dim] - width, cells.shape[dim], axis=dim)
        cells = jnp.concatenate(
            [
                lax.ppermute(tail, axis, [(i, (i + 1) % count) for i in range(ends)]),
                cells,
                lax.ppermute(head, axis, [((i + 1) % count, i) for i in range(ends)]),
            ],
            axis=dim,
        )
    return cells


def embed_steps(timesteps, time_width):
    half_dim = time_width // 2
    frequency = jnp.exp(-math.log(10000.0) * jnp.arange(half_dim, dtype=jnp.float32) / half_dim)
    angles = timesteps.astype(jnp.float32)[:, None] * frequency[None, :]
    return jnp.concatenate([jnp.cos(angles), jnp.sin(angles)], axis=1)


def silu_slope(pre_act):
    sigmoid = jax.nn.sigmoid(pre_act)
    return sigmoid * (1.0 + pre_act * (1.0 - sigmoid))


def with_rims(field_in):
    return with_halo(field_in, (("row", 1),), 1)


def conv_rows(padded, kernel):
    return lax.conv_general_dilated(
        padded,
        kernel,
        (1, 1),
        ((0, 0), (1, 1)),
        dimension_numbers=("NHWC", "HWIO", "NHWC"),
        preferred_element_type=jnp.float32,
    )


def flipped(kernel):
    return jnp.transpose(kernel[::-1, ::-1], (0, 1, 3, 2))


def kernel_grad(padded, grad_field):
    row_count = grad_field.shape[1]
    col_count = grad_field.shape[2]
    widened = jnp.pad(padded, ((0, 0), (0, 0), (1, 1), (0, 0)))
    tap_rows = []
    for tap_row in range(3):
        tap_line = []
        for tap_col in range(3):
            window = widened[:, tap_row : tap_row + row_count, tap_col : tap_col + col_count, :]
            tap_line.append(
                jnp.einsum("brwc,brwd->cd", window, grad_field, preferred_element_type=jnp.float32)
            )
        tap_rows.append(jnp.stack(tap_line))
    return jnp.stack(tap_rows)


def norm_forward(field_in, cell_mask, cell_count, group_count):
    shaped = field_in.reshape(field_in.shape[:3] + (group_count, field_in.shape[3] // group_count))
    first_sum = lax.psum(jnp.sum(shaped * cell_mask, axis=(1, 2, 4)), "row")
    center = first_sum / cell_count[:, None]
    centred = shaped - center[:, None, None, :, None]
    spread_sum = lax.psum(jnp.sum(jnp.square(centred * cell_mask), axis=(1, 2, 4)), "row")
    spread = spread_sum / cell_count[:, None]
    inverse = lax.rsqrt(spread + EPSILON)
    return (centred * inverse[:, None, None, :, None], inverse)


def norm_backward(grad_normed, normalized, inverse, gain_in, cell_mask, cell_count):
    full_shape = grad_normed.shape
    flat_norm = normalized.reshape(full_shape)
    gain_grad = jnp.sum(grad_normed * flat_norm, axis=(0, 1, 2))
    shift_grad = jnp.sum(grad_normed, axis=(0, 1, 2))
    scaled = (grad_normed * gain_in).reshape(normalized.shape)
    sum_plain, sum_cross = lax.psum(
        (
            jnp.sum(scaled * cell_mask, axis=(1, 2, 4)),
            jnp.sum(scaled * normalized * cell_mask, axis=(1, 2, 4)),
        ),
        "row",
    )
    mean_plain = sum_plain / cell_count[:, None]
    mean_cross = sum_cross / cell_count[:, None]
    grad_in = (
        (
            scaled
            - mean_plain[:, None, None, :, None]
            - normalized * mean_cross[:, None, None, :, None]
        )
        * inverse[:, None, None, :, None]
        * cell_mask
    )
    return (grad_in.reshape(full_shape), gain_grad, shift_grad)


def local_rows(
    pixels,
    heights,
    timesteps,
    norm1_gain,
    norm1_bias,
    conv1_weight,
    conv1_bias,
    time_weight,
    time_bias,
    norm2_gain,
    norm2_bias,
    conv2_weight,
    conv2_bias,
    norm3_gain,
    norm3_bias,
    qkv_weight,
    qv_bias,
    out_weight,
    out_bias,
    grad_out,
):
    image_count, row_count, col_count, channels = pixels.shape
    group_count = GROUPS
    head_count = HEADS
    head_width = channels // head_count
    query_count = row_count * col_count
    scaling = head_width ** (-0.5)
    head_shape = (image_count, query_count, head_count, head_width)
    row_ids = lax.axis_index("row") * row_count + jnp.arange(row_count, dtype=jnp.int32)
    row_valid = row_ids[None, :] < heights[:, None]
    row_mask = row_valid.astype(jnp.float32)
    cell_rows = row_mask[:, :, None, None]
    cell_mask = row_mask[:, :, None, None, None]
    own_valid = jnp.repeat(row_valid, col_count, axis=1)[:, None, None, :]
    cell_count = heights.astype(jnp.float32) * (col_count * (channels // group_count))
    gain_one = norm1_gain.astype(jnp.float32)
    gain_two = norm2_gain.astype(jnp.float32)
    gain_three = norm3_gain.astype(jnp.float32)
    field_in = pixels.astype(jnp.float32)
    normed_one, inverse_one = norm_forward(field_in, cell_mask, cell_count, group_count)
    pre_one = normed_one.reshape(field_in.shape) * gain_one + norm1_bias.astype(jnp.float32)
    act_one = (jax.nn.silu(pre_one) * cell_rows).astype(jnp.bfloat16)
    padded_one = with_rims(act_one)
    conv_one = conv_rows(padded_one, conv1_weight) + conv1_bias.astype(jnp.float32)
    time_act = jax.nn.silu(embed_steps(timesteps, time_weight.shape[0]))
    shifts = jnp.dot(
        time_act, time_weight.astype(jnp.float32), precision=PRECISE
    ) + time_bias.astype(jnp.float32)
    scale_part = 1.0 + shifts[:, None, None, :channels]
    shift_part = shifts[:, None, None, channels:]
    normed_two, inverse_two = norm_forward(conv_one, cell_mask, cell_count, group_count)
    affine_two = normed_two.reshape(field_in.shape) * gain_two + norm2_bias.astype(jnp.float32)
    pre_two = affine_two * scale_part + shift_part
    act_two = (jax.nn.silu(pre_two) * cell_rows).astype(jnp.bfloat16)
    padded_two = with_rims(act_two)
    residual = field_in + (conv_rows(padded_two, conv2_weight) + conv2_bias.astype(jnp.float32))
    normed_three, inverse_three = norm_forward(residual, cell_mask, cell_count, group_count)
    act_three = (
        normed_three.reshape(field_in.shape) * gain_three + norm3_bias.astype(jnp.float32)
    ).astype(jnp.bfloat16)
    projected = jnp.einsum(
        "brwc,cd->brwd", act_three, qkv_weight, preferred_element_type=jnp.float32
    )
    qv_float = qv_bias.astype(jnp.float32)
    queries = (projected[..., :channels] + qv_float[:channels]).astype(jnp.bfloat16)
    keys_own = projected[..., channels : 2 * channels].astype(jnp.bfloat16)
    values_own = (projected[..., 2 * channels :] + qv_float[channels:]).astype(jnp.bfloat16)
    query_heads = queries.reshape(head_shape)
    key_heads = keys_own.reshape(head_shape)
    value_heads = values_own.reshape(head_shape)

    def flatten_rows(piece_arr):
        return piece_arr.reshape(
            image_count, piece_arr.shape[1] * col_count, head_count, head_width
        )

    def key_mask(span_rows):
        key_rows = jnp.arange(span_rows, dtype=jnp.int32)
        return jnp.repeat(key_rows[None, :] < heights[:, None], col_count, axis=1)[:, None, None, :]

    top_init = jnp.full((image_count, query_count, head_count), MASKED, jnp.float32)
    piece_keys = lax.all_gather(keys_own, "row", axis=1, tiled=True)
    piece_values = lax.all_gather(values_own, "row", axis=1, tiled=True)
    key_valid = key_mask(piece_keys.shape[1])
    scores = (
        jnp.einsum(
            "bqhd,bkhd->bqhk",
            query_heads,
            flatten_rows(piece_keys),
            preferred_element_type=jnp.float32,
        )
        * scaling
    )
    scores = jnp.where(key_valid, scores, MASKED)
    new_top = jnp.maximum(top_init, jnp.max(scores, axis=3))
    weights = jnp.where(key_valid, jnp.exp(scores - new_top[..., None]), 0.0)
    running_total = jnp.sum(weights, axis=3)
    running_acc = jnp.einsum(
        "bqhk,bkhd->bqhd",
        weights.astype(jnp.bfloat16),
        flatten_rows(piece_values),
        preferred_element_type=jnp.float32,
    )
    attn_float = running_acc / running_total[..., None]
    log_total = new_top + jnp.log(running_total)
    attended = attn_float.reshape(pixels.shape).astype(jnp.bfloat16)
    output_proj = jnp.einsum(
        "brwc,cd->brwd", attended, out_weight, preferred_element_type=jnp.float32
    ) + out_bias.astype(jnp.float32)
    block_out = ((residual + output_proj) * cell_rows).astype(jnp.bfloat16)
    grad_proj = grad_out.astype(jnp.float32) * cell_rows
    grad_proj_low = grad_proj.astype(jnp.bfloat16)
    out_weight_grad = jnp.einsum(
        "brwc,brwd->cd", attended, grad_proj_low, preferred_element_type=jnp.float32
    )
    out_bias_grad = jnp.sum(grad_proj, axis=(0, 1, 2))
    grad_attended = jnp.einsum(
        "brwd,cd->brwc", grad_proj_low, out_weight, preferred_element_type=jnp.float32
    ).astype(jnp.bfloat16)
    grad_heads = grad_attended.reshape(head_shape)
    delta_own = jnp.sum(grad_heads.astype(jnp.float32) * attn_float, axis=3)
    stat_shape = (image_count, row_count, col_count, head_count)
    all_lse, all_delta = (
        lax.all_gather(log_total.reshape(stat_shape), "row", axis=1, tiled=True),
        lax.all_gather(delta_own.reshape(stat_shape), "row", axis=1, tiled=True),
    )
    piece_keys = lax.all_gather(keys_own, "row", axis=1, tiled=True)
    piece_values = lax.all_gather(values_own, "row", axis=1, tiled=True)
    flat_keys = flatten_rows(piece_keys)
    key_valid = key_mask(piece_keys.shape[1])
    scores = (
        jnp.einsum("bqhd,bkhd->bqhk", query_heads, flat_keys, preferred_element_type=jnp.float32)
        * scaling
    )
    soft_weights = jnp.where(key_valid, jnp.exp(scores - log_total[..., None]), 0.0)
    grad_probs = jnp.einsum(
        "bqhd,bkhd->bqhk",
        grad_heads,
        flatten_rows(piece_values),
        preferred_element_type=jnp.float32,
    )
    grad_scores = (soft_weights * (grad_probs - delta_own[..., None])).astype(jnp.bfloat16)
    grad_query_sum = jnp.einsum(
        "bqhk,bkhd->bqhd", grad_scores, flat_keys, preferred_element_type=jnp.float32
    )
    piece_queries = lax.all_gather(queries, "row", axis=1, tiled=True)
    piece_grads = lax.all_gather(grad_attended, "row", axis=1, tiled=True)
    flat_queries = flatten_rows(piece_queries)
    flat_grads = flatten_rows(piece_grads)
    span_rows = piece_queries.shape[1]
    piece_lse = all_lse.reshape(image_count, span_rows * col_count, head_count)
    piece_delta = all_delta.reshape(image_count, span_rows * col_count, head_count)
    scores = (
        jnp.einsum("bqhd,bkhd->bqhk", flat_queries, key_heads, preferred_element_type=jnp.float32)
        * scaling
    )
    soft_weights = jnp.where(own_valid, jnp.exp(scores - piece_lse[..., None]), 0.0)
    value_term = jnp.einsum(
        "bqhk,bqhd->bkhd",
        soft_weights.astype(jnp.bfloat16),
        flat_grads,
        preferred_element_type=jnp.float32,
    )
    grad_probs = jnp.einsum(
        "bqhd,bkhd->bqhk", flat_grads, value_heads, preferred_element_type=jnp.float32
    )
    grad_scores = (soft_weights * (grad_probs - piece_delta[..., None])).astype(jnp.bfloat16)
    key_term = jnp.einsum(
        "bqhk,bqhd->bkhd", grad_scores, flat_queries, preferred_element_type=jnp.float32
    )
    key_term, value_term = (key_term, value_term)
    grad_queries = (grad_query_sum * scaling).reshape(pixels.shape).astype(jnp.bfloat16)
    grad_keys = (key_term * scaling).reshape(pixels.shape).astype(jnp.bfloat16)
    grad_values = value_term.reshape(pixels.shape).astype(jnp.bfloat16)
    grad_projected = jnp.concatenate([grad_queries, grad_keys, grad_values], axis=3)
    qkv_weight_grad = jnp.einsum(
        "brwc,brwd->cd", act_three, grad_projected, preferred_element_type=jnp.float32
    )
    qv_bias_grad = jnp.concatenate(
        [
            jnp.sum(grad_queries.astype(jnp.float32), axis=(0, 1, 2)),
            jnp.sum(grad_values.astype(jnp.float32), axis=(0, 1, 2)),
        ]
    )
    grad_act_three = jnp.einsum(
        "brwd,cd->brwc", grad_projected, qkv_weight, preferred_element_type=jnp.float32
    )
    grad_res_attn, norm3_gain_grad, norm3_bias_grad = norm_backward(
        grad_act_three, normed_three, inverse_three, gain_three, cell_mask, cell_count
    )
    grad_residual = grad_proj + grad_res_attn
    grad_conv_two = grad_residual.astype(jnp.bfloat16)
    conv2_bias_grad = jnp.sum(grad_residual, axis=(0, 1, 2))
    conv2_weight_grad = kernel_grad(padded_two, grad_conv_two)
    grad_act_two = conv_rows(with_rims(grad_conv_two), flipped(conv2_weight)) * cell_rows
    grad_pre_two = grad_act_two * silu_slope(pre_two)
    scale_grad = jnp.sum(grad_pre_two * affine_two, axis=(1, 2))
    shift_grad = jnp.sum(grad_pre_two, axis=(1, 2))
    shift_grads = jnp.concatenate([scale_grad, shift_grad], axis=1)
    grad_conv_one, norm2_gain_grad, norm2_bias_grad = norm_backward(
        grad_pre_two * scale_part, normed_two, inverse_two, gain_two, cell_mask, cell_count
    )
    conv_one_low = grad_conv_one.astype(jnp.bfloat16)
    conv1_bias_grad = jnp.sum(grad_conv_one, axis=(0, 1, 2))
    conv1_weight_grad = kernel_grad(padded_one, conv_one_low)
    grad_act_one = conv_rows(with_rims(conv_one_low), flipped(conv1_weight)) * cell_rows
    grad_pre_one = grad_act_one * silu_slope(pre_one)
    grad_field_norm, norm1_gain_grad, norm1_bias_grad = norm_backward(
        grad_pre_one, normed_one, inverse_one, gain_one, cell_mask, cell_count
    )
    grad_pixels = (grad_residual + grad_field_norm).astype(jnp.bfloat16)
    time_weight_grad = jnp.dot(time_act.T, shift_grads, precision=PRECISE)
    time_bias_grad = jnp.sum(shift_grads, axis=0)
    summed = lax.psum(
        (
            norm1_gain_grad,
            norm1_bias_grad,
            conv1_weight_grad,
            conv1_bias_grad,
            time_weight_grad,
            time_bias_grad,
            norm2_gain_grad,
            norm2_bias_grad,
            conv2_weight_grad,
            conv2_bias_grad,
            norm3_gain_grad,
            norm3_bias_grad,
            qkv_weight_grad,
            qv_bias_grad,
            out_weight_grad,
            out_bias_grad,
        ),
        ("img", "row"),
    )
    return (
        block_out,
        grad_pixels,
        summed[0],
        summed[1],
        summed[2],
        summed[3],
        summed[4],
        summed[5],
        summed[6],
        summed[7],
        summed[8],
        summed[9],
        summed[10],
        summed[11],
        summed[12],
        summed[13],
        summed[14],
        summed[15],
    )


ARRIVAL = (3, 5, 7, 0, 1, 2, 4, 6)


def mib(count):
    return pltpu.CompilerParams(vmem_limit_bytes=count * 2**20)


def dot(left, right):
    return jnp.dot(left, right, preferred_element_type=jnp.float32)


def dot_rows(left, right):
    return lax.dot_general(
        left, right, (((1,), (1,)), ((), ())), preferred_element_type=jnp.float32
    )


def fold(tile):
    return jnp.sum(tile.reshape(-1, 8, tile.shape[1]), axis=0)


def group_sums(row, width):
    channels = row.shape[1]
    rows = lax.broadcasted_iota(jnp.int32, (channels, channels), 0) // width
    cols = lax.broadcasted_iota(jnp.int32, (channels, channels), 1) // width
    same = jnp.where(rows == cols, 1.0, 0.0).astype(jnp.bfloat16)
    wide = jnp.broadcast_to(row, (16, channels))
    total = None
    for _ in range(3):
        term = wide.astype(jnp.bfloat16)
        wide = wide - term.astype(jnp.float32)
        part = dot(term, same)
        total = part if total is None else total + part
    return total[0:1]


def row_at(index, cols):
    return pl.ds(pl.multiple_of(index * cols, cols), cols)


def total_of(tile):
    return jnp.sum(tile, axis=0, keepdims=True)


def cell_sums(tiles, about, height):
    first, square = 0.0, 0.0
    for index, tile in tiles:
        off = (tile - about) * valid_row(index, height)
        first, square = first + fold(off), square + fold(off * off)
    return first, square


def stats_of(first, square, about, height, cols):
    width = about.shape[1] // GROUPS
    each = (height * cols).astype(jnp.float32)
    first, square = total_of(first), total_of(square)
    mean = group_sums(first + about * each, width) / (each * width)
    shift = about - mean
    spread = group_sums(square + 2.0 * first * shift + each * shift * shift, width)
    return mean, lax.rsqrt(spread / (each * width) + EPSILON)


def row_mean(tile):
    return jnp.sum(tile, axis=0, keepdims=True) * (1.0 / tile.shape[0])


def in_turn(count, before, main, after):
    for step in range(count + 2):
        if step < count:
            before(step)
        if 0 <= step - 1 < count:
            main(step - 1)
        if 0 <= step - 2:
            after(step - 2)


def conv_block(shifted, weight, block, size, cols):
    base = block * size
    total = dot(shifted[base : base + size, :], weight[0])
    for tap in (1, 2):
        at = base + tap * cols
        total = total + dot(shifted[at : at + size, :], weight[tap])
    return total


def half_line(mean, inverse, gain, bias, scale=1.0, shift=0.0):
    slope = inverse * gain
    start = bias - mean * slope
    return 0.5 * slope * scale, 0.5 * (start * scale + shift)


def put_shifted(ref, index, tile, cols):
    channels = tile.shape[1]
    column = lax.broadcasted_iota(jnp.int32, tile.shape, 0)
    before = jnp.where(column == 0, 0.0, pltpu.roll(tile, 1, 0))
    after = jnp.where(column == cols - 1, 0.0, pltpu.roll(tile, cols - 1, 0))
    at = row_at(index + 1, cols)
    ref[at, 0:channels] = before.astype(jnp.bfloat16)
    ref[at, channels : 2 * channels] = tile.astype(jnp.bfloat16)
    ref[at, 2 * channels : 3 * channels] = after.astype(jnp.bfloat16)


def clear_rims(ref, cols):
    edge = jnp.zeros((cols, ref.shape[1]), ref.dtype)
    ref[0:cols, :] = edge
    ref[ref.shape[0] - cols : ref.shape[0], :] = edge


def conv_shifted(shifted, weight, out, bias, cols, added=None):
    step = 8 * cols

    def block(index, carry):
        base = index * step
        total = bias
        for tap in range(3):
            at = pl.ds(pl.multiple_of(base + tap * cols, cols), step)
            total = total + dot(shifted[at, :], weight[tap])
        if added is not None:
            total = total + added[pl.ds(pl.multiple_of(base, step), step), :].astype(jnp.float32)
        out[pl.ds(pl.multiple_of(base, step), step), :] = total
        return carry

    lax.fori_loop(0, out.shape[0] // step, block, 0, unroll=True)


def put_quarter(parts, payload, start):
    half = parts[0].shape[0] // 3
    unit = half // 4
    for line, part in enumerate(parts):
        part = part.astype(jnp.bfloat16)
        for shift in range(3):
            at = start + (3 * line + shift) * unit
            for chunk in range(4):
                base = shift * half + chunk * unit
                payload[chunk, at : at + unit, :] = part[base : base + unit]


def own_place(vec):
    spot = lax.axis_index("row")
    image, head = spot // HEADS, spot % HEADS
    return spot, head, image, jnp.max(vec[11:12, :]).astype(jnp.int32)


def started(sems, *pairs):
    copies = [pltpu.make_async_copy(src, dst, sems.at[k]) for k, (src, dst) in enumerate(pairs)]
    for copy in copies:
        copy.start()
    return copies


def finish_all(copies):
    for copy in copies:
        copy.wait()


def valid_row(index, height):
    return jnp.where(index < height, 1.0, 0.0).astype(jnp.float32)


def forward_kernel(vec, *refs):
    blocks, (w_one_far, w_two_far) = refs[:8], refs[8:10]
    act_three, pix_far, conv_far, residual_far, act_one_far, act_two_far, stats_far = refs[10:17]
    pix, conv_one, residual, stats, w_one, w_two, shift_one, shift_two, in_sems, out_sems = refs[17:]
    cells, channels = pix.shape
    block_cells = blocks[0].shape[0]
    cols = (shift_one.shape[0] - cells) // 2
    rows = cells // cols
    spot, _, _, height = own_place(vec)
    pairs = []
    for step, block in zip(ARRIVAL, blocks):
        base = pl.multiple_of((spot ^ step) * block_cells, block_cells)
        pairs.append((block, pix.at[pl.ds(base, block_cells), :]))
    arriving = started(in_sems, *pairs, (w_one_far, w_one), (w_two_far, w_two))
    gain_one, bias_one, conv_bias_one, gain_two, bias_two = (vec[k : k + 1, :] for k in range(5))
    scale, shift, conv_bias_two, gain_three, bias_three = (vec[k : k + 1, :] for k in range(5, 10))
    inner = (pl.ds(cols, cells), pl.ds(channels, channels))

    group = 4
    size = group * cols
    count = rows // group
    zero = jnp.zeros((8, channels), jnp.float32)

    def tile_of(ref, index):
        return ref[index * cols : (index + 1) * cols, :].astype(jnp.float32)

    def tiles_of(ref, block):
        return [(k, tile_of(ref, k)) for k in range(block * group, (block + 1) * group)]

    def stage(source, line, shifted, weight, out, bias, added=None):
        sums = [zero, zero, None]

        def activate(block):
            for index, tile in tiles_of(source, block):
                part = tile * line[0] + line[1]
                part = (part + part * jnp.tanh(part)) * valid_row(index, height)
                put_shifted(shifted, index, part, cols)

        def conv(block):
            total = conv_block(shifted, weight, block, size, cols) + bias
            if added is not None:
                total = total + added[block * size : (block + 1) * size, :].astype(jnp.float32)
            out[block * size : (block + 1) * size, :] = total

        def measure(block):
            if block == 0:
                sums[2] = row_mean(tile_of(out, 0))
            first, square = cell_sums(tiles_of(out, block), sums[2], height)
            sums[0], sums[1] = sums[0] + first, sums[1] + square

        in_turn(count, activate, conv, measure)
        return stats_of(*sums, height, cols)

    clear_rims(shift_one, cols)
    clear_rims(shift_two, cols)
    finish_all(arriving[:8])
    leaving = started(out_sems, (pix, pix_far))
    about = row_mean(tile_of(pix, 0))
    first, square = zero, zero
    for block in range(count):
        more = cell_sums(tiles_of(pix, block), about, height)
        first, square = first + more[0], square + more[1]
    mean_one, inv_one = stats_of(first, square, about, height, cols)
    arriving[8].wait()
    line = half_line(mean_one, inv_one, gain_one, bias_one)
    mean_two, inv_two = stage(pix, line, shift_one, w_one, conv_one, conv_bias_one)
    leaving += started(
        out_sems.at[1:3], (shift_one.at[inner], act_one_far), (conv_one, conv_far)
    )
    arriving[9].wait()
    line = half_line(mean_two, inv_two, gain_two, bias_two, scale, shift)
    mean_three, inv_three = stage(conv_one, line, shift_two, w_two, residual, conv_bias_two, pix)
    leaving += started(
        out_sems.at[3:5], (shift_two.at[inner], act_two_far), (residual, residual_far)
    )
    stats[...] = jnp.concatenate(
        [mean_one, inv_one, mean_two, inv_two, mean_three, inv_three, mean_one, mean_one], axis=0
    )
    leaving += started(out_sems.at[5:6], (stats, stats_far))
    slope = inv_three * gain_three
    start = bias_three - mean_three * slope

    def third(index, carry):
        at = row_at(index, cols)
        act_three[at, :] = (residual[at, :] * slope + start).astype(jnp.bfloat16)
        return carry

    lax.fori_loop(0, rows, third, 0, unroll=4)
    finish_all(leaving)


def project_kernel(act_three, w_heads, biases, query_only, key_pad, value_pad, sizes):
    cells, lanes = query_only.shape
    scaling = (lanes // 2) ** -0.5

    def project(index, carry):
        at = pl.ds(pl.multiple_of(index * 512, 512), 512)
        parts = dot(act_three[at, :], w_heads[...]) + biases[0:1, :]
        query, key, value = (parts[:, k * lanes : (k + 1) * lanes] for k in range(3))
        query_only[at, :] = query.astype(jnp.bfloat16) * jnp.bfloat16(scaling)
        key_pad[at, :] = key.astype(jnp.bfloat16)
        value_pad[at, :] = value.astype(jnp.bfloat16)
        query_size = jnp.sum(query * query, axis=1, keepdims=True) * (scaling * scaling)
        key_size = jnp.sum(key * key, axis=1, keepdims=True)
        return jnp.maximum(carry[0], jnp.max(query_size)), jnp.maximum(carry[1], jnp.max(key_size))

    start = (jnp.float32(0.0), jnp.float32(0.0))
    query_most, key_most = lax.fori_loop(0, cells // 512, project, start)
    line = lax.broadcasted_iota(jnp.int32, sizes.shape, 0)
    sizes[...] = jnp.where(line == 0, query_most, key_most)


def attention_kernel(columns, vec, query_only, key_pad, value_pad, sizes, w_out, *refs):
    blocks = refs[:8]
    value_key_far, query_far, grad_far, mixed_far, sums_far = refs[8:13]
    (
        grad_blocks, grad_proj, value_key, query_part, sums,
        query_grad, heads_t, mixed, mask_row, in_sems, out_sems,
    ) = refs[13:]
    cells, channels = grad_proj.shape
    block_cells = blocks[0].shape[0]
    spot, _, _, height = own_place(vec)
    half = mixed.shape[1] // 2
    cols = columns
    scaling = half**-0.5
    valid_cells = height * cols
    step = 256
    pairs = []
    for index, block in zip(ARRIVAL, blocks):
        base = pl.multiple_of((spot ^ index) * block_cells, block_cells)
        pairs.append((block, grad_blocks.at[pl.ds(base, block_cells), :]))
    arriving = started(in_sems, *pairs)

    lane = lax.broadcasted_iota(jnp.int32, (1, cells), 1)
    mask_row[...] = jnp.where(lane < valid_cells, 0.0, MASKED)
    heads_t[...] = jnp.zeros(heads_t.shape, jnp.float32)
    mixed[...] = jnp.zeros(mixed.shape, jnp.bfloat16)
    finish_all(arriving)

    def clean(index, total):
        at = pl.ds(pl.multiple_of(index * block_cells, block_cells), block_cells)
        cell = index * block_cells + lax.broadcasted_iota(jnp.int32, (block_cells, channels), 0)
        kept = jnp.where(cell < valid_cells, grad_blocks[at, :].astype(jnp.float32), 0.0)
        low = kept.astype(jnp.bfloat16)
        grad_proj[at, :] = low
        query_grad[at, :] = query_only[at, :] + dot(low, w_out[...]).astype(jnp.bfloat16)
        return total + fold(kept)

    start = jnp.zeros((8, channels), jnp.float32)
    total = lax.fori_loop(0, cells // block_cells, clean, start, unroll=True)
    sums[...] = jnp.concatenate([total_of(total), jnp.zeros((7, channels), jnp.float32)], axis=0)
    leaving = started(out_sems, (grad_proj, grad_far), (sums, sums_far))

    def query_block(shifted, index, carry):
        at = pl.ds(pl.multiple_of(index * step, step), step)
        both = query_grad[at, :]
        scores = dot_rows(both, key_pad[...]) + mask_row[...]
        if shifted:
            scores = scores - jnp.max(scores, axis=1, keepdims=True)
        weights = jnp.exp(scores)
        total = jnp.zeros((step, 2 * half), jnp.float32)
        for start in range(0, cells, 2 * half):
            total = total + weights[:, start : start + 2 * half]
        inverse = 1.0 / jnp.sum(total, axis=1, keepdims=True)
        low = weights.astype(jnp.bfloat16)
        out = dot(low, value_pad[...]) * inverse
        wide = both.astype(jnp.float32)
        delta = jnp.sum(wide * out, axis=1, keepdims=True)
        turned = jnp.transpose(wide * inverse).astype(jnp.bfloat16)
        grad_probs = dot_rows(both, value_pad[...])
        grad_scores = (low.astype(jnp.float32) * (grad_probs - delta)).astype(jnp.bfloat16)
        grad_query = dot(grad_scores, key_pad[...]) * (inverse * scaling)
        mixed[at, :] = (out + grad_query).astype(jnp.bfloat16)
        heads_t[0:half, :] += dot(turned[0:half], grad_scores)
        heads_t[half : 2 * half, :] += dot(turned[half : 2 * half], low)
        return carry

    narrow = jnp.max(sizes[0:1, :]) * jnp.max(sizes[1:2, :]) <= 3600.0

    @pl.when(narrow)
    def _():
        lax.fori_loop(0, cells // step, functools.partial(query_block, False), 0, unroll=2)

    @pl.when(jnp.logical_not(narrow))
    def _():
        count = (valid_cells + step - 1) // step
        lax.fori_loop(0, count, functools.partial(query_block, True), 0)

    for start in range(0, cells, step):
        value_key[start : start + step, :] = jnp.transpose(heads_t[:, start : start + step]).astype(
            jnp.bfloat16
        )
    query_part[:, 0:half] = mixed[0 : cells // 2, 0:half]
    query_part[:, half : 2 * half] = mixed[cells // 2 : cells, 0:half]
    leaving += started(
        out_sems.at[2:5], (value_key, value_key_far), (query_part, query_far), (mixed, mixed_far)
    )
    finish_all(leaving)


def aside_kernel(vec, *refs):
    act_far, (mixed_far, value_key_far, act_three_far, grad_far) = refs[0:2], refs[2:6]
    own_far, weight_far, sends = refs[6:8], refs[8], refs[9:13]
    acts, mixed, value_key, act_three, grad_proj, padded, own, weight_rows, in_sems, out_sems = (
        refs[13:]
    )
    cells, channels = act_three.shape
    cols = (padded.shape[0] - cells) // 2
    lanes = mixed.shape[1]
    half = lanes // 2
    spot, head, image, _ = own_place(vec)
    arriving = started(
        in_sems,
        (mixed_far, mixed),
        (value_key_far, value_key),
        (act_three_far, act_three),
        (grad_far, grad_proj),
        (act_far[0], acts.at[0]),
        (act_far[1], acts.at[1]),
    )
    block_cells = sends[0].shape[0]
    step = 256
    arriving[0].wait()
    for k, send in enumerate(sends):
        tiles = []
        for part in range(2):
            block = (head ^ k) + HEADS * (image ^ part)
            at = pl.ds(pl.multiple_of(block * block_cells, block_cells), block_cells)
            tiles.append(mixed[at, half:lanes])
        send[...] = jnp.concatenate(tiles, axis=1)
    finish_all(arriving[1:4])

    def gather(index, totals):
        at = pl.ds(pl.multiple_of(index * step, step), step)
        low_mixed, low_heads, act = mixed[at, :], value_key[at, :], act_three[at, :]
        mixed_t = jnp.transpose(low_mixed.astype(jnp.float32)).astype(jnp.bfloat16)
        heads_t = jnp.transpose(low_heads.astype(jnp.float32)).astype(jnp.bfloat16)
        return (
            totals[0] + dot(mixed_t, act),
            totals[1] + dot(heads_t, act),
            totals[2] + dot(mixed_t, grad_proj[at, :]),
            totals[3] + fold(low_mixed.astype(jnp.float32)),
            totals[4] + fold(low_heads.astype(jnp.float32)),
        )

    square = jnp.zeros((lanes, channels), jnp.float32)
    line = jnp.zeros((8, lanes), jnp.float32)
    from_query, from_heads, from_out, query_sum, value_sum = lax.fori_loop(
        0, cells // step, gather, (square, square, square, line, line)
    )
    unit = half // 4
    parts = (from_query[0:half], from_heads[0:half], from_heads[half:lanes], from_out[half:lanes])
    for chunk in range(4):
        for k, part in enumerate(parts):
            piece = part[chunk * unit : (chunk + 1) * unit].astype(jnp.bfloat16)
            weight_rows[chunk, k * unit : (k + 1) * unit, :] = piece
    weight_rows[:, half:, :] = jnp.zeros((4, 16, channels), jnp.bfloat16)
    which = lax.axis_index("img") * 2 + image
    lane = lax.broadcasted_iota(jnp.int32, (1, channels), 1)
    now = jnp.max(vec[12:13, :]).astype(jnp.int32)
    high = jnp.where(lane == which, (now // 32).astype(jnp.float32), 0.0)
    rest = jnp.where(lane == which, (now % 32).astype(jnp.float32), 0.0)
    row = jnp.concatenate([total_of(query_sum), total_of(value_sum)], axis=1)
    below = jnp.zeros((13, channels), jnp.float32)
    weight_rows[2, half:, :] = jnp.concatenate([row, high, rest, below], axis=0).astype(
        jnp.bfloat16
    )
    source = lax.broadcasted_iota(jnp.int32, (channels, 3 * half), 0)
    target = lax.broadcasted_iota(jnp.int32, (channels, 3 * half), 1)
    chosen = jnp.where(source == head * half + target % half, 1.0, 0.0).astype(jnp.bfloat16)
    lane = lax.broadcasted_iota(jnp.int32, (step, 3 * half), 1)
    column = lax.broadcasted_iota(jnp.int32, (step, 3 * half), 0) % cols
    leaving = started(out_sems.at[2:3], (weight_rows, weight_far))
    for k in range(2):
        arriving[4 + k].wait()
        clear_rims(padded, cols)

        def widen(index, carry):
            at = pl.ds(pl.multiple_of(index * step, step), step)
            tile = dot(acts[k, at, :], chosen)
            before = jnp.where(column == 0, 0.0, pltpu.roll(tile, 1, 0))
            after = jnp.where(column == cols - 1, 0.0, pltpu.roll(tile, step - 1, 0))
            tile = jnp.where(lane < half, before, jnp.where(lane < 2 * half, tile, after))
            padded[pl.ds(pl.multiple_of(index * step + cols, cols), step), :] = tile
            return carry

        lax.fori_loop(0, cells // step, widen, 0)
        for tap in range(3):

            def turn(index, carry):
                at = pl.ds(pl.multiple_of(index * step + tap * cols, cols), step)
                to = pl.ds(pl.multiple_of(index * step, step), step)
                own[k, tap, :, to] = jnp.transpose(padded[at, :]).astype(jnp.bfloat16)
                return carry

            lax.fori_loop(0, cells // step, turn, 0)
        leaving += started(out_sems.at[k : k + 1], (own.at[k], own_far[k]))
    finish_all(leaving)


def middle_kernel(vec, qkv_t, *refs):
    heads_far = (refs[4], refs[0], refs[6], refs[2])
    sides_far = (refs[5], refs[1], refs[7], refs[3])
    grad_far, residual_far, stats_far, own_two_far, rows_far = refs[8:13]
    weight_far, conv_far, own_one_far, out_sums_far = refs[13:17]
    shifted_one, grad_res_far, payload_far = refs[17], refs[18], refs[19:23]
    (
        heads, sides, grad_proj, residual, stats, own_two, grad_res, payload, grad_act, shifted,
        weight, conv_one, own_one, out_sums, in_sems, out_sems,
    ) = refs[23:]
    cells, channels = grad_proj.shape
    cols = (shifted.shape[0] - cells) // 2
    rows = cells // cols
    _, head, image, height = own_place(vec)
    column = lax.axis_index("img")
    width = channels // GROUPS
    count = (height * (cols * width)).astype(jnp.float32)
    half = qkv_t.shape[1]
    unit = half // 4
    small_at = 18 * unit + half
    pairs = [(far, heads.at[head ^ k]) for k, far in enumerate(heads_far)]
    pairs += [(far, sides.at[head ^ k]) for k, far in enumerate(sides_far)]
    arriving = started(
        in_sems,
        *pairs,
        (stats_far, stats),
        (residual_far, residual),
        (grad_far, grad_proj),
        (own_two_far, own_two),
        (rows_far.at[:, pl.ds(0, half), :], payload.at[:, pl.ds(9 * unit, half), :]),
        (rows_far.at[:, pl.ds(half, 16), :], payload.at[:, pl.ds(small_at, 16), :]),
        (weight_far, weight),
        (conv_far, conv_one),
        (own_one_far, own_one),
        (out_sums_far, out_sums),
    )
    finish_all(arriving[:10])
    zeros = jnp.zeros((half, channels), jnp.bfloat16)
    halfway = cells // 2
    step = 512
    pairs = ((0, 1), (2, 3))
    w_main = []
    for a, b in pairs:
        order = [HEADS + a, 2 * HEADS + a, HEADS + b, 2 * HEADS + b]
        w_main.append(jnp.concatenate([qkv_t[k] for k in order], axis=0))
    mean, inverse = stats[4:5, :], stats[5:6, :]
    gain = vec[8:9, :]
    zero = jnp.zeros((8, channels), jnp.float32)
    plain, cross = zero, zero

    def normed(index):
        return (residual[index * cols : (index + 1) * cols, :] - mean) * inverse

    for part in range(2):
        w_side = []
        for a, b in pairs:
            left, right = qkv_t[a], qkv_t[b]
            order = [left, zeros, right, zeros] if part == 0 else [zeros, left, zeros, right]
            w_side.append(jnp.concatenate(order, axis=0))
        for base in range(0, halfway, step):
            start = part * halfway + base
            total = None
            for k, (a, b) in enumerate(pairs):
                main = jnp.concatenate(
                    [heads[a][start : start + step, :], heads[b][start : start + step, :]], axis=1
                )
                side = jnp.concatenate(
                    [sides[a][base : base + step, :], sides[b][base : base + step, :]], axis=1
                )
                term = dot(main, w_main[k]) + dot(side, w_side[k])
                total = term if total is None else total + term
            grad_act[start : start + step, :] = total
            for index in range(start // cols, (start + step) // cols):
                tile = total[index * cols - start : (index + 1) * cols - start]
                plain = plain + fold(tile)
                cross = cross + fold(tile * normed(index))
    plain, cross = total_of(plain), total_of(cross)
    mean_plain = group_sums(plain * gain, width) / count
    mean_cross = group_sums(cross * gain, width) / count
    clear_rims(shifted, cols)
    clear_rims(shifted_one, cols)
    finish_all(arriving[10:16])
    group = 4
    size = group * cols
    steps = rows // group
    totals = [zero, zero, zero, zero]
    one, two = gain * inverse, mean_cross * inverse * inverse
    three = (mean_plain - mean * inverse * mean_cross) * inverse
    gain_two, bias_two, scale, shift = (vec[k : k + 1, :] for k in range(3, 7))
    mean_two, inverse_two = stats[2:3, :], stats[3:4, :]
    line = half_line(mean_two, inverse_two, gain_two, bias_two, scale, shift)
    begin_two = mean_two * inverse_two

    def tiles(block):
        for index in range(block * group, (block + 1) * group):
            yield index, slice(index * cols, (index + 1) * cols)

    def through_three(block):
        for index, at in tiles(block):
            inner = grad_act[at, :] * one - residual[at, :] * two - three
            grad = grad_proj[at, :].astype(jnp.float32) + inner * valid_row(index, height)
            grad_res[at, :] = grad
            put_shifted(shifted, index, grad, cols)
            totals[0] = totals[0] + fold(grad)

    def conv_back(block):
        grad_act[block * size : (block + 1) * size, :] = conv_block(
            shifted, weight, block, size, cols
        )

    def through_act(block):
        for index, at in tiles(block):
            value = conv_one[at, :]
            unit_value = value * inverse_two - begin_two
            part = value * line[0] + line[1]
            sigmoid = 0.5 + 0.5 * jnp.tanh(part)
            slope = sigmoid + 2.0 * part * sigmoid * (1.0 - sigmoid)
            grad = grad_act[at, :] * valid_row(index, height) * slope
            grad_act[at, :] = grad
            totals[1] = totals[1] + fold(grad)
            totals[2] = totals[2] + fold(grad * unit_value)

    in_turn(steps, through_three, conv_back, through_act)
    total = total_of(totals[0])
    three_lines = [cross, plain, total]
    leaving = started(out_sems, (grad_res, grad_res_far))
    plain, cross = total_of(totals[1]), total_of(totals[2])
    gain, bias = gain_two, bias_two
    factor = gain * scale
    mean_plain = group_sums(plain * factor, width) / count
    mean_cross = group_sums(cross * factor, width) / count
    one, two = factor * inverse_two, mean_cross * inverse_two * inverse_two
    three = (mean_plain - begin_two * mean_cross) * inverse_two
    finish_all(arriving[16:])
    parts = [[None] * 3, [None] * 3]

    def through_two(block):
        for index, at in tiles(block):
            grad = grad_act[at, :] * one - conv_one[at, :] * two - three
            grad = grad * valid_row(index, height)
            put_shifted(shifted_one, index, grad, cols)
            totals[3] = totals[3] + fold(grad)

    def weigh(block):
        at = slice(block * size, (block + 1) * size)
        inner = slice(cols + block * size, cols + (block + 1) * size)
        for k, (own, moved) in enumerate(((own_two, shifted), (own_one, shifted_one))):
            grad = moved[inner, channels : 2 * channels]
            for tap in range(3):
                part = dot(own[tap, :, at], grad)
                parts[k][tap] = part if block == 0 else parts[k][tap] + part

    in_turn(steps, through_two, weigh, lambda block: None)
    put_quarter(parts[0], payload, 0)
    put_quarter(parts[1], payload, 9 * unit + half)
    total = total_of(totals[3])
    lines = [
        *three_lines, out_sums[0:1, :], cross * scale, plain * scale, total,
        jnp.zeros((9, channels), jnp.float32),
    ]
    mine = 2 * (column * 2 + image)
    place = lax.broadcasted_iota(jnp.int32, (16, channels), 0)
    both = jnp.where(place == mine, gain * cross + bias * plain, 0.0)
    payload[0, small_at:, :] = jnp.concatenate(lines, axis=0).astype(jnp.bfloat16)
    payload[1, small_at:, :] = jnp.where(place == mine + 1, plain, both).astype(jnp.bfloat16)
    leaving += started(
        out_sems.at[1:5],
        *[(payload.at[column ^ k], far) for k, far in enumerate(payload_far)],
    )
    finish_all(leaving)


def first_kernel(vec, shifted, weight_far, pix_far, grad_far, stats_far, *refs):
    out_own_far, out_away_far, sums_far = refs[:3]
    weight, pix, grad_res, stats, out, sums, grad_act, in_sems, out_sems = refs[3:]
    cells, channels = pix.shape
    block_cells = out.shape[1]
    cols = (shifted.shape[0] - cells) // 2
    rows = cells // cols
    spot, _, _, height = own_place(vec)
    width = channels // GROUPS
    count = (height * (cols * width)).astype(jnp.float32)
    arriving = started(
        in_sems,
        (weight_far, weight),
        (stats_far, stats),
        (pix_far, pix),
        (grad_far, grad_res),
    )
    gain, bias = vec[0:1, :], vec[1:2, :]
    zero = jnp.zeros((8, channels), jnp.float32)
    arriving[0].wait()
    conv_shifted(shifted, weight, grad_act, 0.0, cols)
    finish_all(arriving[1:])
    mean, inverse = stats[0:1, :], stats[1:2, :]
    line = half_line(mean, inverse, gain, bias)
    begin = mean * inverse

    def normed(at):
        return pix[at, :].astype(jnp.float32) * inverse - begin

    def add(index, totals):
        at = row_at(index, cols)
        value = pix[at, :].astype(jnp.float32)
        unit = value * inverse - begin
        part = value * line[0] + line[1]
        sigmoid = 0.5 + 0.5 * jnp.tanh(part)
        slope = sigmoid + 2.0 * part * sigmoid * (1.0 - sigmoid)
        grad = grad_act[at, :] * valid_row(index, height) * slope
        grad_act[at, :] = grad
        return totals[0] + fold(grad), totals[1] + fold(grad * unit)

    plain, cross = lax.fori_loop(0, rows, add, (zero, zero), unroll=2)
    plain, cross = total_of(plain), total_of(cross)
    mean_plain = group_sums(plain * gain, width) / count
    mean_cross = group_sums(cross * gain, width) / count
    block_rows = block_cells // cols
    for part in range(2):
        first_row = (spot ^ (4 * part)) * block_rows
        for line in range(block_rows):
            at = row_at(first_row + line, cols)
            grad = (grad_act[at, :] * gain - mean_plain - normed(at) * mean_cross) * inverse
            grad = grad_res[at, :] + grad * valid_row(first_row + line, height)
            out[part, line * cols : (line + 1) * cols, :] = grad.astype(jnp.bfloat16)
    sums[...] = jnp.concatenate([cross, plain, jnp.zeros((6, channels), jnp.float32)], axis=0)
    finish_all(
        started(
            out_sems, (out.at[0], out_own_far), (out.at[1], out_away_far), (sums, sums_far)
        )
    )


def block_kernel(columns, vec, w_out, *refs):
    heads, residual_far = refs[:4], refs[4]
    out_own, out_away, residual, in_sems = refs[5:]
    block_cells, channels = out_own.shape
    spot, head, _, height = own_place(vec)
    cols = columns
    bases = [
        pl.multiple_of((spot ^ (4 * part)) * block_cells, block_cells) for part in range(2)
    ]
    pairs = [
        (residual_far.at[pl.ds(base, block_cells), :], residual.at[part])
        for part, base in enumerate(bases)
    ]
    finish_all(started(in_sems, *pairs))
    for part, out in enumerate((out_own, out_away)):
        total = residual[part] + vec[10:11, :]
        for step in range(4):
            width = w_out.shape[1]
            tile = heads[step][:, part * width : (part + 1) * width]
            total = total + dot(tile, w_out[head ^ step])
        cell = bases[part] + lax.broadcasted_iota(jnp.int32, (block_cells, channels), 0)
        out[...] = jnp.where(cell < height * cols, total, 0.0).astype(jnp.bfloat16)


def prepare_kernel(*refs):
    shifts, lines_far, kernels_far = refs[0], refs[1:15], refs[15:17]
    vec, w_heads, w_out, biases, qkv_t = refs[17:22]
    backs_far = refs[22:24]
    kernels, backs, qkv_weight, out_weight, heights, timesteps, qv_bias, *lines = refs[24:40]
    line_sems, in_sems, out_sems = refs[40:]
    channels = out_weight.shape[0]
    half = channels // HEADS
    small = started(
        line_sems,
        *zip(lines_far, (*lines, qv_bias, qkv_weight, out_weight, heights, timesteps)),
    )
    arriving = started(
        in_sems, *[(far, kernels.at[k]) for k, far in enumerate(kernels_far)]
    )
    finish_all(small)
    spot = lax.axis_index("row")
    image, head = spot // HEADS, spot % HEADS
    shift_row = shifts[pl.ds(image, 1), :]
    order = list(range(5)) + [None, None] + list(range(5, 9))
    for line, k in enumerate(order):
        if k is not None:
            vec[line : line + 1, :] = lines[k][...].astype(jnp.float32).reshape(1, channels)
    vec[5:6, :] = 1.0 + shift_row[:, :channels]
    vec[6:7, :] = shift_row[:, channels:]
    vec[11:12, :] = jnp.full((1, channels), heights[image].astype(jnp.float32))
    vec[12:13, :] = jnp.full((1, channels), timesteps[image].astype(jnp.float32))
    vec[13:16, :] = jnp.zeros((3, channels), jnp.float32)
    source = lax.broadcasted_iota(jnp.int32, (channels, 2 * half), 0)
    lane = lax.broadcasted_iota(jnp.int32, (channels, 2 * half), 1)
    first = jnp.where((lane < half) & (source == head * half + lane), 1.0, 0.0)
    second = jnp.where((lane >= half) & (source == head * half + lane - half), 1.0, 0.0)
    first, second = first.astype(jnp.bfloat16), second.astype(jnp.bfloat16)
    lanes = 2 * half
    for part, taken in enumerate((first, first, second)):
        whole = qkv_weight[:, part * channels : (part + 1) * channels]
        w_heads[:, part * lanes : (part + 1) * lanes] = dot(whole, taken).astype(jnp.bfloat16)
    turned = jnp.transpose(out_weight[...].astype(jnp.float32)).astype(jnp.bfloat16)
    w_out[...] = dot(turned, second).astype(jnp.bfloat16)
    both = qv_bias[...].astype(jnp.float32).reshape(1, 2 * channels)
    wide = jnp.broadcast_to(both, (16, 2 * channels)).astype(jnp.bfloat16)
    biases[:, 0:lanes] = dot(wide[:, :channels], first)[0:8]
    biases[:, lanes : 2 * lanes] = jnp.zeros((8, lanes), jnp.float32)
    biases[:, 2 * lanes : 3 * lanes] = dot(wide[:, channels:], second)[0:8]
    for block in range(0, 3 * HEADS, 2):
        whole = qkv_weight[:, block // 2 * lanes : (block // 2 + 1) * lanes].astype(jnp.float32)
        whole = jnp.transpose(whole).astype(jnp.bfloat16)
        qkv_t[block] = whole[0:half]
        qkv_t[block + 1] = whole[half:lanes]
    leaving = []
    for k in range(2):
        arriving[k].wait()

        def turn(tap, carry):
            tile = kernels[k, 2 - tap // 3, 2 - tap % 3].astype(jnp.float32)
            at = pl.ds(pl.multiple_of(tap % 3 * channels, channels), channels)
            backs[k, tap // 3, at, :] = jnp.transpose(tile).astype(jnp.bfloat16)
            return carry

        lax.fori_loop(0, 9, turn, 0)
        leaving += started(out_sems.at[k : k + 1], (backs.at[k], backs_far[k]))
    finish_all(leaving)


def final_kernel(*refs):
    parts, frequency = refs[:8], refs[8]
    one_far, two_far, qkv_far, out_far, time_far = refs[9:14]
    bias_out, time_bias, rows = refs[14], refs[15], refs[16:25]
    one, two, qkv_rows, qkv_out, out_out, time_out, small, norm_one, sems, out_sems = refs[25:]
    channels = one.shape[1]
    half = channels // HEADS
    unit = half // 4
    lines = 18 * unit + half + 16
    spot = lax.axis_index("row")
    head, column = spot % HEADS, lax.axis_index("img")
    leaving = []
    for index, part in enumerate(parts):
        away = column ^ (index // 2)
        for pair in range(2):
            quarter, base = head ^ (index % 2 + 2 * pair), pair * lines
            first = pl.multiple_of(quarter * half + away * unit, unit)
            at = pl.ds(first, unit)
            shape = (9, unit, channels)
            late = base + 9 * unit + half
            two[:, at, :] = part[base : base + 9 * unit].astype(jnp.float32).reshape(shape)
            one[:, at, :] = part[late : late + 9 * unit].astype(jnp.float32).reshape(shape)
            here = len(leaving)
            leaving += started(
                sems.at[here : here + 2],
                (two.at[:, at, :], two_far.at[:, at, :]),
                (one.at[:, at, :], one_far.at[:, at, :]),
            )
            middle = base + 9 * unit
            for k in range(3):
                to = pl.ds(pl.multiple_of(first + k * channels, unit), unit)
                piece = part[middle + k * unit : middle + (k + 1) * unit]
                qkv_rows[to, :] = piece.astype(jnp.float32)
            out_out[at, :] = part[middle + 3 * unit : middle + half].astype(jnp.float32)
            small[quarter, away] = part[base + lines - 16 : base + lines].astype(jnp.float32)
    for part in range(3):
        across = slice(part * channels, (part + 1) * channels)
        qkv_out[:, across] = jnp.transpose(qkv_rows[across, :])
    leaving += started(out_sems, (qkv_out, qkv_far), (out_out, out_far))
    sums = [small[quarter, 2] for quarter in range(HEADS)]
    pieces = [part[0:1, :half] for part in sums] + [part[0:1, 3 * half :] for part in sums]
    bias_out[...] = jnp.concatenate(pieces, axis=1).reshape(bias_out.shape)
    for step in range(4):
        norm_one[column ^ step] = parts[2 * step][2 * lines : 2 * lines + 16].astype(jnp.float32)
    total = norm_one[0] + norm_one[1] + norm_one[2] + norm_one[3]
    whole = jnp.concatenate([total[0:2], small[0, 0, 0:7, :]], axis=0)
    for k, row in enumerate(rows):
        row[...] = whole[k : k + 1].reshape(row.shape)
    shifts = small[0, 1]
    pair = jnp.concatenate([shifts[k : k + 1, :] for k in range(0, 16, 2)], axis=0)
    other = jnp.concatenate([shifts[k : k + 1, :] for k in range(1, 16, 2)], axis=0)
    both = jnp.concatenate([pair, other], axis=1)
    time_bias[...] = total_of(both).reshape(time_bias.shape)
    steps = sums[0][1:2, :] * 32.0 + sums[0][2:3, :]
    image = lax.broadcasted_iota(jnp.int32, (8, steps.shape[1]), 0)
    lane = lax.broadcasted_iota(jnp.int32, (8, steps.shape[1]), 1)
    now = jnp.sum(jnp.where(image == lane, steps, 0.0), axis=1, keepdims=True)
    angles = now * frequency[...]
    left = jnp.concatenate([jnp.cos(angles), jnp.sin(angles)], axis=1)
    left = left / (1.0 + jnp.exp(-left))
    terms = []
    for _ in range(3):
        terms.append(left.astype(jnp.bfloat16).astype(jnp.float32))
        left = left - terms[-1]
    terms = jnp.concatenate(terms + [jnp.zeros_like(left)], axis=0)
    both = jnp.concatenate([both] * 3 + [jnp.zeros_like(both)], axis=0).astype(jnp.bfloat16)
    time_out[...] = lax.dot_general(
        terms.astype(jnp.bfloat16), both, (((0,), (0,)), ((), ())),
        preferred_element_type=jnp.float32,
    )
    leaving += started(out_sems.at[2:3], (time_out, time_far))
    finish_all(leaving)


def swap(value, axis, step):
    count = lax.axis_size(axis)
    return lax.ppermute(value, axis, [(k, k ^ step) for k in range(count)])


def pick(stacked, index):
    return lax.dynamic_index_in_dim(stacked, index, 0, keepdims=False)


def add_up(*parts):
    total = parts[0].astype(jnp.float32)
    for part in parts[1:]:
        total = total + part.astype(jnp.float32)
    return total.astype(jnp.bfloat16)


def from_columns(pair):
    return [pair] + [swap(pair, "img", step) for step in (1, 2, 3)]


def with_mates(columns):
    return [part for mine in columns for part in (mine, swap(mine, "row", 1))]


def gather_columns(pair):
    return with_mates(from_columns(pair))


def call(kernel, near_outs, far_outs, scratch, limit, work, scalars, near, far, last_outs=()):
    close = pl.BlockSpec(memory_space=pltpu.VMEM)
    distant = pl.BlockSpec(memory_space=pltpu.HBM)
    operands = list(near) + [pltpu.with_memory_space_constraint(array, pltpu.HBM) for array in far]
    moved = sum(array.size * array.dtype.itemsize for array in operands)
    return pl.pallas_call(
        kernel,
        out_shape=[jax.ShapeDtypeStruct(*kind) for kind in near_outs]
        + [pltpu.HBM(*kind) for kind in far_outs]
        + [jax.ShapeDtypeStruct(*kind) for kind in last_outs],
        in_specs=[pl.BlockSpec(memory_space=pltpu.SMEM)] * len(scalars)
        + [close] * len(near)
        + [distant] * len(far),
        out_specs=[close] * len(near_outs)
        + [distant] * len(far_outs)
        + [close] * len(last_outs),
        scratch_shapes=[pltpu.VMEM(*kind) if isinstance(kind, tuple) else kind for kind in scratch],
        compiler_params=mib(limit),
        cost_estimate=pl.CostEstimate(flops=work, bytes_accessed=moved, transcendentals=0),
    )(*scalars, *operands)


def sems(count):
    return pltpu.SemaphoreType.DMA((count,))


def gather_field(mine, theirs):
    far, far_near = swap(theirs, "row", 4), swap(theirs, "row", 6)
    return [mine, swap(mine, "row", 1), swap(mine, "row", 2), None, far, None, far_near, None]


def relayed(blocks, after=None):
    sent = [blocks[2], blocks[4], blocks[6]]
    if after is not None:
        sent = lax.optimization_barrier((*sent, after))[:3]
    odd = [swap(block, "row", 1) for block in sent]
    return odd, [blocks[step] for step in ARRIVAL[3:]]


def local_image(
    pixels,
    heights,
    timesteps,
    norm1_gain,
    norm1_bias,
    conv1_weight,
    conv1_bias,
    time_weight,
    time_bias,
    norm2_gain,
    norm2_bias,
    conv2_weight,
    conv2_bias,
    norm3_gain,
    norm3_bias,
    qkv_weight,
    qv_bias,
    out_weight,
    out_bias,
    grad_out,
):
    images, row_count, cols, channels = pixels.shape
    block_cells = row_count * cols
    cells = block_cells * lax.axis_size("row")
    half = channels // HEADS
    column = lax.axis_index("img")
    image = lax.axis_index("row") // HEADS
    low, full = jnp.bfloat16, jnp.float32
    pixel_blocks = pixels.reshape(images, block_cells, channels)
    grad_blocks = grad_out.reshape(images, block_cells, channels)
    field = gather_field(pick(pixel_blocks, image), pick(pixel_blocks, 1 - image))
    later = (pick(grad_blocks, image), pick(grad_blocks, 1 - image), field[4], field[6])
    later = lax.optimization_barrier(later)
    grads = gather_field(later[0], later[1])
    field[4], field[6] = later[2], later[3]
    time_act = jax.nn.silu(embed_steps(timesteps, time_weight.shape[0]))
    shifts = jnp.dot(time_act, time_weight.astype(full), precision=PRECISE) + time_bias.astype(full)
    kernel_shape = (3, 3 * channels, channels)
    lanes = 2 * half
    vec, w_heads, w_out, biases, qkv_t, w_one_back, w_two_back = call(
        prepare_kernel,
        [
            ((16, channels), full), ((channels, 3 * lanes), low), ((channels, lanes), low),
            ((8, 3 * lanes), full), ((3 * HEADS, half, channels), low),
        ],
        [(kernel_shape, low), (kernel_shape, low)],
        [
            ((2, 3, 3, channels, channels), low), ((2,) + kernel_shape, low),
            ((channels, 3 * channels), low), ((channels, channels), low),
            pltpu.SMEM((images,), jnp.int32), pltpu.SMEM((images,), jnp.int32),
            ((2 * channels,), low), *[((channels,), low)] * 9,
            sems(14), sems(2), sems(2),
        ],
        16,
        channels,
        [],
        [shifts],
        [
            norm1_gain, norm1_bias, conv1_bias, norm2_gain, norm2_bias, conv2_bias, norm3_gain,
            norm3_bias, out_bias, qv_bias, qkv_weight, out_weight, heights, timesteps,
            conv1_weight,
            conv2_weight,
        ],
    )
    field_late, field = relayed(field, vec)
    w_one, w_two = conv1_weight.reshape(kernel_shape), conv2_weight.reshape(kernel_shape)
    rim_cells = cells + 2 * cols
    cost = 9 * cells * channels * channels // 2

    wide, tall = (cells, channels), (rim_cells, 3 * channels)
    rows_eight = ((8, channels), full)
    act_three, pix, conv_one, residual, act_one, act_two, stats = call(
        forward_kernel,
        [(wide, low)],
        [(wide, low), (wide, full), (wide, full), (wide, low), (wide, low), rows_eight],
        [
            (wide, low), (wide, full), (wide, full), rows_eight, (kernel_shape, low),
            (kernel_shape, low), (tall, low), (tall, low), sems(10), sems(6),
        ],
        28,
        cost * 25,
        [],
        [vec, *field_late],
        [*field, w_one, w_two],
    )
    grads_late, grads = relayed(grads, act_three)
    query_shape, head_shape = (cells // 2, lanes), (cells, lanes)
    query_only, key_pad, value_pad, sizes = call(
        project_kernel,
        [(head_shape, low), (head_shape, low), (head_shape, low), ((8, lanes), full)],
        [],
        [],
        12,
        cost * 2,
        [],
        [act_three, w_heads, biases],
        [],
    )
    value_key, query_part, grad_proj, mixed, out_sums = call(
        functools.partial(attention_kernel, cols),
        [],
        [(head_shape, low), (query_shape, low), (wide, low), (head_shape, low), rows_eight],
        [
            (wide, low), (wide, low), (head_shape, low), (query_shape, low), rows_eight,
            (head_shape, low), ((lanes, cells), full), (head_shape, low), ((1, cells), full),
            sems(8), sems(5),
        ],
        36,
        cost * 34,
        [],
        [vec, query_only, key_pad, value_pad, sizes, w_out, *grads_late],
        grads,
    )

    key_near, query_near = swap(value_key, "row", 2), swap(query_part, "row", 2)
    key_mate, query_mate = swap(value_key, "row", 1), swap(query_part, "row", 1)
    own_shape = (3, 3 * half, cells)
    send_shape = ((block_cells, lanes), low)
    own_one, own_two, weight_rows, *sends = call(
        aside_kernel,
        [],
        [(own_shape, low), (own_shape, low), ((4, half + 16, channels), low)],
        [
            ((2,) + wide, low), (head_shape, low), (head_shape, low), (wide, low), (wide, low),
            ((rim_cells, 3 * half), full), ((2,) + own_shape, low), ((4, half + 16, channels), low),
            sems(6), sems(3),
        ],
        28,
        cost * 27,
        [],
        [vec],
        [act_one, act_two, mixed, value_key, act_three, grad_proj],
        [send_shape] * 4,
    )
    key_near, query_near, own_two = lax.optimization_barrier((key_near, query_near, own_two))
    relays = [key_mate, query_mate, swap(key_near, "row", 1), swap(query_near, "row", 1)]
    packed = [value_key, query_part, key_near, query_near]
    lines = 18 * (half // 4) + half + 16
    shifted_one, grad_res, *payload = call(
        middle_kernel,
        [(tall, low)],
        [(wide, full)] + [((lines, channels), low)] * 4,
        [
            ((HEADS,) + head_shape, low), ((HEADS,) + query_shape, low),
            (wide, low), (wide, full), rows_eight, (own_shape, low), (wide, full),
            ((4, lines, channels), low), (wide, full), (tall, low), (kernel_shape, low),
            (wide, full), (own_shape, low), rows_eight, sems(18), sems(5),
        ],
        40,
        cost * 26,
        [],
        [vec, qkv_t, *relays],
        [
            *packed, grad_proj, residual, stats, own_two, weight_rows, w_two_back, conv_one,
            own_one, out_sums,
        ],
    )
    *sends, shifted_one = lax.optimization_barrier((*sends, shifted_one))
    total = add_up(payload[0], *[swap(payload[step], "img", step) for step in (1, 2, 3)])
    heads_got = [sends[0]] + [swap(sends[step], "row", step) for step in (1, 2, 3)]
    shifted_one, total, *heads_got = lax.optimization_barrier((shifted_one, total, *heads_got))
    both = add_up(total, swap(total, "row", 4))
    grad_own, grad_away, sums_one = call(
        first_kernel,
        [],
        [((block_cells, channels), low), ((block_cells, channels), low), rows_eight],
        [
            (kernel_shape, low), (wide, low), (wide, full), rows_eight,
            ((2, block_cells, channels), low), rows_eight, (wide, full), sems(4), sems(3),
        ],
        20,
        cost * 12,
        [],
        [vec, shifted_one],
        [w_one_back, pix, grad_res, stats],
    )
    block_own, block_away = call(
        functools.partial(block_kernel, cols),
        [((block_cells, channels), low), ((block_cells, channels), low)],
        [],
        [((2, block_cells, channels), full), sems(2)],
        8,
        cost,
        [],
        [vec, out_weight.reshape(HEADS, half, channels), *heads_got],
        [residual],
    )
    out_pair = jnp.stack([block_own, grad_own])
    away_pair = swap(jnp.stack([block_away, grad_away]), "row", 4)
    first_pair = jnp.where(image == 0, out_pair, away_pair)
    second_pair = jnp.where(image == 0, away_pair, out_pair)
    finished = jnp.stack([first_pair, second_pair], axis=1).reshape((2,) + pixels.shape)
    norm_one = jnp.concatenate([sums_one, jnp.zeros_like(sums_one)], axis=0).astype(low)
    norm_one = add_up(norm_one, swap(norm_one, "row", 4))
    other = swap(both, "row", 2)
    pair = jnp.concatenate([both, other, norm_one], axis=0)
    parts = gather_columns(pair)
    line = ((channels,), full)
    kernel_out = ((9, channels, channels), full)
    time_out = ((time_weight.shape[0], 2 * channels), full)
    qkv_out, out_out = ((channels, 3 * channels), full), ((channels, channels), full)
    half_time = time_weight.shape[0] // 2
    frequency = jnp.exp(-math.log(10000.0) * jnp.arange(half_time, dtype=full) / half_time)
    (
        conv1_weight_grad, conv2_weight_grad, qkv_weight_grad, out_weight_grad, time_weight_grad,
        qv_bias_grad, time_bias_grad, *lines,
    ) = call(
        final_kernel,
        [],
        [kernel_out, kernel_out, qkv_out, out_out, time_out],
        [
            kernel_out, kernel_out, ((3 * channels, channels), full), qkv_out, out_out, time_out,
            ((HEADS, 4, 16, channels), full), ((4, 16, channels), full), sems(32), sems(3),
        ],
        28,
        cost,
        [],
        [*parts, frequency[None, :]],
        [],
        [((2 * channels,), full)] * 2 + [line] * 9,
    )
    norm1_gain_grad, norm1_bias_grad, norm3_gain_grad, norm3_bias_grad, conv2_bias_grad = lines[:5]
    out_bias_grad, norm2_gain_grad, norm2_bias_grad, conv1_bias_grad = lines[5:]
    return (
        finished[0],
        finished[1],
        norm1_gain_grad,
        norm1_bias_grad,
        conv1_weight_grad.reshape(conv1_weight.shape),
        conv1_bias_grad,
        time_weight_grad,
        time_bias_grad,
        norm2_gain_grad,
        norm2_bias_grad,
        conv2_weight_grad.reshape(conv2_weight.shape),
        conv2_bias_grad,
        norm3_gain_grad,
        norm3_bias_grad,
        qkv_weight_grad,
        qv_bias_grad,
        out_weight_grad,
        out_bias_grad,
    )


def local(*arrays):
    pixels = arrays[0]
    if lax.axis_size("row") == pixels.shape[0] * HEADS and lax.axis_size("img") == 4:
        return local_image(*arrays)
    return local_rows(*arrays)


def solution(mesh):
    placed = (
        P("img", "row", None, None),
        P("img"),
        P("img"),
        P(),
        P(),
        P(),
        P(),
        P(),
        P(),
        P(),
        P(),
        P(),
        P(),
        P(),
        P(),
        P(),
        P(),
        P(),
        P(),
        P("img", "row", None, None),
    )
    return jax.shard_map(
        local,
        mesh=mesh,
        in_specs=placed,
        out_specs=(
            P("img", "row", None, None),
            P("img", "row", None, None),
            P(),
            P(),
            P(),
            P(),
            P(),
            P(),
            P(),
            P(),
            P(),
            P(),
            P(),
            P(),
            P(),
            P(),
            P(),
            P(),
        ),
        check_vma=False,
    )
```

```python
import functools
import math

import jax
import jax.numpy as jnp
from jax import lax
from jax.experimental import pallas as pl
from jax.experimental.pallas import tpu as pltpu
from jax.sharding import PartitionSpec as P

GROUPS = 32
HEADS = 4


EPSILON = 1e-05
MASKED = -1000000000.0
PRECISE = lax.Precision.HIGHEST


def with_halo(cells, sides, width):
    for axis, dim in sides:
        count = lax.axis_size(axis)
        ends = count - 1
        head = lax.slice_in_dim(cells, 0, width, axis=dim)
        tail = lax.slice_in_dim(cells, cells.shape[dim] - width, cells.shape[dim], axis=dim)
        cells = jnp.concatenate(
            [
                lax.ppermute(tail, axis, [(i, (i + 1) % count) for i in range(ends)]),
                cells,
                lax.ppermute(head, axis, [((i + 1) % count, i) for i in range(ends)]),
            ],
            axis=dim,
        )
    return cells


def embed_steps(timesteps, time_width):
    half_dim = time_width // 2
    frequency = jnp.exp(-math.log(10000.0) * jnp.arange(half_dim, dtype=jnp.float32) / half_dim)
    angles = timesteps.astype(jnp.float32)[:, None] * frequency[None, :]
    return jnp.concatenate([jnp.cos(angles), jnp.sin(angles)], axis=1)


def silu_slope(pre_act):
    sigmoid = jax.nn.sigmoid(pre_act)
    return sigmoid * (1.0 + pre_act * (1.0 - sigmoid))


def with_rims(field_in):
    return with_halo(field_in, (("row", 1),), 1)


def conv_rows(padded, kernel):
    return lax.conv_general_dilated(
        padded,
        kernel,
        (1, 1),
        ((0, 0), (1, 1)),
        dimension_numbers=("NHWC", "HWIO", "NHWC"),
        preferred_element_type=jnp.float32,
    )


def flipped(kernel):
    return jnp.transpose(kernel[::-1, ::-1], (0, 1, 3, 2))


def kernel_grad(padded, grad_field):
    row_count = grad_field.shape[1]
    col_count = grad_field.shape[2]
    widened = jnp.pad(padded, ((0, 0), (0, 0), (1, 1), (0, 0)))
    tap_rows = []
    for tap_row in range(3):
        tap_line = []
        for tap_col in range(3):
            window = widened[:, tap_row : tap_row + row_count, tap_col : tap_col + col_count, :]
            tap_line.append(
                jnp.einsum("brwc,brwd->cd", window, grad_field, preferred_element_type=jnp.float32)
            )
        tap_rows.append(jnp.stack(tap_line))
    return jnp.stack(tap_rows)


def norm_forward(field_in, cell_mask, cell_count, group_count):
    shaped = field_in.reshape(field_in.shape[:3] + (group_count, field_in.shape[3] // group_count))
    first_sum = lax.psum(jnp.sum(shaped * cell_mask, axis=(1, 2, 4)), "row")
    center = first_sum / cell_count[:, None]
    centred = shaped - center[:, None, None, :, None]
    spread_sum = lax.psum(jnp.sum(jnp.square(centred * cell_mask), axis=(1, 2, 4)), "row")
    spread = spread_sum / cell_count[:, None]
    inverse = lax.rsqrt(spread + EPSILON)
    return (centred * inverse[:, None, None, :, None], inverse)


def norm_backward(grad_normed, normalized, inverse, gain_in, cell_mask, cell_count):
    full_shape = grad_normed.shape
    flat_norm = normalized.reshape(full_shape)
    gain_grad = jnp.sum(grad_normed * flat_norm, axis=(0, 1, 2))
    shift_grad = jnp.sum(grad_normed, axis=(0, 1, 2))
    scaled = (grad_normed * gain_in).reshape(normalized.shape)
    sum_plain, sum_cross = lax.psum(
        (
            jnp.sum(scaled * cell_mask, axis=(1, 2, 4)),
            jnp.sum(scaled * normalized * cell_mask, axis=(1, 2, 4)),
        ),
        "row",
    )
    mean_plain = sum_plain / cell_count[:, None]
    mean_cross = sum_cross / cell_count[:, None]
    grad_in = (
        (
            scaled
            - mean_plain[:, None, None, :, None]
            - normalized * mean_cross[:, None, None, :, None]
        )
        * inverse[:, None, None, :, None]
        * cell_mask
    )
    return (grad_in.reshape(full_shape), gain_grad, shift_grad)


def local_rows(
    pixels,
    heights,
    timesteps,
    norm1_gain,
    norm1_bias,
    conv1_weight,
    conv1_bias,
    time_weight,
    time_bias,
    norm2_gain,
    norm2_bias,
    conv2_weight,
    conv2_bias,
    norm3_gain,
    norm3_bias,
    qkv_weight,
    qv_bias,
    out_weight,
    out_bias,
    grad_out,
):
    image_count, row_count, col_count, channels = pixels.shape
    group_count = GROUPS
    head_count = HEADS
    head_width = channels // head_count
    query_count = row_count * col_count
    scaling = head_width ** (-0.5)
    head_shape = (image_count, query_count, head_count, head_width)
    row_ids = lax.axis_index("row") * row_count + jnp.arange(row_count, dtype=jnp.int32)
    row_valid = row_ids[None, :] < heights[:, None]
    row_mask = row_valid.astype(jnp.float32)
    cell_rows = row_mask[:, :, None, None]
    cell_mask = row_mask[:, :, None, None, None]
    own_valid = jnp.repeat(row_valid, col_count, axis=1)[:, None, None, :]
    cell_count = heights.astype(jnp.float32) * (col_count * (channels // group_count))
    gain_one = norm1_gain.astype(jnp.float32)
    gain_two = norm2_gain.astype(jnp.float32)
    gain_three = norm3_gain.astype(jnp.float32)
    field_in = pixels.astype(jnp.float32)
    normed_one, inverse_one = norm_forward(field_in, cell_mask, cell_count, group_count)
    pre_one = normed_one.reshape(field_in.shape) * gain_one + norm1_bias.astype(jnp.float32)
    act_one = (jax.nn.silu(pre_one) * cell_rows).astype(jnp.bfloat16)
    padded_one = with_rims(act_one)
    conv_one = conv_rows(padded_one, conv1_weight) + conv1_bias.astype(jnp.float32)
    time_act = jax.nn.silu(embed_steps(timesteps, time_weight.shape[0]))
    shifts = jnp.dot(
        time_act, time_weight.astype(jnp.float32), precision=PRECISE
    ) + time_bias.astype(jnp.float32)
    scale_part = 1.0 + shifts[:, None, None, :channels]
    shift_part = shifts[:, None, None, channels:]
    normed_two, inverse_two = norm_forward(conv_one, cell_mask, cell_count, group_count)
    affine_two = normed_two.reshape(field_in.shape) * gain_two + norm2_bias.astype(jnp.float32)
    pre_two = affine_two * scale_part + shift_part
    act_two = (jax.nn.silu(pre_two) * cell_rows).astype(jnp.bfloat16)
    padded_two = with_rims(act_two)
    residual = field_in + (conv_rows(padded_two, conv2_weight) + conv2_bias.astype(jnp.float32))
    normed_three, inverse_three = norm_forward(residual, cell_mask, cell_count, group_count)
    act_three = (
        normed_three.reshape(field_in.shape) * gain_three + norm3_bias.astype(jnp.float32)
    ).astype(jnp.bfloat16)
    projected = jnp.einsum(
        "brwc,cd->brwd", act_three, qkv_weight, preferred_element_type=jnp.float32
    )
    qv_float = qv_bias.astype(jnp.float32)
    queries = (projected[..., :channels] + qv_float[:channels]).astype(jnp.bfloat16)
    keys_own = projected[..., channels : 2 * channels].astype(jnp.bfloat16)
    values_own = (projected[..., 2 * channels :] + qv_float[channels:]).astype(jnp.bfloat16)
    query_heads = queries.reshape(head_shape)
    key_heads = keys_own.reshape(head_shape)
    value_heads = values_own.reshape(head_shape)

    def flatten_rows(piece_arr):
        return piece_arr.reshape(
            image_count, piece_arr.shape[1] * col_count, head_count, head_width
        )

    def key_mask(span_rows):
        key_rows = jnp.arange(span_rows, dtype=jnp.int32)
        return jnp.repeat(key_rows[None, :] < heights[:, None], col_count, axis=1)[:, None, None, :]

    top_init = jnp.full((image_count, query_count, head_count), MASKED, jnp.float32)
    piece_keys = lax.all_gather(keys_own, "row", axis=1, tiled=True)
    piece_values = lax.all_gather(values_own, "row", axis=1, tiled=True)
    key_valid = key_mask(piece_keys.shape[1])
    scores = (
        jnp.einsum(
            "bqhd,bkhd->bqhk",
            query_heads,
            flatten_rows(piece_keys),
            preferred_element_type=jnp.float32,
        )
        * scaling
    )
    scores = jnp.where(key_valid, scores, MASKED)
    new_top = jnp.maximum(top_init, jnp.max(scores, axis=3))
    weights = jnp.where(key_valid, jnp.exp(scores - new_top[..., None]), 0.0)
    running_total = jnp.sum(weights, axis=3)
    running_acc = jnp.einsum(
        "bqhk,bkhd->bqhd",
        weights.astype(jnp.bfloat16),
        flatten_rows(piece_values),
        preferred_element_type=jnp.float32,
    )
    attn_float = running_acc / running_total[..., None]
    log_total = new_top + jnp.log(running_total)
    attended = attn_float.reshape(pixels.shape).astype(jnp.bfloat16)
    output_proj = jnp.einsum(
        "brwc,cd->brwd", attended, out_weight, preferred_element_type=jnp.float32
    ) + out_bias.astype(jnp.float32)
    block_out = ((residual + output_proj) * cell_rows).astype(jnp.bfloat16)
    grad_proj = grad_out.astype(jnp.float32) * cell_rows
    grad_proj_low = grad_proj.astype(jnp.bfloat16)
    out_weight_grad = jnp.einsum(
        "brwc,brwd->cd", attended, grad_proj_low, preferred_element_type=jnp.float32
    )
    out_bias_grad = jnp.sum(grad_proj, axis=(0, 1, 2))
    grad_attended = jnp.einsum(
        "brwd,cd->brwc", grad_proj_low, out_weight, preferred_element_type=jnp.float32
    ).astype(jnp.bfloat16)
    grad_heads = grad_attended.reshape(head_shape)
    delta_own = jnp.sum(grad_heads.astype(jnp.float32) * attn_float, axis=3)
    stat_shape = (image_count, row_count, col_count, head_count)
    all_lse, all_delta = (
        lax.all_gather(log_total.reshape(stat_shape), "row", axis=1, tiled=True),
        lax.all_gather(delta_own.reshape(stat_shape), "row", axis=1, tiled=True),
    )
    piece_keys = lax.all_gather(keys_own, "row", axis=1, tiled=True)
    piece_values = lax.all_gather(values_own, "row", axis=1, tiled=True)
    flat_keys = flatten_rows(piece_keys)
    key_valid = key_mask(piece_keys.shape[1])
    scores = (
        jnp.einsum("bqhd,bkhd->bqhk", query_heads, flat_keys, preferred_element_type=jnp.float32)
        * scaling
    )
    soft_weights = jnp.where(key_valid, jnp.exp(scores - log_total[..., None]), 0.0)
    grad_probs = jnp.einsum(
        "bqhd,bkhd->bqhk",
        grad_heads,
        flatten_rows(piece_values),
        preferred_element_type=jnp.float32,
    )
    grad_scores = (soft_weights * (grad_probs - delta_own[..., None])).astype(jnp.bfloat16)
    grad_query_sum = jnp.einsum(
        "bqhk,bkhd->bqhd", grad_scores, flat_keys, preferred_element_type=jnp.float32
    )
    piece_queries = lax.all_gather(queries, "row", axis=1, tiled=True)
    piece_grads = lax.all_gather(grad_attended, "row", axis=1, tiled=True)
    flat_queries = flatten_rows(piece_queries)
    flat_grads = flatten_rows(piece_grads)
    span_rows = piece_queries.shape[1]
    piece_lse = all_lse.reshape(image_count, span_rows * col_count, head_count)
    piece_delta = all_delta.reshape(image_count, span_rows * col_count, head_count)
    scores = (
        jnp.einsum("bqhd,bkhd->bqhk", flat_queries, key_heads, preferred_element_type=jnp.float32)
        * scaling
    )
    soft_weights = jnp.where(own_valid, jnp.exp(scores - piece_lse[..., None]), 0.0)
    value_term = jnp.einsum(
        "bqhk,bqhd->bkhd",
        soft_weights.astype(jnp.bfloat16),
        flat_grads,
        preferred_element_type=jnp.float32,
    )
    grad_probs = jnp.einsum(
        "bqhd,bkhd->bqhk", flat_grads, value_heads, preferred_element_type=jnp.float32
    )
    grad_scores = (soft_weights * (grad_probs - piece_delta[..., None])).astype(jnp.bfloat16)
    key_term = jnp.einsum(
        "bqhk,bqhd->bkhd", grad_scores, flat_queries, preferred_element_type=jnp.float32
    )
    key_term, value_term = (key_term, value_term)
    grad_queries = (grad_query_sum * scaling).reshape(pixels.shape).astype(jnp.bfloat16)
    grad_keys = (key_term * scaling).reshape(pixels.shape).astype(jnp.bfloat16)
    grad_values = value_term.reshape(pixels.shape).astype(jnp.bfloat16)
    grad_projected = jnp.concatenate([grad_queries, grad_keys, grad_values], axis=3)
    qkv_weight_grad = jnp.einsum(
        "brwc,brwd->cd", act_three, grad_projected, preferred_element_type=jnp.float32
    )
    qv_bias_grad = jnp.concatenate(
        [
            jnp.sum(grad_queries.astype(jnp.float32), axis=(0, 1, 2)),
            jnp.sum(grad_values.astype(jnp.float32), axis=(0, 1, 2)),
        ]
    )
    grad_act_three = jnp.einsum(
        "brwd,cd->brwc", grad_projected, qkv_weight, preferred_element_type=jnp.float32
    )
    grad_res_attn, norm3_gain_grad, norm3_bias_grad = norm_backward(
        grad_act_three, normed_three, inverse_three, gain_three, cell_mask, cell_count
    )
    grad_residual = grad_proj + grad_res_attn
    grad_conv_two = grad_residual.astype(jnp.bfloat16)
    conv2_bias_grad = jnp.sum(grad_residual, axis=(0, 1, 2))
    conv2_weight_grad = kernel_grad(padded_two, grad_conv_two)
    grad_act_two = conv_rows(with_rims(grad_conv_two), flipped(conv2_weight)) * cell_rows
    grad_pre_two = grad_act_two * silu_slope(pre_two)
    scale_grad = jnp.sum(grad_pre_two * affine_two, axis=(1, 2))
    shift_grad = jnp.sum(grad_pre_two, axis=(1, 2))
    shift_grads = jnp.concatenate([scale_grad, shift_grad], axis=1)
    grad_conv_one, norm2_gain_grad, norm2_bias_grad = norm_backward(
        grad_pre_two * scale_part, normed_two, inverse_two, gain_two, cell_mask, cell_count
    )
    conv_one_low = grad_conv_one.astype(jnp.bfloat16)
    conv1_bias_grad = jnp.sum(grad_conv_one, axis=(0, 1, 2))
    conv1_weight_grad = kernel_grad(padded_one, conv_one_low)
    grad_act_one = conv_rows(with_rims(conv_one_low), flipped(conv1_weight)) * cell_rows
    grad_pre_one = grad_act_one * silu_slope(pre_one)
    grad_field_norm, norm1_gain_grad, norm1_bias_grad = norm_backward(
        grad_pre_one, normed_one, inverse_one, gain_one, cell_mask, cell_count
    )
    grad_pixels = (grad_residual + grad_field_norm).astype(jnp.bfloat16)
    time_weight_grad = jnp.dot(time_act.T, shift_grads, precision=PRECISE)
    time_bias_grad = jnp.sum(shift_grads, axis=0)
    summed = lax.psum(
        (
            norm1_gain_grad,
            norm1_bias_grad,
            conv1_weight_grad,
            conv1_bias_grad,
            time_weight_grad,
            time_bias_grad,
            norm2_gain_grad,
            norm2_bias_grad,
            conv2_weight_grad,
            conv2_bias_grad,
            norm3_gain_grad,
            norm3_bias_grad,
            qkv_weight_grad,
            qv_bias_grad,
            out_weight_grad,
            out_bias_grad,
        ),
        ("img", "row"),
    )
    return (
        block_out,
        grad_pixels,
        summed[0],
        summed[1],
        summed[2],
        summed[3],
        summed[4],
        summed[5],
        summed[6],
        summed[7],
        summed[8],
        summed[9],
        summed[10],
        summed[11],
        summed[12],
        summed[13],
        summed[14],
        summed[15],
    )


ARRIVAL = (3, 5, 7, 0, 1, 2, 4, 6)


def mib(count):
    return pltpu.CompilerParams(vmem_limit_bytes=count * 2**20)


def dot(left, right):
    return jnp.dot(left, right, preferred_element_type=jnp.float32)


def dot_rows(left, right):
    return lax.dot_general(
        left, right, (((1,), (1,)), ((), ())), preferred_element_type=jnp.float32
    )


def fold(tile):
    return jnp.sum(tile.reshape(-1, 8, tile.shape[1]), axis=0)


def group_sums(row, width):
    channels = row.shape[1]
    rows = lax.broadcasted_iota(jnp.int32, (channels, channels), 0) // width
    cols = lax.broadcasted_iota(jnp.int32, (channels, channels), 1) // width
    same = jnp.where(rows == cols, 1.0, 0.0).astype(jnp.bfloat16)
    wide = jnp.broadcast_to(row, (16, channels))
    total = None
    for _ in range(3):
        term = wide.astype(jnp.bfloat16)
        wide = wide - term.astype(jnp.float32)
        part = dot(term, same)
        total = part if total is None else total + part
    return total[0:1]


def row_at(index, cols):
    return pl.ds(pl.multiple_of(index * cols, cols), cols)


def total_of(tile):
    return jnp.sum(tile, axis=0, keepdims=True)


def cell_sums(tiles, about, height):
    first, square = 0.0, 0.0
    for index, tile in tiles:
        off = (tile - about) * valid_row(index, height)
        first, square = first + fold(off), square + fold(off * off)
    return first, square


def stats_of(first, square, about, height, cols):
    width = about.shape[1] // GROUPS
    each = (height * cols).astype(jnp.float32)
    first, square = total_of(first), total_of(square)
    mean = group_sums(first + about * each, width) / (each * width)
    shift = about - mean
    spread = group_sums(square + 2.0 * first * shift + each * shift * shift, width)
    return mean, lax.rsqrt(spread / (each * width) + EPSILON)


def row_mean(tile):
    return jnp.sum(tile, axis=0, keepdims=True) * (1.0 / tile.shape[0])


def in_turn(count, before, main, after):
    for step in range(count + 2):
        if step < count:
            before(step)
        if 0 <= step - 1 < count:
            main(step - 1)
        if 0 <= step - 2:
            after(step - 2)


def conv_block(shifted, weight, block, size, cols):
    base = block * size
    total = dot(shifted[base : base + size, :], weight[0])
    for tap in (1, 2):
        at = base + tap * cols
        total = total + dot(shifted[at : at + size, :], weight[tap])
    return total


def half_line(mean, inverse, gain, bias, scale=1.0, shift=0.0):
    slope = inverse * gain
    start = bias - mean * slope
    return 0.5 * slope * scale, 0.5 * (start * scale + shift)


def put_shifted(ref, index, tile, cols):
    channels = tile.shape[1]
    column = lax.broadcasted_iota(jnp.int32, tile.shape, 0)
    before = jnp.where(column == 0, 0.0, pltpu.roll(tile, 1, 0))
    after = jnp.where(column == cols - 1, 0.0, pltpu.roll(tile, cols - 1, 0))
    at = row_at(index + 1, cols)
    ref[at, 0:channels] = before.astype(jnp.bfloat16)
    ref[at, channels : 2 * channels] = tile.astype(jnp.bfloat16)
    ref[at, 2 * channels : 3 * channels] = after.astype(jnp.bfloat16)


def clear_rims(ref, cols):
    edge = jnp.zeros((cols, ref.shape[1]), ref.dtype)
    ref[0:cols, :] = edge
    ref[ref.shape[0] - cols : ref.shape[0], :] = edge


def conv_shifted(shifted, weight, out, bias, cols, added=None):
    step = 8 * cols

    def block(index, carry):
        base = index * step
        total = bias
        for tap in range(3):
            at = pl.ds(pl.multiple_of(base + tap * cols, cols), step)
            total = total + dot(shifted[at, :], weight[tap])
        if added is not None:
            total = total + added[pl.ds(pl.multiple_of(base, step), step), :].astype(jnp.float32)
        out[pl.ds(pl.multiple_of(base, step), step), :] = total
        return carry

    lax.fori_loop(0, out.shape[0] // step, block, 0, unroll=True)


def put_quarter(parts, payload, start):
    half = parts[0].shape[0] // 3
    unit = half // 4
    for line, part in enumerate(parts):
        part = part.astype(jnp.bfloat16)
        for shift in range(3):
            at = start + (3 * line + shift) * unit
            for chunk in range(4):
                base = shift * half + chunk * unit
                payload[chunk, at : at + unit, :] = part[base : base + unit]


def own_place(vec):
    spot = lax.axis_index("row")
    image, head = spot // HEADS, spot % HEADS
    return spot, head, image, jnp.max(vec[11:12, :]).astype(jnp.int32)


def started(sems, *pairs):
    copies = [pltpu.make_async_copy(src, dst, sems.at[k]) for k, (src, dst) in enumerate(pairs)]
    for copy in copies:
        copy.start()
    return copies


def finish_all(copies):
    for copy in copies:
        copy.wait()


def valid_row(index, height):
    return jnp.where(index < height, 1.0, 0.0).astype(jnp.float32)


def forward_kernel(vec, *refs):
    blocks, (w_one_far, w_two_far) = refs[:8], refs[8:10]
    act_three, pix_far, conv_far, residual_far, act_one_far, act_two_far, stats_far = refs[10:17]
    pix, conv_one, residual, stats, w_one, w_two, shift_one, shift_two, in_sems, out_sems = refs[17:]
    cells, channels = pix.shape
    block_cells = blocks[0].shape[0]
    cols = (shift_one.shape[0] - cells) // 2
    rows = cells // cols
    spot, _, _, height = own_place(vec)
    pairs = []
    for step, block in zip(ARRIVAL, blocks):
        base = pl.multiple_of((spot ^ step) * block_cells, block_cells)
        pairs.append((block, pix.at[pl.ds(base, block_cells), :]))
    arriving = started(in_sems, *pairs, (w_one_far, w_one), (w_two_far, w_two))
    gain_one, bias_one, conv_bias_one, gain_two, bias_two = (vec[k : k + 1, :] for k in range(5))
    scale, shift, conv_bias_two, gain_three, bias_three = (vec[k : k + 1, :] for k in range(5, 10))
    inner = (pl.ds(cols, cells), pl.ds(channels, channels))

    group = 4
    size = group * cols
    count = rows // group
    zero = jnp.zeros((8, channels), jnp.float32)

    def tile_of(ref, index):
        return ref[index * cols : (index + 1) * cols, :].astype(jnp.float32)

    def tiles_of(ref, block):
        return [(k, tile_of(ref, k)) for k in range(block * group, (block + 1) * group)]

    def stage(source, line, shifted, weight, out, bias, added=None):
        sums = [zero, zero, None]

        def activate(block):
            for index, tile in tiles_of(source, block):
                part = tile * line[0] + line[1]
                part = (part + part * jnp.tanh(part)) * valid_row(index, height)
                put_shifted(shifted, index, part, cols)

        def conv(block):
            total = conv_block(shifted, weight, block, size, cols) + bias
            if added is not None:
                total = total + added[block * size : (block + 1) * size, :].astype(jnp.float32)
            out[block * size : (block + 1) * size, :] = total

        def measure(block):
            if block == 0:
                sums[2] = row_mean(tile_of(out, 0))
            first, square = cell_sums(tiles_of(out, block), sums[2], height)
            sums[0], sums[1] = sums[0] + first, sums[1] + square

        in_turn(count, activate, conv, measure)
        return stats_of(*sums, height, cols)

    clear_rims(shift_one, cols)
    clear_rims(shift_two, cols)
    finish_all(arriving[:8])
    leaving = started(out_sems, (pix, pix_far))
    about = row_mean(tile_of(pix, 0))
    first, square = zero, zero
    for block in range(count):
        more = cell_sums(tiles_of(pix, block), about, height)
        first, square = first + more[0], square + more[1]
    mean_one, inv_one = stats_of(first, square, about, height, cols)
    arriving[8].wait()
    line = half_line(mean_one, inv_one, gain_one, bias_one)
    mean_two, inv_two = stage(pix, line, shift_one, w_one, conv_one, conv_bias_one)
    leaving += started(
        out_sems.at[1:3], (shift_one.at[inner], act_one_far), (conv_one, conv_far)
    )
    arriving[9].wait()
    line = half_line(mean_two, inv_two, gain_two, bias_two, scale, shift)
    mean_three, inv_three = stage(conv_one, line, shift_two, w_two, residual, conv_bias_two, pix)
    leaving += started(
        out_sems.at[3:5], (shift_two.at[inner], act_two_far), (residual, residual_far)
    )
    stats[...] = jnp.concatenate(
        [mean_one, inv_one, mean_two, inv_two, mean_three, inv_three, mean_one, mean_one], axis=0
    )
    leaving += started(out_sems.at[5:6], (stats, stats_far))
    slope = inv_three * gain_three
    start = bias_three - mean_three * slope

    def third(index, carry):
        at = row_at(index, cols)
        act_three[at, :] = (residual[at, :] * slope + start).astype(jnp.bfloat16)
        return carry

    lax.fori_loop(0, rows, third, 0, unroll=4)
    finish_all(leaving)


def attention_kernel(columns, vec, act_three, w_heads, w_out, biases, *refs):
    blocks = refs[:8]
    value_key_far, query_far, grad_far, mixed_far, sums_far = refs[8:13]
    (
        grad_blocks, grad_proj, value_key, query_part, sums,
        query_grad, key_pad, value_pad, heads_t, mixed, mask_row, in_sems, out_sems,
    ) = refs[13:]
    cells, channels = grad_proj.shape
    block_cells = blocks[0].shape[0]
    spot, _, _, height = own_place(vec)
    half = mixed.shape[1] // 2
    cols = columns
    scaling = half**-0.5
    valid_cells = height * cols
    step = 256
    pairs = []
    for index, block in zip(ARRIVAL, blocks):
        base = pl.multiple_of((spot ^ index) * block_cells, block_cells)
        pairs.append((block, grad_blocks.at[pl.ds(base, block_cells), :]))
    arriving = started(in_sems, *pairs)

    sizes = []
    for start in range(0, cells, 512):
        at = slice(start, start + 512)
        parts = dot(act_three[at, :], w_heads[...]) + biases[0:1, :]
        query, key, value = (parts[:, 2 * half * k : 2 * half * (k + 1)] for k in range(3))
        query_grad[at, :] = query.astype(jnp.bfloat16) * jnp.bfloat16(scaling)
        key_pad[at, :] = key.astype(jnp.bfloat16)
        value_pad[at, :] = value.astype(jnp.bfloat16)
        query_size = jnp.sum(query * query, axis=1, keepdims=True) * (scaling * scaling)
        key_size = jnp.sum(key * key, axis=1, keepdims=True)
        sizes.append((jnp.max(query_size), jnp.max(key_size)))
    lane = lax.broadcasted_iota(jnp.int32, (1, cells), 1)
    mask_row[...] = jnp.where(lane < valid_cells, 0.0, MASKED)
    heads_t[...] = jnp.zeros(heads_t.shape, jnp.float32)
    mixed[...] = jnp.zeros(mixed.shape, jnp.bfloat16)
    finish_all(arriving)

    def clean(index, total):
        at = pl.ds(pl.multiple_of(index * block_cells, block_cells), block_cells)
        cell = index * block_cells + lax.broadcasted_iota(jnp.int32, (block_cells, channels), 0)
        kept = jnp.where(cell < valid_cells, grad_blocks[at, :].astype(jnp.float32), 0.0)
        low = kept.astype(jnp.bfloat16)
        grad_proj[at, :] = low
        query_grad[at, :] = query_grad[at, :] + dot(low, w_out[...]).astype(jnp.bfloat16)
        return total + fold(kept)

    start = jnp.zeros((8, channels), jnp.float32)
    total = lax.fori_loop(0, cells // block_cells, clean, start, unroll=True)
    sums[...] = jnp.concatenate([total_of(total), jnp.zeros((7, channels), jnp.float32)], axis=0)
    leaving = started(out_sems, (grad_proj, grad_far), (sums, sums_far))

    def query_block(shifted, index, carry):
        at = pl.ds(pl.multiple_of(index * step, step), step)
        both = query_grad[at, :]
        scores = dot_rows(both, key_pad[...]) + mask_row[...]
        if shifted:
            scores = scores - jnp.max(scores, axis=1, keepdims=True)
        weights = jnp.exp(scores)
        total = jnp.zeros((step, 2 * half), jnp.float32)
        for start in range(0, cells, 2 * half):
            total = total + weights[:, start : start + 2 * half]
        inverse = 1.0 / jnp.sum(total, axis=1, keepdims=True)
        low = weights.astype(jnp.bfloat16)
        out = dot(low, value_pad[...]) * inverse
        wide = both.astype(jnp.float32)
        delta = jnp.sum(wide * out, axis=1, keepdims=True)
        turned = jnp.transpose(wide * inverse).astype(jnp.bfloat16)
        grad_probs = dot_rows(both, value_pad[...])
        grad_scores = (low.astype(jnp.float32) * (grad_probs - delta)).astype(jnp.bfloat16)
        grad_query = dot(grad_scores, key_pad[...]) * (inverse * scaling)
        mixed[at, :] = (out + grad_query).astype(jnp.bfloat16)
        heads_t[0:half, :] += dot(turned[0:half], grad_scores)
        heads_t[half : 2 * half, :] += dot(turned[half : 2 * half], low)
        return carry

    query_most, key_most = (functools.reduce(jnp.maximum, size) for size in zip(*sizes))
    narrow = query_most * key_most <= 3600.0

    @pl.when(narrow)
    def _():
        lax.fori_loop(0, cells // step, functools.partial(query_block, False), 0, unroll=2)

    @pl.when(jnp.logical_not(narrow))
    def _():
        count = (valid_cells + step - 1) // step
        lax.fori_loop(0, count, functools.partial(query_block, True), 0)

    for start in range(0, cells, step):
        value_key[start : start + step, :] = jnp.transpose(heads_t[:, start : start + step]).astype(
            jnp.bfloat16
        )
    query_part[:, 0:half] = mixed[0 : cells // 2, 0:half]
    query_part[:, half : 2 * half] = mixed[cells // 2 : cells, 0:half]
    leaving += started(
        out_sems.at[2:5], (value_key, value_key_far), (query_part, query_far), (mixed, mixed_far)
    )
    finish_all(leaving)


def aside_kernel(vec, *refs):
    act_far, (mixed_far, value_key_far, act_three_far, grad_far) = refs[0:2], refs[2:6]
    own_far, weight_far, sends = refs[6:8], refs[8], refs[9:13]
    acts, mixed, value_key, act_three, grad_proj, padded, own, weight_rows, in_sems, out_sems = (
        refs[13:]
    )
    cells, channels = act_three.shape
    cols = (padded.shape[0] - cells) // 2
    lanes = mixed.shape[1]
    half = lanes // 2
    spot, head, image, _ = own_place(vec)
    arriving = started(
        in_sems,
        (mixed_far, mixed),
        (value_key_far, value_key),
        (act_three_far, act_three),
        (grad_far, grad_proj),
        (act_far[0], acts.at[0]),
        (act_far[1], acts.at[1]),
    )
    block_cells = sends[0].shape[0]
    step = 256
    arriving[0].wait()
    for k, send in enumerate(sends):
        tiles = []
        for part in range(2):
            block = (head ^ k) + HEADS * (image ^ part)
            at = pl.ds(pl.multiple_of(block * block_cells, block_cells), block_cells)
            tiles.append(mixed[at, half:lanes])
        send[...] = jnp.concatenate(tiles, axis=1)
    finish_all(arriving[1:4])

    def gather(index, totals):
        at = pl.ds(pl.multiple_of(index * step, step), step)
        low_mixed, low_heads, act = mixed[at, :], value_key[at, :], act_three[at, :]
        mixed_t = jnp.transpose(low_mixed.astype(jnp.float32)).astype(jnp.bfloat16)
        heads_t = jnp.transpose(low_heads.astype(jnp.float32)).astype(jnp.bfloat16)
        return (
            totals[0] + dot(mixed_t, act),
            totals[1] + dot(heads_t, act),
            totals[2] + dot(mixed_t, grad_proj[at, :]),
            totals[3] + fold(low_mixed.astype(jnp.float32)),
            totals[4] + fold(low_heads.astype(jnp.float32)),
        )

    square = jnp.zeros((lanes, channels), jnp.float32)
    line = jnp.zeros((8, lanes), jnp.float32)
    from_query, from_heads, from_out, query_sum, value_sum = lax.fori_loop(
        0, cells // step, gather, (square, square, square, line, line)
    )
    unit = half // 4
    parts = (from_query[0:half], from_heads[0:half], from_heads[half:lanes], from_out[half:lanes])
    for chunk in range(4):
        for k, part in enumerate(parts):
            piece = part[chunk * unit : (chunk + 1) * unit].astype(jnp.bfloat16)
            weight_rows[chunk, k * unit : (k + 1) * unit, :] = piece
    weight_rows[:, half:, :] = jnp.zeros((4, 16, channels), jnp.bfloat16)
    which = lax.axis_index("img") * 2 + image
    lane = lax.broadcasted_iota(jnp.int32, (1, channels), 1)
    now = jnp.max(vec[12:13, :]).astype(jnp.int32)
    high = jnp.where(lane == which, (now // 32).astype(jnp.float32), 0.0)
    rest = jnp.where(lane == which, (now % 32).astype(jnp.float32), 0.0)
    row = jnp.concatenate([total_of(query_sum), total_of(value_sum)], axis=1)
    below = jnp.zeros((13, channels), jnp.float32)
    weight_rows[2, half:, :] = jnp.concatenate([row, high, rest, below], axis=0).astype(
        jnp.bfloat16
    )
    source = lax.broadcasted_iota(jnp.int32, (channels, 3 * half), 0)
    target = lax.broadcasted_iota(jnp.int32, (channels, 3 * half), 1)
    chosen = jnp.where(source == head * half + target % half, 1.0, 0.0).astype(jnp.bfloat16)
    lane = lax.broadcasted_iota(jnp.int32, (step, 3 * half), 1)
    column = lax.broadcasted_iota(jnp.int32, (step, 3 * half), 0) % cols
    leaving = started(out_sems.at[2:3], (weight_rows, weight_far))
    for k in range(2):
        arriving[4 + k].wait()
        clear_rims(padded, cols)

        def widen(index, carry):
            at = pl.ds(pl.multiple_of(index * step, step), step)
            tile = dot(acts[k, at, :], chosen)
            before = jnp.where(column == 0, 0.0, pltpu.roll(tile, 1, 0))
            after = jnp.where(column == cols - 1, 0.0, pltpu.roll(tile, step - 1, 0))
            tile = jnp.where(lane < half, before, jnp.where(lane < 2 * half, tile, after))
            padded[pl.ds(pl.multiple_of(index * step + cols, cols), step), :] = tile
            return carry

        lax.fori_loop(0, cells // step, widen, 0)
        for tap in range(3):

            def turn(index, carry):
                at = pl.ds(pl.multiple_of(index * step + tap * cols, cols), step)
                to = pl.ds(pl.multiple_of(index * step, step), step)
                own[k, tap, :, to] = jnp.transpose(padded[at, :]).astype(jnp.bfloat16)
                return carry

            lax.fori_loop(0, cells // step, turn, 0)
        leaving += started(out_sems.at[k : k + 1], (own.at[k], own_far[k]))
    finish_all(leaving)


def middle_kernel(vec, qkv_t, *refs):
    heads_far = (refs[4], refs[0], refs[6], refs[2])
    sides_far = (refs[5], refs[1], refs[7], refs[3])
    grad_far, residual_far, stats_far, own_two_far, rows_far = refs[8:13]
    weight_far, conv_far, own_one_far, out_sums_far = refs[13:17]
    shifted_one, grad_res_far, payload_far = refs[17], refs[18], refs[19:23]
    (
        heads, sides, grad_proj, residual, stats, own_two, grad_res, payload, grad_act, shifted,
        weight, conv_one, own_one, out_sums, in_sems, out_sems,
    ) = refs[23:]
    cells, channels = grad_proj.shape
    cols = (shifted.shape[0] - cells) // 2
    rows = cells // cols
    _, head, image, height = own_place(vec)
    column = lax.axis_index("img")
    width = channels // GROUPS
    count = (height * (cols * width)).astype(jnp.float32)
    half = qkv_t.shape[1]
    unit = half // 4
    small_at = 18 * unit + half
    pairs = [(far, heads.at[head ^ k]) for k, far in enumerate(heads_far)]
    pairs += [(far, sides.at[head ^ k]) for k, far in enumerate(sides_far)]
    arriving = started(
        in_sems,
        *pairs,
        (stats_far, stats),
        (residual_far, residual),
        (grad_far, grad_proj),
        (own_two_far, own_two),
        (rows_far.at[:, pl.ds(0, half), :], payload.at[:, pl.ds(9 * unit, half), :]),
        (rows_far.at[:, pl.ds(half, 16), :], payload.at[:, pl.ds(small_at, 16), :]),
        (weight_far, weight),
        (conv_far, conv_one),
        (own_one_far, own_one),
        (out_sums_far, out_sums),
    )
    finish_all(arriving[:10])
    zeros = jnp.zeros((half, channels), jnp.bfloat16)
    halfway = cells // 2
    step = 512
    pairs = ((0, 1), (2, 3))
    w_main = []
    for a, b in pairs:
        order = [HEADS + a, 2 * HEADS + a, HEADS + b, 2 * HEADS + b]
        w_main.append(jnp.concatenate([qkv_t[k] for k in order], axis=0))
    mean, inverse = stats[4:5, :], stats[5:6, :]
    gain = vec[8:9, :]
    zero = jnp.zeros((8, channels), jnp.float32)
    plain, cross = zero, zero

    def normed(index):
        return (residual[index * cols : (index + 1) * cols, :] - mean) * inverse

    for part in range(2):
        w_side = []
        for a, b in pairs:
            left, right = qkv_t[a], qkv_t[b]
            order = [left, zeros, right, zeros] if part == 0 else [zeros, left, zeros, right]
            w_side.append(jnp.concatenate(order, axis=0))
        for base in range(0, halfway, step):
            start = part * halfway + base
            total = None
            for k, (a, b) in enumerate(pairs):
                main = jnp.concatenate(
                    [heads[a][start : start + step, :], heads[b][start : start + step, :]], axis=1
                )
                side = jnp.concatenate(
                    [sides[a][base : base + step, :], sides[b][base : base + step, :]], axis=1
                )
                term = dot(main, w_main[k]) + dot(side, w_side[k])
                total = term if total is None else total + term
            grad_act[start : start + step, :] = total
            for index in range(start // cols, (start + step) // cols):
                tile = total[index * cols - start : (index + 1) * cols - start]
                plain = plain + fold(tile)
                cross = cross + fold(tile * normed(index))
    plain, cross = total_of(plain), total_of(cross)
    mean_plain = group_sums(plain * gain, width) / count
    mean_cross = group_sums(cross * gain, width) / count
    clear_rims(shifted, cols)
    clear_rims(shifted_one, cols)
    finish_all(arriving[10:16])
    group = 4
    size = group * cols
    steps = rows // group
    totals = [zero, zero, zero, zero]
    one, two = gain * inverse, mean_cross * inverse * inverse
    three = (mean_plain - mean * inverse * mean_cross) * inverse
    gain_two, bias_two, scale, shift = (vec[k : k + 1, :] for k in range(3, 7))
    mean_two, inverse_two = stats[2:3, :], stats[3:4, :]
    line = half_line(mean_two, inverse_two, gain_two, bias_two, scale, shift)
    begin_two = mean_two * inverse_two

    def tiles(block):
        for index in range(block * group, (block + 1) * group):
            yield index, slice(index * cols, (index + 1) * cols)

    def through_three(block):
        for index, at in tiles(block):
            inner = grad_act[at, :] * one - residual[at, :] * two - three
            grad = grad_proj[at, :].astype(jnp.float32) + inner * valid_row(index, height)
            grad_res[at, :] = grad
            put_shifted(shifted, index, grad, cols)
            totals[0] = totals[0] + fold(grad)

    def conv_back(block):
        grad_act[block * size : (block + 1) * size, :] = conv_block(
            shifted, weight, block, size, cols
        )

    def through_act(block):
        for index, at in tiles(block):
            value = conv_one[at, :]
            unit_value = value * inverse_two - begin_two
            part = value * line[0] + line[1]
            sigmoid = 0.5 + 0.5 * jnp.tanh(part)
            slope = sigmoid + 2.0 * part * sigmoid * (1.0 - sigmoid)
            grad = grad_act[at, :] * valid_row(index, height) * slope
            grad_act[at, :] = grad
            totals[1] = totals[1] + fold(grad)
            totals[2] = totals[2] + fold(grad * unit_value)

    in_turn(steps, through_three, conv_back, through_act)
    total = total_of(totals[0])
    three_lines = [cross, plain, total]
    leaving = started(out_sems, (grad_res, grad_res_far))
    plain, cross = total_of(totals[1]), total_of(totals[2])
    gain, bias = gain_two, bias_two
    factor = gain * scale
    mean_plain = group_sums(plain * factor, width) / count
    mean_cross = group_sums(cross * factor, width) / count
    one, two = factor * inverse_two, mean_cross * inverse_two * inverse_two
    three = (mean_plain - begin_two * mean_cross) * inverse_two
    finish_all(arriving[16:])
    parts = [[None] * 3, [None] * 3]

    def through_two(block):
        for index, at in tiles(block):
            grad = grad_act[at, :] * one - conv_one[at, :] * two - three
            grad = grad * valid_row(index, height)
            put_shifted(shifted_one, index, grad, cols)
            totals[3] = totals[3] + fold(grad)

    def weigh(block):
        at = slice(block * size, (block + 1) * size)
        inner = slice(cols + block * size, cols + (block + 1) * size)
        for k, (own, moved) in enumerate(((own_two, shifted), (own_one, shifted_one))):
            grad = moved[inner, channels : 2 * channels]
            for tap in range(3):
                part = dot(own[tap, :, at], grad)
                parts[k][tap] = part if block == 0 else parts[k][tap] + part

    in_turn(steps, through_two, weigh, lambda block: None)
    put_quarter(parts[0], payload, 0)
    put_quarter(parts[1], payload, 9 * unit + half)
    total = total_of(totals[3])
    lines = [
        *three_lines, out_sums[0:1, :], cross * scale, plain * scale, total,
        jnp.zeros((9, channels), jnp.float32),
    ]
    mine = 2 * (column * 2 + image)
    place = lax.broadcasted_iota(jnp.int32, (16, channels), 0)
    both = jnp.where(place == mine, gain * cross + bias * plain, 0.0)
    payload[0, small_at:, :] = jnp.concatenate(lines, axis=0).astype(jnp.bfloat16)
    payload[1, small_at:, :] = jnp.where(place == mine + 1, plain, both).astype(jnp.bfloat16)
    leaving += started(
        out_sems.at[1:5],
        *[(payload.at[column ^ k], far) for k, far in enumerate(payload_far)],
    )
    finish_all(leaving)


def first_kernel(vec, shifted, weight_far, pix_far, grad_far, stats_far, *refs):
    out_own_far, out_away_far, sums_far = refs[:3]
    weight, pix, grad_res, stats, out, sums, grad_act, in_sems, out_sems = refs[3:]
    cells, channels = pix.shape
    block_cells = out.shape[1]
    cols = (shifted.shape[0] - cells) // 2
    rows = cells // cols
    spot, _, _, height = own_place(vec)
    width = channels // GROUPS
    count = (height * (cols * width)).astype(jnp.float32)
    arriving = started(
        in_sems,
        (weight_far, weight),
        (stats_far, stats),
        (pix_far, pix),
        (grad_far, grad_res),
    )
    gain, bias = vec[0:1, :], vec[1:2, :]
    zero = jnp.zeros((8, channels), jnp.float32)
    arriving[0].wait()
    conv_shifted(shifted, weight, grad_act, 0.0, cols)
    finish_all(arriving[1:])
    mean, inverse = stats[0:1, :], stats[1:2, :]
    line = half_line(mean, inverse, gain, bias)
    begin = mean * inverse

    def normed(at):
        return pix[at, :].astype(jnp.float32) * inverse - begin

    def add(index, totals):
        at = row_at(index, cols)
        value = pix[at, :].astype(jnp.float32)
        unit = value * inverse - begin
        part = value * line[0] + line[1]
        sigmoid = 0.5 + 0.5 * jnp.tanh(part)
        slope = sigmoid + 2.0 * part * sigmoid * (1.0 - sigmoid)
        grad = grad_act[at, :] * valid_row(index, height) * slope
        grad_act[at, :] = grad
        return totals[0] + fold(grad), totals[1] + fold(grad * unit)

    plain, cross = lax.fori_loop(0, rows, add, (zero, zero), unroll=2)
    plain, cross = total_of(plain), total_of(cross)
    mean_plain = group_sums(plain * gain, width) / count
    mean_cross = group_sums(cross * gain, width) / count
    block_rows = block_cells // cols
    for part in range(2):
        first_row = (spot ^ (4 * part)) * block_rows
        for line in range(block_rows):
            at = row_at(first_row + line, cols)
            grad = (grad_act[at, :] * gain - mean_plain - normed(at) * mean_cross) * inverse
            grad = grad_res[at, :] + grad * valid_row(first_row + line, height)
            out[part, line * cols : (line + 1) * cols, :] = grad.astype(jnp.bfloat16)
    sums[...] = jnp.concatenate([cross, plain, jnp.zeros((6, channels), jnp.float32)], axis=0)
    finish_all(
        started(
            out_sems, (out.at[0], out_own_far), (out.at[1], out_away_far), (sums, sums_far)
        )
    )


def block_kernel(columns, vec, w_out, *refs):
    heads, residual_far = refs[:4], refs[4]
    out_own, out_away, residual, in_sems = refs[5:]
    block_cells, channels = out_own.shape
    spot, head, _, height = own_place(vec)
    cols = columns
    bases = [
        pl.multiple_of((spot ^ (4 * part)) * block_cells, block_cells) for part in range(2)
    ]
    pairs = [
        (residual_far.at[pl.ds(base, block_cells), :], residual.at[part])
        for part, base in enumerate(bases)
    ]
    finish_all(started(in_sems, *pairs))
    for part, out in enumerate((out_own, out_away)):
        total = residual[part] + vec[10:11, :]
        for step in range(4):
            width = w_out.shape[1]
            tile = heads[step][:, part * width : (part + 1) * width]
            total = total + dot(tile, w_out[head ^ step])
        cell = bases[part] + lax.broadcasted_iota(jnp.int32, (block_cells, channels), 0)
        out[...] = jnp.where(cell < height * cols, total, 0.0).astype(jnp.bfloat16)


def prepare_kernel(*refs):
    shifts, lines_far, kernels_far = refs[0], refs[1:15], refs[15:17]
    vec, w_heads, w_out, biases, qkv_t = refs[17:22]
    backs_far = refs[22:24]
    kernels, backs, qkv_weight, out_weight, heights, timesteps, qv_bias, *lines = refs[24:40]
    line_sems, in_sems, out_sems = refs[40:]
    channels = out_weight.shape[0]
    half = channels // HEADS
    small = started(
        line_sems,
        *zip(lines_far, (*lines, qv_bias, qkv_weight, out_weight, heights, timesteps)),
    )
    arriving = started(
        in_sems, *[(far, kernels.at[k]) for k, far in enumerate(kernels_far)]
    )
    finish_all(small)
    spot = lax.axis_index("row")
    image, head = spot // HEADS, spot % HEADS
    shift_row = shifts[pl.ds(image, 1), :]
    order = list(range(5)) + [None, None] + list(range(5, 9))
    for line, k in enumerate(order):
        if k is not None:
            vec[line : line + 1, :] = lines[k][...].astype(jnp.float32).reshape(1, channels)
    vec[5:6, :] = 1.0 + shift_row[:, :channels]
    vec[6:7, :] = shift_row[:, channels:]
    vec[11:12, :] = jnp.full((1, channels), heights[image].astype(jnp.float32))
    vec[12:13, :] = jnp.full((1, channels), timesteps[image].astype(jnp.float32))
    vec[13:16, :] = jnp.zeros((3, channels), jnp.float32)
    source = lax.broadcasted_iota(jnp.int32, (channels, 2 * half), 0)
    lane = lax.broadcasted_iota(jnp.int32, (channels, 2 * half), 1)
    first = jnp.where((lane < half) & (source == head * half + lane), 1.0, 0.0)
    second = jnp.where((lane >= half) & (source == head * half + lane - half), 1.0, 0.0)
    first, second = first.astype(jnp.bfloat16), second.astype(jnp.bfloat16)
    lanes = 2 * half
    for part, taken in enumerate((first, first, second)):
        whole = qkv_weight[:, part * channels : (part + 1) * channels]
        w_heads[:, part * lanes : (part + 1) * lanes] = dot(whole, taken).astype(jnp.bfloat16)
    turned = jnp.transpose(out_weight[...].astype(jnp.float32)).astype(jnp.bfloat16)
    w_out[...] = dot(turned, second).astype(jnp.bfloat16)
    both = qv_bias[...].astype(jnp.float32).reshape(1, 2 * channels)
    wide = jnp.broadcast_to(both, (16, 2 * channels)).astype(jnp.bfloat16)
    biases[:, 0:lanes] = dot(wide[:, :channels], first)[0:8]
    biases[:, lanes : 2 * lanes] = jnp.zeros((8, lanes), jnp.float32)
    biases[:, 2 * lanes : 3 * lanes] = dot(wide[:, channels:], second)[0:8]
    for block in range(0, 3 * HEADS, 2):
        whole = qkv_weight[:, block // 2 * lanes : (block // 2 + 1) * lanes].astype(jnp.float32)
        whole = jnp.transpose(whole).astype(jnp.bfloat16)
        qkv_t[block] = whole[0:half]
        qkv_t[block + 1] = whole[half:lanes]
    leaving = []
    for k in range(2):
        arriving[k].wait()

        def turn(tap, carry):
            tile = kernels[k, 2 - tap // 3, 2 - tap % 3].astype(jnp.float32)
            at = pl.ds(pl.multiple_of(tap % 3 * channels, channels), channels)
            backs[k, tap // 3, at, :] = jnp.transpose(tile).astype(jnp.bfloat16)
            return carry

        lax.fori_loop(0, 9, turn, 0)
        leaving += started(out_sems.at[k : k + 1], (backs.at[k], backs_far[k]))
    finish_all(leaving)


def final_kernel(*refs):
    parts, frequency = refs[:8], refs[8]
    one_far, two_far, qkv_far, out_far, time_far = refs[9:14]
    bias_out, time_bias, rows = refs[14], refs[15], refs[16:25]
    one, two, qkv_rows, qkv_out, out_out, time_out, small, norm_one, sems, out_sems = refs[25:]
    channels = one.shape[1]
    half = channels // HEADS
    unit = half // 4
    lines = 18 * unit + half + 16
    spot = lax.axis_index("row")
    head, column = spot % HEADS, lax.axis_index("img")
    leaving = []
    for index, part in enumerate(parts):
        away = column ^ (index // 2)
        for pair in range(2):
            quarter, base = head ^ (index % 2 + 2 * pair), pair * lines
            first = pl.multiple_of(quarter * half + away * unit, unit)
            at = pl.ds(first, unit)
            shape = (9, unit, channels)
            late = base + 9 * unit + half
            two[:, at, :] = part[base : base + 9 * unit].astype(jnp.float32).reshape(shape)
            one[:, at, :] = part[late : late + 9 * unit].astype(jnp.float32).reshape(shape)
            here = len(leaving)
            leaving += started(
                sems.at[here : here + 2],
                (two.at[:, at, :], two_far.at[:, at, :]),
                (one.at[:, at, :], one_far.at[:, at, :]),
            )
            middle = base + 9 * unit
            for k in range(3):
                to = pl.ds(pl.multiple_of(first + k * channels, unit), unit)
                piece = part[middle + k * unit : middle + (k + 1) * unit]
                qkv_rows[to, :] = piece.astype(jnp.float32)
            out_out[at, :] = part[middle + 3 * unit : middle + half].astype(jnp.float32)
            small[quarter, away] = part[base + lines - 16 : base + lines].astype(jnp.float32)
    for part in range(3):
        across = slice(part * channels, (part + 1) * channels)
        qkv_out[:, across] = jnp.transpose(qkv_rows[across, :])
    leaving += started(out_sems, (qkv_out, qkv_far), (out_out, out_far))
    sums = [small[quarter, 2] for quarter in range(HEADS)]
    pieces = [part[0:1, :half] for part in sums] + [part[0:1, 3 * half :] for part in sums]
    bias_out[...] = jnp.concatenate(pieces, axis=1).reshape(bias_out.shape)
    for step in range(4):
        norm_one[column ^ step] = parts[2 * step][2 * lines : 2 * lines + 16].astype(jnp.float32)
    total = norm_one[0] + norm_one[1] + norm_one[2] + norm_one[3]
    whole = jnp.concatenate([total[0:2], small[0, 0, 0:7, :]], axis=0)
    for k, row in enumerate(rows):
        row[...] = whole[k : k + 1].reshape(row.shape)
    shifts = small[0, 1]
    pair = jnp.concatenate([shifts[k : k + 1, :] for k in range(0, 16, 2)], axis=0)
    other = jnp.concatenate([shifts[k : k + 1, :] for k in range(1, 16, 2)], axis=0)
    both = jnp.concatenate([pair, other], axis=1)
    time_bias[...] = total_of(both).reshape(time_bias.shape)
    steps = sums[0][1:2, :] * 32.0 + sums[0][2:3, :]
    image = lax.broadcasted_iota(jnp.int32, (8, steps.shape[1]), 0)
    lane = lax.broadcasted_iota(jnp.int32, (8, steps.shape[1]), 1)
    now = jnp.sum(jnp.where(image == lane, steps, 0.0), axis=1, keepdims=True)
    angles = now * frequency[...]
    left = jnp.concatenate([jnp.cos(angles), jnp.sin(angles)], axis=1)
    left = left / (1.0 + jnp.exp(-left))
    terms = []
    for _ in range(3):
        terms.append(left.astype(jnp.bfloat16).astype(jnp.float32))
        left = left - terms[-1]
    terms = jnp.concatenate(terms + [jnp.zeros_like(left)], axis=0)
    both = jnp.concatenate([both] * 3 + [jnp.zeros_like(both)], axis=0).astype(jnp.bfloat16)
    time_out[...] = lax.dot_general(
        terms.astype(jnp.bfloat16), both, (((0,), (0,)), ((), ())),
        preferred_element_type=jnp.float32,
    )
    leaving += started(out_sems.at[2:3], (time_out, time_far))
    finish_all(leaving)


def swap(value, axis, step):
    count = lax.axis_size(axis)
    return lax.ppermute(value, axis, [(k, k ^ step) for k in range(count)])


def pick(stacked, index):
    return lax.dynamic_index_in_dim(stacked, index, 0, keepdims=False)


def add_up(*parts):
    total = parts[0].astype(jnp.float32)
    for part in parts[1:]:
        total = total + part.astype(jnp.float32)
    return total.astype(jnp.bfloat16)


def from_columns(pair):
    return [pair] + [swap(pair, "img", step) for step in (1, 2, 3)]


def with_mates(columns):
    return [part for mine in columns for part in (mine, swap(mine, "row", 1))]


def gather_columns(pair):
    return with_mates(from_columns(pair))


def call(kernel, near_outs, far_outs, scratch, limit, work, scalars, near, far, last_outs=()):
    close = pl.BlockSpec(memory_space=pltpu.VMEM)
    distant = pl.BlockSpec(memory_space=pltpu.HBM)
    operands = list(near) + [pltpu.with_memory_space_constraint(array, pltpu.HBM) for array in far]
    moved = sum(array.size * array.dtype.itemsize for array in operands)
    return pl.pallas_call(
        kernel,
        out_shape=[jax.ShapeDtypeStruct(*kind) for kind in near_outs]
        + [pltpu.HBM(*kind) for kind in far_outs]
        + [jax.ShapeDtypeStruct(*kind) for kind in last_outs],
        in_specs=[pl.BlockSpec(memory_space=pltpu.SMEM)] * len(scalars)
        + [close] * len(near)
        + [distant] * len(far),
        out_specs=[close] * len(near_outs)
        + [distant] * len(far_outs)
        + [close] * len(last_outs),
        scratch_shapes=[pltpu.VMEM(*kind) if isinstance(kind, tuple) else kind for kind in scratch],
        compiler_params=mib(limit),
        cost_estimate=pl.CostEstimate(flops=work, bytes_accessed=moved, transcendentals=0),
    )(*scalars, *operands)


def sems(count):
    return pltpu.SemaphoreType.DMA((count,))


def gather_field(mine, theirs):
    far, far_near = swap(theirs, "row", 4), swap(theirs, "row", 6)
    return [mine, swap(mine, "row", 1), swap(mine, "row", 2), None, far, None, far_near, None]


def relayed(blocks, after=None):
    sent = [blocks[2], blocks[4], blocks[6]]
    if after is not None:
        sent = lax.optimization_barrier((*sent, after))[:3]
    odd = [swap(block, "row", 1) for block in sent]
    return odd, [blocks[step] for step in ARRIVAL[3:]]


def local_image(
    pixels,
    heights,
    timesteps,
    norm1_gain,
    norm1_bias,
    conv1_weight,
    conv1_bias,
    time_weight,
    time_bias,
    norm2_gain,
    norm2_bias,
    conv2_weight,
    conv2_bias,
    norm3_gain,
    norm3_bias,
    qkv_weight,
    qv_bias,
    out_weight,
    out_bias,
    grad_out,
):
    images, row_count, cols, channels = pixels.shape
    block_cells = row_count * cols
    cells = block_cells * lax.axis_size("row")
    half = channels // HEADS
    column = lax.axis_index("img")
    image = lax.axis_index("row") // HEADS
    low, full = jnp.bfloat16, jnp.float32
    pixel_blocks = pixels.reshape(images, block_cells, channels)
    grad_blocks = grad_out.reshape(images, block_cells, channels)
    field = gather_field(pick(pixel_blocks, image), pick(pixel_blocks, 1 - image))
    later = (pick(grad_blocks, image), pick(grad_blocks, 1 - image), field[4], field[6])
    later = lax.optimization_barrier(later)
    grads = gather_field(later[0], later[1])
    field[4], field[6] = later[2], later[3]
    time_act = jax.nn.silu(embed_steps(timesteps, time_weight.shape[0]))
    shifts = jnp.dot(time_act, time_weight.astype(full), precision=PRECISE) + time_bias.astype(full)
    kernel_shape = (3, 3 * channels, channels)
    lanes = 2 * half
    vec, w_heads, w_out, biases, qkv_t, w_one_back, w_two_back = call(
        prepare_kernel,
        [
            ((16, channels), full), ((channels, 3 * lanes), low), ((channels, lanes), low),
            ((8, 3 * lanes), full), ((3 * HEADS, half, channels), low),
        ],
        [(kernel_shape, low), (kernel_shape, low)],
        [
            ((2, 3, 3, channels, channels), low), ((2,) + kernel_shape, low),
            ((channels, 3 * channels), low), ((channels, channels), low),
            pltpu.SMEM((images,), jnp.int32), pltpu.SMEM((images,), jnp.int32),
            ((2 * channels,), low), *[((channels,), low)] * 9,
            sems(14), sems(2), sems(2),
        ],
        16,
        channels,
        [],
        [shifts],
        [
            norm1_gain, norm1_bias, conv1_bias, norm2_gain, norm2_bias, conv2_bias, norm3_gain,
            norm3_bias, out_bias, qv_bias, qkv_weight, out_weight, heights, timesteps,
            conv1_weight,
            conv2_weight,
        ],
    )
    field_late, field = relayed(field, vec)
    w_one, w_two = conv1_weight.reshape(kernel_shape), conv2_weight.reshape(kernel_shape)
    rim_cells = cells + 2 * cols
    cost = 9 * cells * channels * channels // 2

    wide, tall = (cells, channels), (rim_cells, 3 * channels)
    rows_eight = ((8, channels), full)
    act_three, pix, conv_one, residual, act_one, act_two, stats = call(
        forward_kernel,
        [(wide, low)],
        [(wide, low), (wide, full), (wide, full), (wide, low), (wide, low), rows_eight],
        [
            (wide, low), (wide, full), (wide, full), rows_eight, (kernel_shape, low),
            (kernel_shape, low), (tall, low), (tall, low), sems(10), sems(6),
        ],
        28,
        cost * 25,
        [],
        [vec, *field_late],
        [*field, w_one, w_two],
    )
    grads_late, grads = relayed(grads, act_three)
    query_shape, head_shape = (cells // 2, lanes), (cells, lanes)
    value_key, query_part, grad_proj, mixed, out_sums = call(
        functools.partial(attention_kernel, cols),
        [],
        [(head_shape, low), (query_shape, low), (wide, low), (head_shape, low), rows_eight],
        [
            (wide, low), (wide, low), (head_shape, low), (query_shape, low), rows_eight,
            (head_shape, low), (head_shape, low), (head_shape, low), ((lanes, cells), full),
            (head_shape, low), ((1, cells), full), sems(8), sems(5),
        ],
        36,
        cost * 34,
        [],
        [vec, act_three, w_heads, w_out, biases, *grads_late],
        grads,
    )

    key_near, query_near = swap(value_key, "row", 2), swap(query_part, "row", 2)
    key_mate, query_mate = swap(value_key, "row", 1), swap(query_part, "row", 1)
    own_shape = (3, 3 * half, cells)
    send_shape = ((block_cells, lanes), low)
    own_one, own_two, weight_rows, *sends = call(
        aside_kernel,
        [],
        [(own_shape, low), (own_shape, low), ((4, half + 16, channels), low)],
        [
            ((2,) + wide, low), (head_shape, low), (head_shape, low), (wide, low), (wide, low),
            ((rim_cells, 3 * half), full), ((2,) + own_shape, low), ((4, half + 16, channels), low),
            sems(6), sems(3),
        ],
        28,
        cost * 27,
        [],
        [vec],
        [act_one, act_two, mixed, value_key, act_three, grad_proj],
        [send_shape] * 4,
    )
    key_near, query_near, key_mate, query_mate, own_two = lax.optimization_barrier(
        (key_near, query_near, key_mate, query_mate, own_two)
    )
    relays = [key_mate, query_mate, swap(key_near, "row", 1), swap(query_near, "row", 1)]
    packed = [value_key, query_part, key_near, query_near]
    lines = 18 * (half // 4) + half + 16
    shifted_one, grad_res, *payload = call(
        middle_kernel,
        [(tall, low)],
        [(wide, full)] + [((lines, channels), low)] * 4,
        [
            ((HEADS,) + head_shape, low), ((HEADS,) + query_shape, low),
            (wide, low), (wide, full), rows_eight, (own_shape, low), (wide, full),
            ((4, lines, channels), low), (wide, full), (tall, low), (kernel_shape, low),
            (wide, full), (own_shape, low), rows_eight, sems(18), sems(5),
        ],
        40,
        cost * 26,
        [],
        [vec, qkv_t, *relays],
        [
            *packed, grad_proj, residual, stats, own_two, weight_rows, w_two_back, conv_one,
            own_one, out_sums,
        ],
    )
    *sends, shifted_one = lax.optimization_barrier((*sends, shifted_one))
    total = add_up(payload[0], *[swap(payload[step], "img", step) for step in (1, 2, 3)])
    heads_got = [sends[0]] + [swap(sends[step], "row", step) for step in (1, 2, 3)]
    shifted_one, total, *heads_got = lax.optimization_barrier((shifted_one, total, *heads_got))
    both = add_up(total, swap(total, "row", 4))
    grad_own, grad_away, sums_one = call(
        first_kernel,
        [],
        [((block_cells, channels), low), ((block_cells, channels), low), rows_eight],
        [
            (kernel_shape, low), (wide, low), (wide, full), rows_eight,
            ((2, block_cells, channels), low), rows_eight, (wide, full), sems(4), sems(3),
        ],
        20,
        cost * 12,
        [],
        [vec, shifted_one],
        [w_one_back, pix, grad_res, stats],
    )
    block_own, block_away = call(
        functools.partial(block_kernel, cols),
        [((block_cells, channels), low), ((block_cells, channels), low)],
        [],
        [((2, block_cells, channels), full), sems(2)],
        8,
        cost,
        [],
        [vec, out_weight.reshape(HEADS, half, channels), *heads_got],
        [residual],
    )
    out_pair = jnp.stack([block_own, grad_own])
    away_pair = swap(jnp.stack([block_away, grad_away]), "row", 4)
    first_pair = jnp.where(image == 0, out_pair, away_pair)
    second_pair = jnp.where(image == 0, away_pair, out_pair)
    finished = jnp.stack([first_pair, second_pair], axis=1).reshape((2,) + pixels.shape)
    norm_one = jnp.concatenate([sums_one, jnp.zeros_like(sums_one)], axis=0).astype(low)
    norm_one = add_up(norm_one, swap(norm_one, "row", 4))
    other = swap(both, "row", 2)
    pair = jnp.concatenate([both, other, norm_one], axis=0)
    parts = gather_columns(pair)
    line = ((channels,), full)
    kernel_out = ((9, channels, channels), full)
    time_out = ((time_weight.shape[0], 2 * channels), full)
    qkv_out, out_out = ((channels, 3 * channels), full), ((channels, channels), full)
    half_time = time_weight.shape[0] // 2
    frequency = jnp.exp(-math.log(10000.0) * jnp.arange(half_time, dtype=full) / half_time)
    (
        conv1_weight_grad, conv2_weight_grad, qkv_weight_grad, out_weight_grad, time_weight_grad,
        qv_bias_grad, time_bias_grad, *lines,
    ) = call(
        final_kernel,
        [],
        [kernel_out, kernel_out, qkv_out, out_out, time_out],
        [
            kernel_out, kernel_out, ((3 * channels, channels), full), qkv_out, out_out, time_out,
            ((HEADS, 4, 16, channels), full), ((4, 16, channels), full), sems(32), sems(3),
        ],
        28,
        cost,
        [],
        [*parts, frequency[None, :]],
        [],
        [((2 * channels,), full)] * 2 + [line] * 9,
    )
    norm1_gain_grad, norm1_bias_grad, norm3_gain_grad, norm3_bias_grad, conv2_bias_grad = lines[:5]
    out_bias_grad, norm2_gain_grad, norm2_bias_grad, conv1_bias_grad = lines[5:]
    return (
        finished[0],
        finished[1],
        norm1_gain_grad,
        norm1_bias_grad,
        conv1_weight_grad.reshape(conv1_weight.shape),
        conv1_bias_grad,
        time_weight_grad,
        time_bias_grad,
        norm2_gain_grad,
        norm2_bias_grad,
        conv2_weight_grad.reshape(conv2_weight.shape),
        conv2_bias_grad,
        norm3_gain_grad,
        norm3_bias_grad,
        qkv_weight_grad,
        qv_bias_grad,
        out_weight_grad,
        out_bias_grad,
    )


def local(*arrays):
    pixels = arrays[0]
    if lax.axis_size("row") == pixels.shape[0] * HEADS and lax.axis_size("img") == 4:
        return local_image(*arrays)
    return local_rows(*arrays)


def solution(mesh):
    placed = (
        P("img", "row", None, None),
        P("img"),
        P("img"),
        P(),
        P(),
        P(),
        P(),
        P(),
        P(),
        P(),
        P(),
        P(),
        P(),
        P(),
        P(),
        P(),
        P(),
        P(),
        P(),
        P("img", "row", None, None),
    )
    return jax.shard_map(
        local,
        mesh=mesh,
        in_specs=placed,
        out_specs=(
            P("img", "row", None, None),
            P("img", "row", None, None),
            P(),
            P(),
            P(),
            P(),
            P(),
            P(),
            P(),
            P(),
            P(),
            P(),
            P(),
            P(),
            P(),
            P(),
            P(),
            P(),
        ),
        check_vma=False,
    )
```

```python
import functools
import math

import jax
import jax.numpy as jnp
from jax import lax
from jax.experimental import pallas as pl
from jax.experimental.pallas import tpu as pltpu
from jax.sharding import PartitionSpec as P

GROUPS = 32
HEADS = 4


EPSILON = 1e-05
MASKED = -1000000000.0
PRECISE = lax.Precision.HIGHEST


def with_halo(cells, sides, width):
    for axis, dim in sides:
        count = lax.axis_size(axis)
        ends = count - 1
        head = lax.slice_in_dim(cells, 0, width, axis=dim)
        tail = lax.slice_in_dim(cells, cells.shape[dim] - width, cells.shape[dim], axis=dim)
        cells = jnp.concatenate(
            [
                lax.ppermute(tail, axis, [(i, (i + 1) % count) for i in range(ends)]),
                cells,
                lax.ppermute(head, axis, [((i + 1) % count, i) for i in range(ends)]),
            ],
            axis=dim,
        )
    return cells


def embed_steps(timesteps, time_width):
    half_dim = time_width // 2
    frequency = jnp.exp(-math.log(10000.0) * jnp.arange(half_dim, dtype=jnp.float32) / half_dim)
    angles = timesteps.astype(jnp.float32)[:, None] * frequency[None, :]
    return jnp.concatenate([jnp.cos(angles), jnp.sin(angles)], axis=1)


def silu_slope(pre_act):
    sigmoid = jax.nn.sigmoid(pre_act)
    return sigmoid * (1.0 + pre_act * (1.0 - sigmoid))


def with_rims(field_in):
    return with_halo(field_in, (("row", 1),), 1)


def conv_rows(padded, kernel):
    return lax.conv_general_dilated(
        padded,
        kernel,
        (1, 1),
        ((0, 0), (1, 1)),
        dimension_numbers=("NHWC", "HWIO", "NHWC"),
        preferred_element_type=jnp.float32,
    )


def flipped(kernel):
    return jnp.transpose(kernel[::-1, ::-1], (0, 1, 3, 2))


def kernel_grad(padded, grad_field):
    row_count = grad_field.shape[1]
    col_count = grad_field.shape[2]
    widened = jnp.pad(padded, ((0, 0), (0, 0), (1, 1), (0, 0)))
    tap_rows = []
    for tap_row in range(3):
        tap_line = []
        for tap_col in range(3):
            window = widened[:, tap_row : tap_row + row_count, tap_col : tap_col + col_count, :]
            tap_line.append(
                jnp.einsum("brwc,brwd->cd", window, grad_field, preferred_element_type=jnp.float32)
            )
        tap_rows.append(jnp.stack(tap_line))
    return jnp.stack(tap_rows)


def norm_forward(field_in, cell_mask, cell_count, group_count):
    shaped = field_in.reshape(field_in.shape[:3] + (group_count, field_in.shape[3] // group_count))
    first_sum = lax.psum(jnp.sum(shaped * cell_mask, axis=(1, 2, 4)), "row")
    center = first_sum / cell_count[:, None]
    centred = shaped - center[:, None, None, :, None]
    spread_sum = lax.psum(jnp.sum(jnp.square(centred * cell_mask), axis=(1, 2, 4)), "row")
    spread = spread_sum / cell_count[:, None]
    inverse = lax.rsqrt(spread + EPSILON)
    return (centred * inverse[:, None, None, :, None], inverse)


def norm_backward(grad_normed, normalized, inverse, gain_in, cell_mask, cell_count):
    full_shape = grad_normed.shape
    flat_norm = normalized.reshape(full_shape)
    gain_grad = jnp.sum(grad_normed * flat_norm, axis=(0, 1, 2))
    shift_grad = jnp.sum(grad_normed, axis=(0, 1, 2))
    scaled = (grad_normed * gain_in).reshape(normalized.shape)
    sum_plain, sum_cross = lax.psum(
        (
            jnp.sum(scaled * cell_mask, axis=(1, 2, 4)),
            jnp.sum(scaled * normalized * cell_mask, axis=(1, 2, 4)),
        ),
        "row",
    )
    mean_plain = sum_plain / cell_count[:, None]
    mean_cross = sum_cross / cell_count[:, None]
    grad_in = (
        (
            scaled
            - mean_plain[:, None, None, :, None]
            - normalized * mean_cross[:, None, None, :, None]
        )
        * inverse[:, None, None, :, None]
        * cell_mask
    )
    return (grad_in.reshape(full_shape), gain_grad, shift_grad)


def local_rows(
    pixels,
    heights,
    timesteps,
    norm1_gain,
    norm1_bias,
    conv1_weight,
    conv1_bias,
    time_weight,
    time_bias,
    norm2_gain,
    norm2_bias,
    conv2_weight,
    conv2_bias,
    norm3_gain,
    norm3_bias,
    qkv_weight,
    qv_bias,
    out_weight,
    out_bias,
    grad_out,
):
    image_count, row_count, col_count, channels = pixels.shape
    group_count = GROUPS
    head_count = HEADS
    head_width = channels // head_count
    query_count = row_count * col_count
    scaling = head_width ** (-0.5)
    head_shape = (image_count, query_count, head_count, head_width)
    row_ids = lax.axis_index("row") * row_count + jnp.arange(row_count, dtype=jnp.int32)
    row_valid = row_ids[None, :] < heights[:, None]
    row_mask = row_valid.astype(jnp.float32)
    cell_rows = row_mask[:, :, None, None]
    cell_mask = row_mask[:, :, None, None, None]
    own_valid = jnp.repeat(row_valid, col_count, axis=1)[:, None, None, :]
    cell_count = heights.astype(jnp.float32) * (col_count * (channels // group_count))
    gain_one = norm1_gain.astype(jnp.float32)
    gain_two = norm2_gain.astype(jnp.float32)
    gain_three = norm3_gain.astype(jnp.float32)
    field_in = pixels.astype(jnp.float32)
    normed_one, inverse_one = norm_forward(field_in, cell_mask, cell_count, group_count)
    pre_one = normed_one.reshape(field_in.shape) * gain_one + norm1_bias.astype(jnp.float32)
    act_one = (jax.nn.silu(pre_one) * cell_rows).astype(jnp.bfloat16)
    padded_one = with_rims(act_one)
    conv_one = conv_rows(padded_one, conv1_weight) + conv1_bias.astype(jnp.float32)
    time_act = jax.nn.silu(embed_steps(timesteps, time_weight.shape[0]))
    shifts = jnp.dot(
        time_act, time_weight.astype(jnp.float32), precision=PRECISE
    ) + time_bias.astype(jnp.float32)
    scale_part = 1.0 + shifts[:, None, None, :channels]
    shift_part = shifts[:, None, None, channels:]
    normed_two, inverse_two = norm_forward(conv_one, cell_mask, cell_count, group_count)
    affine_two = normed_two.reshape(field_in.shape) * gain_two + norm2_bias.astype(jnp.float32)
    pre_two = affine_two * scale_part + shift_part
    act_two = (jax.nn.silu(pre_two) * cell_rows).astype(jnp.bfloat16)
    padded_two = with_rims(act_two)
    residual = field_in + (conv_rows(padded_two, conv2_weight) + conv2_bias.astype(jnp.float32))
    normed_three, inverse_three = norm_forward(residual, cell_mask, cell_count, group_count)
    act_three = (
        normed_three.reshape(field_in.shape) * gain_three + norm3_bias.astype(jnp.float32)
    ).astype(jnp.bfloat16)
    projected = jnp.einsum(
        "brwc,cd->brwd", act_three, qkv_weight, preferred_element_type=jnp.float32
    )
    qv_float = qv_bias.astype(jnp.float32)
    queries = (projected[..., :channels] + qv_float[:channels]).astype(jnp.bfloat16)
    keys_own = projected[..., channels : 2 * channels].astype(jnp.bfloat16)
    values_own = (projected[..., 2 * channels :] + qv_float[channels:]).astype(jnp.bfloat16)
    query_heads = queries.reshape(head_shape)
    key_heads = keys_own.reshape(head_shape)
    value_heads = values_own.reshape(head_shape)

    def flatten_rows(piece_arr):
        return piece_arr.reshape(
            image_count, piece_arr.shape[1] * col_count, head_count, head_width
        )

    def key_mask(span_rows):
        key_rows = jnp.arange(span_rows, dtype=jnp.int32)
        return jnp.repeat(key_rows[None, :] < heights[:, None], col_count, axis=1)[:, None, None, :]

    top_init = jnp.full((image_count, query_count, head_count), MASKED, jnp.float32)
    piece_keys = lax.all_gather(keys_own, "row", axis=1, tiled=True)
    piece_values = lax.all_gather(values_own, "row", axis=1, tiled=True)
    key_valid = key_mask(piece_keys.shape[1])
    scores = (
        jnp.einsum(
            "bqhd,bkhd->bqhk",
            query_heads,
            flatten_rows(piece_keys),
            preferred_element_type=jnp.float32,
        )
        * scaling
    )
    scores = jnp.where(key_valid, scores, MASKED)
    new_top = jnp.maximum(top_init, jnp.max(scores, axis=3))
    weights = jnp.where(key_valid, jnp.exp(scores - new_top[..., None]), 0.0)
    running_total = jnp.sum(weights, axis=3)
    running_acc = jnp.einsum(
        "bqhk,bkhd->bqhd",
        weights.astype(jnp.bfloat16),
        flatten_rows(piece_values),
        preferred_element_type=jnp.float32,
    )
    attn_float = running_acc / running_total[..., None]
    log_total = new_top + jnp.log(running_total)
    attended = attn_float.reshape(pixels.shape).astype(jnp.bfloat16)
    output_proj = jnp.einsum(
        "brwc,cd->brwd", attended, out_weight, preferred_element_type=jnp.float32
    ) + out_bias.astype(jnp.float32)
    block_out = ((residual + output_proj) * cell_rows).astype(jnp.bfloat16)
    grad_proj = grad_out.astype(jnp.float32) * cell_rows
    grad_proj_low = grad_proj.astype(jnp.bfloat16)
    out_weight_grad = jnp.einsum(
        "brwc,brwd->cd", attended, grad_proj_low, preferred_element_type=jnp.float32
    )
    out_bias_grad = jnp.sum(grad_proj, axis=(0, 1, 2))
    grad_attended = jnp.einsum(
        "brwd,cd->brwc", grad_proj_low, out_weight, preferred_element_type=jnp.float32
    ).astype(jnp.bfloat16)
    grad_heads = grad_attended.reshape(head_shape)
    delta_own = jnp.sum(grad_heads.astype(jnp.float32) * attn_float, axis=3)
    stat_shape = (image_count, row_count, col_count, head_count)
    all_lse, all_delta = (
        lax.all_gather(log_total.reshape(stat_shape), "row", axis=1, tiled=True),
        lax.all_gather(delta_own.reshape(stat_shape), "row", axis=1, tiled=True),
    )
    piece_keys = lax.all_gather(keys_own, "row", axis=1, tiled=True)
    piece_values = lax.all_gather(values_own, "row", axis=1, tiled=True)
    flat_keys = flatten_rows(piece_keys)
    key_valid = key_mask(piece_keys.shape[1])
    scores = (
        jnp.einsum("bqhd,bkhd->bqhk", query_heads, flat_keys, preferred_element_type=jnp.float32)
        * scaling
    )
    soft_weights = jnp.where(key_valid, jnp.exp(scores - log_total[..., None]), 0.0)
    grad_probs = jnp.einsum(
        "bqhd,bkhd->bqhk",
        grad_heads,
        flatten_rows(piece_values),
        preferred_element_type=jnp.float32,
    )
    grad_scores = (soft_weights * (grad_probs - delta_own[..., None])).astype(jnp.bfloat16)
    grad_query_sum = jnp.einsum(
        "bqhk,bkhd->bqhd", grad_scores, flat_keys, preferred_element_type=jnp.float32
    )
    piece_queries = lax.all_gather(queries, "row", axis=1, tiled=True)
    piece_grads = lax.all_gather(grad_attended, "row", axis=1, tiled=True)
    flat_queries = flatten_rows(piece_queries)
    flat_grads = flatten_rows(piece_grads)
    span_rows = piece_queries.shape[1]
    piece_lse = all_lse.reshape(image_count, span_rows * col_count, head_count)
    piece_delta = all_delta.reshape(image_count, span_rows * col_count, head_count)
    scores = (
        jnp.einsum("bqhd,bkhd->bqhk", flat_queries, key_heads, preferred_element_type=jnp.float32)
        * scaling
    )
    soft_weights = jnp.where(own_valid, jnp.exp(scores - piece_lse[..., None]), 0.0)
    value_term = jnp.einsum(
        "bqhk,bqhd->bkhd",
        soft_weights.astype(jnp.bfloat16),
        flat_grads,
        preferred_element_type=jnp.float32,
    )
    grad_probs = jnp.einsum(
        "bqhd,bkhd->bqhk", flat_grads, value_heads, preferred_element_type=jnp.float32
    )
    grad_scores = (soft_weights * (grad_probs - piece_delta[..., None])).astype(jnp.bfloat16)
    key_term = jnp.einsum(
        "bqhk,bqhd->bkhd", grad_scores, flat_queries, preferred_element_type=jnp.float32
    )
    key_term, value_term = (key_term, value_term)
    grad_queries = (grad_query_sum * scaling).reshape(pixels.shape).astype(jnp.bfloat16)
    grad_keys = (key_term * scaling).reshape(pixels.shape).astype(jnp.bfloat16)
    grad_values = value_term.reshape(pixels.shape).astype(jnp.bfloat16)
    grad_projected = jnp.concatenate([grad_queries, grad_keys, grad_values], axis=3)
    qkv_weight_grad = jnp.einsum(
        "brwc,brwd->cd", act_three, grad_projected, preferred_element_type=jnp.float32
    )
    qv_bias_grad = jnp.concatenate(
        [
            jnp.sum(grad_queries.astype(jnp.float32), axis=(0, 1, 2)),
            jnp.sum(grad_values.astype(jnp.float32), axis=(0, 1, 2)),
        ]
    )
    grad_act_three = jnp.einsum(
        "brwd,cd->brwc", grad_projected, qkv_weight, preferred_element_type=jnp.float32
    )
    grad_res_attn, norm3_gain_grad, norm3_bias_grad = norm_backward(
        grad_act_three, normed_three, inverse_three, gain_three, cell_mask, cell_count
    )
    grad_residual = grad_proj + grad_res_attn
    grad_conv_two = grad_residual.astype(jnp.bfloat16)
    conv2_bias_grad = jnp.sum(grad_residual, axis=(0, 1, 2))
    conv2_weight_grad = kernel_grad(padded_two, grad_conv_two)
    grad_act_two = conv_rows(with_rims(grad_conv_two), flipped(conv2_weight)) * cell_rows
    grad_pre_two = grad_act_two * silu_slope(pre_two)
    scale_grad = jnp.sum(grad_pre_two * affine_two, axis=(1, 2))
    shift_grad = jnp.sum(grad_pre_two, axis=(1, 2))
    shift_grads = jnp.concatenate([scale_grad, shift_grad], axis=1)
    grad_conv_one, norm2_gain_grad, norm2_bias_grad = norm_backward(
        grad_pre_two * scale_part, normed_two, inverse_two, gain_two, cell_mask, cell_count
    )
    conv_one_low = grad_conv_one.astype(jnp.bfloat16)
    conv1_bias_grad = jnp.sum(grad_conv_one, axis=(0, 1, 2))
    conv1_weight_grad = kernel_grad(padded_one, conv_one_low)
    grad_act_one = conv_rows(with_rims(conv_one_low), flipped(conv1_weight)) * cell_rows
    grad_pre_one = grad_act_one * silu_slope(pre_one)
    grad_field_norm, norm1_gain_grad, norm1_bias_grad = norm_backward(
        grad_pre_one, normed_one, inverse_one, gain_one, cell_mask, cell_count
    )
    grad_pixels = (grad_residual + grad_field_norm).astype(jnp.bfloat16)
    time_weight_grad = jnp.dot(time_act.T, shift_grads, precision=PRECISE)
    time_bias_grad = jnp.sum(shift_grads, axis=0)
    summed = lax.psum(
        (
            norm1_gain_grad,
            norm1_bias_grad,
            conv1_weight_grad,
            conv1_bias_grad,
            time_weight_grad,
            time_bias_grad,
            norm2_gain_grad,
            norm2_bias_grad,
            conv2_weight_grad,
            conv2_bias_grad,
            norm3_gain_grad,
            norm3_bias_grad,
            qkv_weight_grad,
            qv_bias_grad,
            out_weight_grad,
            out_bias_grad,
        ),
        ("img", "row"),
    )
    return (
        block_out,
        grad_pixels,
        summed[0],
        summed[1],
        summed[2],
        summed[3],
        summed[4],
        summed[5],
        summed[6],
        summed[7],
        summed[8],
        summed[9],
        summed[10],
        summed[11],
        summed[12],
        summed[13],
        summed[14],
        summed[15],
    )


ARRIVAL = (3, 5, 7, 0, 1, 2, 4, 6)


def mib(count):
    return pltpu.CompilerParams(vmem_limit_bytes=count * 2**20)


def dot(left, right):
    return jnp.dot(left, right, preferred_element_type=jnp.float32)


def dot_rows(left, right):
    return lax.dot_general(
        left, right, (((1,), (1,)), ((), ())), preferred_element_type=jnp.float32
    )


def fold(tile):
    return jnp.sum(tile.reshape(-1, 8, tile.shape[1]), axis=0)


def group_sums(row, width):
    channels = row.shape[1]
    rows = lax.broadcasted_iota(jnp.int32, (channels, channels), 0) // width
    cols = lax.broadcasted_iota(jnp.int32, (channels, channels), 1) // width
    same = jnp.where(rows == cols, 1.0, 0.0).astype(jnp.bfloat16)
    wide = jnp.broadcast_to(row, (16, channels))
    total = None
    for _ in range(3):
        term = wide.astype(jnp.bfloat16)
        wide = wide - term.astype(jnp.float32)
        part = dot(term, same)
        total = part if total is None else total + part
    return total[0:1]


def row_at(index, cols):
    return pl.ds(pl.multiple_of(index * cols, cols), cols)


def total_of(tile):
    return jnp.sum(tile, axis=0, keepdims=True)


def cell_sums(tiles, about, height):
    first, square = 0.0, 0.0
    for index, tile in tiles:
        off = (tile - about) * valid_row(index, height)
        first, square = first + fold(off), square + fold(off * off)
    return first, square


def stats_of(first, square, about, height, cols):
    width = about.shape[1] // GROUPS
    each = (height * cols).astype(jnp.float32)
    first, square = total_of(first), total_of(square)
    mean = group_sums(first + about * each, width) / (each * width)
    shift = about - mean
    spread = group_sums(square + 2.0 * first * shift + each * shift * shift, width)
    return mean, lax.rsqrt(spread / (each * width) + EPSILON)


def row_mean(tile):
    return jnp.sum(tile, axis=0, keepdims=True) * (1.0 / tile.shape[0])


def in_turn(count, before, main, after):
    for step in range(count + 2):
        if step < count:
            before(step)
        if 0 <= step - 1 < count:
            main(step - 1)
        if 0 <= step - 2:
            after(step - 2)


def conv_block(shifted, weight, block, size, cols):
    base = block * size
    total = dot(shifted[base : base + size, :], weight[0])
    for tap in (1, 2):
        at = base + tap * cols
        total = total + dot(shifted[at : at + size, :], weight[tap])
    return total


def half_line(mean, inverse, gain, bias, scale=1.0, shift=0.0):
    slope = inverse * gain
    start = bias - mean * slope
    return 0.5 * slope * scale, 0.5 * (start * scale + shift)


def put_shifted(ref, index, tile, cols):
    channels = tile.shape[1]
    column = lax.broadcasted_iota(jnp.int32, tile.shape, 0)
    before = jnp.where(column == 0, 0.0, pltpu.roll(tile, 1, 0))
    after = jnp.where(column == cols - 1, 0.0, pltpu.roll(tile, cols - 1, 0))
    at = row_at(index + 1, cols)
    ref[at, 0:channels] = before.astype(jnp.bfloat16)
    ref[at, channels : 2 * channels] = tile.astype(jnp.bfloat16)
    ref[at, 2 * channels : 3 * channels] = after.astype(jnp.bfloat16)


def clear_rims(ref, cols):
    edge = jnp.zeros((cols, ref.shape[1]), ref.dtype)
    ref[0:cols, :] = edge
    ref[ref.shape[0] - cols : ref.shape[0], :] = edge


def conv_shifted(shifted, weight, out, bias, cols, added=None):
    step = 8 * cols

    def block(index, carry):
        base = index * step
        total = bias
        for tap in range(3):
            at = pl.ds(pl.multiple_of(base + tap * cols, cols), step)
            total = total + dot(shifted[at, :], weight[tap])
        if added is not None:
            total = total + added[pl.ds(pl.multiple_of(base, step), step), :].astype(jnp.float32)
        out[pl.ds(pl.multiple_of(base, step), step), :] = total
        return carry

    lax.fori_loop(0, out.shape[0] // step, block, 0, unroll=True)


def put_quarter(parts, payload, start):
    half = parts[0].shape[0] // 3
    unit = half // 4
    for line, part in enumerate(parts):
        part = part.astype(jnp.bfloat16)
        for shift in range(3):
            at = start + (3 * line + shift) * unit
            for chunk in range(4):
                base = shift * half + chunk * unit
                payload[chunk, at : at + unit, :] = part[base : base + unit]


def own_place(vec):
    spot = lax.axis_index("row")
    image, head = spot // HEADS, spot % HEADS
    return spot, head, image, jnp.max(vec[11:12, :]).astype(jnp.int32)


def started(sems, *pairs):
    copies = [pltpu.make_async_copy(src, dst, sems.at[k]) for k, (src, dst) in enumerate(pairs)]
    for copy in copies:
        copy.start()
    return copies


def finish_all(copies):
    for copy in copies:
        copy.wait()


def valid_row(index, height):
    return jnp.where(index < height, 1.0, 0.0).astype(jnp.float32)


def forward_kernel(vec, *refs):
    blocks, (w_one_far, w_two_far) = refs[:8], refs[8:10]
    act_three, pix_far, conv_far, residual_far, act_one_far, act_two_far, stats_far = refs[10:17]
    pix, conv_one, residual, stats, w_one, w_two, shift_one, shift_two, in_sems, out_sems = refs[17:]
    cells, channels = pix.shape
    block_cells = blocks[0].shape[0]
    cols = (shift_one.shape[0] - cells) // 2
    rows = cells // cols
    spot, _, _, height = own_place(vec)
    pairs = []
    for step, block in zip(ARRIVAL, blocks):
        base = pl.multiple_of((spot ^ step) * block_cells, block_cells)
        pairs.append((block, pix.at[pl.ds(base, block_cells), :]))
    arriving = started(in_sems, *pairs, (w_one_far, w_one), (w_two_far, w_two))
    gain_one, bias_one, conv_bias_one, gain_two, bias_two = (vec[k : k + 1, :] for k in range(5))
    scale, shift, conv_bias_two, gain_three, bias_three = (vec[k : k + 1, :] for k in range(5, 10))
    inner = (pl.ds(cols, cells), pl.ds(channels, channels))

    group = 2
    size = group * cols
    count = rows // group
    zero = jnp.zeros((8, channels), jnp.float32)

    def tile_of(ref, index):
        return ref[index * cols : (index + 1) * cols, :].astype(jnp.float32)

    def tiles_of(ref, block):
        return [(k, tile_of(ref, k)) for k in range(block * group, (block + 1) * group)]

    def stage(source, line, shifted, weight, out, bias, added=None):
        sums = [zero, zero, None]

        def activate(block):
            for index, tile in tiles_of(source, block):
                part = tile * line[0] + line[1]
                part = (part + part * jnp.tanh(part)) * valid_row(index, height)
                put_shifted(shifted, index, part, cols)

        def conv(block):
            total = conv_block(shifted, weight, block, size, cols) + bias
            if added is not None:
                total = total + added[block * size : (block + 1) * size, :].astype(jnp.float32)
            out[block * size : (block + 1) * size, :] = total

        def measure(block):
            if block == 0:
                sums[2] = row_mean(tile_of(out, 0))
            first, square = cell_sums(tiles_of(out, block), sums[2], height)
            sums[0], sums[1] = sums[0] + first, sums[1] + square

        in_turn(count, activate, conv, measure)
        return stats_of(*sums, height, cols)

    clear_rims(shift_one, cols)
    clear_rims(shift_two, cols)
    finish_all(arriving[:8])
    leaving = started(out_sems, (pix, pix_far))
    about = row_mean(tile_of(pix, 0))
    first, square = zero, zero
    for block in range(count):
        more = cell_sums(tiles_of(pix, block), about, height)
        first, square = first + more[0], square + more[1]
    mean_one, inv_one = stats_of(first, square, about, height, cols)
    arriving[8].wait()
    line = half_line(mean_one, inv_one, gain_one, bias_one)
    mean_two, inv_two = stage(pix, line, shift_one, w_one, conv_one, conv_bias_one)
    leaving += started(
        out_sems.at[1:3], (shift_one.at[inner], act_one_far), (conv_one, conv_far)
    )
    arriving[9].wait()
    line = half_line(mean_two, inv_two, gain_two, bias_two, scale, shift)
    mean_three, inv_three = stage(conv_one, line, shift_two, w_two, residual, conv_bias_two, pix)
    leaving += started(
        out_sems.at[3:5], (shift_two.at[inner], act_two_far), (residual, residual_far)
    )
    stats[...] = jnp.concatenate(
        [mean_one, inv_one, mean_two, inv_two, mean_three, inv_three, mean_one, mean_one], axis=0
    )
    leaving += started(out_sems.at[5:6], (stats, stats_far))
    slope = inv_three * gain_three
    start = bias_three - mean_three * slope

    def third(index, carry):
        at = row_at(index, cols)
        act_three[at, :] = (residual[at, :] * slope + start).astype(jnp.bfloat16)
        return carry

    lax.fori_loop(0, rows, third, 0, unroll=True)
    finish_all(leaving)


def attention_kernel(columns, vec, act_three, w_heads, w_out, biases, *refs):
    blocks = refs[:8]
    value_key_far, query_far, grad_far, mixed_far, sums_far = refs[8:13]
    (
        grad_blocks, grad_proj, value_key, query_part, sums,
        query_grad, key_pad, value_pad, heads_t, mixed, mask_row, in_sems, out_sems,
    ) = refs[13:]
    cells, channels = grad_proj.shape
    block_cells = blocks[0].shape[0]
    spot, _, _, height = own_place(vec)
    half = mixed.shape[1] // 2
    cols = columns
    scaling = half**-0.5
    valid_cells = height * cols
    step = 256
    pairs = []
    for index, block in zip(ARRIVAL, blocks):
        base = pl.multiple_of((spot ^ index) * block_cells, block_cells)
        pairs.append((block, grad_blocks.at[pl.ds(base, block_cells), :]))
    arriving = started(in_sems, *pairs)

    sizes = []
    for start in range(0, cells, 512):
        at = slice(start, start + 512)
        parts = dot(act_three[at, :], w_heads[...]) + biases[0:1, :]
        query, key, value = (parts[:, 2 * half * k : 2 * half * (k + 1)] for k in range(3))
        query_grad[at, :] = query.astype(jnp.bfloat16) * jnp.bfloat16(scaling)
        key_pad[at, :] = key.astype(jnp.bfloat16)
        value_pad[at, :] = value.astype(jnp.bfloat16)
        query_size = jnp.sum(query * query, axis=1, keepdims=True) * (scaling * scaling)
        key_size = jnp.sum(key * key, axis=1, keepdims=True)
        sizes.append((jnp.max(query_size), jnp.max(key_size)))
    lane = lax.broadcasted_iota(jnp.int32, (1, cells), 1)
    mask_row[...] = jnp.where(lane < valid_cells, 0.0, MASKED)
    heads_t[...] = jnp.zeros(heads_t.shape, jnp.float32)
    mixed[...] = jnp.zeros(mixed.shape, jnp.bfloat16)
    finish_all(arriving)

    def clean(index, total):
        at = pl.ds(pl.multiple_of(index * block_cells, block_cells), block_cells)
        cell = index * block_cells + lax.broadcasted_iota(jnp.int32, (block_cells, channels), 0)
        kept = jnp.where(cell < valid_cells, grad_blocks[at, :].astype(jnp.float32), 0.0)
        low = kept.astype(jnp.bfloat16)
        grad_proj[at, :] = low
        query_grad[at, :] = query_grad[at, :] + dot(low, w_out[...]).astype(jnp.bfloat16)
        return total + fold(kept)

    start = jnp.zeros((8, channels), jnp.float32)
    total = lax.fori_loop(0, cells // block_cells, clean, start, unroll=True)
    sums[...] = jnp.concatenate([total_of(total), jnp.zeros((7, channels), jnp.float32)], axis=0)
    leaving = started(out_sems, (grad_proj, grad_far), (sums, sums_far))

    def query_block(shifted, index, carry):
        at = pl.ds(pl.multiple_of(index * step, step), step)
        both = query_grad[at, :]
        scores = dot_rows(both, key_pad[...]) + mask_row[...]
        if shifted:
            scores = scores - jnp.max(scores, axis=1, keepdims=True)
        weights = jnp.exp(scores)
        total = jnp.zeros((step, 2 * half), jnp.float32)
        for start in range(0, cells, 2 * half):
            total = total + weights[:, start : start + 2 * half]
        inverse = 1.0 / jnp.sum(total, axis=1, keepdims=True)
        low = weights.astype(jnp.bfloat16)
        out = dot(low, value_pad[...]) * inverse
        wide = both.astype(jnp.float32)
        delta = jnp.sum(wide * out, axis=1, keepdims=True)
        turned = jnp.transpose(wide * inverse).astype(jnp.bfloat16)
        grad_probs = dot_rows(both, value_pad[...])
        grad_scores = (low.astype(jnp.float32) * (grad_probs - delta)).astype(jnp.bfloat16)
        grad_query = dot(grad_scores, key_pad[...]) * (inverse * scaling)
        mixed[at, :] = (out + grad_query).astype(jnp.bfloat16)
        heads_t[0:half, :] += dot(turned[0:half], grad_scores)
        heads_t[half : 2 * half, :] += dot(turned[half : 2 * half], low)
        return carry

    query_most, key_most = (functools.reduce(jnp.maximum, size) for size in zip(*sizes))
    narrow = query_most * key_most <= 3600.0

    @pl.when(narrow)
    def _():
        lax.fori_loop(0, cells // step, functools.partial(query_block, False), 0, unroll=2)

    @pl.when(jnp.logical_not(narrow))
    def _():
        count = (valid_cells + step - 1) // step
        lax.fori_loop(0, count, functools.partial(query_block, True), 0)

    for start in range(0, cells, step):
        value_key[start : start + step, :] = jnp.transpose(heads_t[:, start : start + step]).astype(
            jnp.bfloat16
        )
    query_part[:, 0:half] = mixed[0 : cells // 2, 0:half]
    query_part[:, half : 2 * half] = mixed[cells // 2 : cells, 0:half]
    leaving += started(
        out_sems.at[2:5], (value_key, value_key_far), (query_part, query_far), (mixed, mixed_far)
    )
    finish_all(leaving)


def aside_kernel(vec, *refs):
    act_far, (mixed_far, value_key_far, act_three_far, grad_far) = refs[0:2], refs[2:6]
    own_far, weight_far, sends = refs[6:8], refs[8], refs[9:13]
    acts, mixed, value_key, act_three, grad_proj, padded, own, weight_rows, in_sems, out_sems = (
        refs[13:]
    )
    cells, channels = act_three.shape
    cols = (padded.shape[0] - cells) // 2
    lanes = mixed.shape[1]
    half = lanes // 2
    spot, head, image, _ = own_place(vec)
    arriving = started(
        in_sems,
        (mixed_far, mixed),
        (value_key_far, value_key),
        (act_three_far, act_three),
        (grad_far, grad_proj),
        (act_far[0], acts.at[0]),
        (act_far[1], acts.at[1]),
    )
    block_cells = sends[0].shape[0]
    step = 256
    arriving[0].wait()
    for k, send in enumerate(sends):
        tiles = []
        for part in range(2):
            block = (head ^ k) + HEADS * (image ^ part)
            at = pl.ds(pl.multiple_of(block * block_cells, block_cells), block_cells)
            tiles.append(mixed[at, half:lanes])
        send[...] = jnp.concatenate(tiles, axis=1)
    finish_all(arriving[1:4])

    def gather(index, totals):
        at = pl.ds(pl.multiple_of(index * step, step), step)
        low_mixed, low_heads, act = mixed[at, :], value_key[at, :], act_three[at, :]
        mixed_t = jnp.transpose(low_mixed.astype(jnp.float32)).astype(jnp.bfloat16)
        heads_t = jnp.transpose(low_heads.astype(jnp.float32)).astype(jnp.bfloat16)
        return (
            totals[0] + dot(mixed_t, act),
            totals[1] + dot(heads_t, act),
            totals[2] + dot(mixed_t, grad_proj[at, :]),
            totals[3] + fold(low_mixed.astype(jnp.float32)),
            totals[4] + fold(low_heads.astype(jnp.float32)),
        )

    square = jnp.zeros((lanes, channels), jnp.float32)
    line = jnp.zeros((8, lanes), jnp.float32)
    from_query, from_heads, from_out, query_sum, value_sum = lax.fori_loop(
        0, cells // step, gather, (square, square, square, line, line)
    )
    unit = half // 4
    parts = (from_query[0:half], from_heads[0:half], from_heads[half:lanes], from_out[half:lanes])
    for chunk in range(4):
        for k, part in enumerate(parts):
            piece = part[chunk * unit : (chunk + 1) * unit].astype(jnp.bfloat16)
            weight_rows[chunk, k * unit : (k + 1) * unit, :] = piece
    weight_rows[:, half:, :] = jnp.zeros((4, 16, channels), jnp.bfloat16)
    which = lax.axis_index("img") * 2 + image
    lane = lax.broadcasted_iota(jnp.int32, (1, channels), 1)
    now = jnp.max(vec[12:13, :]).astype(jnp.int32)
    high = jnp.where(lane == which, (now // 32).astype(jnp.float32), 0.0)
    rest = jnp.where(lane == which, (now % 32).astype(jnp.float32), 0.0)
    row = jnp.concatenate([total_of(query_sum), total_of(value_sum)], axis=1)
    below = jnp.zeros((13, channels), jnp.float32)
    weight_rows[2, half:, :] = jnp.concatenate([row, high, rest, below], axis=0).astype(
        jnp.bfloat16
    )
    source = lax.broadcasted_iota(jnp.int32, (channels, 3 * half), 0)
    target = lax.broadcasted_iota(jnp.int32, (channels, 3 * half), 1)
    chosen = jnp.where(source == head * half + target % half, 1.0, 0.0).astype(jnp.bfloat16)
    lane = lax.broadcasted_iota(jnp.int32, (step, 3 * half), 1)
    column = lax.broadcasted_iota(jnp.int32, (step, 3 * half), 0) % cols
    leaving = started(out_sems.at[2:3], (weight_rows, weight_far))
    for k in range(2):
        arriving[4 + k].wait()
        clear_rims(padded, cols)

        def widen(index, carry):
            at = pl.ds(pl.multiple_of(index * step, step), step)
            tile = dot(acts[k, at, :], chosen)
            before = jnp.where(column == 0, 0.0, pltpu.roll(tile, 1, 0))
            after = jnp.where(column == cols - 1, 0.0, pltpu.roll(tile, step - 1, 0))
            tile = jnp.where(lane < half, before, jnp.where(lane < 2 * half, tile, after))
            padded[pl.ds(pl.multiple_of(index * step + cols, cols), step), :] = tile
            return carry

        lax.fori_loop(0, cells // step, widen, 0)
        for tap in range(3):

            def turn(index, carry):
                at = pl.ds(pl.multiple_of(index * step + tap * cols, cols), step)
                to = pl.ds(pl.multiple_of(index * step, step), step)
                own[k, tap, :, to] = jnp.transpose(padded[at, :]).astype(jnp.bfloat16)
                return carry

            lax.fori_loop(0, cells // step, turn, 0)
        leaving += started(out_sems.at[k : k + 1], (own.at[k], own_far[k]))
    finish_all(leaving)


def middle_kernel(vec, qkv_t, *refs):
    heads_far = (refs[4], refs[0], refs[6], refs[2])
    sides_far = (refs[5], refs[1], refs[7], refs[3])
    grad_far, residual_far, stats_far, own_two_far, rows_far = refs[8:13]
    weight_far, conv_far, own_one_far, out_sums_far = refs[13:17]
    shifted_one, grad_res_far, payload_far = refs[17], refs[18], refs[19:23]
    (
        heads, sides, grad_proj, residual, stats, own_two, grad_res, payload, grad_act, shifted,
        weight, conv_one, own_one, out_sums, in_sems, out_sems,
    ) = refs[23:]
    cells, channels = grad_proj.shape
    cols = (shifted.shape[0] - cells) // 2
    rows = cells // cols
    _, head, image, height = own_place(vec)
    column = lax.axis_index("img")
    width = channels // GROUPS
    count = (height * (cols * width)).astype(jnp.float32)
    half = qkv_t.shape[1]
    unit = half // 4
    small_at = 18 * unit + half
    pairs = [(far, heads.at[head ^ k]) for k, far in enumerate(heads_far)]
    pairs += [(far, sides.at[head ^ k]) for k, far in enumerate(sides_far)]
    arriving = started(
        in_sems,
        *pairs,
        (stats_far, stats),
        (residual_far, residual),
        (grad_far, grad_proj),
        (own_two_far, own_two),
        (rows_far.at[:, pl.ds(0, half), :], payload.at[:, pl.ds(9 * unit, half), :]),
        (rows_far.at[:, pl.ds(half, 16), :], payload.at[:, pl.ds(small_at, 16), :]),
        (weight_far, weight),
        (conv_far, conv_one),
        (own_one_far, own_one),
        (out_sums_far, out_sums),
    )
    finish_all(arriving[:10])
    zeros = jnp.zeros((half, channels), jnp.bfloat16)
    halfway = cells // 2
    step = 512
    pairs = ((0, 1), (2, 3))
    w_main = []
    for a, b in pairs:
        order = [HEADS + a, 2 * HEADS + a, HEADS + b, 2 * HEADS + b]
        w_main.append(jnp.concatenate([qkv_t[k] for k in order], axis=0))
    mean, inverse = stats[4:5, :], stats[5:6, :]
    gain = vec[8:9, :]
    zero = jnp.zeros((8, channels), jnp.float32)
    plain, cross = zero, zero

    def normed(index):
        return (residual[index * cols : (index + 1) * cols, :] - mean) * inverse

    for part in range(2):
        w_side = []
        for a, b in pairs:
            left, right = qkv_t[a], qkv_t[b]
            order = [left, zeros, right, zeros] if part == 0 else [zeros, left, zeros, right]
            w_side.append(jnp.concatenate(order, axis=0))
        for base in range(0, halfway, step):
            start = part * halfway + base
            total = None
            for k, (a, b) in enumerate(pairs):
                main = jnp.concatenate(
                    [heads[a][start : start + step, :], heads[b][start : start + step, :]], axis=1
                )
                side = jnp.concatenate(
                    [sides[a][base : base + step, :], sides[b][base : base + step, :]], axis=1
                )
                term = dot(main, w_main[k]) + dot(side, w_side[k])
                total = term if total is None else total + term
            grad_act[start : start + step, :] = total
            for index in range(start // cols, (start + step) // cols):
                tile = total[index * cols - start : (index + 1) * cols - start]
                plain = plain + fold(tile)
                cross = cross + fold(tile * normed(index))
    plain, cross = total_of(plain), total_of(cross)
    mean_plain = group_sums(plain * gain, width) / count
    mean_cross = group_sums(cross * gain, width) / count
    clear_rims(shifted, cols)
    clear_rims(shifted_one, cols)
    finish_all(arriving[10:16])
    group = 4
    size = group * cols
    steps = rows // group
    totals = [zero, zero, zero, zero]
    one, two = gain * inverse, mean_cross * inverse * inverse
    three = (mean_plain - mean * inverse * mean_cross) * inverse
    gain_two, bias_two, scale, shift = (vec[k : k + 1, :] for k in range(3, 7))
    mean_two, inverse_two = stats[2:3, :], stats[3:4, :]
    line = half_line(mean_two, inverse_two, gain_two, bias_two, scale, shift)
    begin_two = mean_two * inverse_two

    def tiles(block):
        for index in range(block * group, (block + 1) * group):
            yield index, slice(index * cols, (index + 1) * cols)

    def through_three(block):
        for index, at in tiles(block):
            inner = grad_act[at, :] * one - residual[at, :] * two - three
            grad = grad_proj[at, :].astype(jnp.float32) + inner * valid_row(index, height)
            grad_res[at, :] = grad
            put_shifted(shifted, index, grad, cols)
            totals[0] = totals[0] + fold(grad)

    def conv_back(block):
        grad_act[block * size : (block + 1) * size, :] = conv_block(
            shifted, weight, block, size, cols
        )

    def through_act(block):
        for index, at in tiles(block):
            value = conv_one[at, :]
            unit_value = value * inverse_two - begin_two
            part = value * line[0] + line[1]
            sigmoid = 0.5 + 0.5 * jnp.tanh(part)
            slope = sigmoid + 2.0 * part * sigmoid * (1.0 - sigmoid)
            grad = grad_act[at, :] * valid_row(index, height) * slope
            grad_act[at, :] = grad
            totals[1] = totals[1] + fold(grad)
            totals[2] = totals[2] + fold(grad * unit_value)

    in_turn(steps, through_three, conv_back, through_act)
    total = total_of(totals[0])
    three_lines = [cross, plain, total]
    leaving = started(out_sems, (grad_res, grad_res_far))
    plain, cross = total_of(totals[1]), total_of(totals[2])
    gain, bias = gain_two, bias_two
    factor = gain * scale
    mean_plain = group_sums(plain * factor, width) / count
    mean_cross = group_sums(cross * factor, width) / count
    one, two = factor * inverse_two, mean_cross * inverse_two * inverse_two
    three = (mean_plain - begin_two * mean_cross) * inverse_two
    finish_all(arriving[16:])
    parts = [[None] * 3, [None] * 3]

    def through_two(block):
        for index, at in tiles(block):
            grad = grad_act[at, :] * one - conv_one[at, :] * two - three
            grad = grad * valid_row(index, height)
            put_shifted(shifted_one, index, grad, cols)
            totals[3] = totals[3] + fold(grad)

    def weigh(block):
        at = slice(block * size, (block + 1) * size)
        inner = slice(cols + block * size, cols + (block + 1) * size)
        for k, (own, moved) in enumerate(((own_two, shifted), (own_one, shifted_one))):
            grad = moved[inner, channels : 2 * channels]
            for tap in range(3):
                part = dot(own[tap, :, at], grad)
                parts[k][tap] = part if block == 0 else parts[k][tap] + part

    in_turn(steps, through_two, weigh, lambda block: None)
    put_quarter(parts[0], payload, 0)
    put_quarter(parts[1], payload, 9 * unit + half)
    total = total_of(totals[3])
    lines = [
        *three_lines, out_sums[0:1, :], cross * scale, plain * scale, total,
        jnp.zeros((9, channels), jnp.float32),
    ]
    mine = 2 * (column * 2 + image)
    place = lax.broadcasted_iota(jnp.int32, (16, channels), 0)
    both = jnp.where(place == mine, gain * cross + bias * plain, 0.0)
    payload[0, small_at:, :] = jnp.concatenate(lines, axis=0).astype(jnp.bfloat16)
    payload[1, small_at:, :] = jnp.where(place == mine + 1, plain, both).astype(jnp.bfloat16)
    leaving += started(
        out_sems.at[1:5],
        *[(payload.at[column ^ k], far) for k, far in enumerate(payload_far)],
    )
    finish_all(leaving)


def first_kernel(vec, shifted, weight_far, pix_far, grad_far, stats_far, *refs):
    out_own_far, out_away_far, sums_far = refs[:3]
    weight, pix, grad_res, stats, out, sums, grad_act, in_sems, out_sems = refs[3:]
    cells, channels = pix.shape
    block_cells = out.shape[1]
    cols = (shifted.shape[0] - cells) // 2
    rows = cells // cols
    spot, _, _, height = own_place(vec)
    width = channels // GROUPS
    count = (height * (cols * width)).astype(jnp.float32)
    arriving = started(
        in_sems,
        (weight_far, weight),
        (stats_far, stats),
        (pix_far, pix),
        (grad_far, grad_res),
    )
    gain, bias = vec[0:1, :], vec[1:2, :]
    zero = jnp.zeros((8, channels), jnp.float32)
    arriving[0].wait()
    conv_shifted(shifted, weight, grad_act, 0.0, cols)
    finish_all(arriving[1:])
    mean, inverse = stats[0:1, :], stats[1:2, :]
    line = half_line(mean, inverse, gain, bias)
    begin = mean * inverse

    def normed(at):
        return pix[at, :].astype(jnp.float32) * inverse - begin

    def add(index, totals):
        at = row_at(index, cols)
        value = pix[at, :].astype(jnp.float32)
        unit = value * inverse - begin
        part = value * line[0] + line[1]
        sigmoid = 0.5 + 0.5 * jnp.tanh(part)
        slope = sigmoid + 2.0 * part * sigmoid * (1.0 - sigmoid)
        grad = grad_act[at, :] * valid_row(index, height) * slope
        grad_act[at, :] = grad
        return totals[0] + fold(grad), totals[1] + fold(grad * unit)

    plain, cross = lax.fori_loop(0, rows, add, (zero, zero), unroll=2)
    plain, cross = total_of(plain), total_of(cross)
    mean_plain = group_sums(plain * gain, width) / count
    mean_cross = group_sums(cross * gain, width) / count
    block_rows = block_cells // cols
    for part in range(2):
        first_row = (spot ^ (4 * part)) * block_rows
        for line in range(block_rows):
            at = row_at(first_row + line, cols)
            grad = (grad_act[at, :] * gain - mean_plain - normed(at) * mean_cross) * inverse
            grad = grad_res[at, :] + grad * valid_row(first_row + line, height)
            out[part, line * cols : (line + 1) * cols, :] = grad.astype(jnp.bfloat16)
    sums[...] = jnp.concatenate([cross, plain, jnp.zeros((6, channels), jnp.float32)], axis=0)
    finish_all(
        started(
            out_sems, (out.at[0], out_own_far), (out.at[1], out_away_far), (sums, sums_far)
        )
    )


def block_kernel(columns, vec, w_out, *refs):
    heads, residual_far = refs[:4], refs[4]
    out_own, out_away, residual, in_sems = refs[5:]
    block_cells, channels = out_own.shape
    spot, head, _, height = own_place(vec)
    cols = columns
    bases = [
        pl.multiple_of((spot ^ (4 * part)) * block_cells, block_cells) for part in range(2)
    ]
    pairs = [
        (residual_far.at[pl.ds(base, block_cells), :], residual.at[part])
        for part, base in enumerate(bases)
    ]
    finish_all(started(in_sems, *pairs))
    for part, out in enumerate((out_own, out_away)):
        total = residual[part] + vec[10:11, :]
        for step in range(4):
            width = w_out.shape[1]
            tile = heads[step][:, part * width : (part + 1) * width]
            total = total + dot(tile, w_out[head ^ step])
        cell = bases[part] + lax.broadcasted_iota(jnp.int32, (block_cells, channels), 0)
        out[...] = jnp.where(cell < height * cols, total, 0.0).astype(jnp.bfloat16)


def prepare_kernel(*refs):
    shifts, lines_far, kernels_far = refs[0], refs[1:15], refs[15:17]
    vec, w_heads, w_out, biases, qkv_t = refs[17:22]
    backs_far = refs[22:24]
    kernels, backs, qkv_weight, out_weight, heights, timesteps, qv_bias, *lines = refs[24:40]
    line_sems, in_sems, out_sems = refs[40:]
    channels = out_weight.shape[0]
    half = channels // HEADS
    small = started(
        line_sems,
        *zip(lines_far, (*lines, qv_bias, qkv_weight, out_weight, heights, timesteps)),
    )
    arriving = started(
        in_sems, *[(far, kernels.at[k]) for k, far in enumerate(kernels_far)]
    )
    finish_all(small)
    spot = lax.axis_index("row")
    image, head = spot // HEADS, spot % HEADS
    shift_row = shifts[pl.ds(image, 1), :]
    order = list(range(5)) + [None, None] + list(range(5, 9))
    for line, k in enumerate(order):
        if k is not None:
            vec[line : line + 1, :] = lines[k][...].astype(jnp.float32).reshape(1, channels)
    vec[5:6, :] = 1.0 + shift_row[:, :channels]
    vec[6:7, :] = shift_row[:, channels:]
    vec[11:12, :] = jnp.full((1, channels), heights[image].astype(jnp.float32))
    vec[12:13, :] = jnp.full((1, channels), timesteps[image].astype(jnp.float32))
    vec[13:16, :] = jnp.zeros((3, channels), jnp.float32)
    source = lax.broadcasted_iota(jnp.int32, (channels, 2 * half), 0)
    lane = lax.broadcasted_iota(jnp.int32, (channels, 2 * half), 1)
    first = jnp.where((lane < half) & (source == head * half + lane), 1.0, 0.0)
    second = jnp.where((lane >= half) & (source == head * half + lane - half), 1.0, 0.0)
    first, second = first.astype(jnp.bfloat16), second.astype(jnp.bfloat16)
    lanes = 2 * half
    for part, taken in enumerate((first, first, second)):
        whole = qkv_weight[:, part * channels : (part + 1) * channels]
        w_heads[:, part * lanes : (part + 1) * lanes] = dot(whole, taken).astype(jnp.bfloat16)
    turned = jnp.transpose(out_weight[...].astype(jnp.float32)).astype(jnp.bfloat16)
    w_out[...] = dot(turned, second).astype(jnp.bfloat16)
    both = qv_bias[...].astype(jnp.float32).reshape(1, 2 * channels)
    wide = jnp.broadcast_to(both, (16, 2 * channels)).astype(jnp.bfloat16)
    biases[:, 0:lanes] = dot(wide[:, :channels], first)[0:8]
    biases[:, lanes : 2 * lanes] = jnp.zeros((8, lanes), jnp.float32)
    biases[:, 2 * lanes : 3 * lanes] = dot(wide[:, channels:], second)[0:8]
    for block in range(0, 3 * HEADS, 2):
        whole = qkv_weight[:, block // 2 * lanes : (block // 2 + 1) * lanes].astype(jnp.float32)
        whole = jnp.transpose(whole).astype(jnp.bfloat16)
        qkv_t[block] = whole[0:half]
        qkv_t[block + 1] = whole[half:lanes]
    leaving = []
    for k in range(2):
        arriving[k].wait()

        def turn(tap, carry):
            tile = kernels[k, 2 - tap // 3, 2 - tap % 3].astype(jnp.float32)
            at = pl.ds(pl.multiple_of(tap % 3 * channels, channels), channels)
            backs[k, tap // 3, at, :] = jnp.transpose(tile).astype(jnp.bfloat16)
            return carry

        lax.fori_loop(0, 9, turn, 0)
        leaving += started(out_sems.at[k : k + 1], (backs.at[k], backs_far[k]))
    finish_all(leaving)


def final_kernel(*refs):
    parts, frequency = refs[:8], refs[8]
    one_far, two_far, qkv_far, out_far, time_far = refs[9:14]
    bias_out, time_bias, rows = refs[14], refs[15], refs[16:25]
    one, two, qkv_rows, qkv_out, out_out, time_out, small, norm_one, sems, out_sems = refs[25:]
    channels = one.shape[1]
    half = channels // HEADS
    unit = half // 4
    lines = 18 * unit + half + 16
    spot = lax.axis_index("row")
    head, column = spot % HEADS, lax.axis_index("img")
    leaving = []
    for index, part in enumerate(parts):
        away = column ^ (index // 2)
        for pair in range(2):
            quarter, base = head ^ (index % 2 + 2 * pair), pair * lines
            first = pl.multiple_of(quarter * half + away * unit, unit)
            at = pl.ds(first, unit)
            shape = (9, unit, channels)
            late = base + 9 * unit + half
            two[:, at, :] = part[base : base + 9 * unit].astype(jnp.float32).reshape(shape)
            one[:, at, :] = part[late : late + 9 * unit].astype(jnp.float32).reshape(shape)
            here = len(leaving)
            leaving += started(
                sems.at[here : here + 2],
                (two.at[:, at, :], two_far.at[:, at, :]),
                (one.at[:, at, :], one_far.at[:, at, :]),
            )
            middle = base + 9 * unit
            for k in range(3):
                to = pl.ds(pl.multiple_of(first + k * channels, unit), unit)
                piece = part[middle + k * unit : middle + (k + 1) * unit]
                qkv_rows[to, :] = piece.astype(jnp.float32)
            out_out[at, :] = part[middle + 3 * unit : middle + half].astype(jnp.float32)
            small[quarter, away] = part[base + lines - 16 : base + lines].astype(jnp.float32)
    for part in range(3):
        across = slice(part * channels, (part + 1) * channels)
        qkv_out[:, across] = jnp.transpose(qkv_rows[across, :])
    leaving += started(out_sems, (qkv_out, qkv_far), (out_out, out_far))
    sums = [small[quarter, 2] for quarter in range(HEADS)]
    pieces = [part[0:1, :half] for part in sums] + [part[0:1, 3 * half :] for part in sums]
    bias_out[...] = jnp.concatenate(pieces, axis=1).reshape(bias_out.shape)
    for step in range(4):
        norm_one[column ^ step] = parts[2 * step][2 * lines : 2 * lines + 16].astype(jnp.float32)
    total = norm_one[0] + norm_one[1] + norm_one[2] + norm_one[3]
    whole = jnp.concatenate([total[0:2], small[0, 0, 0:7, :]], axis=0)
    for k, row in enumerate(rows):
        row[...] = whole[k : k + 1].reshape(row.shape)
    shifts = small[0, 1]
    pair = jnp.concatenate([shifts[k : k + 1, :] for k in range(0, 16, 2)], axis=0)
    other = jnp.concatenate([shifts[k : k + 1, :] for k in range(1, 16, 2)], axis=0)
    both = jnp.concatenate([pair, other], axis=1)
    time_bias[...] = total_of(both).reshape(time_bias.shape)
    steps = sums[0][1:2, :] * 32.0 + sums[0][2:3, :]
    image = lax.broadcasted_iota(jnp.int32, (8, steps.shape[1]), 0)
    lane = lax.broadcasted_iota(jnp.int32, (8, steps.shape[1]), 1)
    now = jnp.sum(jnp.where(image == lane, steps, 0.0), axis=1, keepdims=True)
    angles = now * frequency[...]
    left = jnp.concatenate([jnp.cos(angles), jnp.sin(angles)], axis=1)
    left = left / (1.0 + jnp.exp(-left))
    terms = []
    for _ in range(3):
        terms.append(left.astype(jnp.bfloat16).astype(jnp.float32))
        left = left - terms[-1]
    terms = jnp.concatenate(terms + [jnp.zeros_like(left)], axis=0)
    both = jnp.concatenate([both] * 3 + [jnp.zeros_like(both)], axis=0).astype(jnp.bfloat16)
    time_out[...] = lax.dot_general(
        terms.astype(jnp.bfloat16), both, (((0,), (0,)), ((), ())),
        preferred_element_type=jnp.float32,
    )
    leaving += started(out_sems.at[2:3], (time_out, time_far))
    finish_all(leaving)


def swap(value, axis, step):
    count = lax.axis_size(axis)
    return lax.ppermute(value, axis, [(k, k ^ step) for k in range(count)])


def pick(stacked, index):
    return lax.dynamic_index_in_dim(stacked, index, 0, keepdims=False)


def add_up(*parts):
    total = parts[0].astype(jnp.float32)
    for part in parts[1:]:
        total = total + part.astype(jnp.float32)
    return total.astype(jnp.bfloat16)


def from_columns(pair):
    return [pair] + [swap(pair, "img", step) for step in (1, 2, 3)]


def with_mates(columns):
    return [part for mine in columns for part in (mine, swap(mine, "row", 1))]


def gather_columns(pair):
    return with_mates(from_columns(pair))


def call(kernel, near_outs, far_outs, scratch, limit, work, scalars, near, far, last_outs=()):
    close = pl.BlockSpec(memory_space=pltpu.VMEM)
    distant = pl.BlockSpec(memory_space=pltpu.HBM)
    operands = list(near) + [pltpu.with_memory_space_constraint(array, pltpu.HBM) for array in far]
    moved = sum(array.size * array.dtype.itemsize for array in operands)
    return pl.pallas_call(
        kernel,
        out_shape=[jax.ShapeDtypeStruct(*kind) for kind in near_outs]
        + [pltpu.HBM(*kind) for kind in far_outs]
        + [jax.ShapeDtypeStruct(*kind) for kind in last_outs],
        in_specs=[pl.BlockSpec(memory_space=pltpu.SMEM)] * len(scalars)
        + [close] * len(near)
        + [distant] * len(far),
        out_specs=[close] * len(near_outs)
        + [distant] * len(far_outs)
        + [close] * len(last_outs),
        scratch_shapes=[pltpu.VMEM(*kind) if isinstance(kind, tuple) else kind for kind in scratch],
        compiler_params=mib(limit),
        cost_estimate=pl.CostEstimate(flops=work, bytes_accessed=moved, transcendentals=0),
    )(*scalars, *operands)


def sems(count):
    return pltpu.SemaphoreType.DMA((count,))


def gather_field(mine, theirs):
    far, far_near = swap(theirs, "row", 4), swap(theirs, "row", 6)
    return [mine, swap(mine, "row", 1), swap(mine, "row", 2), None, far, None, far_near, None]


def relayed(blocks, after=None):
    sent = [blocks[2], blocks[4], blocks[6]]
    if after is not None:
        sent = lax.optimization_barrier((*sent, after))[:3]
    odd = [swap(block, "row", 1) for block in sent]
    return odd, [blocks[step] for step in ARRIVAL[3:]]


def local_image(
    pixels,
    heights,
    timesteps,
    norm1_gain,
    norm1_bias,
    conv1_weight,
    conv1_bias,
    time_weight,
    time_bias,
    norm2_gain,
    norm2_bias,
    conv2_weight,
    conv2_bias,
    norm3_gain,
    norm3_bias,
    qkv_weight,
    qv_bias,
    out_weight,
    out_bias,
    grad_out,
):
    images, row_count, cols, channels = pixels.shape
    block_cells = row_count * cols
    cells = block_cells * lax.axis_size("row")
    half = channels // HEADS
    column = lax.axis_index("img")
    image = lax.axis_index("row") // HEADS
    low, full = jnp.bfloat16, jnp.float32
    pixel_blocks = pixels.reshape(images, block_cells, channels)
    grad_blocks = grad_out.reshape(images, block_cells, channels)
    field = gather_field(pick(pixel_blocks, image), pick(pixel_blocks, 1 - image))
    later = (pick(grad_blocks, image), pick(grad_blocks, 1 - image), field[4], field[6])
    later = lax.optimization_barrier(later)
    grads = gather_field(later[0], later[1])
    field[4], field[6] = later[2], later[3]
    time_act = jax.nn.silu(embed_steps(timesteps, time_weight.shape[0]))
    shifts = jnp.dot(time_act, time_weight.astype(full), precision=PRECISE) + time_bias.astype(full)
    kernel_shape = (3, 3 * channels, channels)
    lanes = 2 * half
    vec, w_heads, w_out, biases, qkv_t, w_one_back, w_two_back = call(
        prepare_kernel,
        [
            ((16, channels), full), ((channels, 3 * lanes), low), ((channels, lanes), low),
            ((8, 3 * lanes), full), ((3 * HEADS, half, channels), low),
        ],
        [(kernel_shape, low), (kernel_shape, low)],
        [
            ((2, 3, 3, channels, channels), low), ((2,) + kernel_shape, low),
            ((channels, 3 * channels), low), ((channels, channels), low),
            pltpu.SMEM((images,), jnp.int32), pltpu.SMEM((images,), jnp.int32),
            ((2 * channels,), low), *[((channels,), low)] * 9,
            sems(14), sems(2), sems(2),
        ],
        16,
        channels,
        [],
        [shifts],
        [
            norm1_gain, norm1_bias, conv1_bias, norm2_gain, norm2_bias, conv2_bias, norm3_gain,
            norm3_bias, out_bias, qv_bias, qkv_weight, out_weight, heights, timesteps,
            conv1_weight,
            conv2_weight,
        ],
    )
    field_late, field = relayed(field, vec)
    w_one, w_two = conv1_weight.reshape(kernel_shape), conv2_weight.reshape(kernel_shape)
    rim_cells = cells + 2 * cols
    cost = 9 * cells * channels * channels // 2

    wide, tall = (cells, channels), (rim_cells, 3 * channels)
    rows_eight = ((8, channels), full)
    act_three, pix, conv_one, residual, act_one, act_two, stats = call(
        forward_kernel,
        [(wide, low)],
        [(wide, low), (wide, full), (wide, full), (wide, low), (wide, low), rows_eight],
        [
            (wide, low), (wide, full), (wide, full), rows_eight, (kernel_shape, low),
            (kernel_shape, low), (tall, low), (tall, low), sems(10), sems(6),
        ],
        28,
        cost * 25,
        [],
        [vec, *field_late],
        [*field, w_one, w_two],
    )
    grads_late, grads = relayed(grads, act_three)
    query_shape, head_shape = (cells // 2, lanes), (cells, lanes)
    value_key, query_part, grad_proj, mixed, out_sums = call(
        functools.partial(attention_kernel, cols),
        [],
        [(head_shape, low), (query_shape, low), (wide, low), (head_shape, low), rows_eight],
        [
            (wide, low), (wide, low), (head_shape, low), (query_shape, low), rows_eight,
            (head_shape, low), (head_shape, low), (head_shape, low), ((lanes, cells), full),
            (head_shape, low), ((1, cells), full), sems(8), sems(5),
        ],
        36,
        cost * 34,
        [],
        [vec, act_three, w_heads, w_out, biases, *grads_late],
        grads,
    )

    key_near, query_near = swap(value_key, "row", 2), swap(query_part, "row", 2)
    key_mate, query_mate = swap(value_key, "row", 1), swap(query_part, "row", 1)
    own_shape = (3, 3 * half, cells)
    send_shape = ((block_cells, lanes), low)
    own_one, own_two, weight_rows, *sends = call(
        aside_kernel,
        [],
        [(own_shape, low), (own_shape, low), ((4, half + 16, channels), low)],
        [
            ((2,) + wide, low), (head_shape, low), (head_shape, low), (wide, low), (wide, low),
            ((rim_cells, 3 * half), full), ((2,) + own_shape, low), ((4, half + 16, channels), low),
            sems(6), sems(3),
        ],
        28,
        cost * 27,
        [],
        [vec],
        [act_one, act_two, mixed, value_key, act_three, grad_proj],
        [send_shape] * 4,
    )
    key_near, query_near, key_mate, query_mate, own_two = lax.optimization_barrier(
        (key_near, query_near, key_mate, query_mate, own_two)
    )
    relays = [key_mate, query_mate, swap(key_near, "row", 1), swap(query_near, "row", 1)]
    packed = [value_key, query_part, key_near, query_near]
    lines = 18 * (half // 4) + half + 16
    shifted_one, grad_res, *payload = call(
        middle_kernel,
        [(tall, low)],
        [(wide, full)] + [((lines, channels), low)] * 4,
        [
            ((HEADS,) + head_shape, low), ((HEADS,) + query_shape, low),
            (wide, low), (wide, full), rows_eight, (own_shape, low), (wide, full),
            ((4, lines, channels), low), (wide, full), (tall, low), (kernel_shape, low),
            (wide, full), (own_shape, low), rows_eight, sems(18), sems(5),
        ],
        40,
        cost * 26,
        [],
        [vec, qkv_t, *relays],
        [
            *packed, grad_proj, residual, stats, own_two, weight_rows, w_two_back, conv_one,
            own_one, out_sums,
        ],
    )
    *sends, shifted_one = lax.optimization_barrier((*sends, shifted_one))
    total = add_up(payload[0], *[swap(payload[step], "img", step) for step in (1, 2, 3)])
    heads_got = [sends[0]] + [swap(sends[step], "row", step) for step in (1, 2, 3)]
    shifted_one, total, *heads_got = lax.optimization_barrier((shifted_one, total, *heads_got))
    both = add_up(total, swap(total, "row", 4))
    grad_own, grad_away, sums_one = call(
        first_kernel,
        [],
        [((block_cells, channels), low), ((block_cells, channels), low), rows_eight],
        [
            (kernel_shape, low), (wide, low), (wide, full), rows_eight,
            ((2, block_cells, channels), low), rows_eight, (wide, full), sems(4), sems(3),
        ],
        20,
        cost * 12,
        [],
        [vec, shifted_one],
        [w_one_back, pix, grad_res, stats],
    )
    block_own, block_away = call(
        functools.partial(block_kernel, cols),
        [((block_cells, channels), low), ((block_cells, channels), low)],
        [],
        [((2, block_cells, channels), full), sems(2)],
        8,
        cost,
        [],
        [vec, out_weight.reshape(HEADS, half, channels), *heads_got],
        [residual],
    )
    out_pair = jnp.stack([block_own, grad_own])
    away_pair = swap(jnp.stack([block_away, grad_away]), "row", 4)
    first_pair = jnp.where(image == 0, out_pair, away_pair)
    second_pair = jnp.where(image == 0, away_pair, out_pair)
    finished = jnp.stack([first_pair, second_pair], axis=1).reshape((2,) + pixels.shape)
    norm_one = jnp.concatenate([sums_one, jnp.zeros_like(sums_one)], axis=0).astype(low)
    norm_one = add_up(norm_one, swap(norm_one, "row", 4))
    other = swap(both, "row", 2)
    pair = jnp.concatenate([both, other, norm_one], axis=0)
    parts = gather_columns(pair)
    line = ((channels,), full)
    kernel_out = ((9, channels, channels), full)
    time_out = ((time_weight.shape[0], 2 * channels), full)
    qkv_out, out_out = ((channels, 3 * channels), full), ((channels, channels), full)
    half_time = time_weight.shape[0] // 2
    frequency = jnp.exp(-math.log(10000.0) * jnp.arange(half_time, dtype=full) / half_time)
    (
        conv1_weight_grad, conv2_weight_grad, qkv_weight_grad, out_weight_grad, time_weight_grad,
        qv_bias_grad, time_bias_grad, *lines,
    ) = call(
        final_kernel,
        [],
        [kernel_out, kernel_out, qkv_out, out_out, time_out],
        [
            kernel_out, kernel_out, ((3 * channels, channels), full), qkv_out, out_out, time_out,
            ((HEADS, 4, 16, channels), full), ((4, 16, channels), full), sems(32), sems(3),
        ],
        28,
        cost,
        [],
        [*parts, frequency[None, :]],
        [],
        [((2 * channels,), full)] * 2 + [line] * 9,
    )
    norm1_gain_grad, norm1_bias_grad, norm3_gain_grad, norm3_bias_grad, conv2_bias_grad = lines[:5]
    out_bias_grad, norm2_gain_grad, norm2_bias_grad, conv1_bias_grad = lines[5:]
    return (
        finished[0],
        finished[1],
        norm1_gain_grad,
        norm1_bias_grad,
        conv1_weight_grad.reshape(conv1_weight.shape),
        conv1_bias_grad,
        time_weight_grad,
        time_bias_grad,
        norm2_gain_grad,
        norm2_bias_grad,
        conv2_weight_grad.reshape(conv2_weight.shape),
        conv2_bias_grad,
        norm3_gain_grad,
        norm3_bias_grad,
        qkv_weight_grad,
        qv_bias_grad,
        out_weight_grad,
        out_bias_grad,
    )


def local(*arrays):
    pixels = arrays[0]
    if lax.axis_size("row") == pixels.shape[0] * HEADS and lax.axis_size("img") == 4:
        return local_image(*arrays)
    return local_rows(*arrays)


def solution(mesh):
    placed = (
        P("img", "row", None, None),
        P("img"),
        P("img"),
        P(),
        P(),
        P(),
        P(),
        P(),
        P(),
        P(),
        P(),
        P(),
        P(),
        P(),
        P(),
        P(),
        P(),
        P(),
        P(),
        P("img", "row", None, None),
    )
    return jax.shard_map(
        local,
        mesh=mesh,
        in_specs=placed,
        out_specs=(
            P("img", "row", None, None),
            P("img", "row", None, None),
            P(),
            P(),
            P(),
            P(),
            P(),
            P(),
            P(),
            P(),
            P(),
            P(),
            P(),
            P(),
            P(),
            P(),
            P(),
            P(),
        ),
        check_vma=False,
    )
```

```python
import functools
import math

import jax
import jax.numpy as jnp
from jax import lax
from jax.experimental import pallas as pl
from jax.experimental.pallas import tpu as pltpu
from jax.sharding import PartitionSpec as P

GROUPS = 32
HEADS = 4


EPSILON = 1e-05
MASKED = -1000000000.0
PRECISE = lax.Precision.HIGHEST


def with_halo(cells, sides, width):
    for axis, dim in sides:
        count = lax.axis_size(axis)
        ends = count - 1
        head = lax.slice_in_dim(cells, 0, width, axis=dim)
        tail = lax.slice_in_dim(cells, cells.shape[dim] - width, cells.shape[dim], axis=dim)
        cells = jnp.concatenate(
            [
                lax.ppermute(tail, axis, [(i, (i + 1) % count) for i in range(ends)]),
                cells,
                lax.ppermute(head, axis, [((i + 1) % count, i) for i in range(ends)]),
            ],
            axis=dim,
        )
    return cells


def embed_steps(timesteps, time_width):
    half_dim = time_width // 2
    frequency = jnp.exp(-math.log(10000.0) * jnp.arange(half_dim, dtype=jnp.float32) / half_dim)
    angles = timesteps.astype(jnp.float32)[:, None] * frequency[None, :]
    return jnp.concatenate([jnp.cos(angles), jnp.sin(angles)], axis=1)


def silu_slope(pre_act):
    sigmoid = jax.nn.sigmoid(pre_act)
    return sigmoid * (1.0 + pre_act * (1.0 - sigmoid))


def with_rims(field_in):
    return with_halo(field_in, (("row", 1),), 1)


def conv_rows(padded, kernel):
    return lax.conv_general_dilated(
        padded,
        kernel,
        (1, 1),
        ((0, 0), (1, 1)),
        dimension_numbers=("NHWC", "HWIO", "NHWC"),
        preferred_element_type=jnp.float32,
    )


def flipped(kernel):
    return jnp.transpose(kernel[::-1, ::-1], (0, 1, 3, 2))


def kernel_grad(padded, grad_field):
    row_count = grad_field.shape[1]
    col_count = grad_field.shape[2]
    widened = jnp.pad(padded, ((0, 0), (0, 0), (1, 1), (0, 0)))
    tap_rows = []
    for tap_row in range(3):
        tap_line = []
        for tap_col in range(3):
            window = widened[:, tap_row : tap_row + row_count, tap_col : tap_col + col_count, :]
            tap_line.append(
                jnp.einsum("brwc,brwd->cd", window, grad_field, preferred_element_type=jnp.float32)
            )
        tap_rows.append(jnp.stack(tap_line))
    return jnp.stack(tap_rows)


def norm_forward(field_in, cell_mask, cell_count, group_count):
    shaped = field_in.reshape(field_in.shape[:3] + (group_count, field_in.shape[3] // group_count))
    first_sum = lax.psum(jnp.sum(shaped * cell_mask, axis=(1, 2, 4)), "row")
    center = first_sum / cell_count[:, None]
    centred = shaped - center[:, None, None, :, None]
    spread_sum = lax.psum(jnp.sum(jnp.square(centred * cell_mask), axis=(1, 2, 4)), "row")
    spread = spread_sum / cell_count[:, None]
    inverse = lax.rsqrt(spread + EPSILON)
    return (centred * inverse[:, None, None, :, None], inverse)


def norm_backward(grad_normed, normalized, inverse, gain_in, cell_mask, cell_count):
    full_shape = grad_normed.shape
    flat_norm = normalized.reshape(full_shape)
    gain_grad = jnp.sum(grad_normed * flat_norm, axis=(0, 1, 2))
    shift_grad = jnp.sum(grad_normed, axis=(0, 1, 2))
    scaled = (grad_normed * gain_in).reshape(normalized.shape)
    sum_plain, sum_cross = lax.psum(
        (
            jnp.sum(scaled * cell_mask, axis=(1, 2, 4)),
            jnp.sum(scaled * normalized * cell_mask, axis=(1, 2, 4)),
        ),
        "row",
    )
    mean_plain = sum_plain / cell_count[:, None]
    mean_cross = sum_cross / cell_count[:, None]
    grad_in = (
        (
            scaled
            - mean_plain[:, None, None, :, None]
            - normalized * mean_cross[:, None, None, :, None]
        )
        * inverse[:, None, None, :, None]
        * cell_mask
    )
    return (grad_in.reshape(full_shape), gain_grad, shift_grad)


def local_rows(
    pixels,
    heights,
    timesteps,
    norm1_gain,
    norm1_bias,
    conv1_weight,
    conv1_bias,
    time_weight,
    time_bias,
    norm2_gain,
    norm2_bias,
    conv2_weight,
    conv2_bias,
    norm3_gain,
    norm3_bias,
    qkv_weight,
    qv_bias,
    out_weight,
    out_bias,
    grad_out,
):
    image_count, row_count, col_count, channels = pixels.shape
    group_count = GROUPS
    head_count = HEADS
    head_width = channels // head_count
    query_count = row_count * col_count
    scaling = head_width ** (-0.5)
    head_shape = (image_count, query_count, head_count, head_width)
    row_ids = lax.axis_index("row") * row_count + jnp.arange(row_count, dtype=jnp.int32)
    row_valid = row_ids[None, :] < heights[:, None]
    row_mask = row_valid.astype(jnp.float32)
    cell_rows = row_mask[:, :, None, None]
    cell_mask = row_mask[:, :, None, None, None]
    own_valid = jnp.repeat(row_valid, col_count, axis=1)[:, None, None, :]
    cell_count = heights.astype(jnp.float32) * (col_count * (channels // group_count))
    gain_one = norm1_gain.astype(jnp.float32)
    gain_two = norm2_gain.astype(jnp.float32)
    gain_three = norm3_gain.astype(jnp.float32)
    field_in = pixels.astype(jnp.float32)
    normed_one, inverse_one = norm_forward(field_in, cell_mask, cell_count, group_count)
    pre_one = normed_one.reshape(field_in.shape) * gain_one + norm1_bias.astype(jnp.float32)
    act_one = (jax.nn.silu(pre_one) * cell_rows).astype(jnp.bfloat16)
    padded_one = with_rims(act_one)
    conv_one = conv_rows(padded_one, conv1_weight) + conv1_bias.astype(jnp.float32)
    time_act = jax.nn.silu(embed_steps(timesteps, time_weight.shape[0]))
    shifts = jnp.dot(
        time_act, time_weight.astype(jnp.float32), precision=PRECISE
    ) + time_bias.astype(jnp.float32)
    scale_part = 1.0 + shifts[:, None, None, :channels]
    shift_part = shifts[:, None, None, channels:]
    normed_two, inverse_two = norm_forward(conv_one, cell_mask, cell_count, group_count)
    affine_two = normed_two.reshape(field_in.shape) * gain_two + norm2_bias.astype(jnp.float32)
    pre_two = affine_two * scale_part + shift_part
    act_two = (jax.nn.silu(pre_two) * cell_rows).astype(jnp.bfloat16)
    padded_two = with_rims(act_two)
    residual = field_in + (conv_rows(padded_two, conv2_weight) + conv2_bias.astype(jnp.float32))
    normed_three, inverse_three = norm_forward(residual, cell_mask, cell_count, group_count)
    act_three = (
        normed_three.reshape(field_in.shape) * gain_three + norm3_bias.astype(jnp.float32)
    ).astype(jnp.bfloat16)
    projected = jnp.einsum(
        "brwc,cd->brwd", act_three, qkv_weight, preferred_element_type=jnp.float32
    )
    qv_float = qv_bias.astype(jnp.float32)
    queries = (projected[..., :channels] + qv_float[:channels]).astype(jnp.bfloat16)
    keys_own = projected[..., channels : 2 * channels].astype(jnp.bfloat16)
    values_own = (projected[..., 2 * channels :] + qv_float[channels:]).astype(jnp.bfloat16)
    query_heads = queries.reshape(head_shape)
    key_heads = keys_own.reshape(head_shape)
    value_heads = values_own.reshape(head_shape)

    def flatten_rows(piece_arr):
        return piece_arr.reshape(
            image_count, piece_arr.shape[1] * col_count, head_count, head_width
        )

    def key_mask(span_rows):
        key_rows = jnp.arange(span_rows, dtype=jnp.int32)
        return jnp.repeat(key_rows[None, :] < heights[:, None], col_count, axis=1)[:, None, None, :]

    top_init = jnp.full((image_count, query_count, head_count), MASKED, jnp.float32)
    piece_keys = lax.all_gather(keys_own, "row", axis=1, tiled=True)
    piece_values = lax.all_gather(values_own, "row", axis=1, tiled=True)
    key_valid = key_mask(piece_keys.shape[1])
    scores = (
        jnp.einsum(
            "bqhd,bkhd->bqhk",
            query_heads,
            flatten_rows(piece_keys),
            preferred_element_type=jnp.float32,
        )
        * scaling
    )
    scores = jnp.where(key_valid, scores, MASKED)
    new_top = jnp.maximum(top_init, jnp.max(scores, axis=3))
    weights = jnp.where(key_valid, jnp.exp(scores - new_top[..., None]), 0.0)
    running_total = jnp.sum(weights, axis=3)
    running_acc = jnp.einsum(
        "bqhk,bkhd->bqhd",
        weights.astype(jnp.bfloat16),
        flatten_rows(piece_values),
        preferred_element_type=jnp.float32,
    )
    attn_float = running_acc / running_total[..., None]
    log_total = new_top + jnp.log(running_total)
    attended = attn_float.reshape(pixels.shape).astype(jnp.bfloat16)
    output_proj = jnp.einsum(
        "brwc,cd->brwd", attended, out_weight, preferred_element_type=jnp.float32
    ) + out_bias.astype(jnp.float32)
    block_out = ((residual + output_proj) * cell_rows).astype(jnp.bfloat16)
    grad_proj = grad_out.astype(jnp.float32) * cell_rows
    grad_proj_low = grad_proj.astype(jnp.bfloat16)
    out_weight_grad = jnp.einsum(
        "brwc,brwd->cd", attended, grad_proj_low, preferred_element_type=jnp.float32
    )
    out_bias_grad = jnp.sum(grad_proj, axis=(0, 1, 2))
    grad_attended = jnp.einsum(
        "brwd,cd->brwc", grad_proj_low, out_weight, preferred_element_type=jnp.float32
    ).astype(jnp.bfloat16)
    grad_heads = grad_attended.reshape(head_shape)
    delta_own = jnp.sum(grad_heads.astype(jnp.float32) * attn_float, axis=3)
    stat_shape = (image_count, row_count, col_count, head_count)
    all_lse, all_delta = (
        lax.all_gather(log_total.reshape(stat_shape), "row", axis=1, tiled=True),
        lax.all_gather(delta_own.reshape(stat_shape), "row", axis=1, tiled=True),
    )
    piece_keys = lax.all_gather(keys_own, "row", axis=1, tiled=True)
    piece_values = lax.all_gather(values_own, "row", axis=1, tiled=True)
    flat_keys = flatten_rows(piece_keys)
    key_valid = key_mask(piece_keys.shape[1])
    scores = (
        jnp.einsum("bqhd,bkhd->bqhk", query_heads, flat_keys, preferred_element_type=jnp.float32)
        * scaling
    )
    soft_weights = jnp.where(key_valid, jnp.exp(scores - log_total[..., None]), 0.0)
    grad_probs = jnp.einsum(
        "bqhd,bkhd->bqhk",
        grad_heads,
        flatten_rows(piece_values),
        preferred_element_type=jnp.float32,
    )
    grad_scores = (soft_weights * (grad_probs - delta_own[..., None])).astype(jnp.bfloat16)
    grad_query_sum = jnp.einsum(
        "bqhk,bkhd->bqhd", grad_scores, flat_keys, preferred_element_type=jnp.float32
    )
    piece_queries = lax.all_gather(queries, "row", axis=1, tiled=True)
    piece_grads = lax.all_gather(grad_attended, "row", axis=1, tiled=True)
    flat_queries = flatten_rows(piece_queries)
    flat_grads = flatten_rows(piece_grads)
    span_rows = piece_queries.shape[1]
    piece_lse = all_lse.reshape(image_count, span_rows * col_count, head_count)
    piece_delta = all_delta.reshape(image_count, span_rows * col_count, head_count)
    scores = (
        jnp.einsum("bqhd,bkhd->bqhk", flat_queries, key_heads, preferred_element_type=jnp.float32)
        * scaling
    )
    soft_weights = jnp.where(own_valid, jnp.exp(scores - piece_lse[..., None]), 0.0)
    value_term = jnp.einsum(
        "bqhk,bqhd->bkhd",
        soft_weights.astype(jnp.bfloat16),
        flat_grads,
        preferred_element_type=jnp.float32,
    )
    grad_probs = jnp.einsum(
        "bqhd,bkhd->bqhk", flat_grads, value_heads, preferred_element_type=jnp.float32
    )
    grad_scores = (soft_weights * (grad_probs - piece_delta[..., None])).astype(jnp.bfloat16)
    key_term = jnp.einsum(
        "bqhk,bqhd->bkhd", grad_scores, flat_queries, preferred_element_type=jnp.float32
    )
    key_term, value_term = (key_term, value_term)
    grad_queries = (grad_query_sum * scaling).reshape(pixels.shape).astype(jnp.bfloat16)
    grad_keys = (key_term * scaling).reshape(pixels.shape).astype(jnp.bfloat16)
    grad_values = value_term.reshape(pixels.shape).astype(jnp.bfloat16)
    grad_projected = jnp.concatenate([grad_queries, grad_keys, grad_values], axis=3)
    qkv_weight_grad = jnp.einsum(
        "brwc,brwd->cd", act_three, grad_projected, preferred_element_type=jnp.float32
    )
    qv_bias_grad = jnp.concatenate(
        [
            jnp.sum(grad_queries.astype(jnp.float32), axis=(0, 1, 2)),
            jnp.sum(grad_values.astype(jnp.float32), axis=(0, 1, 2)),
        ]
    )
    grad_act_three = jnp.einsum(
        "brwd,cd->brwc", grad_projected, qkv_weight, preferred_element_type=jnp.float32
    )
    grad_res_attn, norm3_gain_grad, norm3_bias_grad = norm_backward(
        grad_act_three, normed_three, inverse_three, gain_three, cell_mask, cell_count
    )
    grad_residual = grad_proj + grad_res_attn
    grad_conv_two = grad_residual.astype(jnp.bfloat16)
    conv2_bias_grad = jnp.sum(grad_residual, axis=(0, 1, 2))
    conv2_weight_grad = kernel_grad(padded_two, grad_conv_two)
    grad_act_two = conv_rows(with_rims(grad_conv_two), flipped(conv2_weight)) * cell_rows
    grad_pre_two = grad_act_two * silu_slope(pre_two)
    scale_grad = jnp.sum(grad_pre_two * affine_two, axis=(1, 2))
    shift_grad = jnp.sum(grad_pre_two, axis=(1, 2))
    shift_grads = jnp.concatenate([scale_grad, shift_grad], axis=1)
    grad_conv_one, norm2_gain_grad, norm2_bias_grad = norm_backward(
        grad_pre_two * scale_part, normed_two, inverse_two, gain_two, cell_mask, cell_count
    )
    conv_one_low = grad_conv_one.astype(jnp.bfloat16)
    conv1_bias_grad = jnp.sum(grad_conv_one, axis=(0, 1, 2))
    conv1_weight_grad = kernel_grad(padded_one, conv_one_low)
    grad_act_one = conv_rows(with_rims(conv_one_low), flipped(conv1_weight)) * cell_rows
    grad_pre_one = grad_act_one * silu_slope(pre_one)
    grad_field_norm, norm1_gain_grad, norm1_bias_grad = norm_backward(
        grad_pre_one, normed_one, inverse_one, gain_one, cell_mask, cell_count
    )
    grad_pixels = (grad_residual + grad_field_norm).astype(jnp.bfloat16)
    time_weight_grad = jnp.dot(time_act.T, shift_grads, precision=PRECISE)
    time_bias_grad = jnp.sum(shift_grads, axis=0)
    summed = lax.psum(
        (
            norm1_gain_grad,
            norm1_bias_grad,
            conv1_weight_grad,
            conv1_bias_grad,
            time_weight_grad,
            time_bias_grad,
            norm2_gain_grad,
            norm2_bias_grad,
            conv2_weight_grad,
            conv2_bias_grad,
            norm3_gain_grad,
            norm3_bias_grad,
            qkv_weight_grad,
            qv_bias_grad,
            out_weight_grad,
            out_bias_grad,
        ),
        ("img", "row"),
    )
    return (
        block_out,
        grad_pixels,
        summed[0],
        summed[1],
        summed[2],
        summed[3],
        summed[4],
        summed[5],
        summed[6],
        summed[7],
        summed[8],
        summed[9],
        summed[10],
        summed[11],
        summed[12],
        summed[13],
        summed[14],
        summed[15],
    )


ARRIVAL = (3, 5, 7, 0, 1, 2, 4, 6)


def mib(count):
    return pltpu.CompilerParams(vmem_limit_bytes=count * 2**20)


def dot(left, right):
    return jnp.dot(left, right, preferred_element_type=jnp.float32)


def dot_rows(left, right):
    return lax.dot_general(
        left, right, (((1,), (1,)), ((), ())), preferred_element_type=jnp.float32
    )


def fold(tile):
    return jnp.sum(tile.reshape(-1, 8, tile.shape[1]), axis=0)


def group_sums(row, width):
    channels = row.shape[1]
    rows = lax.broadcasted_iota(jnp.int32, (channels, channels), 0) // width
    cols = lax.broadcasted_iota(jnp.int32, (channels, channels), 1) // width
    same = jnp.where(rows == cols, 1.0, 0.0).astype(jnp.bfloat16)
    wide = jnp.broadcast_to(row, (16, channels))
    total = None
    for _ in range(3):
        term = wide.astype(jnp.bfloat16)
        wide = wide - term.astype(jnp.float32)
        part = dot(term, same)
        total = part if total is None else total + part
    return total[0:1]


def row_at(index, cols):
    return pl.ds(pl.multiple_of(index * cols, cols), cols)


def total_of(tile):
    return jnp.sum(tile, axis=0, keepdims=True)


def cell_sums(tiles, about, height):
    first, square = 0.0, 0.0
    for index, tile in tiles:
        off = (tile - about) * valid_row(index, height)
        first, square = first + fold(off), square + fold(off * off)
    return first, square


def stats_of(first, square, about, height, cols):
    width = about.shape[1] // GROUPS
    each = (height * cols).astype(jnp.float32)
    first, square = total_of(first), total_of(square)
    mean = group_sums(first + about * each, width) / (each * width)
    shift = about - mean
    spread = group_sums(square + 2.0 * first * shift + each * shift * shift, width)
    return mean, lax.rsqrt(spread / (each * width) + EPSILON)


def row_mean(tile):
    return jnp.sum(tile, axis=0, keepdims=True) * (1.0 / tile.shape[0])


def in_turn(count, before, main, after):
    for step in range(count + 2):
        if step < count:
            before(step)
        if 0 <= step - 1 < count:
            main(step - 1)
        if 0 <= step - 2:
            after(step - 2)


def conv_block(shifted, weight, block, size, cols):
    base = block * size
    total = dot(shifted[base : base + size, :], weight[0])
    for tap in (1, 2):
        at = base + tap * cols
        total = total + dot(shifted[at : at + size, :], weight[tap])
    return total


def half_line(mean, inverse, gain, bias, scale=1.0, shift=0.0):
    slope = inverse * gain
    start = bias - mean * slope
    return 0.5 * slope * scale, 0.5 * (start * scale + shift)


def put_shifted(ref, index, tile, cols):
    channels = tile.shape[1]
    column = lax.broadcasted_iota(jnp.int32, tile.shape, 0)
    before = jnp.where(column == 0, 0.0, pltpu.roll(tile, 1, 0))
    after = jnp.where(column == cols - 1, 0.0, pltpu.roll(tile, cols - 1, 0))
    at = row_at(index + 1, cols)
    ref[at, 0:channels] = before.astype(jnp.bfloat16)
    ref[at, channels : 2 * channels] = tile.astype(jnp.bfloat16)
    ref[at, 2 * channels : 3 * channels] = after.astype(jnp.bfloat16)


def clear_rims(ref, cols):
    edge = jnp.zeros((cols, ref.shape[1]), ref.dtype)
    ref[0:cols, :] = edge
    ref[ref.shape[0] - cols : ref.shape[0], :] = edge


def conv_shifted(shifted, weight, out, bias, cols, added=None):
    step = 8 * cols

    def block(index, carry):
        base = index * step
        total = bias
        for tap in range(3):
            at = pl.ds(pl.multiple_of(base + tap * cols, cols), step)
            total = total + dot(shifted[at, :], weight[tap])
        if added is not None:
            total = total + added[pl.ds(pl.multiple_of(base, step), step), :].astype(jnp.float32)
        out[pl.ds(pl.multiple_of(base, step), step), :] = total
        return carry

    lax.fori_loop(0, out.shape[0] // step, block, 0, unroll=True)


def put_quarter(parts, payload, start):
    half = parts[0].shape[0] // 3
    unit = half // 4
    for line, part in enumerate(parts):
        part = part.astype(jnp.bfloat16)
        for shift in range(3):
            at = start + (3 * line + shift) * unit
            for chunk in range(4):
                base = shift * half + chunk * unit
                payload[chunk, at : at + unit, :] = part[base : base + unit]


def own_place(vec):
    spot = lax.axis_index("row")
    image, head = spot // HEADS, spot % HEADS
    return spot, head, image, jnp.max(vec[11:12, :]).astype(jnp.int32)


def started(sems, *pairs):
    copies = [pltpu.make_async_copy(src, dst, sems.at[k]) for k, (src, dst) in enumerate(pairs)]
    for copy in copies:
        copy.start()
    return copies


def finish_all(copies):
    for copy in copies:
        copy.wait()


def valid_row(index, height):
    return jnp.where(index < height, 1.0, 0.0).astype(jnp.float32)


def forward_kernel(vec, *refs):
    blocks, (w_one_far, w_two_far) = refs[:8], refs[8:10]
    act_three, pix_far, conv_far, residual_far, act_one_far, act_two_far, stats_far = refs[10:17]
    pix, conv_one, residual, stats, w_one, w_two, shift_one, shift_two, in_sems, out_sems = refs[17:]
    cells, channels = pix.shape
    block_cells = blocks[0].shape[0]
    cols = (shift_one.shape[0] - cells) // 2
    rows = cells // cols
    spot, _, _, height = own_place(vec)
    pairs = []
    for step, block in zip(ARRIVAL, blocks):
        base = pl.multiple_of((spot ^ step) * block_cells, block_cells)
        pairs.append((block, pix.at[pl.ds(base, block_cells), :]))
    arriving = started(in_sems, *pairs, (w_one_far, w_one), (w_two_far, w_two))
    gain_one, bias_one, conv_bias_one, gain_two, bias_two = (vec[k : k + 1, :] for k in range(5))
    scale, shift, conv_bias_two, gain_three, bias_three = (vec[k : k + 1, :] for k in range(5, 10))
    inner = (pl.ds(cols, cells), pl.ds(channels, channels))

    group = 2
    size = group * cols
    count = rows // group
    zero = jnp.zeros((8, channels), jnp.float32)

    def tile_of(ref, index):
        return ref[index * cols : (index + 1) * cols, :].astype(jnp.float32)

    def tiles_of(ref, block):
        return [(k, tile_of(ref, k)) for k in range(block * group, (block + 1) * group)]

    def stage(source, line, shifted, weight, out, bias, added=None):
        sums = [zero, zero, None]

        def activate(block):
            for index, tile in tiles_of(source, block):
                part = tile * line[0] + line[1]
                part = (part + part * jnp.tanh(part)) * valid_row(index, height)
                put_shifted(shifted, index, part, cols)

        def conv(block):
            total = conv_block(shifted, weight, block, size, cols) + bias
            if added is not None:
                total = total + added[block * size : (block + 1) * size, :].astype(jnp.float32)
            out[block * size : (block + 1) * size, :] = total

        def measure(block):
            if block == 0:
                sums[2] = row_mean(tile_of(out, 0))
            first, square = cell_sums(tiles_of(out, block), sums[2], height)
            sums[0], sums[1] = sums[0] + first, sums[1] + square

        in_turn(count, activate, conv, measure)
        return stats_of(*sums, height, cols)

    clear_rims(shift_one, cols)
    clear_rims(shift_two, cols)
    finish_all(arriving[:8])
    leaving = started(out_sems, (pix, pix_far))
    about = row_mean(tile_of(pix, 0))
    first, square = zero, zero
    for block in range(count):
        more = cell_sums(tiles_of(pix, block), about, height)
        first, square = first + more[0], square + more[1]
    mean_one, inv_one = stats_of(first, square, about, height, cols)
    arriving[8].wait()
    line = half_line(mean_one, inv_one, gain_one, bias_one)
    mean_two, inv_two = stage(pix, line, shift_one, w_one, conv_one, conv_bias_one)
    leaving += started(
        out_sems.at[1:3], (shift_one.at[inner], act_one_far), (conv_one, conv_far)
    )
    arriving[9].wait()
    line = half_line(mean_two, inv_two, gain_two, bias_two, scale, shift)
    mean_three, inv_three = stage(conv_one, line, shift_two, w_two, residual, conv_bias_two, pix)
    leaving += started(
        out_sems.at[3:5], (shift_two.at[inner], act_two_far), (residual, residual_far)
    )
    stats[...] = jnp.concatenate(
        [mean_one, inv_one, mean_two, inv_two, mean_three, inv_three, mean_one, mean_one], axis=0
    )
    leaving += started(out_sems.at[5:6], (stats, stats_far))
    slope = inv_three * gain_three
    start = bias_three - mean_three * slope

    def third(index, carry):
        at = row_at(index, cols)
        act_three[at, :] = (residual[at, :] * slope + start).astype(jnp.bfloat16)
        return carry

    lax.fori_loop(0, rows, third, 0, unroll=True)
    finish_all(leaving)


def attention_kernel(columns, vec, act_three, w_heads, w_out, biases, *refs):
    blocks = refs[:8]
    value_key_far, query_far, grad_far, mixed_far, sums_far = refs[8:13]
    (
        grad_blocks, grad_proj, value_key, query_part, sums,
        query_grad, key_pad, value_pad, heads_t, mixed, mask_row, in_sems, out_sems,
    ) = refs[13:]
    cells, channels = grad_proj.shape
    block_cells = blocks[0].shape[0]
    spot, _, _, height = own_place(vec)
    half = mixed.shape[1] // 2
    cols = columns
    scaling = half**-0.5
    valid_cells = height * cols
    step = 256
    pairs = []
    for index, block in zip(ARRIVAL, blocks):
        base = pl.multiple_of((spot ^ index) * block_cells, block_cells)
        pairs.append((block, grad_blocks.at[pl.ds(base, block_cells), :]))
    arriving = started(in_sems, *pairs)

    sizes = []
    for start in range(0, cells, 512):
        at = slice(start, start + 512)
        parts = dot(act_three[at, :], w_heads[...]) + biases[0:1, :]
        query, key, value = (parts[:, 2 * half * k : 2 * half * (k + 1)] for k in range(3))
        query_grad[at, :] = query.astype(jnp.bfloat16) * jnp.bfloat16(scaling)
        key_pad[at, :] = key.astype(jnp.bfloat16)
        value_pad[at, :] = value.astype(jnp.bfloat16)
        query_size = jnp.sum(query * query, axis=1, keepdims=True) * (scaling * scaling)
        key_size = jnp.sum(key * key, axis=1, keepdims=True)
        sizes.append((jnp.max(query_size), jnp.max(key_size)))
    lane = lax.broadcasted_iota(jnp.int32, (1, cells), 1)
    mask_row[...] = jnp.where(lane < valid_cells, 0.0, MASKED)
    heads_t[...] = jnp.zeros(heads_t.shape, jnp.float32)
    mixed[...] = jnp.zeros(mixed.shape, jnp.bfloat16)
    finish_all(arriving)

    def clean(index, total):
        at = pl.ds(pl.multiple_of(index * block_cells, block_cells), block_cells)
        cell = index * block_cells + lax.broadcasted_iota(jnp.int32, (block_cells, channels), 0)
        kept = jnp.where(cell < valid_cells, grad_blocks[at, :].astype(jnp.float32), 0.0)
        low = kept.astype(jnp.bfloat16)
        grad_proj[at, :] = low
        query_grad[at, :] = query_grad[at, :] + dot(low, w_out[...]).astype(jnp.bfloat16)
        return total + fold(kept)

    start = jnp.zeros((8, channels), jnp.float32)
    total = lax.fori_loop(0, cells // block_cells, clean, start, unroll=True)
    sums[...] = jnp.concatenate([total_of(total), jnp.zeros((7, channels), jnp.float32)], axis=0)
    leaving = started(out_sems, (grad_proj, grad_far), (sums, sums_far))

    def query_block(shifted, index, carry):
        at = pl.ds(pl.multiple_of(index * step, step), step)
        both = query_grad[at, :]
        scores = dot_rows(both, key_pad[...]) + mask_row[...]
        if shifted:
            scores = scores - jnp.max(scores, axis=1, keepdims=True)
        weights = jnp.exp(scores)
        total = jnp.zeros((step, 2 * half), jnp.float32)
        for start in range(0, cells, 2 * half):
            total = total + weights[:, start : start + 2 * half]
        inverse = 1.0 / jnp.sum(total, axis=1, keepdims=True)
        low = weights.astype(jnp.bfloat16)
        out = dot(low, value_pad[...]) * inverse
        wide = both.astype(jnp.float32)
        delta = jnp.sum(wide * out, axis=1, keepdims=True)
        turned = jnp.transpose(wide * inverse).astype(jnp.bfloat16)
        grad_probs = dot_rows(both, value_pad[...])
        grad_scores = (low.astype(jnp.float32) * (grad_probs - delta)).astype(jnp.bfloat16)
        grad_query = dot(grad_scores, key_pad[...]) * (inverse * scaling)
        mixed[at, :] = (out + grad_query).astype(jnp.bfloat16)
        heads_t[0:half, :] += dot(turned[0:half], grad_scores)
        heads_t[half : 2 * half, :] += dot(turned[half : 2 * half], low)
        return carry

    query_most, key_most = (functools.reduce(jnp.maximum, size) for size in zip(*sizes))
    narrow = query_most * key_most <= 3600.0

    @pl.when(narrow)
    def _():
        lax.fori_loop(0, cells // step, functools.partial(query_block, False), 0, unroll=2)

    @pl.when(jnp.logical_not(narrow))
    def _():
        count = (valid_cells + step - 1) // step
        lax.fori_loop(0, count, functools.partial(query_block, True), 0)

    for start in range(0, cells, step):
        value_key[start : start + step, :] = jnp.transpose(heads_t[:, start : start + step]).astype(
            jnp.bfloat16
        )
    query_part[:, 0:half] = mixed[0 : cells // 2, 0:half]
    query_part[:, half : 2 * half] = mixed[cells // 2 : cells, 0:half]
    leaving += started(
        out_sems.at[2:5], (value_key, value_key_far), (query_part, query_far), (mixed, mixed_far)
    )
    finish_all(leaving)


def aside_kernel(vec, *refs):
    act_far, (mixed_far, value_key_far, act_three_far, grad_far) = refs[0:2], refs[2:6]
    own_far, weight_far, sends = refs[6:8], refs[8], refs[9:13]
    acts, mixed, value_key, act_three, grad_proj, padded, own, weight_rows, in_sems, out_sems = (
        refs[13:]
    )
    cells, channels = act_three.shape
    cols = (padded.shape[0] - cells) // 2
    lanes = mixed.shape[1]
    half = lanes // 2
    spot, head, image, _ = own_place(vec)
    arriving = started(
        in_sems,
        (mixed_far, mixed),
        (value_key_far, value_key),
        (act_three_far, act_three),
        (grad_far, grad_proj),
        (act_far[0], acts.at[0]),
        (act_far[1], acts.at[1]),
    )
    block_cells = sends[0].shape[0]
    step = 256
    arriving[0].wait()
    for k, send in enumerate(sends):
        tiles = []
        for part in range(2):
            block = (head ^ k) + HEADS * (image ^ part)
            at = pl.ds(pl.multiple_of(block * block_cells, block_cells), block_cells)
            tiles.append(mixed[at, half:lanes])
        send[...] = jnp.concatenate(tiles, axis=1)
    finish_all(arriving[1:4])

    def gather(index, totals):
        at = pl.ds(pl.multiple_of(index * step, step), step)
        low_mixed, low_heads, act = mixed[at, :], value_key[at, :], act_three[at, :]
        mixed_t = jnp.transpose(low_mixed.astype(jnp.float32)).astype(jnp.bfloat16)
        heads_t = jnp.transpose(low_heads.astype(jnp.float32)).astype(jnp.bfloat16)
        return (
            totals[0] + dot(mixed_t, act),
            totals[1] + dot(heads_t, act),
            totals[2] + dot(mixed_t, grad_proj[at, :]),
            totals[3] + fold(low_mixed.astype(jnp.float32)),
            totals[4] + fold(low_heads.astype(jnp.float32)),
        )

    square = jnp.zeros((lanes, channels), jnp.float32)
    line = jnp.zeros((8, lanes), jnp.float32)
    from_query, from_heads, from_out, query_sum, value_sum = lax.fori_loop(
        0, cells // step, gather, (square, square, square, line, line)
    )
    unit = half // 4
    parts = (from_query[0:half], from_heads[0:half], from_heads[half:lanes], from_out[half:lanes])
    for chunk in range(4):
        for k, part in enumerate(parts):
            piece = part[chunk * unit : (chunk + 1) * unit].astype(jnp.bfloat16)
            weight_rows[chunk, k * unit : (k + 1) * unit, :] = piece
    weight_rows[:, half:, :] = jnp.zeros((4, 16, channels), jnp.bfloat16)
    which = lax.axis_index("img") * 2 + image
    lane = lax.broadcasted_iota(jnp.int32, (1, channels), 1)
    now = jnp.max(vec[12:13, :]).astype(jnp.int32)
    high = jnp.where(lane == which, (now // 32).astype(jnp.float32), 0.0)
    rest = jnp.where(lane == which, (now % 32).astype(jnp.float32), 0.0)
    row = jnp.concatenate([total_of(query_sum), total_of(value_sum)], axis=1)
    below = jnp.zeros((13, channels), jnp.float32)
    weight_rows[2, half:, :] = jnp.concatenate([row, high, rest, below], axis=0).astype(
        jnp.bfloat16
    )
    source = lax.broadcasted_iota(jnp.int32, (channels, 3 * half), 0)
    target = lax.broadcasted_iota(jnp.int32, (channels, 3 * half), 1)
    chosen = jnp.where(source == head * half + target % half, 1.0, 0.0).astype(jnp.bfloat16)
    lane = lax.broadcasted_iota(jnp.int32, (step, 3 * half), 1)
    column = lax.broadcasted_iota(jnp.int32, (step, 3 * half), 0) % cols
    leaving = started(out_sems.at[2:3], (weight_rows, weight_far))
    for k in range(2):
        arriving[4 + k].wait()
        clear_rims(padded, cols)

        def widen(index, carry):
            at = pl.ds(pl.multiple_of(index * step, step), step)
            tile = dot(acts[k, at, :], chosen)
            before = jnp.where(column == 0, 0.0, pltpu.roll(tile, 1, 0))
            after = jnp.where(column == cols - 1, 0.0, pltpu.roll(tile, step - 1, 0))
            tile = jnp.where(lane < half, before, jnp.where(lane < 2 * half, tile, after))
            padded[pl.ds(pl.multiple_of(index * step + cols, cols), step), :] = tile
            return carry

        lax.fori_loop(0, cells // step, widen, 0)
        for tap in range(3):

            def turn(index, carry):
                at = pl.ds(pl.multiple_of(index * step + tap * cols, cols), step)
                to = pl.ds(pl.multiple_of(index * step, step), step)
                own[k, tap, :, to] = jnp.transpose(padded[at, :]).astype(jnp.bfloat16)
                return carry

            lax.fori_loop(0, cells // step, turn, 0)
        leaving += started(out_sems.at[k : k + 1], (own.at[k], own_far[k]))
    finish_all(leaving)


def middle_kernel(vec, qkv_t, *refs):
    heads_far = (refs[4], refs[0], refs[6], refs[2])
    sides_far = (refs[5], refs[1], refs[7], refs[3])
    grad_far, residual_far, stats_far, own_two_far, rows_far = refs[8:13]
    weight_far, conv_far, own_one_far, out_sums_far = refs[13:17]
    shifted_one, grad_res_far, payload_far = refs[17], refs[18], refs[19:23]
    (
        heads, sides, grad_proj, residual, stats, own_two, grad_res, payload, grad_act, shifted,
        weight, conv_one, own_one, out_sums, in_sems, out_sems,
    ) = refs[23:]
    cells, channels = grad_proj.shape
    cols = (shifted.shape[0] - cells) // 2
    rows = cells // cols
    _, head, image, height = own_place(vec)
    column = lax.axis_index("img")
    width = channels // GROUPS
    count = (height * (cols * width)).astype(jnp.float32)
    half = qkv_t.shape[1]
    unit = half // 4
    small_at = 18 * unit + half
    pairs = [(far, heads.at[head ^ k]) for k, far in enumerate(heads_far)]
    pairs += [(far, sides.at[head ^ k]) for k, far in enumerate(sides_far)]
    arriving = started(
        in_sems,
        *pairs,
        (stats_far, stats),
        (residual_far, residual),
        (grad_far, grad_proj),
        (own_two_far, own_two),
        (rows_far.at[:, pl.ds(0, half), :], payload.at[:, pl.ds(9 * unit, half), :]),
        (rows_far.at[:, pl.ds(half, 16), :], payload.at[:, pl.ds(small_at, 16), :]),
        (weight_far, weight),
        (conv_far, conv_one),
        (own_one_far, own_one),
        (out_sums_far, out_sums),
    )
    finish_all(arriving[:10])
    zeros = jnp.zeros((half, channels), jnp.bfloat16)
    halfway = cells // 2
    step = 512
    pairs = ((0, 1), (2, 3))
    w_main = []
    for a, b in pairs:
        order = [HEADS + a, 2 * HEADS + a, HEADS + b, 2 * HEADS + b]
        w_main.append(jnp.concatenate([qkv_t[k] for k in order], axis=0))
    mean, inverse = stats[4:5, :], stats[5:6, :]
    gain = vec[8:9, :]
    zero = jnp.zeros((8, channels), jnp.float32)
    plain, cross = zero, zero

    def normed(index):
        return (residual[index * cols : (index + 1) * cols, :] - mean) * inverse

    for part in range(2):
        w_side = []
        for a, b in pairs:
            left, right = qkv_t[a], qkv_t[b]
            order = [left, zeros, right, zeros] if part == 0 else [zeros, left, zeros, right]
            w_side.append(jnp.concatenate(order, axis=0))
        for base in range(0, halfway, step):
            start = part * halfway + base
            total = None
            for k, (a, b) in enumerate(pairs):
                main = jnp.concatenate(
                    [heads[a][start : start + step, :], heads[b][start : start + step, :]], axis=1
                )
                side = jnp.concatenate(
                    [sides[a][base : base + step, :], sides[b][base : base + step, :]], axis=1
                )
                term = dot(main, w_main[k]) + dot(side, w_side[k])
                total = term if total is None else total + term
            grad_act[start : start + step, :] = total
            for index in range(start // cols, (start + step) // cols):
                tile = total[index * cols - start : (index + 1) * cols - start]
                plain = plain + fold(tile)
                cross = cross + fold(tile * normed(index))
    plain, cross = total_of(plain), total_of(cross)
    mean_plain = group_sums(plain * gain, width) / count
    mean_cross = group_sums(cross * gain, width) / count
    clear_rims(shifted, cols)
    clear_rims(shifted_one, cols)
    finish_all(arriving[10:16])
    group = 4
    size = group * cols
    steps = rows // group
    totals = [zero, zero, zero, zero]
    one, two = gain * inverse, mean_cross * inverse * inverse
    three = (mean_plain - mean * inverse * mean_cross) * inverse
    gain_two, bias_two, scale, shift = (vec[k : k + 1, :] for k in range(3, 7))
    mean_two, inverse_two = stats[2:3, :], stats[3:4, :]
    line = half_line(mean_two, inverse_two, gain_two, bias_two, scale, shift)
    begin_two = mean_two * inverse_two

    def tiles(block):
        for index in range(block * group, (block + 1) * group):
            yield index, slice(index * cols, (index + 1) * cols)

    def through_three(block):
        for index, at in tiles(block):
            inner = grad_act[at, :] * one - residual[at, :] * two - three
            grad = grad_proj[at, :].astype(jnp.float32) + inner * valid_row(index, height)
            grad_res[at, :] = grad
            put_shifted(shifted, index, grad, cols)
            totals[0] = totals[0] + fold(grad)

    def conv_back(block):
        grad_act[block * size : (block + 1) * size, :] = conv_block(
            shifted, weight, block, size, cols
        )

    def through_act(block):
        for index, at in tiles(block):
            value = conv_one[at, :]
            unit_value = value * inverse_two - begin_two
            part = value * line[0] + line[1]
            sigmoid = 0.5 + 0.5 * jnp.tanh(part)
            slope = sigmoid + 2.0 * part * sigmoid * (1.0 - sigmoid)
            grad = grad_act[at, :] * valid_row(index, height) * slope
            grad_act[at, :] = grad
            totals[1] = totals[1] + fold(grad)
            totals[2] = totals[2] + fold(grad * unit_value)

    in_turn(steps, through_three, conv_back, through_act)
    total = total_of(totals[0])
    three_lines = [cross, plain, total]
    leaving = started(out_sems, (grad_res, grad_res_far))
    plain, cross = total_of(totals[1]), total_of(totals[2])
    gain, bias = gain_two, bias_two
    factor = gain * scale
    mean_plain = group_sums(plain * factor, width) / count
    mean_cross = group_sums(cross * factor, width) / count
    one, two = factor * inverse_two, mean_cross * inverse_two * inverse_two
    three = (mean_plain - begin_two * mean_cross) * inverse_two
    finish_all(arriving[16:])
    parts = [[None] * 3, [None] * 3]

    def through_two(block):
        for index, at in tiles(block):
            grad = grad_act[at, :] * one - conv_one[at, :] * two - three
            grad = grad * valid_row(index, height)
            put_shifted(shifted_one, index, grad, cols)
            totals[3] = totals[3] + fold(grad)

    def weigh(block):
        at = slice(block * size, (block + 1) * size)
        inner = slice(cols + block * size, cols + (block + 1) * size)
        for k, (own, moved) in enumerate(((own_two, shifted), (own_one, shifted_one))):
            grad = moved[inner, channels : 2 * channels]
            for tap in range(3):
                part = dot(own[tap, :, at], grad)
                parts[k][tap] = part if block == 0 else parts[k][tap] + part

    in_turn(steps, through_two, weigh, lambda block: None)
    put_quarter(parts[0], payload, 0)
    put_quarter(parts[1], payload, 9 * unit + half)
    total = total_of(totals[3])
    lines = [
        *three_lines, out_sums[0:1, :], cross * scale, plain * scale, total,
        jnp.zeros((9, channels), jnp.float32),
    ]
    mine = 2 * (column * 2 + image)
    place = lax.broadcasted_iota(jnp.int32, (16, channels), 0)
    both = jnp.where(place == mine, gain * cross + bias * plain, 0.0)
    payload[0, small_at:, :] = jnp.concatenate(lines, axis=0).astype(jnp.bfloat16)
    payload[1, small_at:, :] = jnp.where(place == mine + 1, plain, both).astype(jnp.bfloat16)
    leaving += started(
        out_sems.at[1:5],
        *[(payload.at[column ^ k], far) for k, far in enumerate(payload_far)],
    )
    finish_all(leaving)


def first_kernel(vec, shifted, weight_far, pix_far, grad_far, stats_far, *refs):
    out_own_far, out_away_far, sums_far = refs[:3]
    weight, pix, grad_res, stats, out, sums, grad_act, in_sems, out_sems = refs[3:]
    cells, channels = pix.shape
    block_cells = out.shape[1]
    cols = (shifted.shape[0] - cells) // 2
    rows = cells // cols
    spot, _, _, height = own_place(vec)
    width = channels // GROUPS
    count = (height * (cols * width)).astype(jnp.float32)
    arriving = started(
        in_sems,
        (weight_far, weight),
        (stats_far, stats),
        (pix_far, pix),
        (grad_far, grad_res),
    )
    gain, bias = vec[0:1, :], vec[1:2, :]
    zero = jnp.zeros((8, channels), jnp.float32)
    arriving[0].wait()
    conv_shifted(shifted, weight, grad_act, 0.0, cols)
    finish_all(arriving[1:])
    mean, inverse = stats[0:1, :], stats[1:2, :]
    line = half_line(mean, inverse, gain, bias)
    begin = mean * inverse

    def normed(at):
        return pix[at, :].astype(jnp.float32) * inverse - begin

    def add(index, totals):
        at = row_at(index, cols)
        value = pix[at, :].astype(jnp.float32)
        unit = value * inverse - begin
        part = value * line[0] + line[1]
        sigmoid = 0.5 + 0.5 * jnp.tanh(part)
        slope = sigmoid + 2.0 * part * sigmoid * (1.0 - sigmoid)
        grad = grad_act[at, :] * valid_row(index, height) * slope
        grad_act[at, :] = grad
        return totals[0] + fold(grad), totals[1] + fold(grad * unit)

    plain, cross = lax.fori_loop(0, rows, add, (zero, zero), unroll=2)
    plain, cross = total_of(plain), total_of(cross)
    mean_plain = group_sums(plain * gain, width) / count
    mean_cross = group_sums(cross * gain, width) / count
    block_rows = block_cells // cols
    for part in range(2):
        first_row = (spot ^ (4 * part)) * block_rows
        for line in range(block_rows):
            at = row_at(first_row + line, cols)
            grad = (grad_act[at, :] * gain - mean_plain - normed(at) * mean_cross) * inverse
            grad = grad_res[at, :] + grad * valid_row(first_row + line, height)
            out[part, line * cols : (line + 1) * cols, :] = grad.astype(jnp.bfloat16)
    sums[...] = jnp.concatenate([cross, plain, jnp.zeros((6, channels), jnp.float32)], axis=0)
    finish_all(
        started(
            out_sems, (out.at[0], out_own_far), (out.at[1], out_away_far), (sums, sums_far)
        )
    )


def block_kernel(columns, vec, w_out, *refs):
    heads, residual_far = refs[:4], refs[4]
    out_own, out_away, residual, in_sems = refs[5:]
    block_cells, channels = out_own.shape
    spot, head, _, height = own_place(vec)
    cols = columns
    bases = [
        pl.multiple_of((spot ^ (4 * part)) * block_cells, block_cells) for part in range(2)
    ]
    pairs = [
        (residual_far.at[pl.ds(base, block_cells), :], residual.at[part])
        for part, base in enumerate(bases)
    ]
    finish_all(started(in_sems, *pairs))
    for part, out in enumerate((out_own, out_away)):
        total = residual[part] + vec[10:11, :]
        for step in range(4):
            width = w_out.shape[1]
            tile = heads[step][:, part * width : (part + 1) * width]
            total = total + dot(tile, w_out[head ^ step])
        cell = bases[part] + lax.broadcasted_iota(jnp.int32, (block_cells, channels), 0)
        out[...] = jnp.where(cell < height * cols, total, 0.0).astype(jnp.bfloat16)


def prepare_kernel(*refs):
    shifts, lines_far, kernels_far = refs[0], refs[1:15], refs[15:17]
    vec, w_heads, w_out, biases, qkv_t = refs[17:22]
    backs_far = refs[22:24]
    kernels, backs, qkv_weight, out_weight, heights, timesteps, qv_bias, *lines = refs[24:40]
    line_sems, in_sems, out_sems = refs[40:]
    channels = out_weight.shape[0]
    half = channels // HEADS
    small = started(
        line_sems,
        *zip(lines_far, (*lines, qv_bias, qkv_weight, out_weight, heights, timesteps)),
    )
    arriving = started(
        in_sems, *[(far, kernels.at[k]) for k, far in enumerate(kernels_far)]
    )
    finish_all(small)
    spot = lax.axis_index("row")
    image, head = spot // HEADS, spot % HEADS
    shift_row = shifts[pl.ds(image, 1), :]
    order = list(range(5)) + [None, None] + list(range(5, 9))
    for line, k in enumerate(order):
        if k is not None:
            vec[line : line + 1, :] = lines[k][...].astype(jnp.float32).reshape(1, channels)
    vec[5:6, :] = 1.0 + shift_row[:, :channels]
    vec[6:7, :] = shift_row[:, channels:]
    vec[11:12, :] = jnp.full((1, channels), heights[image].astype(jnp.float32))
    vec[12:13, :] = jnp.full((1, channels), timesteps[image].astype(jnp.float32))
    vec[13:16, :] = jnp.zeros((3, channels), jnp.float32)
    source = lax.broadcasted_iota(jnp.int32, (channels, 2 * half), 0)
    lane = lax.broadcasted_iota(jnp.int32, (channels, 2 * half), 1)
    first = jnp.where((lane < half) & (source == head * half + lane), 1.0, 0.0)
    second = jnp.where((lane >= half) & (source == head * half + lane - half), 1.0, 0.0)
    first, second = first.astype(jnp.bfloat16), second.astype(jnp.bfloat16)
    lanes = 2 * half
    for part, taken in enumerate((first, first, second)):
        whole = qkv_weight[:, part * channels : (part + 1) * channels]
        w_heads[:, part * lanes : (part + 1) * lanes] = dot(whole, taken).astype(jnp.bfloat16)
    turned = jnp.transpose(out_weight[...].astype(jnp.float32)).astype(jnp.bfloat16)
    w_out[...] = dot(turned, second).astype(jnp.bfloat16)
    both = qv_bias[...].astype(jnp.float32).reshape(1, 2 * channels)
    wide = jnp.broadcast_to(both, (16, 2 * channels)).astype(jnp.bfloat16)
    biases[:, 0:lanes] = dot(wide[:, :channels], first)[0:8]
    biases[:, lanes : 2 * lanes] = jnp.zeros((8, lanes), jnp.float32)
    biases[:, 2 * lanes : 3 * lanes] = dot(wide[:, channels:], second)[0:8]
    for block in range(0, 3 * HEADS, 2):
        whole = qkv_weight[:, block // 2 * lanes : (block // 2 + 1) * lanes].astype(jnp.float32)
        whole = jnp.transpose(whole).astype(jnp.bfloat16)
        qkv_t[block] = whole[0:half]
        qkv_t[block + 1] = whole[half:lanes]
    leaving = []
    for k in range(2):
        arriving[k].wait()

        def turn(tap, carry):
            tile = kernels[k, 2 - tap // 3, 2 - tap % 3].astype(jnp.float32)
            at = pl.ds(pl.multiple_of(tap % 3 * channels, channels), channels)
            backs[k, tap // 3, at, :] = jnp.transpose(tile).astype(jnp.bfloat16)
            return carry

        lax.fori_loop(0, 9, turn, 0)
        leaving += started(out_sems.at[k : k + 1], (backs.at[k], backs_far[k]))
    finish_all(leaving)


def final_kernel(*refs):
    parts, begins, frequency = refs[:8], refs[8:12], refs[12]
    one_far, two_far, qkv_far, out_far, time_far = refs[13:18]
    bias_out, time_bias, rows = refs[18], refs[19], refs[20:29]
    one, two, qkv_rows, qkv_out, out_out, time_out, small, norm_one, sems, out_sems = refs[29:]
    channels = one.shape[1]
    half = channels // HEADS
    unit = half // 4
    lines = 10 * unit + half + 16
    spot = lax.axis_index("row")
    head, column = spot % HEADS, lax.axis_index("img")
    leaving = []
    for index, part in enumerate(parts):
        away = column ^ (index // 2)
        for pair in range(2):
            quarter, base = head ^ (index % 2 + 2 * pair), pair * lines
            first = pl.multiple_of(quarter * half + away * unit, unit)
            at = pl.ds(first, unit)
            shape = (9, unit, channels)
            late = base + unit + half
            begin = begins[2 * pair + index % 2][8 * unit * (index // 2) : 8 * unit * (index // 2 + 1)]
            two[0:8, at, :] = begin.astype(jnp.float32).reshape((8, unit, channels))
            two[8, at, :] = part[base : base + unit].astype(jnp.float32)
            one[:, at, :] = part[late : late + 9 * unit].astype(jnp.float32).reshape(shape)
            here = len(leaving)
            leaving += started(
                sems.at[here : here + 2],
                (two.at[:, at, :], two_far.at[:, at, :]),
                (one.at[:, at, :], one_far.at[:, at, :]),
            )
            middle = base + unit
            for k in range(3):
                to = pl.ds(pl.multiple_of(first + k * channels, unit), unit)
                piece = part[middle + k * unit : middle + (k + 1) * unit]
                qkv_rows[to, :] = piece.astype(jnp.float32)
            out_out[at, :] = part[middle + 3 * unit : middle + half].astype(jnp.float32)
            small[quarter, away] = part[base + lines - 16 : base + lines].astype(jnp.float32)
    for part in range(3):
        across = slice(part * channels, (part + 1) * channels)
        qkv_out[:, across] = jnp.transpose(qkv_rows[across, :])
    leaving += started(out_sems, (qkv_out, qkv_far), (out_out, out_far))
    sums = [small[quarter, 2] for quarter in range(HEADS)]
    pieces = [part[0:1, :half] for part in sums] + [part[0:1, 3 * half :] for part in sums]
    bias_out[...] = jnp.concatenate(pieces, axis=1).reshape(bias_out.shape)
    for step in range(4):
        norm_one[column ^ step] = parts[2 * step][2 * lines : 2 * lines + 16].astype(jnp.float32)
    total = norm_one[0] + norm_one[1] + norm_one[2] + norm_one[3]
    whole = jnp.concatenate([total[0:2], small[0, 0, 0:7, :]], axis=0)
    for k, row in enumerate(rows):
        row[...] = whole[k : k + 1].reshape(row.shape)
    shifts = small[0, 1]
    pair = jnp.concatenate([shifts[k : k + 1, :] for k in range(0, 16, 2)], axis=0)
    other = jnp.concatenate([shifts[k : k + 1, :] for k in range(1, 16, 2)], axis=0)
    both = jnp.concatenate([pair, other], axis=1)
    time_bias[...] = total_of(both).reshape(time_bias.shape)
    steps = sums[0][1:2, :] * 32.0 + sums[0][2:3, :]
    image = lax.broadcasted_iota(jnp.int32, (8, steps.shape[1]), 0)
    lane = lax.broadcasted_iota(jnp.int32, (8, steps.shape[1]), 1)
    now = jnp.sum(jnp.where(image == lane, steps, 0.0), axis=1, keepdims=True)
    angles = now * frequency[...]
    left = jnp.concatenate([jnp.cos(angles), jnp.sin(angles)], axis=1)
    left = left / (1.0 + jnp.exp(-left))
    terms = []
    for _ in range(3):
        terms.append(left.astype(jnp.bfloat16).astype(jnp.float32))
        left = left - terms[-1]
    terms = jnp.concatenate(terms + [jnp.zeros_like(left)], axis=0)
    both = jnp.concatenate([both] * 3 + [jnp.zeros_like(both)], axis=0).astype(jnp.bfloat16)
    time_out[...] = lax.dot_general(
        terms.astype(jnp.bfloat16), both, (((0,), (0,)), ((), ())),
        preferred_element_type=jnp.float32,
    )
    leaving += started(out_sems.at[2:3], (time_out, time_far))
    finish_all(leaving)


def swap(value, axis, step):
    count = lax.axis_size(axis)
    return lax.ppermute(value, axis, [(k, k ^ step) for k in range(count)])


def pick(stacked, index):
    return lax.dynamic_index_in_dim(stacked, index, 0, keepdims=False)


def add_up(*parts):
    total = parts[0].astype(jnp.float32)
    for part in parts[1:]:
        total = total + part.astype(jnp.float32)
    return total.astype(jnp.bfloat16)


def from_columns(pair):
    return [pair] + [swap(pair, "img", step) for step in (1, 2, 3)]


def with_mates(columns):
    return [part for mine in columns for part in (mine, swap(mine, "row", 1))]


def gather_columns(pair):
    return with_mates(from_columns(pair))


def call(kernel, near_outs, far_outs, scratch, limit, work, scalars, near, far, last_outs=()):
    close = pl.BlockSpec(memory_space=pltpu.VMEM)
    distant = pl.BlockSpec(memory_space=pltpu.HBM)
    operands = list(near) + [pltpu.with_memory_space_constraint(array, pltpu.HBM) for array in far]
    moved = sum(array.size * array.dtype.itemsize for array in operands)
    return pl.pallas_call(
        kernel,
        out_shape=[jax.ShapeDtypeStruct(*kind) for kind in near_outs]
        + [pltpu.HBM(*kind) for kind in far_outs]
        + [jax.ShapeDtypeStruct(*kind) for kind in last_outs],
        in_specs=[pl.BlockSpec(memory_space=pltpu.SMEM)] * len(scalars)
        + [close] * len(near)
        + [distant] * len(far),
        out_specs=[close] * len(near_outs)
        + [distant] * len(far_outs)
        + [close] * len(last_outs),
        scratch_shapes=[pltpu.VMEM(*kind) if isinstance(kind, tuple) else kind for kind in scratch],
        compiler_params=mib(limit),
        cost_estimate=pl.CostEstimate(flops=work, bytes_accessed=moved, transcendentals=0),
    )(*scalars, *operands)


def sems(count):
    return pltpu.SemaphoreType.DMA((count,))


def gather_field(mine, theirs):
    far, far_near = swap(theirs, "row", 4), swap(theirs, "row", 6)
    return [mine, swap(mine, "row", 1), swap(mine, "row", 2), None, far, None, far_near, None]


def relayed(blocks, after=None):
    sent = [blocks[2], blocks[4], blocks[6]]
    if after is not None:
        sent = lax.optimization_barrier((*sent, after))[:3]
    odd = [swap(block, "row", 1) for block in sent]
    return odd, [blocks[step] for step in ARRIVAL[3:]]


def local_image(
    pixels,
    heights,
    timesteps,
    norm1_gain,
    norm1_bias,
    conv1_weight,
    conv1_bias,
    time_weight,
    time_bias,
    norm2_gain,
    norm2_bias,
    conv2_weight,
    conv2_bias,
    norm3_gain,
    norm3_bias,
    qkv_weight,
    qv_bias,
    out_weight,
    out_bias,
    grad_out,
):
    images, row_count, cols, channels = pixels.shape
    block_cells = row_count * cols
    cells = block_cells * lax.axis_size("row")
    half = channels // HEADS
    column = lax.axis_index("img")
    image = lax.axis_index("row") // HEADS
    low, full = jnp.bfloat16, jnp.float32
    pixel_blocks = pixels.reshape(images, block_cells, channels)
    grad_blocks = grad_out.reshape(images, block_cells, channels)
    field = gather_field(pick(pixel_blocks, image), pick(pixel_blocks, 1 - image))
    later = (pick(grad_blocks, image), pick(grad_blocks, 1 - image), field[4], field[6])
    later = lax.optimization_barrier(later)
    grads = gather_field(later[0], later[1])
    field[4], field[6] = later[2], later[3]
    time_act = jax.nn.silu(embed_steps(timesteps, time_weight.shape[0]))
    shifts = jnp.dot(time_act, time_weight.astype(full), precision=PRECISE) + time_bias.astype(full)
    kernel_shape = (3, 3 * channels, channels)
    lanes = 2 * half
    vec, w_heads, w_out, biases, qkv_t, w_one_back, w_two_back = call(
        prepare_kernel,
        [
            ((16, channels), full), ((channels, 3 * lanes), low), ((channels, lanes), low),
            ((8, 3 * lanes), full), ((3 * HEADS, half, channels), low),
        ],
        [(kernel_shape, low), (kernel_shape, low)],
        [
            ((2, 3, 3, channels, channels), low), ((2,) + kernel_shape, low),
            ((channels, 3 * channels), low), ((channels, channels), low),
            pltpu.SMEM((images,), jnp.int32), pltpu.SMEM((images,), jnp.int32),
            ((2 * channels,), low), *[((channels,), low)] * 9,
            sems(14), sems(2), sems(2),
        ],
        16,
        channels,
        [],
        [shifts],
        [
            norm1_gain, norm1_bias, conv1_bias, norm2_gain, norm2_bias, conv2_bias, norm3_gain,
            norm3_bias, out_bias, qv_bias, qkv_weight, out_weight, heights, timesteps,
            conv1_weight,
            conv2_weight,
        ],
    )
    field_late, field = relayed(field, vec)
    w_one, w_two = conv1_weight.reshape(kernel_shape), conv2_weight.reshape(kernel_shape)
    rim_cells = cells + 2 * cols
    cost = 9 * cells * channels * channels // 2

    wide, tall = (cells, channels), (rim_cells, 3 * channels)
    rows_eight = ((8, channels), full)
    act_three, pix, conv_one, residual, act_one, act_two, stats = call(
        forward_kernel,
        [(wide, low)],
        [(wide, low), (wide, full), (wide, full), (wide, low), (wide, low), rows_eight],
        [
            (wide, low), (wide, full), (wide, full), rows_eight, (kernel_shape, low),
            (kernel_shape, low), (tall, low), (tall, low), sems(10), sems(6),
        ],
        28,
        cost * 25,
        [],
        [vec, *field_late],
        [*field, w_one, w_two],
    )
    grads_late, grads = relayed(grads, act_three)
    query_shape, head_shape = (cells // 2, lanes), (cells, lanes)
    value_key, query_part, grad_proj, mixed, out_sums = call(
        functools.partial(attention_kernel, cols),
        [],
        [(head_shape, low), (query_shape, low), (wide, low), (head_shape, low), rows_eight],
        [
            (wide, low), (wide, low), (head_shape, low), (query_shape, low), rows_eight,
            (head_shape, low), (head_shape, low), (head_shape, low), ((lanes, cells), full),
            (head_shape, low), ((1, cells), full), sems(8), sems(5),
        ],
        36,
        cost * 34,
        [],
        [vec, act_three, w_heads, w_out, biases, *grads_late],
        grads,
    )

    key_near, query_near = swap(value_key, "row", 2), swap(query_part, "row", 2)
    key_mate, query_mate = swap(value_key, "row", 1), swap(query_part, "row", 1)
    own_shape = (3, 3 * half, cells)
    send_shape = ((block_cells, lanes), low)
    own_one, own_two, weight_rows, *sends = call(
        aside_kernel,
        [],
        [(own_shape, low), (own_shape, low), ((4, half + 16, channels), low)],
        [
            ((2,) + wide, low), (head_shape, low), (head_shape, low), (wide, low), (wide, low),
            ((rim_cells, 3 * half), full), ((2,) + own_shape, low), ((4, half + 16, channels), low),
            sems(6), sems(3),
        ],
        28,
        cost * 27,
        [],
        [vec],
        [act_one, act_two, mixed, value_key, act_three, grad_proj],
        [send_shape] * 4,
    )
    key_near, query_near, key_mate, query_mate, own_two = lax.optimization_barrier(
        (key_near, query_near, key_mate, query_mate, own_two)
    )
    relays = [key_mate, query_mate, swap(key_near, "row", 1), swap(query_near, "row", 1)]
    packed = [value_key, query_part, key_near, query_near]
    lines = 18 * (half // 4) + half + 16
    shifted_one, grad_res, *payload = call(
        middle_kernel,
        [(tall, low)],
        [(wide, full)] + [((lines, channels), low)] * 4,
        [
            ((HEADS,) + head_shape, low), ((HEADS,) + query_shape, low),
            (wide, low), (wide, full), rows_eight, (own_shape, low), (wide, full),
            ((4, lines, channels), low), (wide, full), (tall, low), (kernel_shape, low),
            (wide, full), (own_shape, low), rows_eight, sems(18), sems(5),
        ],
        40,
        cost * 26,
        [],
        [vec, qkv_t, *relays],
        [
            *packed, grad_proj, residual, stats, own_two, weight_rows, w_two_back, conv_one,
            own_one, out_sums,
        ],
    )
    *sends, shifted_one = lax.optimization_barrier((*sends, shifted_one))
    total = add_up(payload[0], *[swap(payload[step], "img", step) for step in (1, 2, 3)])
    heads_got = [sends[0]] + [swap(sends[step], "row", step) for step in (1, 2, 3)]
    shifted_one, total, *heads_got = lax.optimization_barrier((shifted_one, total, *heads_got))
    received = swap(total, "row", 4)
    grad_own, grad_away, sums_one = call(
        first_kernel,
        [],
        [((block_cells, channels), low), ((block_cells, channels), low), rows_eight],
        [
            (kernel_shape, low), (wide, low), (wide, full), rows_eight,
            ((2, block_cells, channels), low), rows_eight, (wide, full), sems(4), sems(3),
        ],
        20,
        cost * 12,
        [],
        [vec, shifted_one],
        [w_one_back, pix, grad_res, stats],
    )
    block_own, block_away = call(
        functools.partial(block_kernel, cols),
        [((block_cells, channels), low), ((block_cells, channels), low)],
        [],
        [((2, block_cells, channels), full), sems(2)],
        8,
        cost,
        [],
        [vec, out_weight.reshape(HEADS, half, channels), *heads_got],
        [residual],
    )
    received, sums_one, block_away = lax.optimization_barrier((received, sums_one, block_away))
    both = add_up(total, received)
    norm_one = jnp.concatenate([sums_one, jnp.zeros_like(sums_one)], axis=0).astype(low)
    norm_one = add_up(norm_one, swap(norm_one, "row", 4))
    other = swap(both[8 * (half // 4) :], "row", 2)
    begin = 8 * (half // 4)
    first = from_columns(both[:begin])
    block_away, grad_away, *first[1:] = lax.optimization_barrier(
        (block_away, grad_away, *first[1:])
    )
    out_pair = jnp.stack([block_own, grad_own])
    away_pair = swap(jnp.stack([block_away, grad_away]), "row", 4)
    first = jnp.concatenate(first, axis=0)
    beside = swap(first, "row", 2)
    pair = jnp.concatenate([both[begin:], other, norm_one], axis=0)
    columns = from_columns(pair)
    away_pair, *columns[1:] = lax.optimization_barrier((away_pair, *columns[1:]))
    first_pair = jnp.where(image == 0, out_pair, away_pair)
    second_pair = jnp.where(image == 0, away_pair, out_pair)
    finished = jnp.stack([first_pair, second_pair], axis=1).reshape((2,) + pixels.shape)
    columns[1], first, beside = lax.optimization_barrier((columns[1], first, beside))
    parts = with_mates(columns) + with_mates([first, beside])
    line = ((channels,), full)
    kernel_out = ((9, channels, channels), full)
    time_out = ((time_weight.shape[0], 2 * channels), full)
    qkv_out, out_out = ((channels, 3 * channels), full), ((channels, channels), full)
    half_time = time_weight.shape[0] // 2
    frequency = jnp.exp(-math.log(10000.0) * jnp.arange(half_time, dtype=full) / half_time)
    (
        conv1_weight_grad, conv2_weight_grad, qkv_weight_grad, out_weight_grad, time_weight_grad,
        qv_bias_grad, time_bias_grad, *lines,
    ) = call(
        final_kernel,
        [],
        [kernel_out, kernel_out, qkv_out, out_out, time_out],
        [
            kernel_out, kernel_out, ((3 * channels, channels), full), qkv_out, out_out, time_out,
            ((HEADS, 4, 16, channels), full), ((4, 16, channels), full), sems(32), sems(3),
        ],
        28,
        cost,
        [],
        [*parts, frequency[None, :]],
        [],
        [((2 * channels,), full)] * 2 + [line] * 9,
    )
    norm1_gain_grad, norm1_bias_grad, norm3_gain_grad, norm3_bias_grad, conv2_bias_grad = lines[:5]
    out_bias_grad, norm2_gain_grad, norm2_bias_grad, conv1_bias_grad = lines[5:]
    return (
        finished[0],
        finished[1],
        norm1_gain_grad,
        norm1_bias_grad,
        conv1_weight_grad.reshape(conv1_weight.shape),
        conv1_bias_grad,
        time_weight_grad,
        time_bias_grad,
        norm2_gain_grad,
        norm2_bias_grad,
        conv2_weight_grad.reshape(conv2_weight.shape),
        conv2_bias_grad,
        norm3_gain_grad,
        norm3_bias_grad,
        qkv_weight_grad,
        qv_bias_grad,
        out_weight_grad,
        out_bias_grad,
    )


def local(*arrays):
    pixels = arrays[0]
    if lax.axis_size("row") == pixels.shape[0] * HEADS and lax.axis_size("img") == 4:
        return local_image(*arrays)
    return local_rows(*arrays)


def solution(mesh):
    placed = (
        P("img", "row", None, None),
        P("img"),
        P("img"),
        P(),
        P(),
        P(),
        P(),
        P(),
        P(),
        P(),
        P(),
        P(),
        P(),
        P(),
        P(),
        P(),
        P(),
        P(),
        P(),
        P("img", "row", None, None),
    )
    return jax.shard_map(
        local,
        mesh=mesh,
        in_specs=placed,
        out_specs=(
            P("img", "row", None, None),
            P("img", "row", None, None),
            P(),
            P(),
            P(),
            P(),
            P(),
            P(),
            P(),
            P(),
            P(),
            P(),
            P(),
            P(),
            P(),
            P(),
            P(),
            P(),
        ),
        check_vma=False,
    )
```
